32 devices in a mesh: dp: 8 (over z, x), seq: 4 (over y, core).
Axes of the slice: x: 2, y: 2, z: 4, core: 2. Of those that a mesh axis runs over, the one named last changes fastest.
Arguments:
- short_in: bfloat16 [2, 32, 256, 768], P(None, 'dp', 'seq'), may hold values from -6 to 6
- long_in: bfloat16 [2, 16, 512, 768], P(None, 'dp', 'seq'), may hold values from -6 to 6
- short_cot: bfloat16 [2, 32, 256, 768], P(None, 'dp', 'seq'), may hold values from -6 to 6
- long_cot: bfloat16 [2, 16, 512, 768], P(None, 'dp', 'seq'), may hold values from -6 to 6
- short_len: int32 [2, 8, 4], P(None, 'dp'), may hold values from 0 to 256, as said below
- long_len: int32 [2, 8, 2], P(None, 'dp'), may hold values from 0 to 512, as said below
- wide_master: float32 [768, 6144], P('dp')
- down_master: float32 [3072, 768], P('dp'), may hold values from -0.109375 to 0.109375
- vector_master: float32 [768, 12], P('dp')
- wide_moment: float32 [768, 6144], P('dp'), may hold values from -256 to 256
- down_moment: float32 [3072, 768], P('dp'), may hold values from -256 to 256
- vector_moment: float32 [768, 12], P('dp'), may hold values from -256 to 256
- wide_average: float32 [768, 6144], P('dp'), may hold values from -0.21875 to 0.21875
- down_average: float32 [3072, 768], P('dp'), may hold values from -0.109375 to 0.109375
- vector_average: float32 [768, 12], P('dp'), may hold values from -6 to 6
Outputs:
- short_out: bfloat16 [2, 32, 256, 768], P(None, 'dp', 'seq')
- long_out: bfloat16 [2, 16, 512, 768], P(None, 'dp', 'seq')
- short_back: bfloat16 [2, 32, 256, 768], P(None, 'dp', 'seq')
- long_back: bfloat16 [2, 16, 512, 768], P(None, 'dp', 'seq')
- wide_grad: float32 [768, 6144], P('dp')
- down_grad: float32 [3072, 768], P('dp')
- vector_grad: float32 [768, 12], P('dp')
- wide_velocity: float32 [768, 6144], P('dp')
- down_velocity: float32 [3072, 768], P('dp')
- vector_velocity: float32 [768, 12], P('dp')
- wide_averaged: float32 [768, 6144], P('dp')
- down_averaged: float32 [3072, 768], P('dp')
- vector_averaged: float32 [768, 12], P('dp')
- wide_updated: float32 [768, 6144], P('dp')
- down_updated: float32 [3072, 768], P('dp')
- vector_updated: float32 [768, 12], P('dp')
- wide_copy: bfloat16 [768, 6144], P('dp')
- down_copy: bfloat16 [3072, 768], P('dp')
- vector_copy: bfloat16 [768, 12], P('dp')
The draws below stay inside these ranges and needn't reach their ends.
Inputs may be any that keep to these rules, and one draw needn't show every extreme that they name: `short_len`: 0 marks an empty slot; in each micro-batch every index of dp has at least half of its slots live and one sequence of exactly 256 tokens. `long_len`: 0 marks an empty slot; in each micro-batch every index of dp has at least half of its slots live and one sequence of exactly 512 tokens.
All inputs are finite; a program needn't handle non-finite values.
Results may differ from the reference program's by a relative error of at most 0.015.
Values may be sent and summed in bfloat16 or wider, within the bound.
A program may use at most 256 MiB of HBM per device.

```python
from functools import partial
import jax
import jax.numpy as jnp
from jax import lax

D = 768
HEADS = 12
HEAD_DIM = 64
FF = 3072
LEN_S = 256
LEN_L = 512
MICRO = 2
SEQ_S = 4
SEQ_L = 2
GROUPS = 8
VEC_COLS = 12
TOKENS = 32768


def ragged_lengths(key, slot_count, longest):
    key_live, key_rank, key_size = jax.random.split(key, 3)
    blocks = MICRO * GROUPS
    live_count = jax.random.randint(key_live, (blocks, 1), (slot_count + 1) // 2, slot_count + 1)
    ranking = jax.random.randint(key_rank, (blocks, slot_count), 0, 1 << 20) * slot_count + jnp.arange(slot_count)[None, :]
    rank_order = jnp.argsort(jnp.argsort(ranking, axis=1), axis=1)
    drawn_sizes = jax.random.randint(key_size, (blocks, slot_count), longest // 2, longest + 1)
    chosen = jnp.where(rank_order == 0, longest, jnp.where(rank_order < live_count, drawn_sizes, 0))
    return chosen.astype(jnp.int32).reshape(MICRO, GROUPS, slot_count)


def draw_short_len(key, part):
    key = jax.random.fold_in(key, 1)
    return ragged_lengths(key, SEQ_S, LEN_S)


def draw_long_len(key, part):
    key = jax.random.fold_in(key, 2)
    return ragged_lengths(key, SEQ_L, LEN_L)


def draw_wide_master(key, part):
    key = jax.random.fold_in(key, 3)
    columns = jnp.arange(4 * D + FF)
    factor = jnp.where((columns >= 3 * D) & (columns < 4 * D), 8.0, 1.0) * D ** (-0.5)
    return jax.random.normal(key, (D, 4 * D + FF), jnp.float32) * factor[None, :]


def draw_vector_master(key, part):
    key = jax.random.fold_in(key, 4)
    key_bias, key_gain = jax.random.split(key)
    biases = jax.random.normal(key_bias, (D, VEC_COLS), jnp.float32) * 0.2
    gains = jax.random.uniform(key_gain, (D, VEC_COLS), jnp.float32, 0.6, 1.4)
    columns = jnp.arange(VEC_COLS)
    is_gain = (columns == 3) | (columns == 6)
    return jnp.where(is_gain[None, :], gains, biases)


def block_scale(own_key, dims, pieces, low, high):
    def one(dim, blocks):
        steps = jax.random.uniform(jax.random.fold_in(jax.random.fold_in(own_key, 6), dim), (blocks,), jnp.float32, low / len(pieces), high / len(pieces))
        return jnp.repeat(jnp.exp(steps), dims[dim] // blocks).reshape((-1,) + (1,) * (len(dims) - dim - 1))

    factor_of = one(*pieces[0])
    for cut in pieces[1:]:
        factor_of = factor_of * one(*cut)
    return factor_of


def scatter_about(stream_key, dims, scale, limit, cuts=(), dtype=jnp.bfloat16):
    entries = scale * jax.random.normal(stream_key, dims, jnp.float32)
    if cuts:
        entries = entries * block_scale(stream_key, dims, cuts, -0.22, 0.18)
    return jnp.clip(entries, -limit, limit).astype(dtype)


def setup_inputs(seed: int = 0) -> dict:
    seeds = jax.random.split(jax.random.key(seed), 16)
    short_in = scatter_about(seeds[0], (MICRO, GROUPS * SEQ_S, LEN_S, D), 1.0, 6.0, ((1, 8), (2, 4)))
    long_in = scatter_about(seeds[1], (MICRO, GROUPS * SEQ_L, LEN_L, D), 1.0, 6.0, ((1, 8), (2, 4)))
    short_cot = scatter_about(seeds[2], (MICRO, GROUPS * SEQ_S, LEN_S, D), 1.0, 6.0, ((1, 8), (2, 4)))
    long_cot = scatter_about(seeds[3], (MICRO, GROUPS * SEQ_L, LEN_L, D), 1.0, 6.0, ((1, 8), (2, 4)))
    short_len = draw_short_len(jax.random.fold_in(seeds[15], 71), 0)
    long_len = draw_long_len(jax.random.fold_in(seeds[15], 71), 0)
    wide_master = draw_wide_master(jax.random.fold_in(seeds[15], 71), 0)
    down_master = scatter_about(seeds[7], (FF, D), FF ** -0.5, 0.109375, ((0, 8),), jnp.float32)
    vector_master = draw_vector_master(jax.random.fold_in(seeds[15], 71), 0)
    wide_moment = scatter_about(seeds[9], (D, 4 * D + FF), (0.25 * TOKENS ** 0.5), 256.0, ((0, 8),), jnp.float32)
    down_moment = scatter_about(seeds[10], (FF, D), (0.25 * TOKENS ** 0.5), 256.0, ((0, 8),), jnp.float32)
    vector_moment = scatter_about(seeds[11], (D, VEC_COLS), (0.25 * TOKENS ** 0.5), 256.0, ((0, 8),), jnp.float32)
    wide_average = scatter_about(seeds[12], (D, 4 * D + FF), D ** -0.5, 0.21875, ((0, 8),), jnp.float32)
    down_average = scatter_about(seeds[13], (FF, D), FF ** -0.5, 0.109375, ((0, 8),), jnp.float32)
    vector_average = scatter_about(seeds[14], (D, VEC_COLS), 0.5, 6.0, ((0, 8),), jnp.float32)
    return dict(short_in=short_in, long_in=long_in, short_cot=short_cot, long_cot=long_cot, short_len=short_len, long_len=long_len, wide_master=wide_master, down_master=down_master, vector_master=vector_master, wide_moment=wide_moment, down_moment=down_moment, vector_moment=vector_moment, wide_average=wide_average, down_average=down_average, vector_average=vector_average)


@jax.custom_vjp
def low(v):
    return lax.optimization_barrier(v.astype(jnp.bfloat16)).astype(jnp.float32)

@jax.custom_vjp
def low_back(v):
    return v

def low_keep(v):
    return (low(v), None)

def low_pass(kept, grad):
    return (grad,)

def back_keep(v):
    return (v, None)

def back_low(kept, grad):
    return (low(grad),)
low.defvjp(low_keep, low_pass)
low_back.defvjp(back_keep, back_low)
highest = lax.Precision.HIGHEST
norm_eps = 1e-12
mask_fill = -10000.0
learning_rate = 0.0002
momentum_rate = 0.9
decay_weight = 0.0001
average_rate = 0.9

def matmul(left, right):
    return jnp.dot(left, right, precision=highest, preferred_element_type=jnp.float32)

def layer_norm(inputs, gain, shift):
    centred = inputs - lax.optimization_barrier(jnp.mean(inputs, axis=-1, keepdims=True))
    spread = lax.optimization_barrier(jnp.mean(centred * centred, axis=-1, keepdims=True))
    return centred * lax.rsqrt(spread + norm_eps) * gain + shift

def forward(wide, down, vector, tokens, lengths):
    wide_low = low(wide)
    down_low = low(down)
    vector_low = low(vector)
    seq_count, full_len, model_width = tokens.shape
    flat_rows = tokens.reshape(seq_count * full_len, model_width)
    bias_one = jnp.transpose(vector_low[:, 8:]).reshape(FF)
    queries = low(low_back(matmul(flat_rows, wide_low[:, :D]) + vector_low[:, 0]))
    key_rows = low(low_back(matmul(flat_rows, wide_low[:, D:2 * D])))
    values = low(low_back(matmul(flat_rows, wide_low[:, 2 * D:3 * D]) + vector_low[:, 1]))
    head_shape = (seq_count, full_len, HEADS, HEAD_DIM)
    queries = queries.reshape(head_shape)
    key_rows = key_rows.reshape(head_shape)
    values = values.reshape(head_shape)
    raw_scores = jnp.einsum('bqhd,bkhd->bhqk', queries, key_rows, precision=highest) * HEAD_DIM ** (-0.5)
    raw_scores = low_back(raw_scores)
    key_live = jnp.arange(full_len)[None, :] < lengths[:, None]
    scores = jnp.where(key_live[:, None, None, :], raw_scores, mask_fill)
    row_top = lax.optimization_barrier(jnp.max(scores, axis=-1, keepdims=True))
    exponent = jnp.exp(scores - row_top)
    probs = low(exponent / lax.optimization_barrier(jnp.sum(exponent, axis=-1, keepdims=True)))
    attended = jnp.einsum('bhqk,bkhd->bqhd', probs, values, precision=highest)
    attended = low(low_back(attended)).reshape(seq_count * full_len, model_width)
    branch = low_back(matmul(attended, wide_low[:, 3 * D:4 * D]) + vector_low[:, 2])
    first = layer_norm(flat_rows + branch, vector_low[:, 3], vector_low[:, 4])
    inner_pre = low_back(matmul(low(first), wide_low[:, 4 * D:]) + bias_one)
    active = low(jax.nn.gelu(inner_pre, approximate=False))
    branch_two = low_back(matmul(active, down_low) + vector_low[:, 5])
    result = layer_norm(first + branch_two, vector_low[:, 6], vector_low[:, 7])
    return result.reshape(seq_count, full_len, model_width)

def bucket_pass(tokens, cotangent, lengths, slot_count, masters, totals):
    full_len = tokens.shape[2]
    blocks = MICRO * GROUPS
    block_tokens = tokens.astype(jnp.float32).reshape(blocks, slot_count, full_len, D)
    block_cot = cotangent.astype(jnp.float32).reshape(blocks, slot_count, full_len, D)
    block_len = lengths.reshape(blocks, slot_count)

    def one_block(carry, item):
        inputs, cot_rows, len_rows = item
        live_rows = (jnp.arange(full_len)[None, :] < len_rows[:, None]).astype(jnp.float32)
        result, pullback = jax.vjp(partial(forward, lengths=len_rows), masters[0], masters[1], masters[2], inputs)
        grads = pullback(cot_rows * live_rows[:, :, None])
        carry = (carry[0] + grads[0], carry[1] + grads[1], carry[2] + grads[2])
        return (carry, (result.astype(jnp.bfloat16), grads[3].astype(jnp.bfloat16)))
    totals, (results, backs) = lax.scan(one_block, totals, (block_tokens, block_cot, block_len))
    out_shape = (MICRO, GROUPS * slot_count, full_len, D)
    return (totals, results.reshape(out_shape), backs.reshape(out_shape))

def update(master, reduced_grad, moment, average):
    step_grad = reduced_grad + decay_weight * master
    velocity = momentum_rate * moment + step_grad
    updated = master - learning_rate * (step_grad + momentum_rate * velocity)
    averaged = average_rate * average + (1.0 - average_rate) * updated
    return (velocity, averaged, updated, updated.astype(jnp.bfloat16))

def reference(short_in, long_in, short_cot, long_cot, short_len, long_len, wide_master, down_master, vector_master, wide_moment, down_moment, vector_moment, wide_average, down_average, vector_average):
    masters = (wide_master, down_master, vector_master)
    totals = tuple((jnp.zeros(master.shape, jnp.float32) for master in masters))
    totals, short_out, short_back = bucket_pass(short_in, short_cot, short_len, SEQ_S, masters, totals)
    totals, long_out, long_back = bucket_pass(long_in, long_cot, long_len, SEQ_L, masters, totals)
    wide_new = update(wide_master, totals[0], wide_moment, wide_average)
    down_new = update(down_master, totals[1], down_moment, down_average)
    vector_new = update(vector_master, totals[2], vector_moment, vector_average)
    return (short_out, long_out, short_back, long_back, totals[0], totals[1], totals[2], wide_new[0], down_new[0], vector_new[0], wide_new[1], down_new[1], vector_new[1], wide_new[2], down_new[2], vector_new[2], wide_new[3], down_new[3], vector_new[3])
```

```python
import jax
import jax.numpy as jnp
from jax import lax
from jax.experimental import pallas as pl
from jax.experimental.pallas import tpu as pltpu
from jax.sharding import PartitionSpec as P

D = 768
HEAD_DIM = 64
FF = 3072
PAIR = 128
LONG_L = 512
SHORT_L = 256
VMEM_BYTES = 56 * 1024 * 1024

norm_eps = 1e-12
mask_fill = -10000.0
learning_rate = 0.0002
momentum_rate = 0.9
decay_weight = 0.0001
average_rate = 0.9
score_scale = HEAD_DIM ** (-0.5)
f32 = jnp.float32
bf16 = jnp.bfloat16


def params():
    return pltpu.CompilerParams(vmem_limit_bytes=VMEM_BYTES)


def dot_nn(a, b):
    return lax.dot_general(a, b, (((1,), (0,)), ((), ())), preferred_element_type=f32)


def dot_nt(a, b):
    return lax.dot_general(a, b, (((1,), (1,)), ((), ())), preferred_element_type=f32)


SEQS = ((0, 128, LONG_L, 0), (128, 64, SHORT_L, 1), (192, 64, SHORT_L, 2))


def attn_forward_kernel(lens_ref, q_ref, k_ref, v_ref, o_ref, long_ref, short_ref):
    for first, rows, length, index in SEQS:
        q = q_ref[:, first : first + rows, :].reshape(length, PAIR)
        k = k_ref[:, first : first + rows, :].reshape(length, PAIR)
        v = v_ref[:, first : first + rows, :].reshape(length, PAIR)
        v_t = jnp.transpose(v)
        head_lane = lax.broadcasted_iota(jnp.int32, (length, PAIR), 1) // HEAD_DIM
        live = lax.broadcasted_iota(jnp.int32, (length, length), 0) < lens_ref[index]
        parts = []
        for h in range(2):
            k_h = jnp.where(head_lane == h, k, jnp.zeros_like(k))
            scores = jnp.where(live, dot_nt(k_h, q) * score_scale, mask_fill)
            top = jnp.max(scores, axis=0, keepdims=True)
            exponent = jnp.exp(scores - top)
            total = jnp.sum(exponent, axis=0, keepdims=True)
            probs = (exponent * (1.0 / total)).astype(bf16)
            if index == 0:
                long_ref[h] = probs
            else:
                short_ref[h, index - 1] = probs
            parts.append(dot_nn(v_t[h * HEAD_DIM : (h + 1) * HEAD_DIM], probs))
        o = jnp.transpose(jnp.concatenate(parts, axis=0))
        o_ref[:, first : first + rows, :] = o.astype(bf16).reshape(4, rows, PAIR)


def attn_forward(lens, qkv):
    pairs = D // PAIR
    col = lambda base: pl.BlockSpec((4, 256, PAIR), lambda i, base=base: (0, 0, base + i))
    return pl.pallas_call(
        attn_forward_kernel,
        grid=(pairs,),
        in_specs=[
            pl.BlockSpec(memory_space=pltpu.SMEM),
            col(0),
            col(pairs),
            col(2 * pairs),
        ],
        out_specs=[
            pl.BlockSpec((4, 256, PAIR), lambda i: (0, 0, i)),
            pl.BlockSpec((2, LONG_L, LONG_L), lambda i: (i, 0, 0)),
            pl.BlockSpec((2, 2, SHORT_L, SHORT_L), lambda i: (i, 0, 0, 0)),
        ],
        out_shape=[
            jax.ShapeDtypeStruct((4, 256, D), bf16),
            jax.ShapeDtypeStruct((2 * pairs, LONG_L, LONG_L), bf16),
            jax.ShapeDtypeStruct((2 * pairs, 2, SHORT_L, SHORT_L), bf16),
        ],
        compiler_params=params(),
        name="attn_forward",
    )(lens, qkv, qkv, qkv)


def attn_backward_kernel(
    lens_ref, q_ref, k_ref, v_ref, do_ref, o_ref, long_ref, short_ref, dq_ref, dk_ref, dv_ref, sum_ref
):
    sum_q = jnp.zeros((1, PAIR), f32)
    sum_v = jnp.zeros((1, PAIR), f32)
    for first, rows, length, index in SEQS:
        q = q_ref[:, first : first + rows, :].reshape(length, PAIR)
        k = k_ref[:, first : first + rows, :].reshape(length, PAIR)
        v = v_ref[:, first : first + rows, :].reshape(length, PAIR)
        do = do_ref[:, first : first + rows, :].reshape(length, PAIR)
        o = o_ref[:, first : first + rows, :].reshape(length, PAIR)
        k_t = jnp.transpose(k)
        inner = jnp.transpose(do.astype(f32) * o.astype(f32))
        head_lane = lax.broadcasted_iota(jnp.int32, (length, PAIR), 1) // HEAD_DIM
        live = lax.broadcasted_iota(jnp.int32, (length, length), 0) < lens_ref[index]
        dq_parts = []
        dk = jnp.zeros((length, PAIR), f32)
        dv = jnp.zeros((length, PAIR), f32)
        for h in range(2):
            keep = head_lane == h
            v_h = jnp.where(keep, v, jnp.zeros_like(v))
            do_h = jnp.where(keep, do, jnp.zeros_like(do))
            q_h = jnp.where(keep, q, jnp.zeros_like(q))
            probs = long_ref[h] if index == 0 else short_ref[h, index - 1]
            delta = jnp.sum(inner[h * HEAD_DIM : (h + 1) * HEAD_DIM], axis=0, keepdims=True)
            d_probs = dot_nt(v_h, do)
            d_scores = jnp.where(live, probs.astype(f32) * (d_probs - delta), 0.0).astype(bf16)
            dv = dv + dot_nn(probs, do_h)
            dk = dk + dot_nn(d_scores, q_h)
            dq_parts.append(dot_nn(k_t[h * HEAD_DIM : (h + 1) * HEAD_DIM], d_scores))
        dq = (jnp.transpose(jnp.concatenate(dq_parts, axis=0)) * score_scale).astype(bf16)
        dk = (dk * score_scale).astype(bf16)
        dv = dv.astype(bf16)
        sum_q = sum_q + jnp.sum(dq.astype(f32), axis=0, keepdims=True)
        sum_v = sum_v + jnp.sum(dv.astype(f32), axis=0, keepdims=True)
        dq_ref[:, first : first + rows, :] = dq.reshape(4, rows, PAIR)
        dk_ref[:, first : first + rows, :] = dk.reshape(4, rows, PAIR)
        dv_ref[:, first : first + rows, :] = dv.reshape(4, rows, PAIR)
    sum_ref[0:1, :] = sum_q
    sum_ref[1:2, :] = sum_v
    sum_ref[2:8, :] = jnp.zeros((6, PAIR), f32)


def attn_backward(lens, qkv, d_attended, attended, long_probs, short_probs):
    pairs = D // PAIR
    col = lambda base: pl.BlockSpec((4, 256, PAIR), lambda i, base=base: (0, 0, base + i))
    return pl.pallas_call(
        attn_backward_kernel,
        grid=(pairs,),
        in_specs=[
            pl.BlockSpec(memory_space=pltpu.SMEM),
            col(0),
            col(pairs),
            col(2 * pairs),
            col(0),
            col(0),
            pl.BlockSpec((2, LONG_L, LONG_L), lambda i: (i, 0, 0)),
            pl.BlockSpec((2, 2, SHORT_L, SHORT_L), lambda i: (i, 0, 0, 0)),
        ],
        out_specs=[col(0), col(0), col(0), pl.BlockSpec((8, PAIR), lambda i: (0, i))],
        out_shape=[jax.ShapeDtypeStruct((4, 256, D), bf16)] * 3 + [jax.ShapeDtypeStruct((8, D), f32)],
        compiler_params=params(),
        name="attn_backward",
    )(lens, qkv, qkv, qkv, d_attended, attended, long_probs, short_probs)


def gelu_pair(u):
    a = jnp.abs(u)
    t = 1.0 / (1.0 + (0.3275911 * 0.5**0.5) * a)
    e = jnp.exp(-0.5 * u * u)
    poly = t * (0.254829592 + t * (-0.284496736 + t * (1.421413741 + t * (-1.453152027 + t * 1.061405429))))
    tail = 0.5 * poly * e
    cdf = jnp.where(u < 0.0, tail, 1.0 - tail)
    pdf = e * (0.5 / jnp.pi) ** 0.5
    return u * cdf, cdf + u * pdf


def row_mean(v):
    return jnp.mean(v, axis=-1, keepdims=True)


def middle_kernel(
    lens_ref,
    o_ref,
    x_ref,
    cot_ref,
    wo_ref,
    w1_ref,
    w2_ref,
    vec_ref,
    out_ref,
    y1b_ref,
    g_ref,
    dfb_ref,
    dub_ref,
    dab_ref,
    dob_ref,
    dh_ref,
    sum_ref,
    slope_ref,
):
    r = pl.program_id(0)
    rows = o_ref.shape[0]

    @pl.when(r == 0)
    def _():
        sum_ref[...] = jnp.zeros_like(sum_ref)

    def add(index, v):
        sum_ref[index : index + 1, :] += jnp.sum(v, axis=0, keepdims=True)

    vec = lambda i: vec_ref[i : i + 1, :]
    h = x_ref[...].astype(f32) + (dot_nn(o_ref[...], wo_ref[...]) + vec(2))
    centred = h - row_mean(h)
    inv1 = lax.rsqrt(row_mean(centred * centred) + norm_eps)
    norm1 = centred * inv1
    y1 = norm1 * vec(3) + vec(4)
    y1b = y1.astype(bf16)
    y1b_ref[...] = y1b
    z = y1 + vec(5)
    for c in range(FF // D):
        cols = slice(c * D, (c + 1) * D)
        act, slope = gelu_pair(dot_nn(y1b, w1_ref[:, cols]) + vec(8 + c))
        act = act.astype(bf16)
        g_ref[:, cols] = act
        slope_ref[:, cols] = slope
        z = z + dot_nn(act, w2_ref[cols, :])
    centred2 = z - row_mean(z)
    inv2 = lax.rsqrt(row_mean(centred2 * centred2) + norm_eps)
    norm2 = centred2 * inv2
    out_ref[...] = (norm2 * vec(6) + vec(7)).astype(bf16)

    j = lax.broadcasted_iota(jnp.int32, (rows, 1), 0)
    long_end = lens_ref[0] - r * 128
    short_end = [lens_ref[i] - r * 64 + first for i, first in ((1, 128), (2, 192))]
    live = j < jnp.where(j < 128, long_end, jnp.where(j < 192, short_end[0], short_end[1]))
    dr = jnp.where(live, cot_ref[...].astype(f32), 0.0)
    e2 = dr * vec(6)
    dz = inv2 * (e2 - row_mean(e2) - norm2 * row_mean(e2 * norm2))
    dfb = dz.astype(bf16)
    dfb_ref[...] = dfb
    add(6, dr * norm2)
    add(7, dr)
    add(5, dfb.astype(f32))
    dy1 = dz
    for c in range(FF // D):
        cols = slice(c * D, (c + 1) * D)
        dub = (dot_nt(dfb, w2_ref[cols, :]) * slope_ref[:, cols]).astype(bf16)
        dub_ref[:, cols] = dub
        add(8 + c, dub.astype(f32))
        dy1 = dy1 + dot_nt(dub, w1_ref[:, cols])
    add(3, dy1 * norm1)
    add(4, dy1)
    e1 = dy1 * vec(3)
    dh = inv1 * (e1 - row_mean(e1) - norm1 * row_mean(e1 * norm1))
    dab = dh.astype(bf16)
    dh_ref[...] = dh
    dab_ref[...] = dab
    add(2, dab.astype(f32))
    dob_ref[...] = dot_nt(dab, wo_ref[...]).astype(bf16)


def middle(lens, attended, tokens, cotangent, w_o, w_1, w_2, vec):
    n = tokens.shape[0]
    rows = 256
    row = lambda width: pl.BlockSpec((rows, width), lambda i: (i, 0))
    whole = lambda a: pl.BlockSpec(a.shape, lambda i: (0, 0), pipeline_mode=pl.Buffered(1))
    shape = jax.ShapeDtypeStruct
    return pl.pallas_call(
        middle_kernel,
        grid=(n // rows,),
        in_specs=[
            pl.BlockSpec(memory_space=pltpu.SMEM),
            row(D),
            row(D),
            row(D),
            whole(w_o),
            whole(w_1),
            whole(w_2),
            whole(vec),
        ],
        out_specs=[
            row(D),
            row(D),
            row(FF),
            row(D),
            row(FF),
            row(D),
            row(D),
            row(D),
            pl.BlockSpec((16, D), lambda i: (0, 0)),
        ],
        out_shape=[
            shape((n, D), bf16),
            shape((n, D), bf16),
            shape((n, FF), bf16),
            shape((n, D), bf16),
            shape((n, FF), bf16),
            shape((n, D), bf16),
            shape((n, D), bf16),
            shape((n, D), f32),
            shape((16, D), f32),
        ],
        scratch_shapes=[pltpu.VMEM((rows, FF), f32)],
        compiler_params=params(),
        name="middle",
    )(lens, attended, tokens, cotangent, w_o, w_1, w_2, vec)


def transpose_dot(left, right):
    return jnp.einsum("ra,rb->ab", left, right, preferred_element_type=f32)


def right_dot(left, right):
    return jnp.einsum("ra,ba->rb", left, right, preferred_element_type=f32)


def flip(v, axis, bit):
    n = lax.axis_size(axis)
    return lax.ppermute(v, axis, [(i, i ^ bit) for i in range(n)])


def half_of(v, dim, which):
    size = v.shape[dim] // 2
    return lax.dynamic_slice_in_dim(v, which * size, size, dim)


def halve(v, axis, bit, dim):
    mine = (lax.axis_index(axis) // bit) % 2
    other = flip(half_of(v, dim, 1 - mine), axis, bit)
    return (half_of(v, dim, mine).astype(f32) + other.astype(f32)).astype(bf16)


def double(v, axis, bit, dim):
    mine = (lax.axis_index(axis) // bit) % 2
    other = flip(v, axis, bit)
    return jnp.where(
        mine == 0, jnp.concatenate([v, other], axis=dim), jnp.concatenate([other, v], axis=dim)
    )


def reduce_rows(grad):
    rows, cols = grad.shape
    dp = lax.axis_size("dp")
    v = grad.reshape(dp, rows // dp, cols)
    v = halve(v, "seq", 1, 2)
    v = halve(v, "seq", 2, 2)
    bit = 1
    while bit < dp:
        blocks = v.shape[0]
        v = v.reshape(blocks // 2, 2, v.shape[1], v.shape[2]) if v.ndim == 3 else v
        v = halve(v, "dp", bit, 1)[:, 0]
        bit *= 2
    v = v[0]
    v = double(v, "seq", 2, 1)
    v = double(v, "seq", 1, 1)
    return v.astype(f32)


def update(master, reduced_grad, moment, average):
    step_grad = reduced_grad + decay_weight * master
    velocity = momentum_rate * moment + step_grad
    updated = master - learning_rate * (step_grad + momentum_rate * velocity)
    averaged = average_rate * average + (1.0 - average_rate) * updated
    return (velocity, averaged, updated, updated.astype(jnp.bfloat16))


def spread_rows(long_part, short_part):
    long_blocks = long_part.reshape(4, 128, D)
    short_blocks = jnp.transpose(short_part, (1, 0, 2, 3)).reshape(4, 128, D)
    return jnp.concatenate([long_blocks, short_blocks], axis=1)


def exchange(v):
    return lax.all_to_all(v, "seq", split_axis=0, concat_axis=0, tiled=True)


def collect_rows(v):
    long_part = v[:, :128].reshape(2, 2, 128, D)
    short_part = jnp.transpose(v[:, 128:].reshape(4, 2, 64, D), (1, 0, 2, 3))
    return short_part, long_part


def body(
    short_in,
    long_in,
    short_cot,
    long_cot,
    short_len,
    long_len,
    wide_master,
    down_master,
    vector_master,
    wide_moment,
    down_moment,
    vector_moment,
    wide_average,
    down_average,
    vector_average,
):
    s = lax.axis_index("seq")
    lens = jnp.stack([long_len[s // 2, 0, s % 2], short_len[0, 0, s], short_len[1, 0, s]])
    tokens = exchange(spread_rows(long_in, short_in))
    cotangent = exchange(spread_rows(long_cot, short_cot))
    wide_w = lax.all_gather(wide_master.astype(bf16), "dp", axis=0, tiled=True)
    down_w = lax.all_gather(down_master.astype(bf16), "dp", axis=0, tiled=True)
    vector_w = lax.all_gather(vector_master.astype(bf16), "dp", axis=0, tiled=True)
    vec = jnp.transpose(vector_w.astype(f32))
    w_qkv = wide_w[:, : 3 * D]
    w_o = wide_w[:, 3 * D : 4 * D]
    w_1 = wide_w[:, 4 * D :]

    rows = tokens.reshape(1024, D)
    proj_bias = jnp.concatenate([vec[0], jnp.zeros((D,), f32), vec[1]])
    qkv = (jnp.dot(rows, w_qkv, preferred_element_type=f32) + proj_bias).astype(bf16)
    qkv = qkv.reshape(4, 256, 3 * D)
    attended, long_probs, short_probs = attn_forward(lens, qkv)
    flat_attended = attended.reshape(1024, D)
    out, y1b, act, dfb, dub, dab, dob, dh, sums = middle(
        lens, flat_attended, rows, cotangent.reshape(1024, D), w_o, w_1, down_w, vec
    )
    d_down = transpose_dot(act, dfb).astype(bf16)
    d_one = transpose_dot(y1b, dub).astype(bf16)
    d_o = transpose_dot(flat_attended, dab).astype(bf16)
    dq, dk, dv, qv_sums = attn_backward(
        lens, qkv, dob.reshape(4, 256, D), attended, long_probs, short_probs
    )
    d_qkv = jnp.concatenate([dq, dk, dv], axis=2).reshape(1024, 3 * D)
    d_wqkv = transpose_dot(rows, d_qkv).astype(bf16)
    back = (dh + right_dot(d_qkv, w_qkv)).astype(bf16).reshape(4, 256, D)

    vector_total = jnp.concatenate([qv_sums[:2], sums[2:12]], axis=0)
    vector_sum = jnp.transpose(lax.psum(vector_total, ("dp", "seq")))
    own_rows = vector_master.shape[0]
    vector_reduced = lax.dynamic_slice_in_dim(vector_sum, lax.axis_index("dp") * own_rows, own_rows, 0)
    wide_reduced = jnp.concatenate([reduce_rows(d_wqkv), reduce_rows(d_o), reduce_rows(d_one)], axis=1)
    down_reduced = reduce_rows(d_down)

    short_out, long_out = collect_rows(exchange(out.reshape(4, 256, D)))
    short_back, long_back = collect_rows(exchange(back))
    wide_new = update(wide_master, wide_reduced, wide_moment, wide_average)
    down_new = update(down_master, down_reduced, down_moment, down_average)
    vector_new = update(vector_master, vector_reduced, vector_moment, vector_average)
    return (
        short_out,
        long_out,
        short_back,
        long_back,
        wide_reduced,
        down_reduced,
        vector_reduced,
        wide_new[0],
        down_new[0],
        vector_new[0],
        wide_new[1],
        down_new[1],
        vector_new[1],
        wide_new[2],
        down_new[2],
        vector_new[2],
        wide_new[3],
        down_new[3],
        vector_new[3],
    )


def solution(mesh):
    tok = P(None, "dp", "seq", None)
    lengths = P(None, "dp", None)
    state = P("dp", None)
    return jax.shard_map(
        body,
        mesh=mesh,
        in_specs=(tok,) * 4 + (lengths,) * 2 + (state,) * 9,
        out_specs=(tok,) * 4 + (state,) * 15,
        check_vma=False,
    )
```

```python
import jax
import jax.numpy as jnp
from jax import lax
from jax.experimental import pallas as pl
from jax.experimental.pallas import tpu as pltpu
from jax.sharding import PartitionSpec as P

D = 768
HEAD_DIM = 64
FF = 3072
PAIR = 128
LONG_L = 512
SHORT_L = 256
VMEM_BYTES = 56 * 1024 * 1024

norm_eps = 1e-12
mask_fill = -10000.0
learning_rate = 0.0002
momentum_rate = 0.9
decay_weight = 0.0001
average_rate = 0.9
score_scale = HEAD_DIM ** (-0.5)
f32 = jnp.float32
bf16 = jnp.bfloat16


def params():
    return pltpu.CompilerParams(vmem_limit_bytes=VMEM_BYTES)


def dot_nn(a, b):
    return lax.dot_general(a, b, (((1,), (0,)), ((), ())), preferred_element_type=f32)


def dot_nt(a, b):
    return lax.dot_general(a, b, (((1,), (1,)), ((), ())), preferred_element_type=f32)


SEQS = ((0, 128, LONG_L, 0), (128, 64, SHORT_L, 1), (192, 64, SHORT_L, 2))


def attn_forward_kernel(lens_ref, q_ref, k_ref, v_ref, o_ref, long_ref, short_ref):
    for first, rows, length, index in SEQS:
        q = q_ref[:, first : first + rows, :].reshape(length, PAIR)
        k = k_ref[:, first : first + rows, :].reshape(length, PAIR)
        v = v_ref[:, first : first + rows, :].reshape(length, PAIR)
        v_t = jnp.transpose(v)
        head_lane = lax.broadcasted_iota(jnp.int32, (length, PAIR), 1) // HEAD_DIM
        live = lax.broadcasted_iota(jnp.int32, (length, length), 0) < lens_ref[index]
        parts = []
        for h in range(2):
            k_h = jnp.where(head_lane == h, k, jnp.zeros_like(k))
            scores = jnp.where(live, dot_nt(k_h, q) * score_scale, mask_fill)
            top = jnp.max(scores, axis=0, keepdims=True)
            exponent = jnp.exp(scores - top)
            total = jnp.sum(exponent, axis=0, keepdims=True)
            probs = (exponent * (1.0 / total)).astype(bf16)
            if index == 0:
                long_ref[h] = probs
            else:
                short_ref[h, index - 1] = probs
            parts.append(dot_nn(v_t[h * HEAD_DIM : (h + 1) * HEAD_DIM], probs))
        o = jnp.transpose(jnp.concatenate(parts, axis=0))
        o_ref[:, first : first + rows, :] = o.astype(bf16).reshape(4, rows, PAIR)


def attn_forward(lens, qkv):
    pairs = D // PAIR
    col = lambda base: pl.BlockSpec((4, 256, PAIR), lambda i, base=base: (0, 0, base + i))
    return pl.pallas_call(
        attn_forward_kernel,
        grid=(pairs,),
        in_specs=[
            pl.BlockSpec(memory_space=pltpu.SMEM),
            col(0),
            col(pairs),
            col(2 * pairs),
        ],
        out_specs=[
            pl.BlockSpec((4, 256, PAIR), lambda i: (0, 0, i)),
            pl.BlockSpec((2, LONG_L, LONG_L), lambda i: (i, 0, 0)),
            pl.BlockSpec((2, 2, SHORT_L, SHORT_L), lambda i: (i, 0, 0, 0)),
        ],
        out_shape=[
            jax.ShapeDtypeStruct((4, 256, D), bf16),
            jax.ShapeDtypeStruct((2 * pairs, LONG_L, LONG_L), bf16),
            jax.ShapeDtypeStruct((2 * pairs, 2, SHORT_L, SHORT_L), bf16),
        ],
        compiler_params=params(),
        name="attn_forward",
    )(lens, qkv, qkv, qkv)


def attn_backward_kernel(
    lens_ref, q_ref, k_ref, v_ref, do_ref, o_ref, long_ref, short_ref, dq_ref, dk_ref, dv_ref, sum_ref
):
    sum_q = jnp.zeros((1, PAIR), f32)
    sum_v = jnp.zeros((1, PAIR), f32)
    for first, rows, length, index in SEQS:
        q = q_ref[:, first : first + rows, :].reshape(length, PAIR)
        k = k_ref[:, first : first + rows, :].reshape(length, PAIR)
        v = v_ref[:, first : first + rows, :].reshape(length, PAIR)
        do = do_ref[:, first : first + rows, :].reshape(length, PAIR)
        o = o_ref[:, first : first + rows, :].reshape(length, PAIR)
        k_t = jnp.transpose(k)
        inner = jnp.transpose(do.astype(f32) * o.astype(f32))
        head_lane = lax.broadcasted_iota(jnp.int32, (length, PAIR), 1) // HEAD_DIM
        live = lax.broadcasted_iota(jnp.int32, (length, length), 0) < lens_ref[index]
        dq_parts = []
        dk = jnp.zeros((length, PAIR), f32)
        dv = jnp.zeros((length, PAIR), f32)
        for h in range(2):
            keep = head_lane == h
            v_h = jnp.where(keep, v, jnp.zeros_like(v))
            do_h = jnp.where(keep, do, jnp.zeros_like(do))
            q_h = jnp.where(keep, q, jnp.zeros_like(q))
            probs = long_ref[h] if index == 0 else short_ref[h, index - 1]
            delta = jnp.sum(inner[h * HEAD_DIM : (h + 1) * HEAD_DIM], axis=0, keepdims=True)
            d_probs = dot_nt(v_h, do)
            d_scores = jnp.where(live, probs.astype(f32) * (d_probs - delta), 0.0).astype(bf16)
            dv = dv + dot_nn(probs, do_h)
            dk = dk + dot_nn(d_scores, q_h)
            dq_parts.append(dot_nn(k_t[h * HEAD_DIM : (h + 1) * HEAD_DIM], d_scores))
        dq = (jnp.transpose(jnp.concatenate(dq_parts, axis=0)) * score_scale).astype(bf16)
        dk = (dk * score_scale).astype(bf16)
        dv = dv.astype(bf16)
        sum_q = sum_q + jnp.sum(dq.astype(f32), axis=0, keepdims=True)
        sum_v = sum_v + jnp.sum(dv.astype(f32), axis=0, keepdims=True)
        dq_ref[:, first : first + rows, :] = dq.reshape(4, rows, PAIR)
        dk_ref[:, first : first + rows, :] = dk.reshape(4, rows, PAIR)
        dv_ref[:, first : first + rows, :] = dv.reshape(4, rows, PAIR)
    sum_ref[0:1, :] = sum_q
    sum_ref[1:2, :] = sum_v
    sum_ref[2:8, :] = jnp.zeros((6, PAIR), f32)


def attn_backward(lens, qkv, d_attended, attended, long_probs, short_probs):
    pairs = D // PAIR
    col = lambda base: pl.BlockSpec((4, 256, PAIR), lambda i, base=base: (0, 0, base + i))
    return pl.pallas_call(
        attn_backward_kernel,
        grid=(pairs,),
        in_specs=[
            pl.BlockSpec(memory_space=pltpu.SMEM),
            col(0),
            col(pairs),
            col(2 * pairs),
            col(0),
            col(0),
            pl.BlockSpec((2, LONG_L, LONG_L), lambda i: (i, 0, 0)),
            pl.BlockSpec((2, 2, SHORT_L, SHORT_L), lambda i: (i, 0, 0, 0)),
        ],
        out_specs=[col(0), col(0), col(0), pl.BlockSpec((8, PAIR), lambda i: (0, i))],
        out_shape=[jax.ShapeDtypeStruct((4, 256, D), bf16)] * 3 + [jax.ShapeDtypeStruct((8, D), f32)],
        compiler_params=params(),
        name="attn_backward",
    )(lens, qkv, qkv, qkv, d_attended, attended, long_probs, short_probs)


def gelu_pair(u):
    a = jnp.abs(u)
    t = 1.0 / (1.0 + (0.3275911 * 0.5**0.5) * a)
    e = jnp.exp(-0.5 * u * u)
    poly = t * (0.254829592 + t * (-0.284496736 + t * (1.421413741 + t * (-1.453152027 + t * 1.061405429))))
    tail = 0.5 * poly * e
    cdf = jnp.where(u < 0.0, tail, 1.0 - tail)
    pdf = e * (0.5 / jnp.pi) ** 0.5
    return u * cdf, cdf + u * pdf


def row_mean(v):
    return jnp.mean(v, axis=-1, keepdims=True)


def middle_kernel(
    lens_ref,
    o_ref,
    x_ref,
    cot_ref,
    wo_ref,
    w1_ref,
    w2_ref,
    vec_ref,
    out_ref,
    y1b_ref,
    g_ref,
    dfb_ref,
    dub_ref,
    dab_ref,
    dob_ref,
    dh_ref,
    sum_ref,
    slope_ref,
):
    r = pl.program_id(0)
    rows = o_ref.shape[0]

    @pl.when(r == 0)
    def _():
        sum_ref[...] = jnp.zeros_like(sum_ref)

    def add(index, v):
        sum_ref[index : index + 1, :] += jnp.sum(v, axis=0, keepdims=True)

    vec = lambda i: vec_ref[i : i + 1, :]
    h = x_ref[...].astype(f32) + (dot_nn(o_ref[...], wo_ref[...]) + vec(2))
    centred = h - row_mean(h)
    inv1 = lax.rsqrt(row_mean(centred * centred) + norm_eps)
    norm1 = centred * inv1
    y1 = norm1 * vec(3) + vec(4)
    y1b = y1.astype(bf16)
    y1b_ref[...] = y1b
    z = y1 + vec(5)
    for c in range(FF // D):
        cols = slice(c * D, (c + 1) * D)
        act, slope = gelu_pair(dot_nn(y1b, w1_ref[:, cols]) + vec(8 + c))
        act = act.astype(bf16)
        g_ref[:, cols] = act
        slope_ref[:, cols] = slope
        z = z + dot_nn(act, w2_ref[cols, :])
    centred2 = z - row_mean(z)
    inv2 = lax.rsqrt(row_mean(centred2 * centred2) + norm_eps)
    norm2 = centred2 * inv2
    out_ref[...] = (norm2 * vec(6) + vec(7)).astype(bf16)

    j = lax.broadcasted_iota(jnp.int32, (rows, 1), 0)
    long_end = lens_ref[0] - r * 128
    short_end = [lens_ref[i] - r * 64 + first for i, first in ((1, 128), (2, 192))]
    live = j < jnp.where(j < 128, long_end, jnp.where(j < 192, short_end[0], short_end[1]))
    dr = jnp.where(live, cot_ref[...].astype(f32), 0.0)
    e2 = dr * vec(6)
    dz = inv2 * (e2 - row_mean(e2) - norm2 * row_mean(e2 * norm2))
    dfb = dz.astype(bf16)
    dfb_ref[...] = dfb
    add(6, dr * norm2)
    add(7, dr)
    add(5, dfb.astype(f32))
    dy1 = dz
    for c in range(FF // D):
        cols = slice(c * D, (c + 1) * D)
        dub = (dot_nt(dfb, w2_ref[cols, :]) * slope_ref[:, cols]).astype(bf16)
        dub_ref[:, cols] = dub
        add(8 + c, dub.astype(f32))
        dy1 = dy1 + dot_nt(dub, w1_ref[:, cols])
    add(3, dy1 * norm1)
    add(4, dy1)
    e1 = dy1 * vec(3)
    dh = inv1 * (e1 - row_mean(e1) - norm1 * row_mean(e1 * norm1))
    dab = dh.astype(bf16)
    dh_ref[...] = dh
    dab_ref[...] = dab
    add(2, dab.astype(f32))
    dob_ref[...] = dot_nt(dab, wo_ref[...]).astype(bf16)


def middle(lens, attended, tokens, cotangent, w_o, w_1, w_2, vec):
    n = tokens.shape[0]
    rows = 256
    row = lambda width: pl.BlockSpec((rows, width), lambda i: (i, 0))
    whole = lambda a: pl.BlockSpec(a.shape, lambda i: (0, 0), pipeline_mode=pl.Buffered(1))
    shape = jax.ShapeDtypeStruct
    return pl.pallas_call(
        middle_kernel,
        grid=(n // rows,),
        in_specs=[
            pl.BlockSpec(memory_space=pltpu.SMEM),
            row(D),
            row(D),
            row(D),
            whole(w_o),
            whole(w_1),
            whole(w_2),
            whole(vec),
        ],
        out_specs=[
            row(D),
            row(D),
            row(FF),
            row(D),
            row(FF),
            row(D),
            row(D),
            row(D),
            pl.BlockSpec((16, D), lambda i: (0, 0)),
        ],
        out_shape=[
            shape((n, D), bf16),
            shape((n, D), bf16),
            shape((n, FF), bf16),
            shape((n, D), bf16),
            shape((n, FF), bf16),
            shape((n, D), bf16),
            shape((n, D), bf16),
            shape((n, D), f32),
            shape((16, D), f32),
        ],
        scratch_shapes=[pltpu.VMEM((rows, FF), f32)],
        compiler_params=params(),
        name="middle",
    )(lens, attended, tokens, cotangent, w_o, w_1, w_2, vec)


MESH = pl.DeviceIdType.MESH
Z_CHIPS = 4


def place():
    dp = lax.axis_index("dp")
    s = lax.axis_index("seq")
    return dp, s, dp // 2, dp % 2, s // 2, s % 2


def remote(src, dst, send, recv, device):
    return pltpu.make_async_remote_copy(
        src_ref=src, dst_ref=dst, send_sem=send, recv_sem=recv, device_id=device, device_id_type=MESH
    )


def greet():
    dp, s = lax.axis_index("dp"), lax.axis_index("seq")
    barrier = pltpu.get_barrier_semaphore()
    for k in range(1, 8):
        pl.semaphore_signal(barrier, inc=1, device_id=((dp + k) % 8, s), device_id_type=MESH)
    for k in range(1, 4):
        pl.semaphore_signal(barrier, inc=1, device_id=(dp, (s + k) % 4), device_id_type=MESH)
    pl.semaphore_wait(barrier, 10)


class Part:
    def __init__(self, own, out, sems):
        self.own, self.out = own, out
        self.z_send, self.z_recv, self.x_send, self.x_recv, self.y_send, self.y_recv, self.c_send, self.c_recv = sems
        self.dp, self.s, self.z, self.x, self.y, self.c = place()
        self.rows, cols = own.shape
        self.half_rows, self.half_cols = self.rows // 2, cols // 2

    def cols(self, core):
        return pl.ds(pl.multiple_of(core * self.half_cols, 128), self.half_cols)

    def some(self, q):
        return pl.ds(pl.multiple_of(q * self.half_rows, 16), self.half_rows)

    def block(self, zs, x, core, q=None):
        rows = slice(None) if q is None else self.some(q)
        return self.out.at[zs * 2 + x, rows, self.cols(core)]

    def source(self, zs, own, q=None):
        if own:
            rows = slice(None) if q is None else self.some(q)
            return self.own.at[rows, self.cols(self.c)]
        return self.block(zs, self.x, self.c, q)

    def up(self, zs, own=False):
        dst = self.block(zs, self.x, self.c)
        return remote(self.source(zs, own), dst, self.z_send.at[zs, 0], self.z_recv.at[zs], (self.dp + 2, self.s))

    def down(self, zs, own=False):
        dst = self.block(zs, self.x, self.c)
        return remote(self.source(zs, own), dst, self.z_send.at[zs, 1], self.z_recv.at[zs], (self.dp - 2, self.s))

    def across(self, zs, own=False):
        dst = self.block(zs, self.x, self.c, self.y)
        device = (self.z * 2 + 1 - self.x, self.s)
        return remote(self.source(zs, own, self.y), dst, self.x_send.at[zs], self.x_recv.at[zs], device)

    def across_in(self, zs):
        ref = self.block(zs, 1 - self.x, self.c, self.y)
        return remote(ref, ref, self.x_send.at[zs], self.x_recv.at[zs], (self.dp, self.s))

    def over(self, zs):
        ref = self.block(zs, 1 - self.x, self.c, self.y)
        return remote(ref, ref, self.y_send.at[zs], self.y_recv.at[zs], (self.dp, (1 - self.y) * 2 + self.c))

    def over_in(self, zs):
        ref = self.block(zs, 1 - self.x, self.c, 1 - self.y)
        return remote(ref, ref, self.y_send.at[zs], self.y_recv.at[zs], (self.dp, self.s))

    def share(self, kind, zs, core):
        if kind == 0:
            ref = self.block(zs, self.x, core)
        else:
            ref = self.block(zs, 1 - self.x, core, self.y if kind == 1 else 1 - self.y)
        j = kind * Z_CHIPS + zs
        return remote(ref, ref, self.c_send.at[j], self.c_recv.at[j], (self.dp, self.s + 1 - 2 * self.c))

    def each(self, k, what):
        if k == 0:
            what(self.z)
            return

        @pl.when(self.z >= k)
        def _():
            what(self.z - k)

        @pl.when(self.z + k < Z_CHIPS)
        def _():
            what(self.z + k)

    def stage(self, k):
        if k == 0:

            @pl.when(self.z < Z_CHIPS - 1)
            def _():
                self.up(self.z, True).start()

            @pl.when(self.z > 0)
            def _():
                self.down(self.z, True).start()

            self.across(self.z, True).start()
        elif k < Z_CHIPS:

            @pl.when(self.z >= k)
            def _():
                zs = self.z - k
                self.up(zs).wait_recv()

                @pl.when(self.z < Z_CHIPS - 1)
                def _():
                    self.up(zs).start()

                self.across(zs).start()
                self.share(0, zs, self.c).start()

            @pl.when(self.z + k < Z_CHIPS)
            def _():
                zs = self.z + k
                self.down(zs).wait_recv()

                @pl.when(self.z > 0)
                def _():
                    self.down(zs).start()

                self.across(zs).start()
                self.share(0, zs, self.c).start()

        if 1 <= k <= Z_CHIPS:

            def pass_x(zs):
                self.across_in(zs).wait_recv()
                self.over(zs).start()
                self.share(1, zs, self.c).start()

            self.each(k - 1, pass_x)
        if 2 <= k <= Z_CHIPS + 1:

            def pass_y(zs):
                self.over_in(zs).wait_recv()
                self.share(2, zs, self.c).start()

            self.each(k - 2, pass_y)

    stages = Z_CHIPS + 2

    def finish(self):
        for kind in range(3):
            for k in range(1 if kind == 0 else 0, Z_CHIPS):
                self.each(k, lambda zs, kind=kind: self.share(kind, zs, 1 - self.c).wait_recv())

    def settle(self):
        for k in range(Z_CHIPS):

            @pl.when((self.z >= k) & (self.z < Z_CHIPS - 1))
            def _():
                self.up(self.z - k, k == 0).wait_send()

            @pl.when((self.z + k < Z_CHIPS) & (self.z > 0))
            def _():
                self.down(self.z + k, k == 0).wait_send()

            self.each(k, lambda zs, k=k: self.across(zs, k == 0).wait_send())
            self.each(k, lambda zs: self.over(zs).wait_send())
            for kind in range(3):
                if kind > 0 or k > 0:
                    self.each(k, lambda zs, kind=kind: self.share(kind, zs, self.c).wait_send())


class Tokens:
    def __init__(self, long_ref, short_ref, out, send, recv, local):
        self.long_ref, self.short_ref, self.out, self.send, self.recv, self.local = long_ref, short_ref, out, send, recv, local
        self.dp, self.s = lax.axis_index("dp"), lax.axis_index("seq")

    def pieces(self, target, source):
        yield self.long_ref.at[target // 2, target % 2], self.out.at[source, pl.ds(0, 128)]
        yield self.short_ref.at[0, target], self.out.at[source, pl.ds(128, 64)]
        yield self.short_ref.at[1, target], self.out.at[source, pl.ds(192, 64)]

    def copies(self, k):
        target = (self.s + k) % 4
        for j, (src, dst) in enumerate(self.pieces(target, self.s)):
            yield remote(src, dst, self.send.at[k, j], self.recv.at[k, j], (self.dp, target))

    def own(self):
        for j, (src, dst) in enumerate(self.pieces(self.s, self.s)):
            yield pltpu.make_async_copy(src, dst, self.local.at[j])

    def start(self):
        for k in range(1, 4):
            for copy in self.copies(k):
                copy.start()
        for copy in self.own():
            copy.start()

    def finish(self):
        for copy in self.own():
            copy.wait()
        for k in range(1, 4):
            source = (self.s + 4 - k) % 4
            for j, (src, dst) in enumerate(self.pieces(self.s, source)):
                remote(src, dst, self.send.at[k, j], self.recv.at[k, j], (self.dp, self.s)).wait_recv()

    def settle(self):
        for k in range(1, 4):
            for copy in self.copies(k):
                copy.wait_send()


def gather_kernel(
    wide_ref,
    down_ref,
    vec_ref,
    long_in,
    short_in,
    long_cot,
    short_cot,
    qkv_out,
    wo_out,
    w1_out,
    w2_out,
    vec_out,
    tok_out,
    cot_out,
    own_wide,
    own_down,
    z_send,
    z_recv,
    x_send,
    x_recv,
    y_send,
    y_recv,
    c_send,
    c_recv,
    v_send,
    v_recv,
    t_send,
    t_recv,
    local,
):
    dp, s, z, x, y, c = place()
    greet()
    tokens = Tokens(long_in, short_in, tok_out, t_send.at[0], t_recv.at[0], local.at[0])
    cots = Tokens(long_cot, short_cot, cot_out, t_send.at[1], t_recv.at[1], local.at[1])
    tokens.start()
    own_wide[...] = wide_ref[...].astype(bf16)
    own_down[...] = down_ref[...].astype(bf16)

    def vec_copy(k, source, target):
        return remote(vec_ref, vec_out.at[source], v_send.at[k], v_recv.at[k], (target, s))

    sems = lambda i: [
        r.at[i] for r in (z_send, z_recv, x_send, x_recv, y_send, y_recv, c_send, c_recv)
    ]
    parts = [
        Part(own_wide.at[:, pl.ds(0, 3 * D)], qkv_out, sems(0)),
        Part(own_wide.at[:, pl.ds(3 * D, D)], wo_out, sems(1)),
        Part(own_wide.at[:, pl.ds(4 * D, FF)], w1_out, sems(2)),
        Part(own_down, w2_out, sems(3)),
    ]
    parts[0].stage(0)
    for k in range(1, 8):
        vec_copy(k, dp, (dp + k) % 8).start()
    own_copies = [
        pltpu.make_async_copy(part.own, part.out.at[dp], local.at[2, i]) for i, part in enumerate(parts)
    ]
    own_copies.append(pltpu.make_async_copy(vec_ref, vec_out.at[dp], local.at[2, 4]))
    for copy in own_copies:
        copy.start()
    for t in range(1, Part.stages + len(parts) - 1):
        for i, part in enumerate(parts):
            if 0 <= t - i < Part.stages:
                part.stage(t - i)
        if t == 4:
            cots.start()
    for copy in own_copies:
        copy.wait()
    for part in parts:
        part.finish()
    tokens.finish()
    cots.finish()
    for k in range(1, 8):
        vec_copy(k, (dp + 8 - k) % 8, dp).wait_recv()
    for k in range(1, 8):
        vec_copy(k, dp, (dp + k) % 8).wait_send()
    for part in parts:
        part.settle()
    tokens.settle()
    cots.settle()


def gather(wide_master, down_master, vec_block, long_in, short_in, long_cot, short_cot):
    any_spec = pl.BlockSpec(memory_space=pl.ANY)
    vmem = pl.BlockSpec(memory_space=pltpu.VMEM)
    shape = jax.ShapeDtypeStruct
    rows, down_rows = wide_master.shape[0], down_master.shape[0]
    dma = pltpu.SemaphoreType.DMA
    return pl.pallas_call(
        gather_kernel,
        in_specs=[vmem, vmem, vmem] + [any_spec] * 4,
        out_specs=[any_spec] * 7,
        out_shape=[
            shape((8, rows, 3 * D), bf16),
            shape((8, rows, D), bf16),
            shape((8, rows, FF), bf16),
            shape((8, down_rows, D), bf16),
            shape((8, 16, 128), f32),
            shape((4, 256, D), bf16),
            shape((4, 256, D), bf16),
        ],
        scratch_shapes=[
            pltpu.VMEM((rows, 4 * D + FF), bf16),
            pltpu.VMEM((down_rows, D), bf16),
            dma((4, 4, 2)),
            dma((4, 4)),
            dma((4, 4)),
            dma((4, 4)),
            dma((4, 4)),
            dma((4, 4)),
            dma((4, 12)),
            dma((4, 12)),
            dma((8,)),
            dma((8,)),
            dma((2, 4, 3)),
            dma((2, 4, 3)),
            dma((3, 5)),
        ],
        compiler_params=pltpu.CompilerParams(
            vmem_limit_bytes=VMEM_BYTES, collective_id=0, has_side_effects=True
        ),
        name="gather",
    )(wide_master, down_master, vec_block, long_in, short_in, long_cot, short_cot)


def transpose_dot(left, right):
    return jnp.einsum("ra,rb->ab", left, right, preferred_element_type=f32)


def right_dot(left, right):
    return jnp.einsum("ra,ba->rb", left, right, preferred_element_type=f32)


def flip(v, axis, bit):
    n = lax.axis_size(axis)
    return lax.ppermute(v, axis, [(i, i ^ bit) for i in range(n)])


def half_of(v, dim, which):
    size = v.shape[dim] // 2
    return lax.dynamic_slice_in_dim(v, which * size, size, dim)


def halve(v, axis, bit, dim):
    mine = (lax.axis_index(axis) // bit) % 2
    other = flip(half_of(v, dim, 1 - mine), axis, bit)
    return (half_of(v, dim, mine).astype(f32) + other.astype(f32)).astype(bf16)


def double(v, axis, bit, dim):
    mine = (lax.axis_index(axis) // bit) % 2
    other = flip(v, axis, bit)
    return jnp.where(
        mine == 0, jnp.concatenate([v, other], axis=dim), jnp.concatenate([other, v], axis=dim)
    )


def reduce_rows(grad):
    rows, cols = grad.shape
    dp = lax.axis_size("dp")
    v = grad.reshape(dp, rows // dp, cols)
    v = halve(v, "seq", 1, 2)
    v = halve(v, "seq", 2, 2)
    bit = 1
    while bit < dp:
        blocks = v.shape[0]
        v = v.reshape(blocks // 2, 2, v.shape[1], v.shape[2]) if v.ndim == 3 else v
        v = halve(v, "dp", bit, 1)[:, 0]
        bit *= 2
    v = v[0]
    v = double(v, "seq", 2, 1)
    v = double(v, "seq", 1, 1)
    return v.astype(f32)


def update(master, reduced_grad, moment, average):
    step_grad = reduced_grad + decay_weight * master
    velocity = momentum_rate * moment + step_grad
    updated = master - learning_rate * (step_grad + momentum_rate * velocity)
    averaged = average_rate * average + (1.0 - average_rate) * updated
    return (velocity, averaged, updated, updated.astype(jnp.bfloat16))


def spread_rows(long_part, short_part):
    long_blocks = long_part.reshape(4, 128, D)
    short_blocks = jnp.transpose(short_part, (1, 0, 2, 3)).reshape(4, 128, D)
    return jnp.concatenate([long_blocks, short_blocks], axis=1)


def exchange(v):
    return lax.all_to_all(v, "seq", split_axis=0, concat_axis=0, tiled=True)


def collect_rows(v):
    long_part = v[:, :128].reshape(2, 2, 128, D)
    short_part = jnp.transpose(v[:, 128:].reshape(4, 2, 64, D), (1, 0, 2, 3))
    return short_part, long_part


def body(
    short_in,
    long_in,
    short_cot,
    long_cot,
    short_len,
    long_len,
    wide_master,
    down_master,
    vector_master,
    wide_moment,
    down_moment,
    vector_moment,
    wide_average,
    down_average,
    vector_average,
):
    s = lax.axis_index("seq")
    lens = jnp.stack([long_len[s // 2, 0, s % 2], short_len[0, 0, s], short_len[1, 0, s]])
    if lax.axis_size("dp") == 8:
        vec_own = jnp.transpose(vector_master).astype(bf16).astype(f32)
        vec_block = jnp.pad(vec_own, ((0, 4), (0, 128 - vec_own.shape[1])))
        w_qkv, w_o, w_1, w_2, vec_blocks, tokens, cotangent = gather(
            wide_master, down_master, vec_block, long_in, short_in, long_cot, short_cot
        )
        w_qkv, w_o, w_1, w_2 = [w.reshape(-1, w.shape[2]) for w in (w_qkv, w_o, w_1, w_2)]
        vec = jnp.transpose(vec_blocks[:, :12, : vec_own.shape[1]], (1, 0, 2)).reshape(12, D)
    else:
        tokens = exchange(spread_rows(long_in, short_in))
        cotangent = exchange(spread_rows(long_cot, short_cot))
        wide_w = lax.all_gather(wide_master.astype(bf16), "dp", axis=0, tiled=True)
        w_2 = lax.all_gather(down_master.astype(bf16), "dp", axis=0, tiled=True)
        vector_w = lax.all_gather(vector_master.astype(bf16), "dp", axis=0, tiled=True)
        vec = jnp.transpose(vector_w.astype(f32))
        w_qkv = wide_w[:, : 3 * D]
        w_o = wide_w[:, 3 * D : 4 * D]
        w_1 = wide_w[:, 4 * D :]

    rows = tokens.reshape(1024, D)
    proj_bias = jnp.concatenate([vec[0], jnp.zeros((D,), f32), vec[1]])
    qkv = (jnp.dot(rows, w_qkv, preferred_element_type=f32) + proj_bias).astype(bf16)
    qkv = qkv.reshape(4, 256, 3 * D)
    attended, long_probs, short_probs = attn_forward(lens, qkv)
    flat_attended = attended.reshape(1024, D)
    out, y1b, act, dfb, dub, dab, dob, dh, sums = middle(
        lens, flat_attended, rows, cotangent.reshape(1024, D), w_o, w_1, w_2, vec
    )
    d_down = transpose_dot(act, dfb).astype(bf16)
    d_one = transpose_dot(y1b, dub).astype(bf16)
    d_o = transpose_dot(flat_attended, dab).astype(bf16)
    dq, dk, dv, qv_sums = attn_backward(
        lens, qkv, dob.reshape(4, 256, D), attended, long_probs, short_probs
    )
    d_qkv = jnp.concatenate([dq, dk, dv], axis=2).reshape(1024, 3 * D)
    d_wqkv = transpose_dot(rows, d_qkv).astype(bf16)
    back = (dh + right_dot(d_qkv, w_qkv)).astype(bf16).reshape(4, 256, D)

    vector_total = jnp.concatenate([qv_sums[:2], sums[2:12]], axis=0)
    vector_sum = jnp.transpose(lax.psum(vector_total, ("dp", "seq")))
    own_rows = vector_master.shape[0]
    vector_reduced = lax.dynamic_slice_in_dim(vector_sum, lax.axis_index("dp") * own_rows, own_rows, 0)
    wide_reduced = jnp.concatenate([reduce_rows(d_wqkv), reduce_rows(d_o), reduce_rows(d_one)], axis=1)
    down_reduced = reduce_rows(d_down)

    short_out, long_out = collect_rows(exchange(out.reshape(4, 256, D)))
    short_back, long_back = collect_rows(exchange(back))
    wide_new = update(wide_master, wide_reduced, wide_moment, wide_average)
    down_new = update(down_master, down_reduced, down_moment, down_average)
    vector_new = update(vector_master, vector_reduced, vector_moment, vector_average)
    return (
        short_out,
        long_out,
        short_back,
        long_back,
        wide_reduced,
        down_reduced,
        vector_reduced,
        wide_new[0],
        down_new[0],
        vector_new[0],
        wide_new[1],
        down_new[1],
        vector_new[1],
        wide_new[2],
        down_new[2],
        vector_new[2],
        wide_new[3],
        down_new[3],
        vector_new[3],
    )


def solution(mesh):
    tok = P(None, "dp", "seq", None)
    lengths = P(None, "dp", None)
    state = P("dp", None)
    return jax.shard_map(
        body,
        mesh=mesh,
        in_specs=(tok,) * 4 + (lengths,) * 2 + (state,) * 9,
        out_specs=(tok,) * 4 + (state,) * 15,
        check_vma=False,
    )
```

```python
import jax
import jax.numpy as jnp
from jax import lax
from jax.experimental import pallas as pl
from jax.experimental.pallas import tpu as pltpu
from jax.sharding import PartitionSpec as P

D = 768
HEAD_DIM = 64
FF = 3072
PAIR = 128
LONG_L = 512
SHORT_L = 256
VMEM_BYTES = 56 * 1024 * 1024

norm_eps = 1e-12
mask_fill = -10000.0
learning_rate = 0.0002
momentum_rate = 0.9
decay_weight = 0.0001
average_rate = 0.9
score_scale = HEAD_DIM ** (-0.5)
f32 = jnp.float32
bf16 = jnp.bfloat16


def params():
    return pltpu.CompilerParams(vmem_limit_bytes=VMEM_BYTES)


def dot_nn(a, b):
    return lax.dot_general(a, b, (((1,), (0,)), ((), ())), preferred_element_type=f32)


def dot_nt(a, b):
    return lax.dot_general(a, b, (((1,), (1,)), ((), ())), preferred_element_type=f32)


SEQS = ((0, 128, LONG_L, 0), (128, 64, SHORT_L, 1), (192, 64, SHORT_L, 2))


def attn_forward_kernel(lens_ref, q_ref, k_ref, v_ref, o_ref, long_ref, short_ref):
    for first, rows, length, index in SEQS:
        q = q_ref[:, first : first + rows, :].reshape(length, PAIR)
        k = k_ref[:, first : first + rows, :].reshape(length, PAIR)
        v = v_ref[:, first : first + rows, :].reshape(length, PAIR)
        v_t = jnp.transpose(v)
        head_lane = lax.broadcasted_iota(jnp.int32, (length, PAIR), 1) // HEAD_DIM
        live = lax.broadcasted_iota(jnp.int32, (length, length), 0) < lens_ref[index]
        parts = []
        for h in range(2):
            k_h = jnp.where(head_lane == h, k, jnp.zeros_like(k))
            scores = jnp.where(live, dot_nt(k_h, q) * score_scale, mask_fill)
            top = jnp.max(scores, axis=0, keepdims=True)
            exponent = jnp.exp(scores - top)
            total = jnp.sum(exponent, axis=0, keepdims=True)
            probs = (exponent * (1.0 / total)).astype(bf16)
            if index == 0:
                long_ref[h] = probs
            else:
                short_ref[h, index - 1] = probs
            parts.append(dot_nn(v_t[h * HEAD_DIM : (h + 1) * HEAD_DIM], probs))
        o = jnp.transpose(jnp.concatenate(parts, axis=0))
        o_ref[:, first : first + rows, :] = o.astype(bf16).reshape(4, rows, PAIR)


def attn_forward(lens, qkv):
    pairs = D // PAIR
    col = lambda base: pl.BlockSpec((4, 256, PAIR), lambda i, base=base: (0, 0, base + i))
    return pl.pallas_call(
        attn_forward_kernel,
        grid=(pairs,),
        in_specs=[
            pl.BlockSpec(memory_space=pltpu.SMEM),
            col(0),
            col(pairs),
            col(2 * pairs),
        ],
        out_specs=[
            pl.BlockSpec((4, 256, PAIR), lambda i: (0, 0, i)),
            pl.BlockSpec((2, LONG_L, LONG_L), lambda i: (i, 0, 0)),
            pl.BlockSpec((2, 2, SHORT_L, SHORT_L), lambda i: (i, 0, 0, 0)),
        ],
        out_shape=[
            jax.ShapeDtypeStruct((4, 256, D), bf16),
            jax.ShapeDtypeStruct((2 * pairs, LONG_L, LONG_L), bf16),
            jax.ShapeDtypeStruct((2 * pairs, 2, SHORT_L, SHORT_L), bf16),
        ],
        compiler_params=params(),
        name="attn_forward",
    )(lens, qkv, qkv, qkv)


def attn_backward_kernel(
    lens_ref, q_ref, k_ref, v_ref, do_ref, o_ref, long_ref, short_ref, dq_ref, dk_ref, dv_ref, sum_ref
):
    sum_q = jnp.zeros((1, PAIR), f32)
    sum_v = jnp.zeros((1, PAIR), f32)
    for first, rows, length, index in SEQS:
        q = q_ref[:, first : first + rows, :].reshape(length, PAIR)
        k = k_ref[:, first : first + rows, :].reshape(length, PAIR)
        v = v_ref[:, first : first + rows, :].reshape(length, PAIR)
        do = do_ref[:, first : first + rows, :].reshape(length, PAIR)
        o = o_ref[:, first : first + rows, :].reshape(length, PAIR)
        k_t = jnp.transpose(k)
        inner = jnp.transpose(do.astype(f32) * o.astype(f32))
        head_lane = lax.broadcasted_iota(jnp.int32, (length, PAIR), 1) // HEAD_DIM
        live = lax.broadcasted_iota(jnp.int32, (length, length), 0) < lens_ref[index]
        dq_parts = []
        dk = jnp.zeros((length, PAIR), f32)
        dv = jnp.zeros((length, PAIR), f32)
        for h in range(2):
            keep = head_lane == h
            v_h = jnp.where(keep, v, jnp.zeros_like(v))
            do_h = jnp.where(keep, do, jnp.zeros_like(do))
            q_h = jnp.where(keep, q, jnp.zeros_like(q))
            probs = long_ref[h] if index == 0 else short_ref[h, index - 1]
            delta = jnp.sum(inner[h * HEAD_DIM : (h + 1) * HEAD_DIM], axis=0, keepdims=True)
            d_probs = dot_nt(v_h, do)
            d_scores = jnp.where(live, probs.astype(f32) * (d_probs - delta), 0.0).astype(bf16)
            dv = dv + dot_nn(probs, do_h)
            dk = dk + dot_nn(d_scores, q_h)
            dq_parts.append(dot_nn(k_t[h * HEAD_DIM : (h + 1) * HEAD_DIM], d_scores))
        dq = (jnp.transpose(jnp.concatenate(dq_parts, axis=0)) * score_scale).astype(bf16)
        dk = (dk * score_scale).astype(bf16)
        dv = dv.astype(bf16)
        sum_q = sum_q + jnp.sum(dq.astype(f32), axis=0, keepdims=True)
        sum_v = sum_v + jnp.sum(dv.astype(f32), axis=0, keepdims=True)
        dq_ref[:, first : first + rows, :] = dq.reshape(4, rows, PAIR)
        dk_ref[:, first : first + rows, :] = dk.reshape(4, rows, PAIR)
        dv_ref[:, first : first + rows, :] = dv.reshape(4, rows, PAIR)
    sum_ref[0:1, :] = sum_q
    sum_ref[1:2, :] = sum_v
    sum_ref[2:8, :] = jnp.zeros((6, PAIR), f32)


def attn_backward(lens, qkv, d_attended, attended, long_probs, short_probs):
    pairs = D // PAIR
    col = lambda base: pl.BlockSpec((4, 256, PAIR), lambda i, base=base: (0, 0, base + i))
    return pl.pallas_call(
        attn_backward_kernel,
        grid=(pairs,),
        in_specs=[
            pl.BlockSpec(memory_space=pltpu.SMEM),
            col(0),
            col(pairs),
            col(2 * pairs),
            col(0),
            col(0),
            pl.BlockSpec((2, LONG_L, LONG_L), lambda i: (i, 0, 0)),
            pl.BlockSpec((2, 2, SHORT_L, SHORT_L), lambda i: (i, 0, 0, 0)),
        ],
        out_specs=[col(0), col(0), col(0), pl.BlockSpec((8, PAIR), lambda i: (0, i))],
        out_shape=[jax.ShapeDtypeStruct((4, 256, D), bf16)] * 3 + [jax.ShapeDtypeStruct((8, D), f32)],
        compiler_params=params(),
        name="attn_backward",
    )(lens, qkv, qkv, qkv, d_attended, attended, long_probs, short_probs)


def gelu_pair(u):
    a = jnp.abs(u)
    t = 1.0 / (1.0 + (0.3275911 * 0.5**0.5) * a)
    e = jnp.exp(-0.5 * u * u)
    poly = t * (0.254829592 + t * (-0.284496736 + t * (1.421413741 + t * (-1.453152027 + t * 1.061405429))))
    tail = 0.5 * poly * e
    cdf = jnp.where(u < 0.0, tail, 1.0 - tail)
    pdf = e * (0.5 / jnp.pi) ** 0.5
    return u * cdf, cdf + u * pdf


def row_mean(v):
    return jnp.mean(v, axis=-1, keepdims=True)


def middle_kernel(
    lens_ref,
    o_ref,
    x_ref,
    cot_ref,
    wo_ref,
    w1_ref,
    w2_ref,
    vec_ref,
    out_ref,
    y1b_ref,
    g_ref,
    dfb_ref,
    dub_ref,
    dab_ref,
    dob_ref,
    dh_ref,
    sum_ref,
    slope_ref,
):
    r = pl.program_id(0)
    rows = o_ref.shape[0]

    @pl.when(r == 0)
    def _():
        sum_ref[...] = jnp.zeros_like(sum_ref)

    def add(index, v):
        sum_ref[index : index + 1, :] += jnp.sum(v, axis=0, keepdims=True)

    vec = lambda i: vec_ref[i : i + 1, :]
    h = x_ref[...].astype(f32) + (dot_nn(o_ref[...], wo_ref[...]) + vec(2))
    centred = h - row_mean(h)
    inv1 = lax.rsqrt(row_mean(centred * centred) + norm_eps)
    norm1 = centred * inv1
    y1 = norm1 * vec(3) + vec(4)
    y1b = y1.astype(bf16)
    y1b_ref[...] = y1b
    z = y1 + vec(5)
    for c in range(FF // D):
        cols = slice(c * D, (c + 1) * D)
        act, slope = gelu_pair(dot_nn(y1b, w1_ref[:, cols]) + vec(8 + c))
        act = act.astype(bf16)
        g_ref[:, cols] = act
        slope_ref[:, cols] = slope
        z = z + dot_nn(act, w2_ref[cols, :])
    centred2 = z - row_mean(z)
    inv2 = lax.rsqrt(row_mean(centred2 * centred2) + norm_eps)
    norm2 = centred2 * inv2
    out_ref[...] = (norm2 * vec(6) + vec(7)).astype(bf16)

    j = lax.broadcasted_iota(jnp.int32, (rows, 1), 0)
    long_end = lens_ref[0] - r * 128
    short_end = [lens_ref[i] - r * 64 + first for i, first in ((1, 128), (2, 192))]
    live = j < jnp.where(j < 128, long_end, jnp.where(j < 192, short_end[0], short_end[1]))
    dr = jnp.where(live, cot_ref[...].astype(f32), 0.0)
    e2 = dr * vec(6)
    dz = inv2 * (e2 - row_mean(e2) - norm2 * row_mean(e2 * norm2))
    dfb = dz.astype(bf16)
    dfb_ref[...] = dfb
    add(6, dr * norm2)
    add(7, dr)
    add(5, dfb.astype(f32))
    dy1 = dz
    for c in range(FF // D):
        cols = slice(c * D, (c + 1) * D)
        dub = (dot_nt(dfb, w2_ref[cols, :]) * slope_ref[:, cols]).astype(bf16)
        dub_ref[:, cols] = dub
        add(8 + c, dub.astype(f32))
        dy1 = dy1 + dot_nt(dub, w1_ref[:, cols])
    add(3, dy1 * norm1)
    add(4, dy1)
    e1 = dy1 * vec(3)
    dh = inv1 * (e1 - row_mean(e1) - norm1 * row_mean(e1 * norm1))
    dab = dh.astype(bf16)
    dh_ref[...] = dh
    dab_ref[...] = dab
    add(2, dab.astype(f32))
    dob_ref[...] = dot_nt(dab, wo_ref[...]).astype(bf16)


def middle(lens, attended, tokens, cotangent, w_o, w_1, w_2, vec):
    n = tokens.shape[0]
    rows = 256
    row = lambda width: pl.BlockSpec((rows, width), lambda i: (i, 0))
    whole = lambda a: pl.BlockSpec(a.shape, lambda i: (0, 0), pipeline_mode=pl.Buffered(1))
    shape = jax.ShapeDtypeStruct
    return pl.pallas_call(
        middle_kernel,
        grid=(n // rows,),
        in_specs=[
            pl.BlockSpec(memory_space=pltpu.SMEM),
            row(D),
            row(D),
            row(D),
            whole(w_o),
            whole(w_1),
            whole(w_2),
            whole(vec),
        ],
        out_specs=[
            row(D),
            row(D),
            row(FF),
            row(D),
            row(FF),
            row(D),
            row(D),
            row(D),
            pl.BlockSpec((16, D), lambda i: (0, 0)),
        ],
        out_shape=[
            shape((n, D), bf16),
            shape((n, D), bf16),
            shape((n, FF), bf16),
            shape((n, D), bf16),
            shape((n, FF), bf16),
            shape((n, D), bf16),
            shape((n, D), bf16),
            shape((n, D), f32),
            shape((16, D), f32),
        ],
        scratch_shapes=[pltpu.VMEM((rows, FF), f32)],
        compiler_params=params(),
        name="middle",
    )(lens, attended, tokens, cotangent, w_o, w_1, w_2, vec)


MESH = pl.DeviceIdType.MESH
Z_CHIPS = 4


def place():
    dp = lax.axis_index("dp")
    s = lax.axis_index("seq")
    return dp, s, dp // 2, dp % 2, s // 2, s % 2


def remote(src, dst, send, recv, device):
    return pltpu.make_async_remote_copy(
        src_ref=src, dst_ref=dst, send_sem=send, recv_sem=recv, device_id=device, device_id_type=MESH
    )


def greet():
    dp, s = lax.axis_index("dp"), lax.axis_index("seq")
    barrier = pltpu.get_barrier_semaphore()
    for k in range(1, 8):
        pl.semaphore_signal(barrier, inc=1, device_id=((dp + k) % 8, s), device_id_type=MESH)
    for k in range(1, 4):
        pl.semaphore_signal(barrier, inc=1, device_id=(dp, (s + k) % 4), device_id_type=MESH)
    pl.semaphore_wait(barrier, 10)


class Part:
    def __init__(self, own, out, sems):
        self.own, self.out = own, out
        self.z_send, self.z_recv, self.x_send, self.x_recv, self.y_send, self.y_recv, self.c_send, self.c_recv = sems
        self.dp, self.s, self.z, self.x, self.y, self.c = place()
        self.rows, cols = own.shape
        self.half_rows, self.half_cols = self.rows // 2, cols // 2

    def cols(self, core):
        return pl.ds(pl.multiple_of(core * self.half_cols, 128), self.half_cols)

    def some(self, q):
        return pl.ds(pl.multiple_of(q * self.half_rows, 16), self.half_rows)

    def block(self, zs, x, core, q=None):
        rows = slice(None) if q is None else self.some(q)
        return self.out.at[zs * 2 + x, rows, self.cols(core)]

    def source(self, zs, own, q=None):
        if own:
            rows = slice(None) if q is None else self.some(q)
            return self.own.at[rows, self.cols(self.c)]
        return self.block(zs, self.x, self.c, q)

    def up(self, zs, own=False):
        dst = self.block(zs, self.x, self.c)
        return remote(self.source(zs, own), dst, self.z_send.at[zs, 0], self.z_recv.at[zs], (self.dp + 2, self.s))

    def down(self, zs, own=False):
        dst = self.block(zs, self.x, self.c)
        return remote(self.source(zs, own), dst, self.z_send.at[zs, 1], self.z_recv.at[zs], (self.dp - 2, self.s))

    def across(self, zs, own=False):
        dst = self.block(zs, self.x, self.c, self.y)
        device = (self.z * 2 + 1 - self.x, self.s)
        return remote(self.source(zs, own, self.y), dst, self.x_send.at[zs], self.x_recv.at[zs], device)

    def across_in(self, zs):
        ref = self.block(zs, 1 - self.x, self.c, self.y)
        return remote(ref, ref, self.x_send.at[zs], self.x_recv.at[zs], (self.dp, self.s))

    def over(self, zs):
        ref = self.block(zs, 1 - self.x, self.c, self.y)
        return remote(ref, ref, self.y_send.at[zs], self.y_recv.at[zs], (self.dp, (1 - self.y) * 2 + self.c))

    def over_in(self, zs):
        ref = self.block(zs, 1 - self.x, self.c, 1 - self.y)
        return remote(ref, ref, self.y_send.at[zs], self.y_recv.at[zs], (self.dp, self.s))

    def share(self, kind, zs, core):
        if kind == 0:
            ref = self.block(zs, self.x, core)
        else:
            ref = self.block(zs, 1 - self.x, core, self.y if kind == 1 else 1 - self.y)
        j = kind * Z_CHIPS + zs
        return remote(ref, ref, self.c_send.at[j], self.c_recv.at[j], (self.dp, self.s + 1 - 2 * self.c))

    def each(self, k, what):
        if k == 0:
            what(self.z)
            return

        @pl.when(self.z >= k)
        def _():
            what(self.z - k)

        @pl.when(self.z + k < Z_CHIPS)
        def _():
            what(self.z + k)

    def stage(self, k):
        if k == 0:

            @pl.when(self.z < Z_CHIPS - 1)
            def _():
                self.up(self.z, True).start()

            @pl.when(self.z > 0)
            def _():
                self.down(self.z, True).start()

            self.across(self.z, True).start()
        elif k < Z_CHIPS:

            @pl.when(self.z >= k)
            def _():
                zs = self.z - k
                self.up(zs).wait_recv()

                @pl.when(self.z < Z_CHIPS - 1)
                def _():
                    self.up(zs).start()

                self.across(zs).start()
                self.share(0, zs, self.c).start()

            @pl.when(self.z + k < Z_CHIPS)
            def _():
                zs = self.z + k
                self.down(zs).wait_recv()

                @pl.when(self.z > 0)
                def _():
                    self.down(zs).start()

                self.across(zs).start()
                self.share(0, zs, self.c).start()

        if 1 <= k <= Z_CHIPS:

            def pass_x(zs):
                self.across_in(zs).wait_recv()
                self.over(zs).start()
                self.share(1, zs, self.c).start()

            self.each(k - 1, pass_x)
        if 2 <= k <= Z_CHIPS + 1:

            def pass_y(zs):
                self.over_in(zs).wait_recv()
                self.share(2, zs, self.c).start()

            self.each(k - 2, pass_y)

    stages = Z_CHIPS + 2

    def finish(self):
        for kind in range(3):
            for k in range(1 if kind == 0 else 0, Z_CHIPS):
                self.each(k, lambda zs, kind=kind: self.share(kind, zs, 1 - self.c).wait_recv())

    def settle(self):
        for k in range(Z_CHIPS):

            @pl.when((self.z >= k) & (self.z < Z_CHIPS - 1))
            def _():
                self.up(self.z - k, k == 0).wait_send()

            @pl.when((self.z + k < Z_CHIPS) & (self.z > 0))
            def _():
                self.down(self.z + k, k == 0).wait_send()

            self.each(k, lambda zs, k=k: self.across(zs, k == 0).wait_send())
            self.each(k, lambda zs: self.over(zs).wait_send())
            for kind in range(3):
                if kind > 0 or k > 0:
                    self.each(k, lambda zs, kind=kind: self.share(kind, zs, self.c).wait_send())


class Tokens:
    def __init__(self, long_ref, short_ref, out, send, recv, local):
        self.long_ref, self.short_ref, self.out, self.send, self.recv, self.local = long_ref, short_ref, out, send, recv, local
        self.dp, self.s = lax.axis_index("dp"), lax.axis_index("seq")

    def pieces(self, target, source):
        yield self.long_ref.at[target // 2, target % 2], self.out.at[source, pl.ds(0, 128)]
        yield self.short_ref.at[0, target], self.out.at[source, pl.ds(128, 64)]
        yield self.short_ref.at[1, target], self.out.at[source, pl.ds(192, 64)]

    def copies(self, k):
        target = (self.s + k) % 4
        for j, (src, dst) in enumerate(self.pieces(target, self.s)):
            yield remote(src, dst, self.send.at[k, j], self.recv.at[k, j], (self.dp, target))

    def own(self):
        for j, (src, dst) in enumerate(self.pieces(self.s, self.s)):
            yield pltpu.make_async_copy(src, dst, self.local.at[j])

    def start(self):
        for k in range(1, 4):
            for copy in self.copies(k):
                copy.start()
        for copy in self.own():
            copy.start()

    def finish(self):
        for copy in self.own():
            copy.wait()
        for k in range(1, 4):
            source = (self.s + 4 - k) % 4
            for j, (src, dst) in enumerate(self.pieces(self.s, source)):
                remote(src, dst, self.send.at[k, j], self.recv.at[k, j], (self.dp, self.s)).wait_recv()

    def settle(self):
        for k in range(1, 4):
            for copy in self.copies(k):
                copy.wait_send()


def gather_kernel(
    wide_ref,
    down_ref,
    vec_ref,
    long_in,
    short_in,
    long_cot,
    short_cot,
    qkv_out,
    wo_out,
    w1_out,
    w2_out,
    vec_out,
    tok_out,
    cot_out,
    own_wide,
    own_down,
    z_send,
    z_recv,
    x_send,
    x_recv,
    y_send,
    y_recv,
    c_send,
    c_recv,
    v_send,
    v_recv,
    t_send,
    t_recv,
    local,
):
    dp, s, z, x, y, c = place()
    greet()
    tokens = Tokens(long_in, short_in, tok_out, t_send.at[0], t_recv.at[0], local.at[0])
    cots = Tokens(long_cot, short_cot, cot_out, t_send.at[1], t_recv.at[1], local.at[1])
    tokens.start()
    own_wide[...] = wide_ref[...].astype(bf16)
    own_down[...] = down_ref[...].astype(bf16)

    def vec_copy(k, source, target):
        return remote(vec_ref, vec_out.at[source], v_send.at[k], v_recv.at[k], (target, s))

    sems = lambda i: [
        r.at[i] for r in (z_send, z_recv, x_send, x_recv, y_send, y_recv, c_send, c_recv)
    ]
    parts = [
        Part(own_wide.at[:, pl.ds(0, 3 * D)], qkv_out, sems(0)),
        Part(own_wide.at[:, pl.ds(3 * D, D)], wo_out, sems(1)),
        Part(own_wide.at[:, pl.ds(4 * D, FF)], w1_out, sems(2)),
        Part(own_down, w2_out, sems(3)),
    ]
    parts[0].stage(0)
    for k in range(1, 8):
        vec_copy(k, dp, (dp + k) % 8).start()
    own_copies = [
        pltpu.make_async_copy(part.own, part.out.at[dp], local.at[2, i]) for i, part in enumerate(parts)
    ]
    own_copies.append(pltpu.make_async_copy(vec_ref, vec_out.at[dp], local.at[2, 4]))
    for copy in own_copies:
        copy.start()
    for t in range(1, Part.stages + len(parts) - 1):
        for i, part in enumerate(parts):
            if 0 <= t - i < Part.stages:
                part.stage(t - i)
        if t == 4:
            cots.start()
    for copy in own_copies:
        copy.wait()
    for part in parts:
        part.finish()
    tokens.finish()
    cots.finish()
    for k in range(1, 8):
        vec_copy(k, (dp + 8 - k) % 8, dp).wait_recv()
    for k in range(1, 8):
        vec_copy(k, dp, (dp + k) % 8).wait_send()
    for part in parts:
        part.settle()
    tokens.settle()
    cots.settle()


def gather(wide_master, down_master, vec_block, long_in, short_in, long_cot, short_cot):
    any_spec = pl.BlockSpec(memory_space=pl.ANY)
    vmem = pl.BlockSpec(memory_space=pltpu.VMEM)
    shape = jax.ShapeDtypeStruct
    rows, down_rows = wide_master.shape[0], down_master.shape[0]
    dma = pltpu.SemaphoreType.DMA
    return pl.pallas_call(
        gather_kernel,
        in_specs=[vmem, vmem, vmem] + [any_spec] * 4,
        out_specs=[any_spec] * 7,
        out_shape=[
            shape((8, rows, 3 * D), bf16),
            shape((8, rows, D), bf16),
            shape((8, rows, FF), bf16),
            shape((8, down_rows, D), bf16),
            shape((8, 16, 128), f32),
            shape((4, 256, D), bf16),
            shape((4, 256, D), bf16),
        ],
        scratch_shapes=[
            pltpu.VMEM((rows, 4 * D + FF), bf16),
            pltpu.VMEM((down_rows, D), bf16),
            dma((4, 4, 2)),
            dma((4, 4)),
            dma((4, 4)),
            dma((4, 4)),
            dma((4, 4)),
            dma((4, 4)),
            dma((4, 12)),
            dma((4, 12)),
            dma((8,)),
            dma((8,)),
            dma((2, 4, 3)),
            dma((2, 4, 3)),
            dma((3, 5)),
        ],
        compiler_params=pltpu.CompilerParams(
            vmem_limit_bytes=VMEM_BYTES, collective_id=0, has_side_effects=True
        ),
        name="gather",
    )(wide_master, down_master, vec_block, long_in, short_in, long_cot, short_cot)


class Grad:
    def __init__(self, src, acc, cbuf, xbuf, ybuf, zbuf, fin, sems, order):
        self.src, self.acc, self.cbuf, self.xbuf, self.ybuf, self.zbuf, self.fin = src, acc, cbuf, xbuf, ybuf, zbuf, fin
        self.c_send, self.c_recv, self.x_send, self.x_recv, self.y_send, self.y_recv = sems[:6]
        self.z_send, self.z_recv, self.f_send, self.f_recv, self.local = sems[6:]
        self.order = order
        self.dp, self.s, self.z, self.x, self.y, self.c = place()
        self.rows, cols = src.shape[2:]
        self.half_rows, self.half_cols = self.rows // 2, cols // 2

    def cols(self, core):
        return pl.ds(pl.multiple_of(core * self.half_cols, 128), self.half_cols)

    def some(self, q):
        return pl.ds(pl.multiple_of(q * self.half_rows, 16), self.half_rows)

    def core_copy(self, j):
        xd = (1 - self.x) if j == 0 else self.x
        return remote(
            self.src.at[:, xd, :, self.cols(1 - self.c)],
            self.cbuf.at[:, xd],
            self.c_send.at[j],
            self.c_recv.at[j],
            (self.dp, self.s + 1 - 2 * self.c),
        )

    def own_copy(self, j):
        xd = (1 - self.x) if j == 0 else self.x
        return pltpu.make_async_copy(self.src.at[:, xd, :, self.cols(self.c)], self.acc.at[:, xd], self.local.at[j])

    def x_copy(self, zd):
        device = (self.z * 2 + 1 - self.x, self.s)
        return remote(
            self.acc.at[zd, 1 - self.x], self.xbuf.at[zd], self.x_send.at[zd], self.x_recv.at[zd], device
        )

    def y_copy(self, zd):
        device = (self.dp, (1 - self.y) * 2 + self.c)
        return remote(
            self.acc.at[zd, self.x, self.some(1 - self.y)],
            self.ybuf.at[zd],
            self.y_send.at[zd],
            self.y_recv.at[zd],
            device,
        )

    def z_copy(self, k):
        zd = (self.z + k) % Z_CHIPS
        src = self.acc.at[zd, self.x, self.some(self.y)] if self.order == "xyz" else self.acc.at[zd]
        return remote(
            src, self.zbuf.at[k], self.z_send.at[k], self.z_recv.at[k], (zd * 2 + self.x, self.s)
        )

    def fin_quarter(self, s):
        return self.fin.at[self.some(s // 2), self.cols(s % 2)]

    def fin_copy(self, k):
        return remote(
            self.fin_quarter(self.s),
            self.fin_quarter(self.s),
            self.f_send.at[k],
            self.f_recv.at[k],
            (self.dp, (self.s + k) % 4),
        )

    def fin_in(self, k):
        ref = self.fin_quarter((self.s + 4 - k) % 4)
        return remote(ref, ref, self.f_send.at[k], self.f_recv.at[k], (self.dp, self.s))

    def core_add(self, j):
        xd = (1 - self.x) if j == 0 else self.x
        self.core_copy(j).wait_recv()
        self.own_copy(j).wait()

        def one(zd, carry):
            self.acc[zd, xd] = (self.acc[zd, xd].astype(f32) + self.cbuf[zd, xd].astype(f32)).astype(bf16)
            return carry

        lax.fori_loop(0, Z_CHIPS, one, 0)

    def publish(self, total):
        self.fin[self.some(self.y), self.cols(self.c)] = total.astype(bf16)
        for k in range(1, 4):
            self.fin_copy(k).start()

    stages = 7

    def stage(self, i):
        if i == 0:
            for j in range(2):
                self.core_copy(j).start()
                self.own_copy(j).start()
        elif self.order == "xyz":
            if i == 1:
                self.core_add(0)
                for k in range(Z_CHIPS):
                    self.x_copy((self.z + k) % Z_CHIPS).start()
            elif i == 2:
                self.core_add(1)
            elif i == 3:
                for k in range(Z_CHIPS):
                    zd = (self.z + k) % Z_CHIPS
                    self.x_copy(zd).wait_recv()
                    self.acc[zd, self.x] = (self.acc[zd, self.x].astype(f32) + self.xbuf[zd].astype(f32)).astype(bf16)
                    self.y_copy(zd).start()
            elif i == 4:
                for k in (1, 2, 3, 0):
                    zd = (self.z + k) % Z_CHIPS
                    self.y_copy(zd).wait_recv()
                    rows = self.some(self.y)
                    self.acc[zd, self.x, rows] = (
                        self.acc[zd, self.x, rows].astype(f32) + self.ybuf[zd].astype(f32)
                    ).astype(bf16)
                    if k:
                        self.z_copy(k).start()
            elif i == 5:
                total = self.acc[self.z, self.x, self.some(self.y)].astype(f32)
                for k in range(1, Z_CHIPS):
                    self.z_copy(k).wait_recv()
                    total = total + self.zbuf[k].astype(f32)
                self.publish(total)
        else:
            if i == 1:
                self.core_add(0)
                self.core_add(1)
                for k in range(1, Z_CHIPS):
                    self.z_copy(k).start()
            elif i == 3:
                for k in range(1, Z_CHIPS):
                    self.z_copy(k).wait_recv()
                for xd in range(2):
                    total = self.acc[self.z, xd].astype(f32)
                    for k in range(1, Z_CHIPS):
                        total = total + self.zbuf[k, xd].astype(f32)
                    self.acc[self.z, xd] = total.astype(bf16)
                self.x_copy(self.z).start()
            elif i == 4:
                self.x_copy(self.z).wait_recv()
                total = self.acc[self.z, self.x].astype(f32) + self.xbuf[self.z].astype(f32)
                self.acc[self.z, self.x] = total.astype(bf16)
                self.y_copy(self.z).start()
            elif i == 5:
                self.y_copy(self.z).wait_recv()
                self.publish(self.acc[self.z, self.x, self.some(self.y)].astype(f32) + self.ybuf[self.z].astype(f32))
        if i == 6:
            for k in range(1, 4):
                self.fin_in(k).wait_recv()

    def settle(self):
        for j in range(2):
            self.core_copy(j).wait_send()
        for k in range(1, Z_CHIPS):
            self.z_copy(k).wait_send()
        for k in range(1, 4):
            self.fin_copy(k).wait_send()
        for k in range(Z_CHIPS if self.order == "xyz" else 1):
            self.x_copy((self.z + k) % Z_CHIPS).wait_send()
            self.y_copy((self.z + k) % Z_CHIPS).wait_send()


class Returns:
    def __init__(self, rows_ref, long_out, short_out, send, recv, local):
        self.rows_ref, self.long_out, self.short_out = rows_ref, long_out, short_out
        self.send, self.recv, self.local = send, recv, local
        self.dp, self.s = lax.axis_index("dp"), lax.axis_index("seq")

    def pieces(self, target, source):
        yield self.rows_ref.at[target, pl.ds(0, 128)], self.long_out.at[source // 2, source % 2]
        yield self.rows_ref.at[target, pl.ds(128, 64)], self.short_out.at[0, source]
        yield self.rows_ref.at[target, pl.ds(192, 64)], self.short_out.at[1, source]

    copies, own, start, finish, settle = Tokens.copies, Tokens.own, Tokens.start, Tokens.finish, Tokens.settle


class Sums:
    def __init__(self, src, sbuf, part, dbuf, out, sems):
        self.src, self.sbuf, self.part, self.dbuf, self.out = src, sbuf, part, dbuf, out
        self.s_send, self.s_recv, self.d_send, self.d_recv = sems
        self.dp, self.s = lax.axis_index("dp"), lax.axis_index("seq")

    def s_copy(self, k, source):
        return remote(self.src, self.sbuf.at[source], self.s_send.at[k], self.s_recv.at[k], (self.dp, (self.s + k) % 4))

    def d_copy(self, k, source):
        target = (self.dp + k) % 8
        return remote(
            self.part.at[target], self.dbuf.at[source], self.d_send.at[k], self.d_recv.at[k], (target, self.s)
        )

    def stage(self, i):
        if i == 0:
            for k in range(1, 4):
                self.s_copy(k, self.s).start()
            self.sbuf[self.s] = self.src[...]
        elif i == 1:
            for k in range(1, 4):
                self.s_copy(k, (self.s + 4 - k) % 4).wait_recv()
            self.part[...] = (self.sbuf[0] + self.sbuf[1]) + (self.sbuf[2] + self.sbuf[3])
            for k in range(1, 8):
                self.d_copy(k, self.dp).start()
            self.dbuf[self.dp] = self.part[self.dp]
        elif i == 2:
            for k in range(1, 8):
                self.d_copy(k, (self.dp + 8 - k) % 8).wait_recv()
            total = self.dbuf[0]
            for d in range(1, 8):
                total = total + self.dbuf[d]
            self.out[...] = total

    def settle(self):
        for k in range(1, 4):
            self.s_copy(k, self.s).wait_send()
        for k in range(1, 8):
            self.d_copy(k, self.dp).wait_send()


ORDERS = ("zxy", "xyz", "xyz", "xyz")


def reduce_kernel(count, *refs):
    grads, refs = refs[:count], refs[count:]
    sums_ref, out_rows, back_rows, refs = refs[0], refs[1], refs[2], refs[3:]
    fins, refs = refs[:count], refs[count:]
    (sums_out, short_out, long_out, short_back, long_back), refs = refs[:5], refs[5:]
    bufs, refs = refs[: 5 * count], refs[5 * count :]
    (sbuf, part, dbuf), refs = refs[:3], refs[3:]
    sems, refs = refs[:11], refs[11:]
    s_sems, (t_send, t_recv, local) = refs[:4], refs[4:]
    greet()
    pieces = []
    for i in range(count):
        acc, cbuf, xbuf, ybuf, zbuf = bufs[5 * i : 5 * i + 5]
        pieces.append(
            Grad(grads[i], acc, cbuf, xbuf, ybuf, zbuf, fins[i], [r.at[i] for r in sems], ORDERS[i])
        )
    sums = Sums(sums_ref, sbuf, part, dbuf, sums_out, s_sems)
    outs = Returns(out_rows, long_out, short_out, t_send.at[0], t_recv.at[0], local.at[0])
    backs = Returns(back_rows, long_back, short_back, t_send.at[1], t_recv.at[1], local.at[1])
    outs.start()
    for t in range(Grad.stages + count - 1):
        for i, piece in enumerate(pieces):
            if 0 <= t - i < Grad.stages:
                piece.stage(t - i)
        if t < 3:
            sums.stage(t)
        if t == 2:
            backs.start()
    outs.finish()
    backs.finish()
    for piece in pieces:
        piece.settle()
    sums.settle()
    outs.settle()
    backs.settle()


def reduce_all(grads, sums, out_rows, back_rows):
    count = len(grads)
    any_spec = pl.BlockSpec(memory_space=pl.ANY)
    vmem = pl.BlockSpec(memory_space=pltpu.VMEM)
    shape = jax.ShapeDtypeStruct
    dma = pltpu.SemaphoreType.DMA
    bufs = []
    for g, order in zip(grads, ORDERS):
        rows, cols = g.shape[2:]
        half, cut = cols // 2, rows // 2
        bufs += [
            pltpu.VMEM((4, 2, rows, half), bf16),
            pltpu.VMEM((4, 2, rows, half), bf16),
            pltpu.VMEM((4, rows, half), bf16),
            pltpu.VMEM((4, cut, half), bf16),
            pltpu.VMEM((4, cut, half) if order == "xyz" else (4, 2, rows, half), bf16),
        ]
    return pl.pallas_call(
        lambda *refs: reduce_kernel(count, *refs),
        in_specs=[any_spec] * count + [vmem, any_spec, any_spec],
        out_specs=[vmem] * count + [vmem] + [any_spec] * 4,
        out_shape=[shape(g.shape[2:], bf16) for g in grads]
        + [
            shape((16, 128), f32),
            shape((2, 4, 64, D), bf16),
            shape((2, 2, 128, D), bf16),
            shape((2, 4, 64, D), bf16),
            shape((2, 2, 128, D), bf16),
        ],
        scratch_shapes=bufs
        + [pltpu.VMEM((4, 8, 16, 128), f32), pltpu.VMEM((8, 16, 128), f32), pltpu.VMEM((8, 16, 128), f32)]
        + [dma((count, 2))] * 2
        + [dma((count, 4))] * 8
        + [dma((count, 2))]
        + [dma((4,)), dma((4,)), dma((8,)), dma((8,))]
        + [dma((2, 4, 3)), dma((2, 4, 3)), dma((2, 3))],
        compiler_params=pltpu.CompilerParams(
            vmem_limit_bytes=VMEM_BYTES, collective_id=1, has_side_effects=True
        ),
        name="reduce",
    )(*grads, sums, out_rows, back_rows)


def transpose_dot(left, right):
    return jnp.einsum("ra,rb->ab", left, right, preferred_element_type=f32)


def right_dot(left, right):
    return jnp.einsum("ra,ba->rb", left, right, preferred_element_type=f32)


def flip(v, axis, bit):
    n = lax.axis_size(axis)
    return lax.ppermute(v, axis, [(i, i ^ bit) for i in range(n)])


def half_of(v, dim, which):
    size = v.shape[dim] // 2
    return lax.dynamic_slice_in_dim(v, which * size, size, dim)


def halve(v, axis, bit, dim):
    mine = (lax.axis_index(axis) // bit) % 2
    other = flip(half_of(v, dim, 1 - mine), axis, bit)
    return (half_of(v, dim, mine).astype(f32) + other.astype(f32)).astype(bf16)


def double(v, axis, bit, dim):
    mine = (lax.axis_index(axis) // bit) % 2
    other = flip(v, axis, bit)
    return jnp.where(
        mine == 0, jnp.concatenate([v, other], axis=dim), jnp.concatenate([other, v], axis=dim)
    )


def reduce_rows(grad):
    rows, cols = grad.shape
    dp = lax.axis_size("dp")
    v = grad.reshape(dp, rows // dp, cols)
    v = halve(v, "seq", 1, 2)
    v = halve(v, "seq", 2, 2)
    bit = 1
    while bit < dp:
        blocks = v.shape[0]
        v = v.reshape(blocks // 2, 2, v.shape[1], v.shape[2]) if v.ndim == 3 else v
        v = halve(v, "dp", bit, 1)[:, 0]
        bit *= 2
    v = v[0]
    v = double(v, "seq", 2, 1)
    v = double(v, "seq", 1, 1)
    return v.astype(f32)


def update(master, reduced_grad, moment, average):
    step_grad = reduced_grad + decay_weight * master
    velocity = momentum_rate * moment + step_grad
    updated = master - learning_rate * (step_grad + momentum_rate * velocity)
    averaged = average_rate * average + (1.0 - average_rate) * updated
    return (velocity, averaged, updated, updated.astype(jnp.bfloat16))


def spread_rows(long_part, short_part):
    long_blocks = long_part.reshape(4, 128, D)
    short_blocks = jnp.transpose(short_part, (1, 0, 2, 3)).reshape(4, 128, D)
    return jnp.concatenate([long_blocks, short_blocks], axis=1)


def exchange(v):
    return lax.all_to_all(v, "seq", split_axis=0, concat_axis=0, tiled=True)


def collect_rows(v):
    long_part = v[:, :128].reshape(2, 2, 128, D)
    short_part = jnp.transpose(v[:, 128:].reshape(4, 2, 64, D), (1, 0, 2, 3))
    return short_part, long_part


def body(
    short_in,
    long_in,
    short_cot,
    long_cot,
    short_len,
    long_len,
    wide_master,
    down_master,
    vector_master,
    wide_moment,
    down_moment,
    vector_moment,
    wide_average,
    down_average,
    vector_average,
):
    s = lax.axis_index("seq")
    lens = jnp.stack([long_len[s // 2, 0, s % 2], short_len[0, 0, s], short_len[1, 0, s]])
    if lax.axis_size("dp") == 8:
        vec_own = jnp.transpose(vector_master).astype(bf16).astype(f32)
        vec_block = jnp.pad(vec_own, ((0, 4), (0, 128 - vec_own.shape[1])))
        w_qkv, w_o, w_1, w_2, vec_blocks, tokens, cotangent = gather(
            wide_master, down_master, vec_block, long_in, short_in, long_cot, short_cot
        )
        w_qkv, w_o, w_1, w_2 = [w.reshape(-1, w.shape[2]) for w in (w_qkv, w_o, w_1, w_2)]
        vec = jnp.transpose(vec_blocks[:, :12, : vec_own.shape[1]], (1, 0, 2)).reshape(12, D)
    else:
        tokens = exchange(spread_rows(long_in, short_in))
        cotangent = exchange(spread_rows(long_cot, short_cot))
        wide_w = lax.all_gather(wide_master.astype(bf16), "dp", axis=0, tiled=True)
        w_2 = lax.all_gather(down_master.astype(bf16), "dp", axis=0, tiled=True)
        vector_w = lax.all_gather(vector_master.astype(bf16), "dp", axis=0, tiled=True)
        vec = jnp.transpose(vector_w.astype(f32))
        w_qkv = wide_w[:, : 3 * D]
        w_o = wide_w[:, 3 * D : 4 * D]
        w_1 = wide_w[:, 4 * D :]

    rows = tokens.reshape(1024, D)
    proj_bias = jnp.concatenate([vec[0], jnp.zeros((D,), f32), vec[1]])
    qkv = (jnp.dot(rows, w_qkv, preferred_element_type=f32) + proj_bias).astype(bf16)
    qkv = qkv.reshape(4, 256, 3 * D)
    attended, long_probs, short_probs = attn_forward(lens, qkv)
    flat_attended = attended.reshape(1024, D)
    out, y1b, act, dfb, dub, dab, dob, dh, sums = middle(
        lens, flat_attended, rows, cotangent.reshape(1024, D), w_o, w_1, w_2, vec
    )
    d_down = transpose_dot(act, dfb).astype(bf16)
    d_one = transpose_dot(y1b, dub).astype(bf16)
    d_o = transpose_dot(flat_attended, dab).astype(bf16)
    dq, dk, dv, qv_sums = attn_backward(
        lens, qkv, dob.reshape(4, 256, D), attended, long_probs, short_probs
    )
    d_qkv = jnp.concatenate([dq, dk, dv], axis=2).reshape(1024, 3 * D)
    d_wqkv = transpose_dot(rows, d_qkv).astype(bf16)
    back = (dh + right_dot(d_qkv, w_qkv)).astype(bf16).reshape(4, 256, D)

    vector_total = jnp.concatenate([qv_sums[:2], sums[2:12]], axis=0)
    own_rows = vector_master.shape[0]
    if lax.axis_size("dp") == 8:
        blocks = lambda g: g.reshape(4, 2, g.shape[0] // 8, g.shape[1])
        spread = jnp.transpose(vector_total.reshape(12, 8, own_rows), (1, 0, 2))
        spread = jnp.pad(spread, ((0, 0), (0, 4), (0, 128 - own_rows)))
        down_low, one_low, o_low, qkv_low, sums_own, short_out, long_out, short_back, long_back = reduce_all(
            [blocks(g) for g in (d_down, d_one, d_o, d_wqkv)], spread, out.reshape(4, 256, D), back
        )
        vector_reduced = jnp.transpose(sums_own[:12, :own_rows])
        wide_reduced = jnp.concatenate([qkv_low, o_low, one_low], axis=1).astype(f32)
        down_reduced = down_low.astype(f32)
    else:
        vector_sum = jnp.transpose(lax.psum(vector_total, ("dp", "seq")))
        vector_reduced = lax.dynamic_slice_in_dim(vector_sum, lax.axis_index("dp") * own_rows, own_rows, 0)
        wide_reduced = jnp.concatenate([reduce_rows(d_wqkv), reduce_rows(d_o), reduce_rows(d_one)], axis=1)
        down_reduced = reduce_rows(d_down)
        short_out, long_out = collect_rows(exchange(out.reshape(4, 256, D)))
        short_back, long_back = collect_rows(exchange(back))
    wide_new = update(wide_master, wide_reduced, wide_moment, wide_average)
    down_new = update(down_master, down_reduced, down_moment, down_average)
    vector_new = update(vector_master, vector_reduced, vector_moment, vector_average)
    return (
        short_out,
        long_out,
        short_back,
        long_back,
        wide_reduced,
        down_reduced,
        vector_reduced,
        wide_new[0],
        down_new[0],
        vector_new[0],
        wide_new[1],
        down_new[1],
        vector_new[1],
        wide_new[2],
        down_new[2],
        vector_new[2],
        wide_new[3],
        down_new[3],
        vector_new[3],
    )


def solution(mesh):
    tok = P(None, "dp", "seq", None)
    lengths = P(None, "dp", None)
    state = P("dp", None)
    return jax.shard_map(
        body,
        mesh=mesh,
        in_specs=(tok,) * 4 + (lengths,) * 2 + (state,) * 9,
        out_specs=(tok,) * 4 + (state,) * 15,
        check_vma=False,
    )
```

```python
import jax
import jax.numpy as jnp
from jax import lax
from jax.experimental import pallas as pl
from jax.experimental.pallas import tpu as pltpu
from jax.sharding import PartitionSpec as P

D = 768
HEAD_DIM = 64
FF = 3072
PAIR = 128
LONG_L = 512
SHORT_L = 256
VMEM_BYTES = 56 * 1024 * 1024

norm_eps = 1e-12
mask_fill = -10000.0
learning_rate = 0.0002
momentum_rate = 0.9
decay_weight = 0.0001
average_rate = 0.9
score_scale = HEAD_DIM ** (-0.5)
f32 = jnp.float32
bf16 = jnp.bfloat16


def params():
    return pltpu.CompilerParams(vmem_limit_bytes=VMEM_BYTES)


def dot_nn(a, b):
    return lax.dot_general(a, b, (((1,), (0,)), ((), ())), preferred_element_type=f32)


def dot_nt(a, b):
    return lax.dot_general(a, b, (((1,), (1,)), ((), ())), preferred_element_type=f32)


SEQS = ((0, 128, LONG_L, 0), (128, 64, SHORT_L, 1), (192, 64, SHORT_L, 2))


def attend(q, k, v, limit, keep_probs):
    length = q.shape[0]
    v_t = jnp.transpose(v)
    head_lane = lax.broadcasted_iota(jnp.int32, (length, PAIR), 1) // HEAD_DIM
    live = lax.broadcasted_iota(jnp.int32, (length, length), 0) < limit
    parts = []
    for h in range(2):
        k_h = jnp.where(head_lane == h, k, jnp.zeros_like(k))
        scores = jnp.where(live, dot_nt(k_h, q) * score_scale, mask_fill)
        top = jnp.max(scores, axis=0, keepdims=True)
        exponent = jnp.exp(scores - top)
        total = jnp.sum(exponent, axis=0, keepdims=True)
        probs = (exponent * (1.0 / total)).astype(bf16)
        keep_probs(h, probs)
        parts.append(dot_nn(v_t[h * HEAD_DIM : (h + 1) * HEAD_DIM], probs))
    return jnp.transpose(jnp.concatenate(parts, axis=0)).astype(bf16)


def attn_forward_kernel(lens_ref, q_ref, k_ref, v_ref, o_ref, long_ref, short_ref):
    for first, rows, length, index in SEQS:
        q, k, v = [r[:, first : first + rows, :].reshape(length, PAIR) for r in (q_ref, k_ref, v_ref)]

        def keep_probs(h, probs, index=index):
            if index == 0:
                long_ref[h] = probs
            else:
                short_ref[h, index - 1] = probs

        o = attend(q, k, v, lens_ref[index], keep_probs)
        o_ref[:, first : first + rows, :] = o.reshape(4, rows, PAIR)


def attn_forward(lens, qkv):
    pairs = D // PAIR
    col = lambda base: pl.BlockSpec((4, 256, PAIR), lambda i, base=base: (0, 0, base + i))
    return pl.pallas_call(
        attn_forward_kernel,
        grid=(pairs,),
        in_specs=[
            pl.BlockSpec(memory_space=pltpu.SMEM),
            col(0),
            col(pairs),
            col(2 * pairs),
        ],
        out_specs=[
            pl.BlockSpec((4, 256, PAIR), lambda i: (0, 0, i)),
            pl.BlockSpec((2, LONG_L, LONG_L), lambda i: (i, 0, 0)),
            pl.BlockSpec((2, 2, SHORT_L, SHORT_L), lambda i: (i, 0, 0, 0)),
        ],
        out_shape=[
            jax.ShapeDtypeStruct((4, 256, D), bf16),
            jax.ShapeDtypeStruct((2 * pairs, LONG_L, LONG_L), bf16),
            jax.ShapeDtypeStruct((2 * pairs, 2, SHORT_L, SHORT_L), bf16),
        ],
        compiler_params=params(),
        name="attn_forward",
    )(lens, qkv, qkv, qkv)


def attn_backward_kernel(
    lens_ref, q_ref, k_ref, v_ref, do_ref, o_ref, long_ref, short_ref, dq_ref, dk_ref, dv_ref, sum_ref
):
    sum_q = jnp.zeros((1, PAIR), f32)
    sum_v = jnp.zeros((1, PAIR), f32)
    for first, rows, length, index in SEQS:
        q = q_ref[:, first : first + rows, :].reshape(length, PAIR)
        k = k_ref[:, first : first + rows, :].reshape(length, PAIR)
        v = v_ref[:, first : first + rows, :].reshape(length, PAIR)
        do = do_ref[:, first : first + rows, :].reshape(length, PAIR)
        o = o_ref[:, first : first + rows, :].reshape(length, PAIR)
        k_t = jnp.transpose(k)
        inner = jnp.transpose(do.astype(f32) * o.astype(f32))
        head_lane = lax.broadcasted_iota(jnp.int32, (length, PAIR), 1) // HEAD_DIM
        live = lax.broadcasted_iota(jnp.int32, (length, length), 0) < lens_ref[index]
        dq_parts = []
        dk = jnp.zeros((length, PAIR), f32)
        dv = jnp.zeros((length, PAIR), f32)
        for h in range(2):
            keep = head_lane == h
            v_h = jnp.where(keep, v, jnp.zeros_like(v))
            do_h = jnp.where(keep, do, jnp.zeros_like(do))
            q_h = jnp.where(keep, q, jnp.zeros_like(q))
            probs = long_ref[h] if index == 0 else short_ref[h, index - 1]
            delta = jnp.sum(inner[h * HEAD_DIM : (h + 1) * HEAD_DIM], axis=0, keepdims=True)
            d_probs = dot_nt(v_h, do)
            d_scores = jnp.where(live, probs.astype(f32) * (d_probs - delta), 0.0).astype(bf16)
            dv = dv + dot_nn(probs, do_h)
            dk = dk + dot_nn(d_scores, q_h)
            dq_parts.append(dot_nn(k_t[h * HEAD_DIM : (h + 1) * HEAD_DIM], d_scores))
        dq = (jnp.transpose(jnp.concatenate(dq_parts, axis=0)) * score_scale).astype(bf16)
        dk = (dk * score_scale).astype(bf16)
        dv = dv.astype(bf16)
        sum_q = sum_q + jnp.sum(dq.astype(f32), axis=0, keepdims=True)
        sum_v = sum_v + jnp.sum(dv.astype(f32), axis=0, keepdims=True)
        dq_ref[:, first : first + rows, :] = dq.reshape(4, rows, PAIR)
        dk_ref[:, first : first + rows, :] = dk.reshape(4, rows, PAIR)
        dv_ref[:, first : first + rows, :] = dv.reshape(4, rows, PAIR)
    sum_ref[0:1, :] = sum_q
    sum_ref[1:2, :] = sum_v
    sum_ref[2:8, :] = jnp.zeros((6, PAIR), f32)


def attn_backward(lens, qkv, d_attended, attended, long_probs, short_probs):
    pairs = D // PAIR
    col = lambda base: pl.BlockSpec((4, 256, PAIR), lambda i, base=base: (0, 0, base + i))
    return pl.pallas_call(
        attn_backward_kernel,
        grid=(pairs,),
        in_specs=[
            pl.BlockSpec(memory_space=pltpu.SMEM),
            col(0),
            col(pairs),
            col(2 * pairs),
            col(0),
            col(0),
            pl.BlockSpec((2, LONG_L, LONG_L), lambda i: (i, 0, 0)),
            pl.BlockSpec((2, 2, SHORT_L, SHORT_L), lambda i: (i, 0, 0, 0)),
        ],
        out_specs=[col(0), col(0), col(0), pl.BlockSpec((8, PAIR), lambda i: (0, i))],
        out_shape=[jax.ShapeDtypeStruct((4, 256, D), bf16)] * 3 + [jax.ShapeDtypeStruct((8, D), f32)],
        compiler_params=params(),
        name="attn_backward",
    )(lens, qkv, qkv, qkv, d_attended, attended, long_probs, short_probs)


def gelu_pair(u):
    a = jnp.abs(u)
    t = 1.0 / (1.0 + (0.3275911 * 0.5**0.5) * a)
    e = jnp.exp(-0.5 * u * u)
    poly = t * (0.254829592 + t * (-0.284496736 + t * (1.421413741 + t * (-1.453152027 + t * 1.061405429))))
    tail = 0.5 * poly * e
    cdf = jnp.where(u < 0.0, tail, 1.0 - tail)
    pdf = e * (0.5 / jnp.pi) ** 0.5
    return u * cdf, cdf + u * pdf


def row_mean(v):
    return jnp.mean(v, axis=-1, keepdims=True)


def middle_kernel(
    lens_ref,
    o_ref,
    x_ref,
    cot_ref,
    wo_ref,
    w1_ref,
    w2_ref,
    vec_ref,
    out_ref,
    y1b_ref,
    g_ref,
    dfb_ref,
    dub_ref,
    dab_ref,
    dob_ref,
    dh_ref,
    sum_ref,
    slope_ref,
):
    r = pl.program_id(0)
    rows = o_ref.shape[0]

    @pl.when(r == 0)
    def _():
        sum_ref[...] = jnp.zeros_like(sum_ref)

    def add(index, v):
        sum_ref[index : index + 1, :] += jnp.sum(v, axis=0, keepdims=True)

    vec = lambda i: vec_ref[i : i + 1, :]
    h = x_ref[...].astype(f32) + (dot_nn(o_ref[...], wo_ref[...]) + vec(2))
    centred = h - row_mean(h)
    inv1 = lax.rsqrt(row_mean(centred * centred) + norm_eps)
    norm1 = centred * inv1
    y1 = norm1 * vec(3) + vec(4)
    y1b = y1.astype(bf16)
    y1b_ref[...] = y1b
    z = y1 + vec(5)
    for c in range(FF // D):
        cols = slice(c * D, (c + 1) * D)
        act, slope = gelu_pair(dot_nn(y1b, w1_ref[:, cols]) + vec(8 + c))
        act = act.astype(bf16)
        g_ref[:, cols] = act
        slope_ref[:, cols] = slope
        z = z + dot_nn(act, w2_ref[cols, :])
    centred2 = z - row_mean(z)
    inv2 = lax.rsqrt(row_mean(centred2 * centred2) + norm_eps)
    norm2 = centred2 * inv2
    out_ref[...] = (norm2 * vec(6) + vec(7)).astype(bf16)

    j = lax.broadcasted_iota(jnp.int32, (rows, 1), 0)
    long_end = lens_ref[0] - r * 128
    short_end = [lens_ref[i] - r * 64 + first for i, first in ((1, 128), (2, 192))]
    live = j < jnp.where(j < 128, long_end, jnp.where(j < 192, short_end[0], short_end[1]))
    dr = jnp.where(live, cot_ref[...].astype(f32), 0.0)
    e2 = dr * vec(6)
    dz = inv2 * (e2 - row_mean(e2) - norm2 * row_mean(e2 * norm2))
    dfb = dz.astype(bf16)
    dfb_ref[...] = dfb
    add(6, dr * norm2)
    add(7, dr)
    add(5, dfb.astype(f32))
    dy1 = dz
    for c in range(FF // D):
        cols = slice(c * D, (c + 1) * D)
        dub = (dot_nt(dfb, w2_ref[cols, :]) * slope_ref[:, cols]).astype(bf16)
        dub_ref[:, cols] = dub
        add(8 + c, dub.astype(f32))
        dy1 = dy1 + dot_nt(dub, w1_ref[:, cols])
    add(3, dy1 * norm1)
    add(4, dy1)
    e1 = dy1 * vec(3)
    dh = inv1 * (e1 - row_mean(e1) - norm1 * row_mean(e1 * norm1))
    dab = dh.astype(bf16)
    dh_ref[...] = dh
    dab_ref[...] = dab
    add(2, dab.astype(f32))
    dob_ref[...] = dot_nt(dab, wo_ref[...]).astype(bf16)


def middle(lens, attended, tokens, cotangent, w_o, w_1, w_2, vec):
    n = tokens.shape[0]
    rows = 256
    row = lambda width: pl.BlockSpec((rows, width), lambda i: (i, 0))
    whole = lambda a: pl.BlockSpec(a.shape, lambda i: (0, 0), pipeline_mode=pl.Buffered(1))
    shape = jax.ShapeDtypeStruct
    return pl.pallas_call(
        middle_kernel,
        grid=(n // rows,),
        in_specs=[
            pl.BlockSpec(memory_space=pltpu.SMEM),
            row(D),
            row(D),
            row(D),
            whole(w_o),
            whole(w_1),
            whole(w_2),
            whole(vec),
        ],
        out_specs=[
            row(D),
            row(D),
            row(FF),
            row(D),
            row(FF),
            row(D),
            row(D),
            row(D),
            pl.BlockSpec((16, D), lambda i: (0, 0)),
        ],
        out_shape=[
            shape((n, D), bf16),
            shape((n, D), bf16),
            shape((n, FF), bf16),
            shape((n, D), bf16),
            shape((n, FF), bf16),
            shape((n, D), bf16),
            shape((n, D), bf16),
            shape((n, D), f32),
            shape((16, D), f32),
        ],
        scratch_shapes=[pltpu.VMEM((rows, FF), f32)],
        compiler_params=params(),
        name="middle",
    )(lens, attended, tokens, cotangent, w_o, w_1, w_2, vec)


MESH = pl.DeviceIdType.MESH
Z_CHIPS = 4


def place():
    dp = lax.axis_index("dp")
    s = lax.axis_index("seq")
    return dp, s, dp // 2, dp % 2, s // 2, s % 2


def remote(src, dst, send, recv, device):
    return pltpu.make_async_remote_copy(
        src_ref=src, dst_ref=dst, send_sem=send, recv_sem=recv, device_id=device, device_id_type=MESH
    )


def greet():
    dp, s = lax.axis_index("dp"), lax.axis_index("seq")
    barrier = pltpu.get_barrier_semaphore()
    for k in range(1, 8):
        pl.semaphore_signal(barrier, inc=1, device_id=((dp + k) % 8, s), device_id_type=MESH)
    for k in range(1, 4):
        pl.semaphore_signal(barrier, inc=1, device_id=(dp, (s + k) % 4), device_id_type=MESH)
    pl.semaphore_wait(barrier, 10)


class Part:
    def __init__(self, own, out, sems, direct=False):
        self.own, self.out, self.direct = own, out, direct
        self.z_send, self.z_recv, self.x_send, self.x_recv, self.y_send, self.y_recv, self.c_send, self.c_recv = sems
        self.dp, self.s, self.z, self.x, self.y, self.c = place()
        self.rows, cols = own.shape
        self.half_rows, self.half_cols = self.rows // 2, cols // 2

    def cols(self, core):
        return pl.ds(pl.multiple_of(core * self.half_cols, 128), self.half_cols)

    def some(self, q):
        return pl.ds(pl.multiple_of(q * self.half_rows, 16), self.half_rows)

    def block(self, zs, x, core, q=None):
        rows = slice(None) if q is None else self.some(q)
        return self.out.at[zs * 2 + x, rows, self.cols(core)]

    def source(self, zs, own, q=None):
        if own:
            rows = slice(None) if q is None else self.some(q)
            return self.own.at[rows, self.cols(self.c)]
        return self.block(zs, self.x, self.c, q)

    def up(self, zs, own=False):
        dst = self.block(zs, self.x, self.c)
        return remote(self.source(zs, own), dst, self.z_send.at[zs, 0], self.z_recv.at[zs], (self.dp + 2, self.s))

    def down(self, zs, own=False):
        dst = self.block(zs, self.x, self.c)
        return remote(self.source(zs, own), dst, self.z_send.at[zs, 1], self.z_recv.at[zs], (self.dp - 2, self.s))

    def across(self, zs, own=False):
        q = None if self.direct else self.y
        dst = self.block(zs, self.x, self.c, q)
        device = (self.z * 2 + 1 - self.x, self.s)
        return remote(self.source(zs, own, q), dst, self.x_send.at[zs], self.x_recv.at[zs], device)

    def across_in(self, zs):
        ref = self.block(zs, 1 - self.x, self.c, None if self.direct else self.y)
        return remote(ref, ref, self.x_send.at[zs], self.x_recv.at[zs], (self.dp, self.s))

    def over(self, zs):
        ref = self.block(zs, 1 - self.x, self.c, self.y)
        return remote(ref, ref, self.y_send.at[zs], self.y_recv.at[zs], (self.dp, (1 - self.y) * 2 + self.c))

    def over_in(self, zs):
        ref = self.block(zs, 1 - self.x, self.c, 1 - self.y)
        return remote(ref, ref, self.y_send.at[zs], self.y_recv.at[zs], (self.dp, self.s))

    def share(self, kind, zs, core):
        if kind == 0:
            ref = self.block(zs, self.x, core)
        else:
            q = self.y if kind == 1 else 1 - self.y
            ref = self.block(zs, 1 - self.x, core, None if self.direct else q)
        j = kind * Z_CHIPS + zs
        return remote(ref, ref, self.c_send.at[j], self.c_recv.at[j], (self.dp, self.s + 1 - 2 * self.c))

    def each(self, k, what):
        if k == 0:
            what(self.z)
            return

        @pl.when(self.z >= k)
        def _():
            what(self.z - k)

        @pl.when(self.z + k < Z_CHIPS)
        def _():
            what(self.z + k)

    def stage(self, k):
        if k == 0:

            @pl.when(self.z < Z_CHIPS - 1)
            def _():
                self.up(self.z, True).start()

            @pl.when(self.z > 0)
            def _():
                self.down(self.z, True).start()

            self.across(self.z, True).start()
        elif k < Z_CHIPS:

            @pl.when(self.z >= k)
            def _():
                zs = self.z - k
                self.up(zs).wait_recv()

                @pl.when(self.z < Z_CHIPS - 1)
                def _():
                    self.up(zs).start()

                self.across(zs).start()
                self.share(0, zs, self.c).start()

            @pl.when(self.z + k < Z_CHIPS)
            def _():
                zs = self.z + k
                self.down(zs).wait_recv()

                @pl.when(self.z > 0)
                def _():
                    self.down(zs).start()

                self.across(zs).start()
                self.share(0, zs, self.c).start()

        if 1 <= k <= Z_CHIPS:

            def pass_x(zs):
                self.across_in(zs).wait_recv()
                if not self.direct:
                    self.over(zs).start()
                self.share(1, zs, self.c).start()

            self.each(k - 1, pass_x)
        if 2 <= k <= Z_CHIPS + 1 and not self.direct:

            def pass_y(zs):
                self.over_in(zs).wait_recv()
                self.share(2, zs, self.c).start()

            self.each(k - 2, pass_y)

    stages = Z_CHIPS + 2

    def finish(self):
        for kind in range(2 if self.direct else 3):
            for k in range(1 if kind == 0 else 0, Z_CHIPS):
                self.each(k, lambda zs, kind=kind: self.share(kind, zs, 1 - self.c).wait_recv())

    def settle(self):
        for k in range(Z_CHIPS):

            @pl.when((self.z >= k) & (self.z < Z_CHIPS - 1))
            def _():
                self.up(self.z - k, k == 0).wait_send()

            @pl.when((self.z + k < Z_CHIPS) & (self.z > 0))
            def _():
                self.down(self.z + k, k == 0).wait_send()

            self.each(k, lambda zs, k=k: self.across(zs, k == 0).wait_send())
            if not self.direct:
                self.each(k, lambda zs: self.over(zs).wait_send())
            for kind in range(2 if self.direct else 3):
                if kind > 0 or k > 0:
                    self.each(k, lambda zs, kind=kind: self.share(kind, zs, self.c).wait_send())


class Tokens:
    def __init__(self, long_ref, short_ref, out, send, recv, local):
        self.long_ref, self.short_ref, self.out, self.send, self.recv, self.local = long_ref, short_ref, out, send, recv, local
        self.dp, self.s = lax.axis_index("dp"), lax.axis_index("seq")

    def pieces(self, target, source):
        yield self.long_ref.at[target // 2, target % 2], self.out.at[source, pl.ds(0, 128)]
        yield self.short_ref.at[0, target], self.out.at[source, pl.ds(128, 64)]
        yield self.short_ref.at[1, target], self.out.at[source, pl.ds(192, 64)]

    def copies(self, k):
        target = (self.s + k) % 4
        for j, (src, dst) in enumerate(self.pieces(target, self.s)):
            yield remote(src, dst, self.send.at[k, j], self.recv.at[k, j], (self.dp, target))

    def own(self):
        for j, (src, dst) in enumerate(self.pieces(self.s, self.s)):
            yield pltpu.make_async_copy(src, dst, self.local.at[j])

    def start(self):
        for k in range(1, 4):
            for copy in self.copies(k):
                copy.start()
        for copy in self.own():
            copy.start()

    def finish(self):
        for copy in self.own():
            copy.wait()
        for k in range(1, 4):
            source = (self.s + 4 - k) % 4
            for j, (src, dst) in enumerate(self.pieces(self.s, source)):
                remote(src, dst, self.send.at[k, j], self.recv.at[k, j], (self.dp, self.s)).wait_recv()

    def settle(self):
        for k in range(1, 4):
            for copy in self.copies(k):
                copy.wait_send()


def forward_kernel(
    lens_ref,
    wide_ref,
    down_ref,
    vec_ref,
    long_in,
    short_in,
    long_cot,
    short_cot,
    qkv_w_out,
    wo_out,
    w1_out,
    w2_out,
    vec_out,
    tok_out,
    cot_out,
    qkv_out,
    att_out,
    long_probs,
    short_probs,
    own_wide,
    own_down,
    w_s,
    x_s,
    qkv_s,
    vec_s,
    bias_s,
    long_s,
    short_s,
    z_send,
    z_recv,
    x_send,
    x_recv,
    y_send,
    y_recv,
    c_send,
    c_recv,
    v_send,
    v_recv,
    t_send,
    t_recv,
    local,
    p_sem,
):
    dp, s, z, x, y, c = place()
    greet()
    tokens = Tokens(long_in, short_in, x_s, t_send.at[0], t_recv.at[0], local.at[0])
    cots = Tokens(long_cot, short_cot, cot_out, t_send.at[1], t_recv.at[1], local.at[1])
    tokens.start()
    own_wide[...] = wide_ref[...].astype(bf16)

    def vec_copy(k, source, target):
        return remote(vec_ref, vec_s.at[source], v_send.at[k], v_recv.at[k], (target, s))

    sems = lambda i: [
        r.at[i] for r in (z_send, z_recv, x_send, x_recv, y_send, y_recv, c_send, c_recv)
    ]
    parts = [
        Part(own_wide.at[:, pl.ds(0, 3 * D)], w_s, sems(0)),
        Part(own_wide.at[:, pl.ds(3 * D, D)], wo_out, sems(1)),
        Part(own_wide.at[:, pl.ds(4 * D, FF)], w1_out, sems(2)),
        Part(own_down, w2_out, sems(3), direct=True),
    ]
    first, others = parts[0], parts[1:]
    first.stage(0)
    for k in range(1, 8):
        vec_copy(k, dp, (dp + k) % 8).start()
    own_down[...] = down_ref[...].astype(bf16)
    own_copies = [
        pltpu.make_async_copy(part.own, part.out.at[dp], local.at[2, i]) for i, part in enumerate(parts)
    ]
    own_copies.append(pltpu.make_async_copy(vec_ref, vec_s.at[dp], local.at[2, 4]))
    for copy in own_copies:
        copy.start()
    first.stage(1)
    parts[1].stage(0)
    first.stage(2)
    parts[2].stage(0)
    first.stage(3)
    first.stage(4)
    parts[3].stage(0)
    first.stage(5)
    cots.start()
    for copy in own_copies:
        copy.wait()
    for k in range(1, 8):
        vec_copy(k, (dp + 8 - k) % 8, dp).wait_recv()
    vec = vec_s[0].astype(f32)
    for d in range(1, 8):
        vec = vec + vec_s[d].astype(f32)
    vec_out[...] = vec
    bias_s[:, 0:D] = jnp.broadcast_to(vec[0:1, :], (8, D))
    bias_s[:, D : 2 * D] = jnp.zeros((8, D), f32)
    bias_s[:, 2 * D : 3 * D] = jnp.broadcast_to(vec[1:2, :], (8, D))
    tokens.finish()
    first.finish()
    keep_tokens = pltpu.make_async_copy(x_s, tok_out, local.at[3, 0])
    keep_weights = pltpu.make_async_copy(w_s, qkv_w_out, local.at[3, 1])
    keep_tokens.start()
    keep_weights.start()

    def during(i, plan):
        for when, jobs in plan:

            @pl.when(i == when)
            def _():
                for index, stage in jobs:
                    parts[index].stage(stage)

    def project(j, carry):
        during(j, ((2, ((1, 1),)), (4, ((2, 1),)), (6, ((1, 2),)), (8, ((3, 1),))))
        cols = pl.ds(pl.multiple_of(j * 256, 256), 256)
        w = w_s[:, :, cols].reshape(D, 256)
        rows = x_s[...].reshape(1024, D)
        qkv_s[:, :, cols] = (dot_nn(rows, w) + bias_s[0:1, cols]).astype(bf16).reshape(4, 256, 256)
        return carry

    lax.fori_loop(0, 3 * D // 256, project, 0)
    keep_qkv = pltpu.make_async_copy(qkv_s, qkv_out, local.at[3, 2])
    keep_qkv.start()
    pairs = D // PAIR

    def keep_probs_copies(i, slot):
        return (
            pltpu.make_async_copy(long_s.at[slot], long_probs.at[pl.ds(2 * i, 2)], p_sem.at[0, slot]),
            pltpu.make_async_copy(short_s.at[slot], short_probs.at[pl.ds(2 * i, 2)], p_sem.at[1, slot]),
        )

    def attention(i, carry):
        during(
            i,
            (
                (0, ((2, 2), (1, 3))),
                (1, ((3, 2), (1, 4))),
                (2, ((2, 3), (1, 5))),
                (3, ((3, 3),)),
                (4, ((2, 4),)),
                (5, ((3, 4), (2, 5))),
            ),
        )
        slot = i % 2

        @pl.when(i >= 2)
        def _():
            for copy in keep_probs_copies(i - 2, slot):
                copy.wait()

        for first_row, rows, length, index in SEQS:
            q, k, v = [
                qkv_s[:, first_row : first_row + rows, pl.ds(pl.multiple_of(base + i * PAIR, PAIR), PAIR)].reshape(
                    length, PAIR
                )
                for base in (0, D, 2 * D)
            ]

            def keep_probs(h, probs, index=index):
                if index == 0:
                    long_s[slot, h] = probs
                else:
                    short_s[slot, h, index - 1] = probs

            o = attend(q, k, v, lens_ref[index], keep_probs)
            att_out[:, first_row : first_row + rows, pl.ds(pl.multiple_of(i * PAIR, PAIR), PAIR)] = o.reshape(
                4, rows, PAIR
            )
        for copy in keep_probs_copies(i, slot):
            copy.start()
        return carry

    lax.fori_loop(0, pairs, attention, 0)
    parts[3].stage(5)
    for part in others:
        part.finish()
    cots.finish()
    keep_tokens.wait()
    keep_weights.wait()
    keep_qkv.wait()
    for i in (pairs - 2, pairs - 1):
        for copy in keep_probs_copies(i, i % 2):
            copy.wait()
    for k in range(1, 8):
        vec_copy(k, dp, (dp + k) % 8).wait_send()
    for part in parts:
        part.settle()
    tokens.settle()
    cots.settle()


def forward(lens, wide_master, down_master, vec_block, long_in, short_in, long_cot, short_cot):
    any_spec = pl.BlockSpec(memory_space=pl.ANY)
    vmem = pl.BlockSpec(memory_space=pltpu.VMEM)
    smem = pl.BlockSpec(memory_space=pltpu.SMEM)
    shape = jax.ShapeDtypeStruct
    rows, down_rows = wide_master.shape[0], down_master.shape[0]
    dma = pltpu.SemaphoreType.DMA
    heads = D // HEAD_DIM
    return pl.pallas_call(
        forward_kernel,
        in_specs=[smem, vmem, vmem, vmem] + [any_spec] * 4,
        out_specs=[any_spec] * 4 + [vmem] + [any_spec] * 3 + [vmem] + [any_spec] * 2,
        out_shape=[
            shape((8, rows, 3 * D), bf16),
            shape((8, rows, D), bf16),
            shape((8, rows, FF), bf16),
            shape((8, down_rows, D), bf16),
            shape((16, D), f32),
            shape((4, 256, D), bf16),
            shape((4, 256, D), bf16),
            shape((4, 256, 3 * D), bf16),
            shape((4, 256, D), bf16),
            shape((heads, LONG_L, LONG_L), bf16),
            shape((heads, 2, SHORT_L, SHORT_L), bf16),
        ],
        scratch_shapes=[
            pltpu.VMEM((rows, 4 * D + FF), bf16),
            pltpu.VMEM((down_rows, D), bf16),
            pltpu.VMEM((8, rows, 3 * D), bf16),
            pltpu.VMEM((4, 256, D), bf16),
            pltpu.VMEM((4, 256, 3 * D), bf16),
            pltpu.VMEM((8, 16, D), bf16),
            pltpu.VMEM((8, 3 * D), f32),
            pltpu.VMEM((2, 2, LONG_L, LONG_L), bf16),
            pltpu.VMEM((2, 2, 2, SHORT_L, SHORT_L), bf16),
            dma((4, 4, 2)),
            dma((4, 4)),
            dma((4, 4)),
            dma((4, 4)),
            dma((4, 4)),
            dma((4, 4)),
            dma((4, 12)),
            dma((4, 12)),
            dma((8,)),
            dma((8,)),
            dma((2, 4, 3)),
            dma((2, 4, 3)),
            dma((4, 5)),
            dma((2, 2)),
        ],
        compiler_params=pltpu.CompilerParams(
            vmem_limit_bytes=VMEM_BYTES, collective_id=0, has_side_effects=True
        ),
        name="forward",
    )(lens, wide_master, down_master, vec_block, long_in, short_in, long_cot, short_cot)


class Grad:
    def __init__(self, src, acc, cbuf, xbuf, ybuf, zbuf, fin, sems, order):
        self.src, self.acc, self.cbuf, self.xbuf, self.ybuf, self.zbuf, self.fin = src, acc, cbuf, xbuf, ybuf, zbuf, fin
        self.c_send, self.c_recv, self.x_send, self.x_recv, self.y_send, self.y_recv = sems[:6]
        self.z_send, self.z_recv, self.f_send, self.f_recv, self.local = sems[6:]
        self.order = order
        self.dp, self.s, self.z, self.x, self.y, self.c = place()
        self.rows, cols = src.shape[2:]
        self.half_rows, self.half_cols = self.rows // 2, cols // 2

    def cols(self, core):
        return pl.ds(pl.multiple_of(core * self.half_cols, 128), self.half_cols)

    def some(self, q):
        return pl.ds(pl.multiple_of(q * self.half_rows, 16), self.half_rows)

    def core_copy(self, j):
        xd = (1 - self.x) if j == 0 else self.x
        return remote(
            self.src.at[:, xd, :, self.cols(1 - self.c)],
            self.cbuf.at[:, xd],
            self.c_send.at[j],
            self.c_recv.at[j],
            (self.dp, self.s + 1 - 2 * self.c),
        )

    def own_copy(self, j):
        xd = (1 - self.x) if j == 0 else self.x
        return pltpu.make_async_copy(self.src.at[:, xd, :, self.cols(self.c)], self.acc.at[:, xd], self.local.at[j])

    def x_copy(self, zd):
        device = (self.z * 2 + 1 - self.x, self.s)
        return remote(
            self.acc.at[zd, 1 - self.x], self.xbuf.at[zd], self.x_send.at[zd], self.x_recv.at[zd], device
        )

    def y_copy(self, zd):
        device = (self.dp, (1 - self.y) * 2 + self.c)
        return remote(
            self.acc.at[zd, self.x, self.some(1 - self.y)],
            self.ybuf.at[zd],
            self.y_send.at[zd],
            self.y_recv.at[zd],
            device,
        )

    def z_copy(self, k):
        zd = (self.z + k) % Z_CHIPS
        src = self.acc.at[zd, self.x, self.some(self.y)] if self.order == "xyz" else self.acc.at[zd]
        return remote(
            src, self.zbuf.at[k], self.z_send.at[k], self.z_recv.at[k], (zd * 2 + self.x, self.s)
        )

    def fin_quarter(self, s):
        return self.fin.at[self.some(s // 2), self.cols(s % 2)]

    def fin_copy(self, k):
        return remote(
            self.fin_quarter(self.s),
            self.fin_quarter(self.s),
            self.f_send.at[k],
            self.f_recv.at[k],
            (self.dp, (self.s + k) % 4),
        )

    def fin_in(self, k):
        ref = self.fin_quarter((self.s + 4 - k) % 4)
        return remote(ref, ref, self.f_send.at[k], self.f_recv.at[k], (self.dp, self.s))

    def core_add(self, j):
        xd = (1 - self.x) if j == 0 else self.x
        self.core_copy(j).wait_recv()
        self.own_copy(j).wait()

        def one(zd, carry):
            self.acc[zd, xd] = (self.acc[zd, xd].astype(f32) + self.cbuf[zd, xd].astype(f32)).astype(bf16)
            return carry

        lax.fori_loop(0, Z_CHIPS, one, 0)

    def publish(self, total):
        self.fin[self.some(self.y), self.cols(self.c)] = total.astype(bf16)
        for k in range(1, 4):
            self.fin_copy(k).start()

    stages = 7

    def stage(self, i):
        if i == 0:
            for j in range(2):
                self.core_copy(j).start()
                self.own_copy(j).start()
        elif self.order == "xyz":
            if i == 1:
                self.core_add(0)
                for k in range(Z_CHIPS):
                    self.x_copy((self.z + k) % Z_CHIPS).start()
            elif i == 2:
                self.core_add(1)
            elif i == 3:
                for k in range(Z_CHIPS):
                    zd = (self.z + k) % Z_CHIPS
                    self.x_copy(zd).wait_recv()
                    self.acc[zd, self.x] = (self.acc[zd, self.x].astype(f32) + self.xbuf[zd].astype(f32)).astype(bf16)
                    self.y_copy(zd).start()
            elif i == 4:
                for k in (1, 2, 3, 0):
                    zd = (self.z + k) % Z_CHIPS
                    self.y_copy(zd).wait_recv()
                    rows = self.some(self.y)
                    self.acc[zd, self.x, rows] = (
                        self.acc[zd, self.x, rows].astype(f32) + self.ybuf[zd].astype(f32)
                    ).astype(bf16)
                    if k:
                        self.z_copy(k).start()
            elif i == 5:
                total = self.acc[self.z, self.x, self.some(self.y)].astype(f32)
                for k in range(1, Z_CHIPS):
                    self.z_copy(k).wait_recv()
                    total = total + self.zbuf[k].astype(f32)
                self.publish(total)
        else:
            if i == 1:
                self.core_add(0)
                self.core_add(1)
                for k in range(1, Z_CHIPS):
                    self.z_copy(k).start()
            elif i == 3:
                for k in range(1, Z_CHIPS):
                    self.z_copy(k).wait_recv()
                for xd in range(2):
                    total = self.acc[self.z, xd].astype(f32)
                    for k in range(1, Z_CHIPS):
                        total = total + self.zbuf[k, xd].astype(f32)
                    self.acc[self.z, xd] = total.astype(bf16)
                self.x_copy(self.z).start()
            elif i == 4:
                self.x_copy(self.z).wait_recv()
                total = self.acc[self.z, self.x].astype(f32) + self.xbuf[self.z].astype(f32)
                self.acc[self.z, self.x] = total.astype(bf16)
                self.y_copy(self.z).start()
            elif i == 5:
                self.y_copy(self.z).wait_recv()
                self.publish(self.acc[self.z, self.x, self.some(self.y)].astype(f32) + self.ybuf[self.z].astype(f32))
        if i == 6:
            for k in range(1, 4):
                self.fin_in(k).wait_recv()

    def settle(self):
        for j in range(2):
            self.core_copy(j).wait_send()
        for k in range(1, Z_CHIPS):
            self.z_copy(k).wait_send()
        for k in range(1, 4):
            self.fin_copy(k).wait_send()
        for k in range(Z_CHIPS if self.order == "xyz" else 1):
            self.x_copy((self.z + k) % Z_CHIPS).wait_send()
            self.y_copy((self.z + k) % Z_CHIPS).wait_send()


class Returns:
    def __init__(self, rows_ref, long_out, short_out, send, recv, local):
        self.rows_ref, self.long_out, self.short_out = rows_ref, long_out, short_out
        self.send, self.recv, self.local = send, recv, local
        self.dp, self.s = lax.axis_index("dp"), lax.axis_index("seq")

    def pieces(self, target, source):
        yield self.rows_ref.at[target, pl.ds(0, 128)], self.long_out.at[source // 2, source % 2]
        yield self.rows_ref.at[target, pl.ds(128, 64)], self.short_out.at[0, source]
        yield self.rows_ref.at[target, pl.ds(192, 64)], self.short_out.at[1, source]

    copies, own, start, finish, settle = Tokens.copies, Tokens.own, Tokens.start, Tokens.finish, Tokens.settle


class Sums:
    def __init__(self, src, sbuf, part, dbuf, out, sems):
        self.src, self.sbuf, self.part, self.dbuf, self.out = src, sbuf, part, dbuf, out
        self.s_send, self.s_recv, self.d_send, self.d_recv = sems
        self.dp, self.s = lax.axis_index("dp"), lax.axis_index("seq")

    def s_copy(self, k, source):
        return remote(self.src, self.sbuf.at[source], self.s_send.at[k], self.s_recv.at[k], (self.dp, (self.s + k) % 4))

    def d_copy(self, k, source):
        target = (self.dp + k) % 8
        return remote(
            self.part.at[target], self.dbuf.at[source], self.d_send.at[k], self.d_recv.at[k], (target, self.s)
        )

    def stage(self, i):
        if i == 0:
            for k in range(1, 4):
                self.s_copy(k, self.s).start()
            self.sbuf[self.s] = self.src[...]
        elif i == 1:
            for k in range(1, 4):
                self.s_copy(k, (self.s + 4 - k) % 4).wait_recv()
            self.part[...] = (self.sbuf[0] + self.sbuf[1]) + (self.sbuf[2] + self.sbuf[3])
            for k in range(1, 8):
                self.d_copy(k, self.dp).start()
            self.dbuf[self.dp] = self.part[self.dp]
        elif i == 2:
            for k in range(1, 8):
                self.d_copy(k, (self.dp + 8 - k) % 8).wait_recv()
            total = self.dbuf[0]
            for d in range(1, 8):
                total = total + self.dbuf[d]
            self.out[...] = total

    def settle(self):
        for k in range(1, 4):
            self.s_copy(k, self.s).wait_send()
        for k in range(1, 8):
            self.d_copy(k, self.dp).wait_send()


ORDERS = ("zxy", "xyz", "xyz", "xyz")


def reduce_kernel(count, *refs):
    grads, refs = refs[:count], refs[count:]
    sums_ref, out_rows, back_rows, refs = refs[0], refs[1], refs[2], refs[3:]
    fins, refs = refs[:count], refs[count:]
    (sums_out, short_out, long_out, short_back, long_back), refs = refs[:5], refs[5:]
    bufs, refs = refs[: 5 * count], refs[5 * count :]
    (sbuf, part, dbuf), refs = refs[:3], refs[3:]
    sems, refs = refs[:11], refs[11:]
    s_sems, (t_send, t_recv, local) = refs[:4], refs[4:]
    greet()
    pieces = []
    for i in range(count):
        acc, cbuf, xbuf, ybuf, zbuf = bufs[5 * i : 5 * i + 5]
        pieces.append(
            Grad(grads[i], acc, cbuf, xbuf, ybuf, zbuf, fins[i], [r.at[i] for r in sems], ORDERS[i])
        )
    sums = Sums(sums_ref, sbuf, part, dbuf, sums_out, s_sems)
    outs = Returns(out_rows, long_out, short_out, t_send.at[0], t_recv.at[0], local.at[0])
    backs = Returns(back_rows, long_back, short_back, t_send.at[1], t_recv.at[1], local.at[1])
    outs.start()
    for t in range(Grad.stages + count - 1):
        for i, piece in enumerate(pieces):
            if 0 <= t - i < Grad.stages:
                piece.stage(t - i)
        if t < 3:
            sums.stage(t)
        if t == 2:
            backs.start()
    outs.finish()
    backs.finish()
    for piece in pieces:
        piece.settle()
    sums.settle()
    outs.settle()
    backs.settle()


def reduce_all(grads, sums, out_rows, back_rows):
    count = len(grads)
    any_spec = pl.BlockSpec(memory_space=pl.ANY)
    vmem = pl.BlockSpec(memory_space=pltpu.VMEM)
    shape = jax.ShapeDtypeStruct
    dma = pltpu.SemaphoreType.DMA
    bufs = []
    for g, order in zip(grads, ORDERS):
        rows, cols = g.shape[2:]
        half, cut = cols // 2, rows // 2
        bufs += [
            pltpu.VMEM((4, 2, rows, half), bf16),
            pltpu.VMEM((4, 2, rows, half), bf16),
            pltpu.VMEM((4, rows, half), bf16),
            pltpu.VMEM((4, cut, half), bf16),
            pltpu.VMEM((4, cut, half) if order == "xyz" else (4, 2, rows, half), bf16),
        ]
    return pl.pallas_call(
        lambda *refs: reduce_kernel(count, *refs),
        in_specs=[any_spec] * count + [vmem, any_spec, any_spec],
        out_specs=[vmem] * count + [vmem] + [any_spec] * 4,
        out_shape=[shape(g.shape[2:], bf16) for g in grads]
        + [
            shape((16, 128), f32),
            shape((2, 4, 64, D), bf16),
            shape((2, 2, 128, D), bf16),
            shape((2, 4, 64, D), bf16),
            shape((2, 2, 128, D), bf16),
        ],
        scratch_shapes=bufs
        + [pltpu.VMEM((4, 8, 16, 128), f32), pltpu.VMEM((8, 16, 128), f32), pltpu.VMEM((8, 16, 128), f32)]
        + [dma((count, 2))] * 2
        + [dma((count, 4))] * 8
        + [dma((count, 2))]
        + [dma((4,)), dma((4,)), dma((8,)), dma((8,))]
        + [dma((2, 4, 3)), dma((2, 4, 3)), dma((2, 3))],
        compiler_params=pltpu.CompilerParams(
            vmem_limit_bytes=VMEM_BYTES, collective_id=1, has_side_effects=True
        ),
        name="reduce",
    )(*grads, sums, out_rows, back_rows)


def transpose_dot(left, right):
    return jnp.einsum("ra,rb->ab", left, right, preferred_element_type=f32)


def right_dot(left, right):
    return jnp.einsum("ra,ba->rb", left, right, preferred_element_type=f32)


def flip(v, axis, bit):
    n = lax.axis_size(axis)
    return lax.ppermute(v, axis, [(i, i ^ bit) for i in range(n)])


def half_of(v, dim, which):
    size = v.shape[dim] // 2
    return lax.dynamic_slice_in_dim(v, which * size, size, dim)


def halve(v, axis, bit, dim):
    mine = (lax.axis_index(axis) // bit) % 2
    other = flip(half_of(v, dim, 1 - mine), axis, bit)
    return (half_of(v, dim, mine).astype(f32) + other.astype(f32)).astype(bf16)


def double(v, axis, bit, dim):
    mine = (lax.axis_index(axis) // bit) % 2
    other = flip(v, axis, bit)
    return jnp.where(
        mine == 0, jnp.concatenate([v, other], axis=dim), jnp.concatenate([other, v], axis=dim)
    )


def reduce_rows(grad):
    rows, cols = grad.shape
    dp = lax.axis_size("dp")
    v = grad.reshape(dp, rows // dp, cols)
    v = halve(v, "seq", 1, 2)
    v = halve(v, "seq", 2, 2)
    bit = 1
    while bit < dp:
        blocks = v.shape[0]
        v = v.reshape(blocks // 2, 2, v.shape[1], v.shape[2]) if v.ndim == 3 else v
        v = halve(v, "dp", bit, 1)[:, 0]
        bit *= 2
    v = v[0]
    v = double(v, "seq", 2, 1)
    v = double(v, "seq", 1, 1)
    return v.astype(f32)


def update(master, reduced_grad, moment, average):
    step_grad = reduced_grad + decay_weight * master
    velocity = momentum_rate * moment + step_grad
    updated = master - learning_rate * (step_grad + momentum_rate * velocity)
    averaged = average_rate * average + (1.0 - average_rate) * updated
    return (velocity, averaged, updated, updated.astype(jnp.bfloat16))


def spread_rows(long_part, short_part):
    long_blocks = long_part.reshape(4, 128, D)
    short_blocks = jnp.transpose(short_part, (1, 0, 2, 3)).reshape(4, 128, D)
    return jnp.concatenate([long_blocks, short_blocks], axis=1)


def exchange(v):
    return lax.all_to_all(v, "seq", split_axis=0, concat_axis=0, tiled=True)


def collect_rows(v):
    long_part = v[:, :128].reshape(2, 2, 128, D)
    short_part = jnp.transpose(v[:, 128:].reshape(4, 2, 64, D), (1, 0, 2, 3))
    return short_part, long_part


def body(
    short_in,
    long_in,
    short_cot,
    long_cot,
    short_len,
    long_len,
    wide_master,
    down_master,
    vector_master,
    wide_moment,
    down_moment,
    vector_moment,
    wide_average,
    down_average,
    vector_average,
):
    s = lax.axis_index("seq")
    lens = jnp.stack([long_len[s // 2, 0, s % 2], short_len[0, 0, s], short_len[1, 0, s]])
    if lax.axis_size("dp") == 8:
        own = vector_master.shape[0]
        vec_own = jnp.pad(jnp.transpose(vector_master).astype(bf16), ((0, 4), (0, 0)))
        vec_block = lax.dynamic_update_slice(
            jnp.zeros((16, D), bf16), vec_own, (0, lax.axis_index("dp") * own)
        )
        w_qkv, w_o, w_1, w_2, vec, tokens, cotangent, qkv, attended, long_probs, short_probs = forward(
            lens, wide_master, down_master, vec_block, long_in, short_in, long_cot, short_cot
        )
        w_qkv, w_o, w_1, w_2 = [w.reshape(-1, w.shape[2]) for w in (w_qkv, w_o, w_1, w_2)]
        rows = tokens.reshape(1024, D)
    else:
        tokens = exchange(spread_rows(long_in, short_in))
        cotangent = exchange(spread_rows(long_cot, short_cot))
        wide_w = lax.all_gather(wide_master.astype(bf16), "dp", axis=0, tiled=True)
        w_2 = lax.all_gather(down_master.astype(bf16), "dp", axis=0, tiled=True)
        vector_w = lax.all_gather(vector_master.astype(bf16), "dp", axis=0, tiled=True)
        vec = jnp.transpose(vector_w.astype(f32))
        w_qkv = wide_w[:, : 3 * D]
        w_o = wide_w[:, 3 * D : 4 * D]
        w_1 = wide_w[:, 4 * D :]
        rows = tokens.reshape(1024, D)
        proj_bias = jnp.concatenate([vec[0], jnp.zeros((D,), f32), vec[1]])
        qkv = (jnp.dot(rows, w_qkv, preferred_element_type=f32) + proj_bias).astype(bf16)
        qkv = qkv.reshape(4, 256, 3 * D)
        attended, long_probs, short_probs = attn_forward(lens, qkv)

    flat_attended = attended.reshape(1024, D)
    out, y1b, act, dfb, dub, dab, dob, dh, sums = middle(
        lens, flat_attended, rows, cotangent.reshape(1024, D), w_o, w_1, w_2, vec
    )
    d_down = transpose_dot(act, dfb).astype(bf16)
    d_one = transpose_dot(y1b, dub).astype(bf16)
    d_o = transpose_dot(flat_attended, dab).astype(bf16)
    dq, dk, dv, qv_sums = attn_backward(
        lens, qkv, dob.reshape(4, 256, D), attended, long_probs, short_probs
    )
    d_qkv = jnp.concatenate([dq, dk, dv], axis=2).reshape(1024, 3 * D)
    d_wqkv = transpose_dot(rows, d_qkv).astype(bf16)
    back = (dh + right_dot(d_qkv, w_qkv)).astype(bf16).reshape(4, 256, D)

    vector_total = jnp.concatenate([qv_sums[:2], sums[2:12]], axis=0)
    own_rows = vector_master.shape[0]
    if lax.axis_size("dp") == 8:
        blocks = lambda g: g.reshape(4, 2, g.shape[0] // 8, g.shape[1])
        spread = jnp.transpose(vector_total.reshape(12, 8, own_rows), (1, 0, 2))
        spread = jnp.pad(spread, ((0, 0), (0, 4), (0, 128 - own_rows)))
        down_low, one_low, o_low, qkv_low, sums_own, short_out, long_out, short_back, long_back = reduce_all(
            [blocks(g) for g in (d_down, d_one, d_o, d_wqkv)], spread, out.reshape(4, 256, D), back
        )
        vector_reduced = jnp.transpose(sums_own[:12, :own_rows])
        wide_reduced = jnp.concatenate([qkv_low, o_low, one_low], axis=1).astype(f32)
        down_reduced = down_low.astype(f32)
    else:
        vector_sum = jnp.transpose(lax.psum(vector_total, ("dp", "seq")))
        vector_reduced = lax.dynamic_slice_in_dim(vector_sum, lax.axis_index("dp") * own_rows, own_rows, 0)
        wide_reduced = jnp.concatenate([reduce_rows(d_wqkv), reduce_rows(d_o), reduce_rows(d_one)], axis=1)
        down_reduced = reduce_rows(d_down)
        short_out, long_out = collect_rows(exchange(out.reshape(4, 256, D)))
        short_back, long_back = collect_rows(exchange(back))
    wide_new = update(wide_master, wide_reduced, wide_moment, wide_average)
    down_new = update(down_master, down_reduced, down_moment, down_average)
    vector_new = update(vector_master, vector_reduced, vector_moment, vector_average)
    return (
        short_out,
        long_out,
        short_back,
        long_back,
        wide_reduced,
        down_reduced,
        vector_reduced,
        wide_new[0],
        down_new[0],
        vector_new[0],
        wide_new[1],
        down_new[1],
        vector_new[1],
        wide_new[2],
        down_new[2],
        vector_new[2],
        wide_new[3],
        down_new[3],
        vector_new[3],
    )


def solution(mesh):
    tok = P(None, "dp", "seq", None)
    lengths = P(None, "dp", None)
    state = P("dp", None)
    return jax.shard_map(
        body,
        mesh=mesh,
        in_specs=(tok,) * 4 + (lengths,) * 2 + (state,) * 9,
        out_specs=(tok,) * 4 + (state,) * 15,
        check_vma=False,
    )
```

```python
import jax
import jax.numpy as jnp
from jax import lax
from jax.experimental import pallas as pl
from jax.experimental.pallas import tpu as pltpu
from jax.sharding import PartitionSpec as P

D = 768
HEAD_DIM = 64
FF = 3072
PAIR = 128
LONG_L = 512
SHORT_L = 256
VMEM_BYTES = 62 * 1024 * 1024

norm_eps = 1e-12
mask_fill = -10000.0
learning_rate = 0.0002
momentum_rate = 0.9
decay_weight = 0.0001
average_rate = 0.9
score_scale = HEAD_DIM ** (-0.5)
f32 = jnp.float32
bf16 = jnp.bfloat16


def params():
    return pltpu.CompilerParams(vmem_limit_bytes=VMEM_BYTES)


def dot_nn(a, b):
    return lax.dot_general(a, b, (((1,), (0,)), ((), ())), preferred_element_type=f32)


def dot_nt(a, b):
    return lax.dot_general(a, b, (((1,), (1,)), ((), ())), preferred_element_type=f32)


SEQS = ((0, 128, LONG_L, 0), (128, 64, SHORT_L, 1), (192, 64, SHORT_L, 2))


def attend(q, k, v, limit, keep_probs):
    length = q.shape[0]
    v_t = jnp.transpose(v)
    head_lane = lax.broadcasted_iota(jnp.int32, (length, PAIR), 1) // HEAD_DIM
    live = lax.broadcasted_iota(jnp.int32, (length, length), 0) < limit
    parts = []
    for h in range(2):
        k_h = jnp.where(head_lane == h, k, jnp.zeros_like(k))
        scores = jnp.where(live, dot_nt(k_h, q) * score_scale, mask_fill)
        top = jnp.max(scores, axis=0, keepdims=True)
        exponent = jnp.exp(scores - top)
        total = jnp.sum(exponent, axis=0, keepdims=True)
        probs = (exponent * (1.0 / total)).astype(bf16)
        keep_probs(h, probs)
        parts.append(dot_nn(v_t[h * HEAD_DIM : (h + 1) * HEAD_DIM], probs))
    return jnp.transpose(jnp.concatenate(parts, axis=0)).astype(bf16)


def attn_forward_kernel(lens_ref, q_ref, k_ref, v_ref, o_ref, long_ref, short_ref):
    for first, rows, length, index in SEQS:
        q, k, v = [r[:, first : first + rows, :].reshape(length, PAIR) for r in (q_ref, k_ref, v_ref)]

        def keep_probs(h, probs, index=index):
            if index == 0:
                long_ref[h] = probs
            else:
                short_ref[h, index - 1] = probs

        o = attend(q, k, v, lens_ref[index], keep_probs)
        o_ref[:, first : first + rows, :] = o.reshape(4, rows, PAIR)


def attn_forward(lens, qkv):
    pairs = D // PAIR
    col = lambda base: pl.BlockSpec((4, 256, PAIR), lambda i, base=base: (0, 0, base + i))
    return pl.pallas_call(
        attn_forward_kernel,
        grid=(pairs,),
        in_specs=[
            pl.BlockSpec(memory_space=pltpu.SMEM),
            col(0),
            col(pairs),
            col(2 * pairs),
        ],
        out_specs=[
            pl.BlockSpec((4, 256, PAIR), lambda i: (0, 0, i)),
            pl.BlockSpec((2, LONG_L, LONG_L), lambda i: (i, 0, 0)),
            pl.BlockSpec((2, 2, SHORT_L, SHORT_L), lambda i: (i, 0, 0, 0)),
        ],
        out_shape=[
            jax.ShapeDtypeStruct((4, 256, D), bf16),
            jax.ShapeDtypeStruct((2 * pairs, LONG_L, LONG_L), bf16),
            jax.ShapeDtypeStruct((2 * pairs, 2, SHORT_L, SHORT_L), bf16),
        ],
        compiler_params=params(),
        name="attn_forward",
    )(lens, qkv, qkv, qkv)


def attend_back(q, k, v, do, o, limit, kept_probs):
    length = q.shape[0]
    k_t = jnp.transpose(k)
    inner = jnp.transpose(do.astype(f32) * o.astype(f32))
    head_lane = lax.broadcasted_iota(jnp.int32, (length, PAIR), 1) // HEAD_DIM
    live = lax.broadcasted_iota(jnp.int32, (length, length), 0) < limit
    dq_parts = []
    dk = jnp.zeros((length, PAIR), f32)
    dv = jnp.zeros((length, PAIR), f32)
    for h in range(2):
        keep = head_lane == h
        v_h, do_h, q_h = [jnp.where(keep, m, jnp.zeros_like(m)) for m in (v, do, q)]
        probs = kept_probs(h)
        delta = jnp.sum(inner[h * HEAD_DIM : (h + 1) * HEAD_DIM], axis=0, keepdims=True)
        d_probs = dot_nt(v_h, do)
        d_scores = jnp.where(live, probs.astype(f32) * (d_probs - delta), 0.0).astype(bf16)
        dv = dv + dot_nn(probs, do_h)
        dk = dk + dot_nn(d_scores, q_h)
        dq_parts.append(dot_nn(k_t[h * HEAD_DIM : (h + 1) * HEAD_DIM], d_scores))
    dq = jnp.transpose(jnp.concatenate(dq_parts, axis=0)) * score_scale
    return dq.astype(bf16), (dk * score_scale).astype(bf16), dv.astype(bf16)


def attn_backward_kernel(
    lens_ref, q_ref, k_ref, v_ref, do_ref, o_ref, long_ref, short_ref, dq_ref, dk_ref, dv_ref, sum_ref
):
    sum_q = jnp.zeros((1, PAIR), f32)
    sum_v = jnp.zeros((1, PAIR), f32)
    for first, rows, length, index in SEQS:
        args = [r[:, first : first + rows, :].reshape(length, PAIR) for r in (q_ref, k_ref, v_ref, do_ref, o_ref)]
        kept = lambda h, index=index: long_ref[h] if index == 0 else short_ref[h, index - 1]
        dq, dk, dv = attend_back(*args, lens_ref[index], kept)
        sum_q = sum_q + jnp.sum(dq.astype(f32), axis=0, keepdims=True)
        sum_v = sum_v + jnp.sum(dv.astype(f32), axis=0, keepdims=True)
        for ref, v in ((dq_ref, dq), (dk_ref, dk), (dv_ref, dv)):
            ref[:, first : first + rows, :] = v.reshape(4, rows, PAIR)
    sum_ref[0:1, :] = sum_q
    sum_ref[1:2, :] = sum_v
    sum_ref[2:8, :] = jnp.zeros((6, PAIR), f32)


def attn_backward(lens, qkv, d_attended, attended, long_probs, short_probs):
    pairs = D // PAIR
    col = lambda base: pl.BlockSpec((4, 256, PAIR), lambda i, base=base: (0, 0, base + i))
    return pl.pallas_call(
        attn_backward_kernel,
        grid=(pairs,),
        in_specs=[
            pl.BlockSpec(memory_space=pltpu.SMEM),
            col(0),
            col(pairs),
            col(2 * pairs),
            col(0),
            col(0),
            pl.BlockSpec((2, LONG_L, LONG_L), lambda i: (i, 0, 0)),
            pl.BlockSpec((2, 2, SHORT_L, SHORT_L), lambda i: (i, 0, 0, 0)),
        ],
        out_specs=[col(0), col(0), col(0), pl.BlockSpec((8, PAIR), lambda i: (0, i))],
        out_shape=[jax.ShapeDtypeStruct((4, 256, D), bf16)] * 3 + [jax.ShapeDtypeStruct((8, D), f32)],
        compiler_params=params(),
        name="attn_backward",
    )(lens, qkv, qkv, qkv, d_attended, attended, long_probs, short_probs)


def gelu_pair(u):
    a = jnp.abs(u)
    t = 1.0 / (1.0 + (0.3275911 * 0.5**0.5) * a)
    e = jnp.exp(-0.5 * u * u)
    poly = t * (0.254829592 + t * (-0.284496736 + t * (1.421413741 + t * (-1.453152027 + t * 1.061405429))))
    tail = 0.5 * poly * e
    cdf = jnp.where(u < 0.0, tail, 1.0 - tail)
    pdf = e * (0.5 / jnp.pi) ** 0.5
    return u * cdf, cdf + u * pdf


def row_mean(v):
    return jnp.mean(v, axis=-1, keepdims=True)


def middle_kernel(
    lens_ref,
    o_ref,
    x_ref,
    cot_ref,
    wo_ref,
    w1_ref,
    w2_ref,
    vec_ref,
    out_ref,
    y1b_ref,
    g_ref,
    dfb_ref,
    dub_ref,
    dab_ref,
    dob_ref,
    dh_ref,
    sum_ref,
    slope_ref,
):
    r = pl.program_id(0)
    rows = o_ref.shape[0]

    @pl.when(r == 0)
    def _():
        sum_ref[...] = jnp.zeros_like(sum_ref)

    def add(index, v):
        sum_ref[index : index + 1, :] += jnp.sum(v, axis=0, keepdims=True)

    vec = lambda i: vec_ref[i : i + 1, :]
    h = x_ref[...].astype(f32) + (dot_nn(o_ref[...], wo_ref[...]) + vec(2))
    centred = h - row_mean(h)
    inv1 = lax.rsqrt(row_mean(centred * centred) + norm_eps)
    norm1 = centred * inv1
    y1 = norm1 * vec(3) + vec(4)
    y1b = y1.astype(bf16)
    y1b_ref[...] = y1b
    z = y1 + vec(5)
    for c in range(FF // D):
        cols = slice(c * D, (c + 1) * D)
        act, slope = gelu_pair(dot_nn(y1b, w1_ref[:, cols]) + vec(8 + c))
        act = act.astype(bf16)
        g_ref[:, cols] = act
        slope_ref[:, cols] = slope
        z = z + dot_nn(act, w2_ref[cols, :])
    centred2 = z - row_mean(z)
    inv2 = lax.rsqrt(row_mean(centred2 * centred2) + norm_eps)
    norm2 = centred2 * inv2
    out_ref[...] = (norm2 * vec(6) + vec(7)).astype(bf16)

    j = lax.broadcasted_iota(jnp.int32, (rows, 1), 0)
    long_end = lens_ref[0] - r * 128
    short_end = [lens_ref[i] - r * 64 + first for i, first in ((1, 128), (2, 192))]
    live = j < jnp.where(j < 128, long_end, jnp.where(j < 192, short_end[0], short_end[1]))
    dr = jnp.where(live, cot_ref[...].astype(f32), 0.0)
    e2 = dr * vec(6)
    dz = inv2 * (e2 - row_mean(e2) - norm2 * row_mean(e2 * norm2))
    dfb = dz.astype(bf16)
    dfb_ref[...] = dfb
    add(6, dr * norm2)
    add(7, dr)
    add(5, dfb.astype(f32))
    dy1 = dz
    for c in range(FF // D):
        cols = slice(c * D, (c + 1) * D)
        dub = (dot_nt(dfb, w2_ref[cols, :]) * slope_ref[:, cols]).astype(bf16)
        dub_ref[:, cols] = dub
        add(8 + c, dub.astype(f32))
        dy1 = dy1 + dot_nt(dub, w1_ref[:, cols])
    add(3, dy1 * norm1)
    add(4, dy1)
    e1 = dy1 * vec(3)
    dh = inv1 * (e1 - row_mean(e1) - norm1 * row_mean(e1 * norm1))
    dab = dh.astype(bf16)
    dh_ref[...] = dh
    dab_ref[...] = dab
    add(2, dab.astype(f32))
    dob_ref[...] = dot_nt(dab, wo_ref[...]).astype(bf16)


def middle(lens, attended, tokens, cotangent, w_o, w_1, w_2, vec):
    n = tokens.shape[0]
    rows = 256
    row = lambda width: pl.BlockSpec((rows, width), lambda i: (i, 0))
    whole = lambda a: pl.BlockSpec(a.shape, lambda i: (0, 0), pipeline_mode=pl.Buffered(1))
    shape = jax.ShapeDtypeStruct
    return pl.pallas_call(
        middle_kernel,
        grid=(n // rows,),
        in_specs=[
            pl.BlockSpec(memory_space=pltpu.SMEM),
            row(D),
            row(D),
            row(D),
            whole(w_o),
            whole(w_1),
            whole(w_2),
            whole(vec),
        ],
        out_specs=[
            row(D),
            row(D),
            row(FF),
            row(D),
            row(FF),
            row(D),
            row(D),
            row(D),
            pl.BlockSpec((16, D), lambda i: (0, 0)),
        ],
        out_shape=[
            shape((n, D), bf16),
            shape((n, D), bf16),
            shape((n, FF), bf16),
            shape((n, D), bf16),
            shape((n, FF), bf16),
            shape((n, D), bf16),
            shape((n, D), bf16),
            shape((n, D), f32),
            shape((16, D), f32),
        ],
        scratch_shapes=[pltpu.VMEM((rows, FF), f32)],
        compiler_params=params(),
        name="middle",
    )(lens, attended, tokens, cotangent, w_o, w_1, w_2, vec)


MESH = pl.DeviceIdType.MESH
Z_CHIPS = 4


def place():
    dp = lax.axis_index("dp")
    s = lax.axis_index("seq")
    return dp, s, dp // 2, dp % 2, s // 2, s % 2


def remote(src, dst, send, recv, device):
    return pltpu.make_async_remote_copy(
        src_ref=src, dst_ref=dst, send_sem=send, recv_sem=recv, device_id=device, device_id_type=MESH
    )


def greet():
    dp, s = lax.axis_index("dp"), lax.axis_index("seq")
    barrier = pltpu.get_barrier_semaphore()
    for k in range(1, 8):
        pl.semaphore_signal(barrier, inc=1, device_id=((dp + k) % 8, s), device_id_type=MESH)
    for k in range(1, 4):
        pl.semaphore_signal(barrier, inc=1, device_id=(dp, (s + k) % 4), device_id_type=MESH)
    pl.semaphore_wait(barrier, 10)


class Part:
    def __init__(self, own, out, sems, direct=False):
        self.own, self.out, self.direct = own, out, direct
        self.z_send, self.z_recv, self.x_send, self.x_recv, self.y_send, self.y_recv, self.c_send, self.c_recv = sems
        self.dp, self.s, self.z, self.x, self.y, self.c = place()
        self.rows, cols = own.shape
        self.half_rows, self.half_cols = self.rows // 2, cols // 2

    def cols(self, core):
        return pl.ds(pl.multiple_of(core * self.half_cols, 128), self.half_cols)

    def some(self, q):
        return pl.ds(pl.multiple_of(q * self.half_rows, 16), self.half_rows)

    def block(self, zs, x, core, q=None):
        rows = slice(None) if q is None else self.some(q)
        return self.out.at[zs * 2 + x, rows, self.cols(core)]

    def source(self, zs, own, q=None):
        if own:
            rows = slice(None) if q is None else self.some(q)
            return self.own.at[rows, self.cols(self.c)]
        return self.block(zs, self.x, self.c, q)

    def up(self, zs, own=False):
        dst = self.block(zs, self.x, self.c)
        return remote(self.source(zs, own), dst, self.z_send.at[zs, 0], self.z_recv.at[zs], (self.dp + 2, self.s))

    def down(self, zs, own=False):
        dst = self.block(zs, self.x, self.c)
        return remote(self.source(zs, own), dst, self.z_send.at[zs, 1], self.z_recv.at[zs], (self.dp - 2, self.s))

    def across(self, zs, own=False):
        q = None if self.direct else self.y
        dst = self.block(zs, self.x, self.c, q)
        device = (self.z * 2 + 1 - self.x, self.s)
        return remote(self.source(zs, own, q), dst, self.x_send.at[zs], self.x_recv.at[zs], device)

    def across_in(self, zs):
        ref = self.block(zs, 1 - self.x, self.c, None if self.direct else self.y)
        return remote(ref, ref, self.x_send.at[zs], self.x_recv.at[zs], (self.dp, self.s))

    def over(self, zs):
        ref = self.block(zs, 1 - self.x, self.c, self.y)
        return remote(ref, ref, self.y_send.at[zs], self.y_recv.at[zs], (self.dp, (1 - self.y) * 2 + self.c))

    def over_in(self, zs):
        ref = self.block(zs, 1 - self.x, self.c, 1 - self.y)
        return remote(ref, ref, self.y_send.at[zs], self.y_recv.at[zs], (self.dp, self.s))

    def share(self, kind, zs, core):
        if kind == 0:
            ref = self.block(zs, self.x, core)
        else:
            q = self.y if kind == 1 else 1 - self.y
            ref = self.block(zs, 1 - self.x, core, None if self.direct else q)
        j = kind * Z_CHIPS + zs
        return remote(ref, ref, self.c_send.at[j], self.c_recv.at[j], (self.dp, self.s + 1 - 2 * self.c))

    def each(self, k, what):
        if k == 0:
            what(self.z)
            return

        @pl.when(self.z >= k)
        def _():
            what(self.z - k)

        @pl.when(self.z + k < Z_CHIPS)
        def _():
            what(self.z + k)

    def stage(self, k):
        if k == 0:

            @pl.when(self.z < Z_CHIPS - 1)
            def _():
                self.up(self.z, True).start()

            @pl.when(self.z > 0)
            def _():
                self.down(self.z, True).start()

            self.across(self.z, True).start()
        elif k < Z_CHIPS:

            @pl.when(self.z >= k)
            def _():
                zs = self.z - k
                self.up(zs).wait_recv()

                @pl.when(self.z < Z_CHIPS - 1)
                def _():
                    self.up(zs).start()

                self.across(zs).start()
                self.share(0, zs, self.c).start()

            @pl.when(self.z + k < Z_CHIPS)
            def _():
                zs = self.z + k
                self.down(zs).wait_recv()

                @pl.when(self.z > 0)
                def _():
                    self.down(zs).start()

                self.across(zs).start()
                self.share(0, zs, self.c).start()

        if 1 <= k <= Z_CHIPS:

            def pass_x(zs):
                self.across_in(zs).wait_recv()
                if not self.direct:
                    self.over(zs).start()
                self.share(1, zs, self.c).start()

            self.each(k - 1, pass_x)
        if 2 <= k <= Z_CHIPS + 1 and not self.direct:

            def pass_y(zs):
                self.over_in(zs).wait_recv()
                self.share(2, zs, self.c).start()

            self.each(k - 2, pass_y)

    stages = Z_CHIPS + 2

    def finish(self):
        for kind in range(2 if self.direct else 3):
            for k in range(1 if kind == 0 else 0, Z_CHIPS):
                self.each(k, lambda zs, kind=kind: self.share(kind, zs, 1 - self.c).wait_recv())

    def settle(self):
        for k in range(Z_CHIPS):

            @pl.when((self.z >= k) & (self.z < Z_CHIPS - 1))
            def _():
                self.up(self.z - k, k == 0).wait_send()

            @pl.when((self.z + k < Z_CHIPS) & (self.z > 0))
            def _():
                self.down(self.z + k, k == 0).wait_send()

            self.each(k, lambda zs, k=k: self.across(zs, k == 0).wait_send())
            if not self.direct:
                self.each(k, lambda zs: self.over(zs).wait_send())
            for kind in range(2 if self.direct else 3):
                if kind > 0 or k > 0:
                    self.each(k, lambda zs, kind=kind: self.share(kind, zs, self.c).wait_send())


class Tokens:
    def __init__(self, long_ref, short_ref, out, send, recv, local):
        self.long_ref, self.short_ref, self.out, self.send, self.recv, self.local = long_ref, short_ref, out, send, recv, local
        self.dp, self.s = lax.axis_index("dp"), lax.axis_index("seq")

    def pieces(self, target, source):
        yield self.long_ref.at[target // 2, target % 2], self.out.at[source, pl.ds(0, 128)]
        yield self.short_ref.at[0, target], self.out.at[source, pl.ds(128, 64)]
        yield self.short_ref.at[1, target], self.out.at[source, pl.ds(192, 64)]

    def copies(self, k):
        target = (self.s + k) % 4
        for j, (src, dst) in enumerate(self.pieces(target, self.s)):
            yield remote(src, dst, self.send.at[k, j], self.recv.at[k, j], (self.dp, target))

    def own(self):
        for j, (src, dst) in enumerate(self.pieces(self.s, self.s)):
            yield pltpu.make_async_copy(src, dst, self.local.at[j])

    def start(self):
        for k in range(1, 4):
            for copy in self.copies(k):
                copy.start()
        for copy in self.own():
            copy.start()

    def finish(self):
        for copy in self.own():
            copy.wait()
        for k in range(1, 4):
            source = (self.s + 4 - k) % 4
            for j, (src, dst) in enumerate(self.pieces(self.s, source)):
                remote(src, dst, self.send.at[k, j], self.recv.at[k, j], (self.dp, self.s)).wait_recv()

    def settle(self):
        for k in range(1, 4):
            for copy in self.copies(k):
                copy.wait_send()


def forward_kernel(
    lens_ref,
    wide_ref,
    down_ref,
    vec_ref,
    long_in,
    short_in,
    long_cot,
    short_cot,
    qkv_w_out,
    wo_out,
    w1_out,
    w2_out,
    vec_out,
    tok_out,
    cot_out,
    qkv_out,
    att_out,
    long_probs,
    short_probs,
    own_wide,
    own_down,
    w_s,
    x_s,
    qkv_s,
    vec_s,
    bias_s,
    long_s,
    short_s,
    z_send,
    z_recv,
    x_send,
    x_recv,
    y_send,
    y_recv,
    c_send,
    c_recv,
    v_send,
    v_recv,
    t_send,
    t_recv,
    local,
    p_sem,
):
    dp, s, z, x, y, c = place()
    greet()
    tokens = Tokens(long_in, short_in, x_s, t_send.at[0], t_recv.at[0], local.at[0])
    cots = Tokens(long_cot, short_cot, cot_out, t_send.at[1], t_recv.at[1], local.at[1])
    tokens.start()
    own_wide[...] = wide_ref[...].astype(bf16)

    def vec_copy(k, source, target):
        return remote(vec_ref, vec_s.at[source], v_send.at[k], v_recv.at[k], (target, s))

    sems = lambda i: [
        r.at[i] for r in (z_send, z_recv, x_send, x_recv, y_send, y_recv, c_send, c_recv)
    ]
    parts = [
        Part(own_wide.at[:, pl.ds(0, 3 * D)], w_s, sems(0)),
        Part(own_wide.at[:, pl.ds(3 * D, D)], wo_out, sems(1)),
        Part(own_wide.at[:, pl.ds(4 * D, FF)], w1_out, sems(2)),
        Part(own_down, w2_out, sems(3), direct=True),
    ]
    first, others = parts[0], parts[1:]
    first.stage(0)
    for k in range(1, 8):
        vec_copy(k, dp, (dp + k) % 8).start()
    own_down[...] = down_ref[...].astype(bf16)
    own_copies = [
        pltpu.make_async_copy(part.own, part.out.at[dp], local.at[2, i]) for i, part in enumerate(parts)
    ]
    own_copies.append(pltpu.make_async_copy(vec_ref, vec_s.at[dp], local.at[2, 4]))
    for copy in own_copies:
        copy.start()
    first.stage(1)
    parts[1].stage(0)
    first.stage(2)
    parts[2].stage(0)
    first.stage(3)
    first.stage(4)
    parts[3].stage(0)
    first.stage(5)
    cots.start()
    for copy in own_copies:
        copy.wait()
    for k in range(1, 8):
        vec_copy(k, (dp + 8 - k) % 8, dp).wait_recv()
    vec = vec_s[0].astype(f32)
    for d in range(1, 8):
        vec = vec + vec_s[d].astype(f32)
    vec_out[...] = vec
    bias_s[:, 0:D] = jnp.broadcast_to(vec[0:1, :], (8, D))
    bias_s[:, D : 2 * D] = jnp.zeros((8, D), f32)
    bias_s[:, 2 * D : 3 * D] = jnp.broadcast_to(vec[1:2, :], (8, D))
    tokens.finish()
    first.finish()
    keep_tokens = pltpu.make_async_copy(x_s, tok_out, local.at[3, 0])
    keep_weights = pltpu.make_async_copy(w_s, qkv_w_out, local.at[3, 1])
    keep_tokens.start()
    keep_weights.start()

    def during(i, plan):
        for when, jobs in plan:

            @pl.when(i == when)
            def _():
                for index, stage in jobs:
                    parts[index].stage(stage)

    def project(j, carry):
        during(j, ((2, ((1, 1),)), (4, ((2, 1),)), (6, ((1, 2),)), (8, ((3, 1),))))
        cols = pl.ds(pl.multiple_of(j * 256, 256), 256)
        w = w_s[:, :, cols].reshape(D, 256)
        rows = x_s[...].reshape(1024, D)
        qkv_s[:, :, cols] = (dot_nn(rows, w) + bias_s[0:1, cols]).astype(bf16).reshape(4, 256, 256)
        return carry

    lax.fori_loop(0, 3 * D // 256, project, 0)
    keep_qkv = pltpu.make_async_copy(qkv_s, qkv_out, local.at[3, 2])
    keep_qkv.start()
    pairs = D // PAIR

    def keep_probs_copies(i, slot):
        return (
            pltpu.make_async_copy(long_s.at[slot], long_probs.at[pl.ds(2 * i, 2)], p_sem.at[0, slot]),
            pltpu.make_async_copy(short_s.at[slot], short_probs.at[pl.ds(2 * i, 2)], p_sem.at[1, slot]),
        )

    def attention(i, carry):
        during(
            i,
            (
                (0, ((2, 2), (1, 3))),
                (1, ((3, 2), (1, 4))),
                (2, ((2, 3), (1, 5))),
                (3, ((3, 3),)),
                (4, ((2, 4),)),
                (5, ((3, 4), (2, 5))),
            ),
        )
        slot = i % 2

        @pl.when(i >= 2)
        def _():
            for copy in keep_probs_copies(i - 2, slot):
                copy.wait()

        for first_row, rows, length, index in SEQS:
            q, k, v = [
                qkv_s[:, first_row : first_row + rows, pl.ds(pl.multiple_of(base + i * PAIR, PAIR), PAIR)].reshape(
                    length, PAIR
                )
                for base in (0, D, 2 * D)
            ]

            def keep_probs(h, probs, index=index):
                if index == 0:
                    long_s[slot, h] = probs
                else:
                    short_s[slot, h, index - 1] = probs

            o = attend(q, k, v, lens_ref[index], keep_probs)
            att_out[:, first_row : first_row + rows, pl.ds(pl.multiple_of(i * PAIR, PAIR), PAIR)] = o.reshape(
                4, rows, PAIR
            )
        for copy in keep_probs_copies(i, slot):
            copy.start()
        return carry

    lax.fori_loop(0, pairs, attention, 0)
    parts[3].stage(5)
    for part in others:
        part.finish()
    cots.finish()
    keep_tokens.wait()
    keep_weights.wait()
    keep_qkv.wait()
    for i in (pairs - 2, pairs - 1):
        for copy in keep_probs_copies(i, i % 2):
            copy.wait()
    for k in range(1, 8):
        vec_copy(k, dp, (dp + k) % 8).wait_send()
    for part in parts:
        part.settle()
    tokens.settle()
    cots.settle()


def forward(lens, wide_master, down_master, vec_block, long_in, short_in, long_cot, short_cot):
    any_spec = pl.BlockSpec(memory_space=pl.ANY)
    vmem = pl.BlockSpec(memory_space=pltpu.VMEM)
    smem = pl.BlockSpec(memory_space=pltpu.SMEM)
    shape = jax.ShapeDtypeStruct
    rows, down_rows = wide_master.shape[0], down_master.shape[0]
    dma = pltpu.SemaphoreType.DMA
    heads = D // HEAD_DIM
    return pl.pallas_call(
        forward_kernel,
        in_specs=[smem, vmem, vmem, vmem] + [any_spec] * 4,
        out_specs=[any_spec] * 4 + [vmem] + [any_spec] * 3 + [vmem] + [any_spec] * 2,
        out_shape=[
            shape((8, rows, 3 * D), bf16),
            shape((8, rows, D), bf16),
            shape((8, rows, FF), bf16),
            shape((8, down_rows, D), bf16),
            shape((16, D), f32),
            shape((4, 256, D), bf16),
            shape((4, 256, D), bf16),
            shape((4, 256, 3 * D), bf16),
            shape((4, 256, D), bf16),
            shape((heads, LONG_L, LONG_L), bf16),
            shape((heads, 2, SHORT_L, SHORT_L), bf16),
        ],
        scratch_shapes=[
            pltpu.VMEM((rows, 4 * D + FF), bf16),
            pltpu.VMEM((down_rows, D), bf16),
            pltpu.VMEM((8, rows, 3 * D), bf16),
            pltpu.VMEM((4, 256, D), bf16),
            pltpu.VMEM((4, 256, 3 * D), bf16),
            pltpu.VMEM((8, 16, D), bf16),
            pltpu.VMEM((8, 3 * D), f32),
            pltpu.VMEM((2, 2, LONG_L, LONG_L), bf16),
            pltpu.VMEM((2, 2, 2, SHORT_L, SHORT_L), bf16),
            dma((4, 4, 2)),
            dma((4, 4)),
            dma((4, 4)),
            dma((4, 4)),
            dma((4, 4)),
            dma((4, 4)),
            dma((4, 12)),
            dma((4, 12)),
            dma((8,)),
            dma((8,)),
            dma((2, 4, 3)),
            dma((2, 4, 3)),
            dma((4, 5)),
            dma((2, 2)),
        ],
        compiler_params=pltpu.CompilerParams(
            vmem_limit_bytes=VMEM_BYTES, collective_id=0, has_side_effects=True
        ),
        name="forward",
    )(lens, wide_master, down_master, vec_block, long_in, short_in, long_cot, short_cot)


class Grad:
    def __init__(self, theirs, acc, cbuf, xbuf, ybuf, zbuf, quarter, fin, sems, order):
        self.theirs, self.acc, self.cbuf, self.xbuf, self.ybuf, self.zbuf = theirs, acc, cbuf, xbuf, ybuf, zbuf
        self.quarter, self.fin, self.order = quarter, fin, order
        self.c_send, self.c_recv, self.x_send, self.x_recv, self.y_send, self.y_recv = sems[:6]
        self.z_send, self.z_recv, self.f_send, self.f_recv, self.local = sems[6:]
        self.dp, self.s, self.z, self.x, self.y, self.c = place()
        self.rows, cols = fin.shape
        self.half_rows, self.half_cols = self.rows // 2, cols // 2
        self.core_pieces = 4 if order == "zxy" else 2

    def cols(self, core):
        return pl.ds(pl.multiple_of(core * self.half_cols, 128), self.half_cols)

    def some(self, q):
        return pl.ds(pl.multiple_of(q * self.half_rows, 16), self.half_rows)

    def core_view(self, ref, j):
        if self.order == "zxy":
            return ref.at[j]
        return ref.at[:, (1 - self.x) if j == 0 else self.x]

    def core_copy(self, j):
        return remote(
            self.core_view(self.theirs, j),
            self.core_view(self.cbuf, j),
            self.c_send.at[j],
            self.c_recv.at[j],
            (self.dp, self.s + 1 - 2 * self.c),
        )

    def x_copy(self, zd):
        device = (self.z * 2 + 1 - self.x, self.s)
        j = zd if self.order == "xyz" else 0
        return remote(self.acc.at[zd, 1 - self.x], self.xbuf.at[j], self.x_send.at[j], self.x_recv.at[j], device)

    def y_copy(self, zd):
        device = (self.dp, (1 - self.y) * 2 + self.c)
        j = zd if self.order == "xyz" else 0
        src = self.acc.at[zd, self.x, self.some(1 - self.y)]
        return remote(src, self.ybuf.at[j], self.y_send.at[j], self.y_recv.at[j], device)

    def z_copy(self, k):
        zd = (self.z + k) % Z_CHIPS
        src = self.acc.at[zd, self.x, self.some(self.y)] if self.order == "xyz" else self.acc.at[zd]
        return remote(
            src, self.zbuf.at[k - 1], self.z_send.at[k], self.z_recv.at[k], (zd * 2 + self.x, self.s)
        )

    def fin_quarter(self, s):
        return self.fin.at[self.some(s // 2), self.cols(s % 2)]

    def fin_copy(self, k):
        return remote(
            self.quarter,
            self.fin_quarter(self.s),
            self.f_send.at[k],
            self.f_recv.at[k],
            (self.dp, (self.s + k) % 4),
        )

    def fin_in(self, k):
        ref = self.fin_quarter((self.s + 4 - k) % 4)
        return remote(self.quarter, ref, self.f_send.at[k], self.f_recv.at[k], (self.dp, self.s))

    def fin_own(self):
        return pltpu.make_async_copy(self.quarter, self.fin_quarter(self.s), self.local)

    def core_start(self, j):
        self.core_copy(j).start()

    def core_sent(self):
        for j in range(self.core_pieces):
            self.core_copy(j).wait_send()

    def z_block(self, k):
        zd = (self.z + k) % Z_CHIPS
        self.core_copy(zd).wait_recv()
        for xd in range(2):
            self.acc[zd, xd] = (self.acc[zd, xd].astype(f32) + self.cbuf[zd, xd].astype(f32)).astype(bf16)

        if k % Z_CHIPS:
            self.z_copy(k % Z_CHIPS).start()

    def core_add(self, j):
        xd = (1 - self.x) if j == 0 else self.x
        self.core_copy(j).wait_recv()

        def one(zd, carry):
            self.acc[zd, xd] = (self.acc[zd, xd].astype(f32) + self.cbuf[zd, xd].astype(f32)).astype(bf16)
            return carry

        lax.fori_loop(0, Z_CHIPS, one, 0)

    def pass_x(self, k):
        zd = (self.z + k + 1) % Z_CHIPS
        self.x_copy(zd).wait_recv()
        self.acc[zd, self.x] = (self.acc[zd, self.x].astype(f32) + self.xbuf[zd].astype(f32)).astype(bf16)
        self.y_copy(zd).start()

    def publish(self, total):
        self.quarter[...] = total.astype(bf16)
        self.fin_own().start()
        for k in range(1, 4):
            self.fin_copy(k).start()

    def stage(self, i):
        if not isinstance(i, int) or i >= 30:
            self.pass_x(i - 30)
        elif self.order == "xyz":
            if i == 1:
                self.core_add(0)
                for k in range(Z_CHIPS):
                    self.x_copy((self.z + k + 1) % Z_CHIPS).start()
            elif i == 2:
                self.core_add(1)
            elif i == 3:

                def pass_x(k, carry):
                    self.pass_x(k)
                    return carry

                lax.fori_loop(0, Z_CHIPS, pass_x, 0)
            elif i == 4:
                rows = self.some(self.y)
                for k in (1, 2, 3, 0):
                    zd = (self.z + k) % Z_CHIPS
                    self.y_copy(zd).wait_recv()
                    self.acc[zd, self.x, rows] = (
                        self.acc[zd, self.x, rows].astype(f32) + self.ybuf[zd].astype(f32)
                    ).astype(bf16)
                    if k:
                        self.z_copy(k).start()
            elif i == 5:
                total = self.acc[self.z, self.x, self.some(self.y)].astype(f32)
                for k in range(1, Z_CHIPS):
                    self.z_copy(k).wait_recv()
                    total = total + self.zbuf[k - 1].astype(f32)
                self.publish(total)
        else:
            if i == 3:
                for k in range(1, Z_CHIPS):
                    self.z_copy(k).wait_recv()
                for xd in range(2):
                    total = self.acc[self.z, xd].astype(f32)
                    for k in range(1, Z_CHIPS):
                        total = total + self.zbuf[k - 1, xd].astype(f32)
                    self.acc[self.z, xd] = total.astype(bf16)
                self.x_copy(self.z).start()
            elif i == 4:
                self.x_copy(self.z).wait_recv()
                total = self.acc[self.z, self.x].astype(f32) + self.xbuf[0].astype(f32)
                self.acc[self.z, self.x] = total.astype(bf16)
                self.y_copy(self.z).start()
            elif i == 5:
                self.y_copy(self.z).wait_recv()
                self.publish(self.acc[self.z, self.x, self.some(self.y)].astype(f32) + self.ybuf[0].astype(f32))
        if i == 6:
            self.fin_own().wait()
            for k in range(1, 4):
                self.fin_in(k).wait_recv()

    def settle(self):
        for k in range(1, Z_CHIPS):
            self.z_copy(k).wait_send()
        for k in range(1, 4):
            self.fin_copy(k).wait_send()
        for k in range(Z_CHIPS if self.order == "xyz" else 1):
            self.x_copy((self.z + k) % Z_CHIPS).wait_send()
            self.y_copy((self.z + k) % Z_CHIPS).wait_send()


class Returns:
    def __init__(self, rows_ref, long_out, short_out, send, recv, local):
        self.rows_ref, self.long_out, self.short_out = rows_ref, long_out, short_out
        self.send, self.recv, self.local = send, recv, local
        self.dp, self.s = lax.axis_index("dp"), lax.axis_index("seq")

    def pieces(self, target, source):
        yield self.rows_ref.at[target, pl.ds(0, 128)], self.long_out.at[source // 2, source % 2]
        yield self.rows_ref.at[target, pl.ds(128, 64)], self.short_out.at[0, source]
        yield self.rows_ref.at[target, pl.ds(192, 64)], self.short_out.at[1, source]

    copies, own, start, finish, settle = Tokens.copies, Tokens.own, Tokens.start, Tokens.finish, Tokens.settle


def sums_window(d):
    return jnp.minimum(d * 96 // 128, 4) * 128


class Sums:
    def __init__(self, src, sbuf, part, dbuf, out, sems):
        self.src, self.sbuf, self.part, self.dbuf, self.out = src, sbuf, part, dbuf, out
        self.s_send, self.s_recv, self.d_send, self.d_recv = sems
        self.dp, self.s = lax.axis_index("dp"), lax.axis_index("seq")

    def s_copy(self, k, source):
        return remote(self.src, self.sbuf.at[source], self.s_send.at[k], self.s_recv.at[k], (self.dp, (self.s + k) % 4))

    def window(self, d):
        return self.part.at[:, pl.ds(pl.multiple_of(sums_window(d), 128), 256)]

    def d_copy(self, k, source):
        target = (self.dp + k) % 8
        return remote(self.window(target), self.dbuf.at[source], self.d_send.at[k], self.d_recv.at[k], (target, self.s))

    def stage(self, i):
        if i == 0:
            for k in range(1, 4):
                self.s_copy(k, self.s).start()
            self.sbuf[self.s] = self.src[...]
        elif i == 1:
            for k in range(1, 4):
                self.s_copy(k, (self.s + 4 - k) % 4).wait_recv()
            self.part[...] = (self.sbuf[0] + self.sbuf[1]) + (self.sbuf[2] + self.sbuf[3])
            for k in range(1, 8):
                self.d_copy(k, self.dp).start()
            self.dbuf[self.dp] = self.window(self.dp)[...]
        elif i == 2:
            for k in range(1, 8):
                self.d_copy(k, (self.dp + 8 - k) % 8).wait_recv()
            total = self.dbuf[0]
            for d in range(1, 8):
                total = total + self.dbuf[d]
            self.out[...] = total

    def settle(self):
        for k in range(1, 4):
            self.s_copy(k, self.s).wait_send()
        for k in range(1, 8):
            self.d_copy(k, self.dp).wait_send()


PIECES = (
    ("down", 384, D, "zxy"),
    ("one", 96, FF, "xyz"),
    ("o", 96, D, "xyz"),
    ("qkv0", 96, D, "xyz"),
    ("qkv1", 96, D, "xyz"),
    ("qkv2", 96, D, "xyz"),
)


def backward_kernel(*refs):
    refs = list(refs)

    def take(n):
        out = refs[:n]
        del refs[:n]
        return out

    lens_ref, sums_in = take(2)
    act_hbm, dfb_hbm, y1b_hbm, dub_hbm, att_hbm, dab_hbm, dob_hbm, qkv_hbm = take(8)
    long_hbm, short_hbm, tok_hbm, dh_hbm, w_hbm, out_rows = take(6)
    fins = take(len(PIECES))
    (sums_out,) = take(1)
    short_out, long_out, short_back, long_back = take(4)
    theirs_a, theirs_b = take(2)
    bufs = [take(6) for _ in PIECES]
    big, dfb_s, y1b_s, att_s, at_s, qkv_s, dob_s, long_s, short_s, dh_s, w_s, dqkv_s, back_s = take(13)
    sums_s, sbuf, part, dbuf = take(4)
    sems = take(11)
    s_sems = take(4)
    t_send, t_recv, local, load_sem, big_sem, p_sem = take(6)

    dp, s, z, x, y, c = place()
    greet()
    outs = Returns(out_rows, long_out, short_out, t_send.at[0], t_recv.at[0], local.at[0])
    backs = Returns(back_s, long_back, short_back, t_send.at[1], t_recv.at[1], local.at[1])

    def load(i, src, dst):
        copy = pltpu.make_async_copy(src, dst, load_sem.at[i])
        copy.start()
        return copy

    def act_chunk(k):
        zd = (z + k) % Z_CHIPS
        return act_hbm.at[:, pl.ds(pl.multiple_of(zd * D, D), D)]

    def dub_chunk(k):
        first = jnp.where(k < 2, (1 - c) * 2 + k, c * 2 + k - 2)
        return dub_hbm.at[:, pl.ds(pl.multiple_of(first * D, D), D)]

    def big_copy(src, slot):
        return pltpu.make_async_copy(src, big.at[slot], big_sem.at[slot])

    big_copy(act_chunk(1), 1).start()
    load_dfb = load(0, dfb_hbm, dfb_s)
    load_y1b = load(1, y1b_hbm, y1b_s)
    load_att = load(2, att_hbm, att_s)
    load_qkv = load(3, qkv_hbm, qkv_s)
    load_dob = load(4, dob_hbm, dob_s)
    load_w = load(5, w_hbm, w_s)
    load_dh = load(6, dh_hbm, dh_s)

    pieces = []
    for i, (name, rows, cols, order) in enumerate(PIECES):
        theirs = (theirs_a, theirs_b)[i] if i < 2 else theirs_a.at[:, :, pl.ds((i - 2) * 96, 96), :]
        pieces.append(Grad(theirs, *bufs[i], fins[i], [r.at[i] for r in sems], order))
    down, one, o_piece = pieces[:3]
    sums = Sums(sums_s, sbuf, part, dbuf, sums_out, s_sems)
    outs.start()

    def columns(core, width):
        return pl.ds(pl.multiple_of(core * width, 128), width)

    load_dfb.wait()

    def down_block(k, carry):
        zd = (z + k) % Z_CHIPS
        slot = k % 2
        big_copy(act_chunk(k), slot).wait()

        @pl.when(k < Z_CHIPS)
        def _():
            big_copy(act_chunk(k + 1), 1 - slot).start()

        @pl.when(k == Z_CHIPS)
        def _():
            big_copy(dub_chunk(0), 1 - slot).start()

        at_s[...] = jnp.transpose(big[slot])
        theirs_a[zd] = dot_nn(at_s[...], dfb_s[:, columns(1 - c, D // 2)]).astype(bf16).reshape(2, 384, D // 2)
        down.core_start(zd)
        down.acc[zd] = dot_nn(at_s[...], dfb_s[:, columns(c, D // 2)]).astype(bf16).reshape(2, 384, D // 2)
        for j in range(2, Z_CHIPS + 1):

            @pl.when(k == j)
            def _():
                down.z_block(j - 1)

        return carry

    lax.fori_loop(1, Z_CHIPS + 1, down_block, 0)
    load_dab = load(0, dab_hbm, dfb_s)

    load_y1b.wait()
    at_s[...] = jnp.transpose(y1b_s[...])
    load_tok = load(1, tok_hbm, y1b_s)

    def one_block(k, carry):
        slot = (k + 1) % 2
        big_copy(dub_chunk(k), slot).wait()

        @pl.when(k < 3)
        def _():
            big_copy(dub_chunk(k + 1), 1 - slot).start()

        grad = dot_nn(at_s[...], big[slot]).astype(bf16).reshape(4, 2, 96, D)
        cols = pl.ds(pl.multiple_of((k % 2) * D, D), D)

        @pl.when(k < 2)
        def _():
            theirs_b[:, :, :, cols] = grad

        @pl.when(k >= 2)
        def _():
            one.acc[:, :, :, cols] = grad

        @pl.when(k == 1)
        def _():
            one.core_start(0)
            one.core_start(1)
            down.z_block(Z_CHIPS)

        return carry

    lax.fori_loop(0, 4, one_block, 0)
    one.stage(1)
    down.core_sent()

    def small_grad(piece, right):
        piece.theirs[...] = dot_nn(at_s[...], right(1 - c)).astype(bf16).reshape(4, 2, 96, D // 2)
        piece.core_start(0)
        piece.core_start(1)
        piece.acc[...] = dot_nn(at_s[...], right(c)).astype(bf16).reshape(4, 2, 96, D // 2)

    load_att.wait()
    at_s[...] = jnp.transpose(att_s[...].reshape(1024, D))
    load_dab.wait()
    small_grad(o_piece, lambda core: dfb_s[:, columns(core, D // 2)])
    one.stage(2)
    o_piece.stage(1)

    load_tok.wait()
    at_s[...] = jnp.transpose(y1b_s[...])
    load_qkv.wait()
    load_dob.wait()
    load_w.wait()
    load_dh.wait()
    sums_s[...] = sums_in[...]
    pairs = D // PAIR

    def probs_copies(i, slot):
        return (
            pltpu.make_async_copy(long_hbm.at[pl.ds(2 * i, 2)], long_s.at[slot], p_sem.at[0, slot]),
            pltpu.make_async_copy(short_hbm.at[pl.ds(2 * i, 2)], short_s.at[slot], p_sem.at[1, slot]),
        )

    for copy in probs_copies(0, 0):
        copy.start()

    def run(jobs):
        for index, stage in jobs:
            pieces[index].stage(stage)

    before = (
        ((2, 2),),
        ((1, 30),),
        ((3, 2),),
        ((1, 31),),
        ((4, 2), (1, 32)),
        ((1, 33),),
    )
    after = (
        ((3, 1),),
        ((4, 1),),
        ((5, 1), (5, 2), (1, 4)),
    )
    tail = (
        (2, 3), (2, 4), (1, 5), (0, 3), (3, 3), (3, 4), (2, 5), (0, 4), (4, 3), (4, 4), (3, 5), (0, 5),
        (5, 3), (5, 4), (4, 5), (5, 5),
    )
    for g in range(3):

        def pair(i, carry, g=g):
            for j in range(2):

                @pl.when(i == 2 * g + j)
                def _():
                    run(before[2 * g + j])

            slot = i % 2
            for copy in probs_copies(i, slot):
                copy.wait()

            @pl.when(i + 1 < pairs)
            def _():
                for copy in probs_copies(i + 1, 1 - slot):
                    copy.start()

            lanes = pl.ds(pl.multiple_of(i * PAIR, PAIR), PAIR)
            sum_q = jnp.zeros((1, PAIR), f32)
            sum_v = jnp.zeros((1, PAIR), f32)
            for first, rows, length, index in SEQS:
                q, k, v = [
                    qkv_s[:, first : first + rows, pl.ds(pl.multiple_of(base + i * PAIR, PAIR), PAIR)].reshape(length, PAIR)
                    for base in (0, D, 2 * D)
                ]
                do, o = [r[:, first : first + rows, lanes].reshape(length, PAIR) for r in (dob_s, att_s)]
                kept = lambda h, index=index: long_s[slot, h] if index == 0 else short_s[slot, h, index - 1]
                grads = attend_back(q, k, v, do, o, lens_ref[index], kept)
                sum_q = sum_q + jnp.sum(grads[0].astype(f32), axis=0, keepdims=True)
                sum_v = sum_v + jnp.sum(grads[2].astype(f32), axis=0, keepdims=True)
                for j in range(3):
                    dst = pl.ds(pl.multiple_of(j * 256 + (i % 2) * PAIR, PAIR), PAIR)
                    dqkv_s[:, first : first + rows, dst] = grads[j].reshape(4, rows, PAIR)
            sums_s[0:1, lanes] = sum_q
            sums_s[1:2, lanes] = sum_v
            return carry

        lax.fori_loop(2 * g, 2 * g + 2, pair, 0)
        small_grad(pieces[3 + g], lambda core: dqkv_s[:, :, columns(core, D // 2)].reshape(1024, D // 2))
        run(after[g])
        if g == 2:
            sums.stage(0)
        total = dh_s[...]
        for j in range(3):
            total = total + dot_nt(
                dqkv_s[:, :, j * 256 : (j + 1) * 256].reshape(1024, 256), w_s[:, j * D + g * 256 : j * D + (g + 1) * 256]
            )
        if g < 2:
            dh_s[...] = total
        else:
            back_s[...] = total.astype(bf16).reshape(4, 256, D)

    backs.start()
    sums.stage(1)
    run(tail)
    sums.stage(2)
    run([(i, 6) for i in range(6)])
    outs.finish()
    backs.finish()
    for i, piece in enumerate(pieces):
        if i > 0:
            piece.core_sent()
        piece.settle()
    sums.settle()
    outs.settle()
    backs.settle()


def backward(lens, sums, arrays, out_rows):
    any_spec = pl.BlockSpec(memory_space=pl.ANY)
    vmem = pl.BlockSpec(memory_space=pltpu.VMEM)
    smem = pl.BlockSpec(memory_space=pltpu.SMEM)
    shape = jax.ShapeDtypeStruct
    dma = pltpu.SemaphoreType.DMA
    count = len(PIECES)
    bufs = []
    for name, rows, cols, order in PIECES:
        half, cut = cols // 2, rows // 2
        blocks = 4 if order == "xyz" else 1
        bufs += [
            pltpu.VMEM((4, 2, rows, half), bf16),
            pltpu.VMEM((4, 2, rows, half), bf16),
            pltpu.VMEM((blocks, rows, half), bf16),
            pltpu.VMEM((blocks, cut, half), bf16),
            pltpu.VMEM((3, cut, half) if order == "xyz" else (3, 2, rows, half), bf16),
            pltpu.VMEM((cut, half), bf16),
        ]
    n = 1024
    return pl.pallas_call(
        backward_kernel,
        in_specs=[smem, vmem] + [any_spec] * (len(arrays) + 1),
        out_specs=[any_spec] * count + [vmem] + [any_spec] * 4,
        out_shape=[shape((rows, cols), bf16) for _, rows, cols, _ in PIECES]
        + [
            shape((16, 256), f32),
            shape((2, 4, 64, D), bf16),
            shape((2, 2, 128, D), bf16),
            shape((2, 4, 64, D), bf16),
            shape((2, 2, 128, D), bf16),
        ],
        scratch_shapes=[pltpu.VMEM((4, 2, 384, D // 2), bf16), pltpu.VMEM((4, 2, 96, FF // 2), bf16)]
        + bufs
        + [
            pltpu.VMEM((2, n, D), bf16),
            pltpu.VMEM((n, D), bf16),
            pltpu.VMEM((n, D), bf16),
            pltpu.VMEM((4, 256, D), bf16),
            pltpu.VMEM((D, n), bf16),
            pltpu.VMEM((4, 256, 3 * D), bf16),
            pltpu.VMEM((4, 256, D), bf16),
            pltpu.VMEM((2, 2, LONG_L, LONG_L), bf16),
            pltpu.VMEM((2, 2, 2, SHORT_L, SHORT_L), bf16),
            pltpu.VMEM((n, D), f32),
            pltpu.VMEM((D, 3 * D), bf16),
            pltpu.VMEM((4, 256, D), bf16),
            pltpu.VMEM((4, 256, D), bf16),
            pltpu.VMEM((16, D), f32),
            pltpu.VMEM((4, 16, D), f32),
            pltpu.VMEM((16, D), f32),
            pltpu.VMEM((8, 16, 256), f32),
        ]
        + [dma((count, 4))] * 10
        + [dma((count,))]
        + [dma((4,)), dma((4,)), dma((8,)), dma((8,))]
        + [dma((2, 4, 3)), dma((2, 4, 3)), dma((2, 3)), dma((7,)), dma((2,)), dma((2, 2))],
        compiler_params=pltpu.CompilerParams(
            vmem_limit_bytes=VMEM_BYTES, collective_id=1, has_side_effects=True
        ),
        name="backward",
    )(lens, sums, *arrays, out_rows)


def transpose_dot(left, right):
    return jnp.einsum("ra,rb->ab", left, right, preferred_element_type=f32)


def right_dot(left, right):
    return jnp.einsum("ra,ba->rb", left, right, preferred_element_type=f32)


def flip(v, axis, bit):
    n = lax.axis_size(axis)
    return lax.ppermute(v, axis, [(i, i ^ bit) for i in range(n)])


def half_of(v, dim, which):
    size = v.shape[dim] // 2
    return lax.dynamic_slice_in_dim(v, which * size, size, dim)


def halve(v, axis, bit, dim):
    mine = (lax.axis_index(axis) // bit) % 2
    other = flip(half_of(v, dim, 1 - mine), axis, bit)
    return (half_of(v, dim, mine).astype(f32) + other.astype(f32)).astype(bf16)


def double(v, axis, bit, dim):
    mine = (lax.axis_index(axis) // bit) % 2
    other = flip(v, axis, bit)
    return jnp.where(
        mine == 0, jnp.concatenate([v, other], axis=dim), jnp.concatenate([other, v], axis=dim)
    )


def reduce_rows(grad):
    rows, cols = grad.shape
    dp = lax.axis_size("dp")
    v = grad.reshape(dp, rows // dp, cols)
    v = halve(v, "seq", 1, 2)
    v = halve(v, "seq", 2, 2)
    bit = 1
    while bit < dp:
        blocks = v.shape[0]
        v = v.reshape(blocks // 2, 2, v.shape[1], v.shape[2]) if v.ndim == 3 else v
        v = halve(v, "dp", bit, 1)[:, 0]
        bit *= 2
    v = v[0]
    v = double(v, "seq", 2, 1)
    v = double(v, "seq", 1, 1)
    return v.astype(f32)


def update(master, reduced_grad, moment, average):
    step_grad = reduced_grad + decay_weight * master
    velocity = momentum_rate * moment + step_grad
    updated = master - learning_rate * (step_grad + momentum_rate * velocity)
    averaged = average_rate * average + (1.0 - average_rate) * updated
    return (velocity, averaged, updated, updated.astype(jnp.bfloat16))


def spread_rows(long_part, short_part):
    long_blocks = long_part.reshape(4, 128, D)
    short_blocks = jnp.transpose(short_part, (1, 0, 2, 3)).reshape(4, 128, D)
    return jnp.concatenate([long_blocks, short_blocks], axis=1)


def exchange(v):
    return lax.all_to_all(v, "seq", split_axis=0, concat_axis=0, tiled=True)


def collect_rows(v):
    long_part = v[:, :128].reshape(2, 2, 128, D)
    short_part = jnp.transpose(v[:, 128:].reshape(4, 2, 64, D), (1, 0, 2, 3))
    return short_part, long_part


def body(
    short_in,
    long_in,
    short_cot,
    long_cot,
    short_len,
    long_len,
    wide_master,
    down_master,
    vector_master,
    wide_moment,
    down_moment,
    vector_moment,
    wide_average,
    down_average,
    vector_average,
):
    s = lax.axis_index("seq")
    lens = jnp.stack([long_len[s // 2, 0, s % 2], short_len[0, 0, s], short_len[1, 0, s]])
    if lax.axis_size("dp") == 8:
        own = vector_master.shape[0]
        vec_own = jnp.pad(jnp.transpose(vector_master).astype(bf16), ((0, 4), (0, 0)))
        vec_block = lax.dynamic_update_slice(
            jnp.zeros((16, D), bf16), vec_own, (0, lax.axis_index("dp") * own)
        )
        w_qkv, w_o, w_1, w_2, vec, tokens, cotangent, qkv, attended, long_probs, short_probs = forward(
            lens, wide_master, down_master, vec_block, long_in, short_in, long_cot, short_cot
        )
        w_qkv, w_o, w_1, w_2 = [w.reshape(-1, w.shape[2]) for w in (w_qkv, w_o, w_1, w_2)]
        rows = tokens.reshape(1024, D)
    else:
        tokens = exchange(spread_rows(long_in, short_in))
        cotangent = exchange(spread_rows(long_cot, short_cot))
        wide_w = lax.all_gather(wide_master.astype(bf16), "dp", axis=0, tiled=True)
        w_2 = lax.all_gather(down_master.astype(bf16), "dp", axis=0, tiled=True)
        vector_w = lax.all_gather(vector_master.astype(bf16), "dp", axis=0, tiled=True)
        vec = jnp.transpose(vector_w.astype(f32))
        w_qkv = wide_w[:, : 3 * D]
        w_o = wide_w[:, 3 * D : 4 * D]
        w_1 = wide_w[:, 4 * D :]
        rows = tokens.reshape(1024, D)
        proj_bias = jnp.concatenate([vec[0], jnp.zeros((D,), f32), vec[1]])
        qkv = (jnp.dot(rows, w_qkv, preferred_element_type=f32) + proj_bias).astype(bf16)
        qkv = qkv.reshape(4, 256, 3 * D)
        attended, long_probs, short_probs = attn_forward(lens, qkv)

    flat_attended = attended.reshape(1024, D)
    out, y1b, act, dfb, dub, dab, dob, dh, sums = middle(
        lens, flat_attended, rows, cotangent.reshape(1024, D), w_o, w_1, w_2, vec
    )
    own_rows = vector_master.shape[0]
    if lax.axis_size("dp") == 8:
        arrays = (
            act, dfb, y1b, dub, attended, dab, dob.reshape(4, 256, D), qkv, long_probs, short_probs, rows, dh, w_qkv
        )
        down_low, one_low, o_low, low_0, low_1, low_2, sums_own, short_out, long_out, short_back, long_back = backward(
            lens, sums, arrays, out.reshape(4, 256, D)
        )
        index = lax.axis_index("dp")
        own_sums = lax.dynamic_slice(sums_own, (0, index * own_rows - sums_window(index)), (12, own_rows))
        vector_reduced = jnp.transpose(own_sums)
        lows = [low[:, j * 256 : (j + 1) * 256] for j in range(3) for low in (low_0, low_1, low_2)]
        wide_reduced = jnp.concatenate(lows + [o_low, one_low], axis=1).astype(f32)
        down_reduced = down_low.astype(f32)
    else:
        d_down = transpose_dot(act, dfb).astype(bf16)
        d_one = transpose_dot(y1b, dub).astype(bf16)
        d_o = transpose_dot(flat_attended, dab).astype(bf16)
        dq, dk, dv, qv_sums = attn_backward(
            lens, qkv, dob.reshape(4, 256, D), attended, long_probs, short_probs
        )
        d_qkv = jnp.concatenate([dq, dk, dv], axis=2).reshape(1024, 3 * D)
        d_wqkv = transpose_dot(rows, d_qkv).astype(bf16)
        back = (dh + right_dot(d_qkv, w_qkv)).astype(bf16).reshape(4, 256, D)
        vector_total = jnp.concatenate([qv_sums[:2], sums[2:12]], axis=0)
        vector_sum = jnp.transpose(lax.psum(vector_total, ("dp", "seq")))
        vector_reduced = lax.dynamic_slice_in_dim(vector_sum, lax.axis_index("dp") * own_rows, own_rows, 0)
        wide_reduced = jnp.concatenate([reduce_rows(d_wqkv), reduce_rows(d_o), reduce_rows(d_one)], axis=1)
        down_reduced = reduce_rows(d_down)
        short_out, long_out = collect_rows(exchange(out.reshape(4, 256, D)))
        short_back, long_back = collect_rows(exchange(back))
    wide_new = update(wide_master, wide_reduced, wide_moment, wide_average)
    down_new = update(down_master, down_reduced, down_moment, down_average)
    vector_new = update(vector_master, vector_reduced, vector_moment, vector_average)
    return (
        short_out,
        long_out,
        short_back,
        long_back,
        wide_reduced,
        down_reduced,
        vector_reduced,
        wide_new[0],
        down_new[0],
        vector_new[0],
        wide_new[1],
        down_new[1],
        vector_new[1],
        wide_new[2],
        down_new[2],
        vector_new[2],
        wide_new[3],
        down_new[3],
        vector_new[3],
    )


def solution(mesh):
    tok = P(None, "dp", "seq", None)
    lengths = P(None, "dp", None)
    state = P("dp", None)
    return jax.shard_map(
        body,
        mesh=mesh,
        in_specs=(tok,) * 4 + (lengths,) * 2 + (state,) * 9,
        out_specs=(tok,) * 4 + (state,) * 15,
        check_vma=False,
    )
```

```python
import jax
import jax.numpy as jnp
from jax import lax
from jax.experimental import pallas as pl
from jax.experimental.pallas import tpu as pltpu
from jax.sharding import PartitionSpec as P

D = 768
HEAD_DIM = 64
FF = 3072
PAIR = 128
LONG_L = 512
SHORT_L = 256
VMEM_BYTES = 62 * 1024 * 1024

norm_eps = 1e-12
mask_fill = -10000.0
learning_rate = 0.0002
momentum_rate = 0.9
decay_weight = 0.0001
average_rate = 0.9
score_scale = HEAD_DIM ** (-0.5)
f32 = jnp.float32
bf16 = jnp.bfloat16


def params():
    return pltpu.CompilerParams(vmem_limit_bytes=VMEM_BYTES)


def dot_nn(a, b):
    return lax.dot_general(a, b, (((1,), (0,)), ((), ())), preferred_element_type=f32)


def dot_nt(a, b):
    return lax.dot_general(a, b, (((1,), (1,)), ((), ())), preferred_element_type=f32)


SEQS = ((0, 128, LONG_L, 0), (128, 64, SHORT_L, 1), (192, 64, SHORT_L, 2))


def attend(q, k, v, limit, keep_probs):
    length = q.shape[0]
    v_t = jnp.transpose(v)
    head_lane = lax.broadcasted_iota(jnp.int32, (length, PAIR), 1) // HEAD_DIM
    live = lax.broadcasted_iota(jnp.int32, (length, length), 0) < limit
    parts = []
    for h in range(2):
        k_h = jnp.where(head_lane == h, k, jnp.zeros_like(k))
        scores = jnp.where(live, dot_nt(k_h, q) * score_scale, mask_fill)
        top = jnp.max(scores, axis=0, keepdims=True)
        exponent = jnp.exp(scores - top)
        total = jnp.sum(exponent, axis=0, keepdims=True)
        probs = (exponent * (1.0 / total)).astype(bf16)
        keep_probs(h, probs)
        parts.append(dot_nn(v_t[h * HEAD_DIM : (h + 1) * HEAD_DIM], probs))
    return jnp.transpose(jnp.concatenate(parts, axis=0)).astype(bf16)


def attn_forward_kernel(lens_ref, q_ref, k_ref, v_ref, o_ref, long_ref, short_ref):
    for first, rows, length, index in SEQS:
        q, k, v = [r[:, first : first + rows, :].reshape(length, PAIR) for r in (q_ref, k_ref, v_ref)]

        def keep_probs(h, probs, index=index):
            if index == 0:
                long_ref[h] = probs
            else:
                short_ref[h, index - 1] = probs

        o = attend(q, k, v, lens_ref[index], keep_probs)
        o_ref[:, first : first + rows, :] = o.reshape(4, rows, PAIR)


def attn_forward(lens, qkv):
    pairs = D // PAIR
    col = lambda base: pl.BlockSpec((4, 256, PAIR), lambda i, base=base: (0, 0, base + i))
    return pl.pallas_call(
        attn_forward_kernel,
        grid=(pairs,),
        in_specs=[
            pl.BlockSpec(memory_space=pltpu.SMEM),
            col(0),
            col(pairs),
            col(2 * pairs),
        ],
        out_specs=[
            pl.BlockSpec((4, 256, PAIR), lambda i: (0, 0, i)),
            pl.BlockSpec((2, LONG_L, LONG_L), lambda i: (i, 0, 0)),
            pl.BlockSpec((2, 2, SHORT_L, SHORT_L), lambda i: (i, 0, 0, 0)),
        ],
        out_shape=[
            jax.ShapeDtypeStruct((4, 256, D), bf16),
            jax.ShapeDtypeStruct((2 * pairs, LONG_L, LONG_L), bf16),
            jax.ShapeDtypeStruct((2 * pairs, 2, SHORT_L, SHORT_L), bf16),
        ],
        compiler_params=params(),
        name="attn_forward",
    )(lens, qkv, qkv, qkv)


def attend_back(q, k, v, do, o, limit, kept_probs):
    length = q.shape[0]
    k_t = jnp.transpose(k)
    inner = jnp.transpose(do.astype(f32) * o.astype(f32))
    head_lane = lax.broadcasted_iota(jnp.int32, (length, PAIR), 1) // HEAD_DIM
    live = lax.broadcasted_iota(jnp.int32, (length, length), 0) < limit
    dq_parts = []
    dk = jnp.zeros((length, PAIR), f32)
    dv = jnp.zeros((length, PAIR), f32)
    for h in range(2):
        keep = head_lane == h
        v_h, do_h, q_h = [jnp.where(keep, m, jnp.zeros_like(m)) for m in (v, do, q)]
        probs = kept_probs(h)
        delta = jnp.sum(inner[h * HEAD_DIM : (h + 1) * HEAD_DIM], axis=0, keepdims=True)
        d_probs = dot_nt(v_h, do)
        d_scores = jnp.where(live, probs.astype(f32) * (d_probs - delta), 0.0).astype(bf16)
        dv = dv + dot_nn(probs, do_h)
        dk = dk + dot_nn(d_scores, q_h)
        dq_parts.append(dot_nn(k_t[h * HEAD_DIM : (h + 1) * HEAD_DIM], d_scores))
    dq = jnp.transpose(jnp.concatenate(dq_parts, axis=0)) * score_scale
    return dq.astype(bf16), (dk * score_scale).astype(bf16), dv.astype(bf16)


def attn_backward_kernel(
    lens_ref, q_ref, k_ref, v_ref, do_ref, o_ref, long_ref, short_ref, dq_ref, dk_ref, dv_ref, sum_ref
):
    sum_q = jnp.zeros((1, PAIR), f32)
    sum_v = jnp.zeros((1, PAIR), f32)
    for first, rows, length, index in SEQS:
        args = [r[:, first : first + rows, :].reshape(length, PAIR) for r in (q_ref, k_ref, v_ref, do_ref, o_ref)]
        kept = lambda h, index=index: long_ref[h] if index == 0 else short_ref[h, index - 1]
        dq, dk, dv = attend_back(*args, lens_ref[index], kept)
        sum_q = sum_q + jnp.sum(dq.astype(f32), axis=0, keepdims=True)
        sum_v = sum_v + jnp.sum(dv.astype(f32), axis=0, keepdims=True)
        for ref, v in ((dq_ref, dq), (dk_ref, dk), (dv_ref, dv)):
            ref[:, first : first + rows, :] = v.reshape(4, rows, PAIR)
    sum_ref[0:1, :] = sum_q
    sum_ref[1:2, :] = sum_v
    sum_ref[2:8, :] = jnp.zeros((6, PAIR), f32)


def attn_backward(lens, qkv, d_attended, attended, long_probs, short_probs):
    pairs = D // PAIR
    col = lambda base: pl.BlockSpec((4, 256, PAIR), lambda i, base=base: (0, 0, base + i))
    return pl.pallas_call(
        attn_backward_kernel,
        grid=(pairs,),
        in_specs=[
            pl.BlockSpec(memory_space=pltpu.SMEM),
            col(0),
            col(pairs),
            col(2 * pairs),
            col(0),
            col(0),
            pl.BlockSpec((2, LONG_L, LONG_L), lambda i: (i, 0, 0)),
            pl.BlockSpec((2, 2, SHORT_L, SHORT_L), lambda i: (i, 0, 0, 0)),
        ],
        out_specs=[col(0), col(0), col(0), pl.BlockSpec((8, PAIR), lambda i: (0, i))],
        out_shape=[jax.ShapeDtypeStruct((4, 256, D), bf16)] * 3 + [jax.ShapeDtypeStruct((8, D), f32)],
        compiler_params=params(),
        name="attn_backward",
    )(lens, qkv, qkv, qkv, d_attended, attended, long_probs, short_probs)


def gelu_pair(u):
    a = jnp.abs(u)
    t = 1.0 / (1.0 + (0.3275911 * 0.5**0.5) * a)
    e = jnp.exp(-0.5 * u * u)
    poly = t * (0.254829592 + t * (-0.284496736 + t * (1.421413741 + t * (-1.453152027 + t * 1.061405429))))
    tail = 0.5 * poly * e
    cdf = jnp.where(u < 0.0, tail, 1.0 - tail)
    pdf = e * (0.5 / jnp.pi) ** 0.5
    return u * cdf, cdf + u * pdf


def row_mean(v):
    return jnp.mean(v, axis=-1, keepdims=True)


def middle_kernel(
    lens_ref,
    o_ref,
    x_ref,
    cot_ref,
    wo_ref,
    w1_ref,
    w2_ref,
    vec_ref,
    out_ref,
    y1b_ref,
    g_ref,
    dfb_ref,
    dub_ref,
    dab_ref,
    dob_ref,
    dh_ref,
    sum_ref,
    slope_ref,
):
    r = pl.program_id(0)
    rows = o_ref.shape[0]

    @pl.when(r == 0)
    def _():
        sum_ref[...] = jnp.zeros_like(sum_ref)

    def add(index, v):
        sum_ref[index : index + 1, :] += jnp.sum(v, axis=0, keepdims=True)

    vec = lambda i: vec_ref[i : i + 1, :]
    h = x_ref[...].astype(f32) + (dot_nn(o_ref[...], wo_ref[...]) + vec(2))
    centred = h - row_mean(h)
    inv1 = lax.rsqrt(row_mean(centred * centred) + norm_eps)
    norm1 = centred * inv1
    y1 = norm1 * vec(3) + vec(4)
    y1b = y1.astype(bf16)
    y1b_ref[...] = y1b
    z = y1 + vec(5)
    for c in range(FF // D):
        cols = slice(c * D, (c + 1) * D)
        act, slope = gelu_pair(dot_nn(y1b, w1_ref[:, cols]) + vec(8 + c))
        act = act.astype(bf16)
        g_ref[:, cols] = act
        slope_ref[:, cols] = slope
        z = z + dot_nn(act, w2_ref[cols, :])
    centred2 = z - row_mean(z)
    inv2 = lax.rsqrt(row_mean(centred2 * centred2) + norm_eps)
    norm2 = centred2 * inv2
    out_ref[...] = (norm2 * vec(6) + vec(7)).astype(bf16)

    j = lax.broadcasted_iota(jnp.int32, (rows, 1), 0)
    long_end = lens_ref[0] - r * 128
    short_end = [lens_ref[i] - r * 64 + first for i, first in ((1, 128), (2, 192))]
    live = j < jnp.where(j < 128, long_end, jnp.where(j < 192, short_end[0], short_end[1]))
    dr = jnp.where(live, cot_ref[...].astype(f32), 0.0)
    e2 = dr * vec(6)
    dz = inv2 * (e2 - row_mean(e2) - norm2 * row_mean(e2 * norm2))
    dfb = dz.astype(bf16)
    dfb_ref[...] = dfb
    add(6, dr * norm2)
    add(7, dr)
    add(5, dfb.astype(f32))
    dy1 = dz
    for c in range(FF // D):
        cols = slice(c * D, (c + 1) * D)
        dub = (dot_nt(dfb, w2_ref[cols, :]) * slope_ref[:, cols]).astype(bf16)
        dub_ref[:, cols] = dub
        add(8 + c, dub.astype(f32))
        dy1 = dy1 + dot_nt(dub, w1_ref[:, cols])
    add(3, dy1 * norm1)
    add(4, dy1)
    e1 = dy1 * vec(3)
    dh = inv1 * (e1 - row_mean(e1) - norm1 * row_mean(e1 * norm1))
    dab = dh.astype(bf16)
    dh_ref[...] = dh
    dab_ref[...] = dab
    add(2, dab.astype(f32))
    dob_ref[...] = dot_nt(dab, wo_ref[...]).astype(bf16)


def middle(lens, attended, tokens, cotangent, w_o, w_1, w_2, vec):
    n = tokens.shape[0]
    rows = 256
    row = lambda width: pl.BlockSpec((rows, width), lambda i: (i, 0))
    whole = lambda a: pl.BlockSpec(a.shape, lambda i: (0, 0), pipeline_mode=pl.Buffered(1))
    shape = jax.ShapeDtypeStruct
    return pl.pallas_call(
        middle_kernel,
        grid=(n // rows,),
        in_specs=[
            pl.BlockSpec(memory_space=pltpu.SMEM),
            row(D),
            row(D),
            row(D),
            whole(w_o),
            whole(w_1),
            whole(w_2),
            whole(vec),
        ],
        out_specs=[
            row(D),
            row(D),
            row(FF),
            row(D),
            row(FF),
            row(D),
            row(D),
            row(D),
            pl.BlockSpec((16, D), lambda i: (0, 0)),
        ],
        out_shape=[
            shape((n, D), bf16),
            shape((n, D), bf16),
            shape((n, FF), bf16),
            shape((n, D), bf16),
            shape((n, FF), bf16),
            shape((n, D), bf16),
            shape((n, D), bf16),
            shape((n, D), f32),
            shape((16, D), f32),
        ],
        scratch_shapes=[pltpu.VMEM((rows, FF), f32)],
        compiler_params=params(),
        name="middle",
    )(lens, attended, tokens, cotangent, w_o, w_1, w_2, vec)


MESH = pl.DeviceIdType.MESH
Z_CHIPS = 4


def place():
    dp = lax.axis_index("dp")
    s = lax.axis_index("seq")
    return dp, s, dp // 2, dp % 2, s // 2, s % 2


def remote(src, dst, send, recv, device):
    return pltpu.make_async_remote_copy(
        src_ref=src, dst_ref=dst, send_sem=send, recv_sem=recv, device_id=device, device_id_type=MESH
    )


def greet():
    dp, s = lax.axis_index("dp"), lax.axis_index("seq")
    barrier = pltpu.get_barrier_semaphore()
    for k in range(1, 8):
        pl.semaphore_signal(barrier, inc=1, device_id=((dp + k) % 8, s), device_id_type=MESH)
    for k in range(1, 4):
        pl.semaphore_signal(barrier, inc=1, device_id=(dp, (s + k) % 4), device_id_type=MESH)
    pl.semaphore_wait(barrier, 10)


def own_lengths(short_ref, long_ref):
    s = lax.axis_index("seq")
    return long_ref[s // 2, 0, s % 2], short_ref[0, 0, s], short_ref[1, 0, s]


class Part:
    def __init__(self, own, out, sems, direct=False):
        self.own, self.out, self.direct = own, out, direct
        self.z_send, self.z_recv, self.x_send, self.x_recv, self.y_send, self.y_recv, self.c_send, self.c_recv = sems
        self.dp, self.s, self.z, self.x, self.y, self.c = place()
        self.rows, cols = own.shape
        self.half_rows, self.half_cols = self.rows // 2, cols // 2

    def cols(self, core):
        return pl.ds(pl.multiple_of(core * self.half_cols, 128), self.half_cols)

    def some(self, q):
        return pl.ds(pl.multiple_of(q * self.half_rows, 16), self.half_rows)

    def block(self, zs, x, core, q=None):
        rows = slice(None) if q is None else self.some(q)
        return self.out.at[zs * 2 + x, rows, self.cols(core)]

    def source(self, zs, own, q=None):
        if own:
            rows = slice(None) if q is None else self.some(q)
            return self.own.at[rows, self.cols(self.c)]
        return self.block(zs, self.x, self.c, q)

    def up(self, zs, own=False):
        dst = self.block(zs, self.x, self.c)
        return remote(self.source(zs, own), dst, self.z_send.at[zs, 0], self.z_recv.at[zs], (self.dp + 2, self.s))

    def down(self, zs, own=False):
        dst = self.block(zs, self.x, self.c)
        return remote(self.source(zs, own), dst, self.z_send.at[zs, 1], self.z_recv.at[zs], (self.dp - 2, self.s))

    def across(self, zs, own=False):
        q = None if self.direct else self.y
        dst = self.block(zs, self.x, self.c, q)
        device = (self.z * 2 + 1 - self.x, self.s)
        return remote(self.source(zs, own, q), dst, self.x_send.at[zs], self.x_recv.at[zs], device)

    def across_in(self, zs):
        ref = self.block(zs, 1 - self.x, self.c, None if self.direct else self.y)
        return remote(ref, ref, self.x_send.at[zs], self.x_recv.at[zs], (self.dp, self.s))

    def over(self, zs):
        ref = self.block(zs, 1 - self.x, self.c, self.y)
        return remote(ref, ref, self.y_send.at[zs], self.y_recv.at[zs], (self.dp, (1 - self.y) * 2 + self.c))

    def over_in(self, zs):
        ref = self.block(zs, 1 - self.x, self.c, 1 - self.y)
        return remote(ref, ref, self.y_send.at[zs], self.y_recv.at[zs], (self.dp, self.s))

    def share(self, kind, zs, core):
        if kind == 0:
            ref = self.block(zs, self.x, core)
        else:
            q = self.y if kind == 1 else 1 - self.y
            ref = self.block(zs, 1 - self.x, core, None if self.direct else q)
        j = kind * Z_CHIPS + zs
        return remote(ref, ref, self.c_send.at[j], self.c_recv.at[j], (self.dp, self.s + 1 - 2 * self.c))

    def each(self, k, what):
        if k == 0:
            what(self.z)
            return

        @pl.when(self.z >= k)
        def _():
            what(self.z - k)

        @pl.when(self.z + k < Z_CHIPS)
        def _():
            what(self.z + k)

    def stage(self, k):
        if k == 0:

            @pl.when(self.z < Z_CHIPS - 1)
            def _():
                self.up(self.z, True).start()

            @pl.when(self.z > 0)
            def _():
                self.down(self.z, True).start()

            self.across(self.z, True).start()
        elif k < Z_CHIPS:

            @pl.when(self.z >= k)
            def _():
                zs = self.z - k
                self.up(zs).wait_recv()

                @pl.when(self.z < Z_CHIPS - 1)
                def _():
                    self.up(zs).start()

                self.across(zs).start()
                self.share(0, zs, self.c).start()

            @pl.when(self.z + k < Z_CHIPS)
            def _():
                zs = self.z + k
                self.down(zs).wait_recv()

                @pl.when(self.z > 0)
                def _():
                    self.down(zs).start()

                self.across(zs).start()
                self.share(0, zs, self.c).start()

        if 1 <= k <= Z_CHIPS:

            def pass_x(zs):
                self.across_in(zs).wait_recv()
                if not self.direct:
                    self.over(zs).start()
                self.share(1, zs, self.c).start()

            self.each(k - 1, pass_x)
        if 2 <= k <= Z_CHIPS + 1 and not self.direct:

            def pass_y(zs):
                self.over_in(zs).wait_recv()
                self.share(2, zs, self.c).start()

            self.each(k - 2, pass_y)

    stages = Z_CHIPS + 2

    def finish(self):
        for kind in range(2 if self.direct else 3):
            for k in range(1 if kind == 0 else 0, Z_CHIPS):
                self.each(k, lambda zs, kind=kind: self.share(kind, zs, 1 - self.c).wait_recv())

    def settle(self):
        for k in range(Z_CHIPS):

            @pl.when((self.z >= k) & (self.z < Z_CHIPS - 1))
            def _():
                self.up(self.z - k, k == 0).wait_send()

            @pl.when((self.z + k < Z_CHIPS) & (self.z > 0))
            def _():
                self.down(self.z + k, k == 0).wait_send()

            self.each(k, lambda zs, k=k: self.across(zs, k == 0).wait_send())
            if not self.direct:
                self.each(k, lambda zs: self.over(zs).wait_send())
            for kind in range(2 if self.direct else 3):
                if kind > 0 or k > 0:
                    self.each(k, lambda zs, kind=kind: self.share(kind, zs, self.c).wait_send())


class Tokens:
    def __init__(self, long_ref, short_ref, out, send, recv, local):
        self.long_ref, self.short_ref, self.out, self.send, self.recv, self.local = long_ref, short_ref, out, send, recv, local
        self.dp, self.s = lax.axis_index("dp"), lax.axis_index("seq")

    def pieces(self, target, source):
        yield self.long_ref.at[target // 2, target % 2], self.out.at[source, pl.ds(0, 128)]
        yield self.short_ref.at[0, target], self.out.at[source, pl.ds(128, 64)]
        yield self.short_ref.at[1, target], self.out.at[source, pl.ds(192, 64)]

    def copies(self, k):
        target = (self.s + k) % 4
        for j, (src, dst) in enumerate(self.pieces(target, self.s)):
            yield remote(src, dst, self.send.at[k, j], self.recv.at[k, j], (self.dp, target))

    def own(self):
        for j, (src, dst) in enumerate(self.pieces(self.s, self.s)):
            yield pltpu.make_async_copy(src, dst, self.local.at[j])

    def start(self):
        for k in range(1, 4):
            for copy in self.copies(k):
                copy.start()
        for copy in self.own():
            copy.start()

    def finish(self):
        for copy in self.own():
            copy.wait()
        for k in range(1, 4):
            source = (self.s + 4 - k) % 4
            for j, (src, dst) in enumerate(self.pieces(self.s, source)):
                remote(src, dst, self.send.at[k, j], self.recv.at[k, j], (self.dp, self.s)).wait_recv()

    def settle(self):
        for k in range(1, 4):
            for copy in self.copies(k):
                copy.wait_send()


def layer_norm_back(grad, normed, inverse):
    return inverse * (grad - row_mean(grad) - normed * row_mean(grad * normed))


def live_rows(r, lens_ref):
    j = lax.broadcasted_iota(jnp.int32, (256, 1), 0)
    ends = [lens_ref[0] - r * 128] + [lens_ref[i] - r * 64 + first for i, first in ((1, 128), (2, 192))]
    return j < jnp.where(j < 128, ends[0], jnp.where(j < 192, ends[1], ends[2]))


DIRECT = (True, False, False, True)
FIRST_JOBS = ((0, 1), (1, 1), (0, 2), (1, 2), (2, 0), (0, 3), (1, 3), (0, 4))
PROJECT_JOBS = {2: ((2, 1),), 4: ((1, 4),), 5: ((1, 5),), 8: ((2, 2), (3, 0))}
ATTENTION_JOBS = {2: ((2, 3),), 3: ((2, 4),), 4: ((2, 5), (3, 1), (4, 0))}
INNER_FIRST_JOBS = ()
INNER_JOBS = {0: ((3, 2),), 3: ((3, 3),)}
OUTER_FIRST_JOBS = ((3, 4),)


def forward_kernel(*refs):
    refs = list(refs)

    def take(n):
        out = refs[:n]
        del refs[:n]
        return out

    short_len_ref, long_len_ref, wide_ref, down_ref, vec_ref = take(5)
    long_in, short_in, long_cot, short_cot = take(4)
    qkv_w_out, wo_out, w1_out, w2_out, tok_out, qkv_out, att_out, probs_out = take(8)
    act_out, slope_out, y1b_out, norm_out, inv_out, dz_out, dfb_out, out_out = take(8)
    vec_out, sums_out = take(2)
    own_wide, own_down, w_s, wo_s, w1_s, w2_s, x_s, cot_s, qkv_s, att_s, vec_s, bias_s = take(12)
    stage_s, act_s, y1_s, y1b_s, norm_s, inv_s, dfb_s, out_s = take(8)
    z_send, z_recv, x_send, x_recv, y_send, y_recv, c_send, c_recv, v_send, v_recv, t_send, t_recv = take(12)
    local, keep_sem, stage_sem = take(3)

    dp, s, z, x, y, c = place()
    lens_ref = own_lengths(short_len_ref, long_len_ref)
    greet()
    tokens = Tokens(long_in, short_in, x_s, t_send.at[0], t_recv.at[0], local.at[0])
    cots = Tokens(long_cot, short_cot, cot_s, t_send.at[1], t_recv.at[1], local.at[1])
    tokens.start()
    own_wide[:, 0 : 3 * D] = wide_ref[:, 0 : 3 * D].astype(bf16)

    def vec_copy(k, source, target):
        return remote(vec_ref, vec_s.at[source], v_send.at[k], v_recv.at[k], (target, s))

    sems = lambda i: [
        r.at[i] for r in (z_send, z_recv, x_send, x_recv, y_send, y_recv, c_send, c_recv)
    ]
    owns = [own_wide.at[:, pl.ds(first, cols)] for first, cols in ((0, 3 * D), (3 * D, D), (4 * D, FF))] + [own_down]
    parts = [
        Part(own, out, sems(i), direct=DIRECT[i]) for i, (own, out) in enumerate(zip(owns, (w_s, wo_s, w1_s, w2_s)))
    ]

    def run(jobs):
        for index, stage in jobs:
            if index == len(parts):
                cots.start()
            else:
                parts[index].stage(stage)

    first = parts[0]
    first.stage(0)
    own_wide[:, 3 * D : 4 * D] = wide_ref[:, 3 * D : 4 * D].astype(bf16)
    parts[1].stage(0)
    for k in range(1, 8):
        vec_copy(k, dp, (dp + k) % 8).start()
    own_wide[:, 4 * D :] = wide_ref[:, 4 * D :].astype(bf16)
    own_down[...] = down_ref[...].astype(bf16)
    own_copies = [
        pltpu.make_async_copy(part.own, part.out.at[dp], local.at[2, i]) for i, part in enumerate(parts)
    ]
    own_copies.append(pltpu.make_async_copy(vec_ref, vec_s.at[dp], local.at[2, 4]))
    for copy in own_copies:
        copy.start()
    run(FIRST_JOBS)
    for copy in own_copies:
        copy.wait()
    for k in range(1, 8):
        vec_copy(k, (dp + 8 - k) % 8, dp).wait_recv()
    vec = vec_s[0].astype(f32)
    for d in range(1, 8):
        vec = vec + vec_s[d].astype(f32)
    vec_out[...] = vec
    bias_s[:, 0:D] = jnp.broadcast_to(vec[0:1, :], (8, D))
    bias_s[:, D : 2 * D] = jnp.zeros((8, D), f32)
    bias_s[:, 2 * D : 3 * D] = jnp.broadcast_to(vec[1:2, :], (8, D))
    sums_out[...] = jnp.zeros_like(sums_out)
    tokens.finish()
    first.finish()
    kept = []

    def keep(src, dst):
        copy = pltpu.make_async_copy(src, dst, keep_sem.at[len(kept)])
        copy.start()
        kept.append(copy)

    keep(x_s, tok_out)
    keep(w_s, qkv_w_out)

    def during(i, plan):
        for when, jobs in plan.items():

            @pl.when(i == when)
            def _():
                run(jobs)

    def project(j, carry):
        during(j, PROJECT_JOBS)
        cols = pl.ds(pl.multiple_of(j * 256, 256), 256)
        w = w_s[:, :, cols].reshape(D, 256)
        rows = x_s[...].reshape(1024, D)
        qkv_s[:, :, cols] = (dot_nn(rows, w) + bias_s[0:1, cols]).astype(bf16).reshape(4, 256, 256)
        return carry

    lax.fori_loop(0, 3 * D // 256, project, 0)
    keep(qkv_s, qkv_out)
    pairs = D // PAIR

    def probs_copy(i, slot):
        return pltpu.make_async_copy(stage_s.at[slot], probs_out.at[i], stage_sem.at[slot])

    def attention(i, carry):
        during(i, ATTENTION_JOBS)
        slot = i % 2

        @pl.when(i >= 2)
        def _():
            probs_copy(i - 2, slot).wait()

        lanes = pl.ds(pl.multiple_of(i * PAIR, PAIR), PAIR)
        for first_row, rows, length, index in SEQS:
            q, k, v = [
                qkv_s[:, first_row : first_row + rows, pl.ds(pl.multiple_of(base + i * PAIR, PAIR), PAIR)].reshape(
                    length, PAIR
                )
                for base in (0, D, 2 * D)
            ]

            def keep_probs(h, probs, index=index):
                if index == 0:
                    stage_s[slot, h * LONG_L : (h + 1) * LONG_L, 0:LONG_L] = probs
                else:
                    row = (2 * h + index - 1) * SHORT_L
                    stage_s[slot, row : row + SHORT_L, LONG_L : LONG_L + SHORT_L] = probs

            o = attend(q, k, v, lens_ref[index], keep_probs)
            att_s[:, first_row : first_row + rows, lanes] = o.reshape(4, rows, PAIR)
        probs_copy(i, slot).start()
        return carry

    lax.fori_loop(0, pairs, attention, 0)
    keep(att_s, att_out)
    run(INNER_FIRST_JOBS)
    parts[1].finish()
    parts[2].finish()
    keep(wo_s, wo_out)
    keep(w1_s, w1_out)
    row_vec = lambda i: vec_out[i : i + 1, :]

    def slope_copy(r, slot):
        return pltpu.make_async_copy(stage_s.at[slot], slope_out.at[r], stage_sem.at[slot])

    def inner(r, carry):
        during(r, INNER_JOBS)
        slot = r % 2

        @pl.when(r < 2)
        def _():
            probs_copy(pairs - 2 + r, slot).wait()

        @pl.when(r >= 2)
        def _():
            slope_copy(r - 2, slot).wait()

        h = x_s[r].astype(f32) + (dot_nn(att_s[r], wo_s[...].reshape(D, D)) + row_vec(2))
        centred = h - row_mean(h)
        inverse = lax.rsqrt(row_mean(centred * centred) + norm_eps)
        normed = centred * inverse
        y1 = normed * row_vec(3) + row_vec(4)
        y1b = y1.astype(bf16)
        y1_s[r] = y1
        y1b_s[r] = y1b
        norm_s[r] = normed.astype(bf16)
        inv_s[r] = jnp.broadcast_to(inverse, (256, 128))
        at = pl.ds(pl.multiple_of(r * 256, 256), 256)
        for k in range(FF // D):
            w = w1_s[:, :, k * D : (k + 1) * D].reshape(D, D)
            act, slope = gelu_pair(dot_nn(y1b, w) + row_vec(8 + k))
            act_s[k, at] = act.astype(bf16)
            stage_s[slot, k * 256 : (k + 1) * 256] = slope.astype(bf16)
        slope_copy(r, slot).start()
        return carry

    lax.fori_loop(0, 4, inner, 0)
    for src, dst in ((act_s, act_out), (y1b_s, y1b_out), (norm_s, norm_out), (inv_s, inv_out)):
        keep(src, dst)
    run(OUTER_FIRST_JOBS)
    parts[3].finish()
    keep(w2_s, w2_out)
    cots.finish()

    def outer(r, carry):
        at = pl.ds(pl.multiple_of(r * 256, 256), 256)
        total = y1_s[r] + row_vec(5)
        for k in range(FF // D):
            total = total + dot_nn(act_s[k, at], w2_s[2 * k : 2 * k + 2].reshape(D, D))
        centred = total - row_mean(total)
        inverse = lax.rsqrt(row_mean(centred * centred) + norm_eps)
        normed = centred * inverse
        out_s[r] = (normed * row_vec(6) + row_vec(7)).astype(bf16)
        dr = jnp.where(live_rows(r, lens_ref), cot_s[r].astype(f32), 0.0)
        dz = layer_norm_back(dr * row_vec(6), normed, inverse)
        dfb = dz.astype(bf16)
        y1_s[r] = dz
        dfb_s[r] = dfb
        for i, v in ((5, dfb.astype(f32)), (6, dr * normed), (7, dr)):
            sums_out[i : i + 1, :] += jnp.sum(v, axis=0, keepdims=True)
        return carry

    lax.fori_loop(0, 4, outer, 0)
    for src, dst in ((y1_s, dz_out), (dfb_s, dfb_out), (out_s, out_out)):
        keep(src, dst)
    for copy in kept:
        copy.wait()
    for r in (2, 3):
        slope_copy(r, r % 2).wait()
    for k in range(1, 8):
        vec_copy(k, dp, (dp + k) % 8).wait_send()
    for part in parts:
        part.settle()
    tokens.settle()
    cots.settle()


def forward(short_len, long_len, wide_master, down_master, vec_block, long_in, short_in, long_cot, short_cot):
    any_spec = pl.BlockSpec(memory_space=pl.ANY)
    vmem = pl.BlockSpec(memory_space=pltpu.VMEM)
    smem = pl.BlockSpec(memory_space=pltpu.SMEM)
    shape = jax.ShapeDtypeStruct
    rows, down_rows = wide_master.shape[0], down_master.shape[0]
    dma = pltpu.SemaphoreType.DMA
    tok = (4, 256, D)
    outs = [
        ((8, rows, 3 * D), bf16),
        ((8, rows, D), bf16),
        ((8, rows, FF), bf16),
        ((8, down_rows, D), bf16),
        (tok, bf16),
        ((4, 256, 3 * D), bf16),
        (tok, bf16),
        ((D // PAIR, 1024, D), bf16),
        ((4, 1024, D), bf16),
        ((4, 1024, D), bf16),
        (tok, bf16),
        (tok, bf16),
        ((4, 256, 128), f32),
        (tok, f32),
        (tok, bf16),
        (tok, bf16),
    ]
    vm = lambda dims, t=bf16: pltpu.VMEM(dims, t)
    return pl.pallas_call(
        forward_kernel,
        in_specs=[smem, smem, vmem, vmem, vmem] + [any_spec] * 4,
        out_specs=[any_spec] * len(outs) + [vmem] * 2,
        out_shape=[shape(dims, t) for dims, t in outs] + [shape((16, D), f32)] * 2,
        scratch_shapes=[
            vm((rows, 4 * D + FF)),
            vm((down_rows, D)),
            vm((8, rows, 3 * D)),
            vm((8, rows, D)),
            vm((8, rows, FF)),
            vm((8, down_rows, D)),
            vm(tok),
            vm(tok),
            vm((4, 256, 3 * D)),
            vm(tok),
            vm((8, 16, D)),
            vm((8, 3 * D), f32),
            vm((2, 1024, D)),
            vm((4, 1024, D)),
            vm(tok, f32),
            vm(tok),
            vm(tok),
            vm((4, 256, 128), f32),
            vm(tok),
            vm(tok),
            dma((4, 4, 2)),
            dma((4, 4)),
            dma((4, 4)),
            dma((4, 4)),
            dma((4, 4)),
            dma((4, 4)),
            dma((4, 12)),
            dma((4, 12)),
            dma((8,)),
            dma((8,)),
            dma((2, 4, 3)),
            dma((2, 4, 3)),
            dma((3, 5)),
            dma((16,)),
            dma((2,)),
        ],
        compiler_params=pltpu.CompilerParams(
            vmem_limit_bytes=VMEM_BYTES, collective_id=0, has_side_effects=True
        ),
        name="forward",
    )(short_len, long_len, wide_master, down_master, vec_block, long_in, short_in, long_cot, short_cot)


class Grad:
    def __init__(self, theirs, acc, cbuf, xbuf, ybuf, zbuf, quarter, fin, sems, order):
        self.theirs, self.acc, self.cbuf, self.xbuf, self.ybuf, self.zbuf = theirs, acc, cbuf, xbuf, ybuf, zbuf
        self.quarter, self.fin, self.order = quarter, fin, order
        self.c_send, self.c_recv, self.x_send, self.x_recv, self.y_send, self.y_recv = sems[:6]
        self.z_send, self.z_recv, self.f_send, self.f_recv, self.local = sems[6:]
        self.dp, self.s, self.z, self.x, self.y, self.c = place()
        self.rows, cols = fin.shape
        self.half_rows, self.half_cols = self.rows // 2, cols // 2
        self.by_z = self.rows == 384
        self.core_pieces = 4 if self.by_z else 2
        self.mine = self.some(self.y)

    def cols(self, core):
        return pl.ds(pl.multiple_of(core * self.half_cols, 128), self.half_cols)

    def some(self, q):
        return pl.ds(pl.multiple_of(q * self.half_rows, 16), self.half_rows)

    def core_view(self, ref, j):
        if self.by_z:
            return ref.at[j]
        if self.order[0] == "x":
            return ref.at[:, (1 - self.x) if j == 0 else self.x]
        return ref.at[:, :, self.some((1 - self.y) if j == 0 else self.y)]

    def core_copy(self, j):
        return remote(
            self.core_view(self.theirs, j),
            self.core_view(self.cbuf, j),
            self.c_send.at[j],
            self.c_recv.at[j],
            (self.dp, self.s + 1 - 2 * self.c),
        )

    def x_copy(self, zd):
        device = (self.z * 2 + 1 - self.x, self.s)
        j = 0 if self.order == "zxy" else zd
        src = self.acc.at[zd, 1 - self.x, self.mine] if self.order == "yxz" else self.acc.at[zd, 1 - self.x]
        return remote(src, self.xbuf.at[j], self.x_send.at[j], self.x_recv.at[j], device)

    def y_copy(self, zd):
        device = (self.dp, (1 - self.y) * 2 + self.c)
        j = 0 if self.order[2] == "y" else zd
        rows = self.some(1 - self.y)
        src = self.acc.at[zd, :, rows] if self.order == "yxz" else self.acc.at[zd, self.x, rows]
        return remote(src, self.ybuf.at[j], self.y_send.at[j], self.y_recv.at[j], device)

    def z_copy(self, k):
        zd = (self.z + k) % Z_CHIPS
        src = self.acc.at[zd, self.x, self.mine]
        if self.order == "zxy":
            src = self.acc.at[zd]
        elif self.order == "xzy":
            src = self.acc.at[zd, self.x]
        return remote(
            src, self.zbuf.at[k - 1], self.z_send.at[k], self.z_recv.at[k], (zd * 2 + self.x, self.s)
        )

    def fin_quarter(self, y, core):
        return self.fin.at[self.some(y), self.cols(core)]

    def fin_copy(self, k):
        device = (self.dp, (1 - self.y) * 2 + self.c) if k == 2 else (self.dp, self.s + 1 - 2 * self.c)
        y = 1 - self.y if k == 3 else self.y
        dst = self.fin_quarter(y, self.c)
        return remote(dst if k == 3 else self.quarter, dst, self.f_send.at[k], self.f_recv.at[k], device)

    def fin_in(self, k):
        ref = self.fin_quarter(self.y if k == 1 else 1 - self.y, self.c if k == 2 else 1 - self.c)
        return remote(self.quarter, ref, self.f_send.at[k], self.f_recv.at[k], (self.dp, self.s))

    def fin_own(self):
        return pltpu.make_async_copy(self.quarter, self.fin_quarter(self.y, self.c), self.local)

    def core_start(self):
        for j in range(self.core_pieces):
            self.core_copy(j).start()

    def core_sent(self):
        for j in range(self.core_pieces):
            self.core_copy(j).wait_send()

    def z_block(self, k):
        zd = (self.z + k) % Z_CHIPS
        self.core_copy(zd).wait_recv()
        for xd in range(2):
            self.acc[zd, xd] = (self.acc[zd, xd].astype(f32) + self.cbuf[zd, xd].astype(f32)).astype(bf16)
        if self.order[0] == "x":
            self.x_copy(zd).start()
        elif k % Z_CHIPS:
            self.z_copy(k % Z_CHIPS).start()

    def core_add(self, j):
        self.core_copy(j).wait_recv()
        if self.order[0] == "x":
            xd = (1 - self.x) if j == 0 else self.x

            def one(zd, carry):
                self.acc[zd, xd] = (self.acc[zd, xd].astype(f32) + self.cbuf[zd, xd].astype(f32)).astype(bf16)
                return carry

        else:
            rows = self.some((1 - self.y) if j == 0 else self.y)

            def one(zd, carry):
                for xd in range(2):
                    self.acc[zd, xd, rows] = (
                        self.acc[zd, xd, rows].astype(f32) + self.cbuf[zd, xd, rows].astype(f32)
                    ).astype(bf16)
                return carry

        lax.fori_loop(0, Z_CHIPS, one, 0)

    def second(self, k):
        zd = (self.z + k + 1) % Z_CHIPS
        if self.order[0] == "x":
            self.x_copy(zd).wait_recv()
            self.acc[zd, self.x] = (self.acc[zd, self.x].astype(f32) + self.xbuf[zd].astype(f32)).astype(bf16)
            if self.order == "xyz":
                self.y_copy(zd).start()
            elif k < 3:
                self.z_copy(k + 1).start()
        else:
            self.y_copy(zd).wait_recv()
            for xd in range(2):
                self.acc[zd, xd, self.mine] = (
                    self.acc[zd, xd, self.mine].astype(f32) + self.ybuf[zd, xd].astype(f32)
                ).astype(bf16)
            self.x_copy(zd).start()

    def third(self, k):
        zd = (self.z + k) % Z_CHIPS
        if self.order == "xyz":
            self.y_copy(zd).wait_recv()
            came = self.ybuf
        else:
            self.x_copy(zd).wait_recv()
            came = self.xbuf
        self.acc[zd, self.x, self.mine] = (
            self.acc[zd, self.x, self.mine].astype(f32) + came[zd].astype(f32)
        ).astype(bf16)
        if k:
            self.z_copy(k).start()

    def publish(self, total):
        self.quarter[...] = total.astype(bf16)
        self.fin_own().start()
        self.fin_copy(1).start()
        self.fin_copy(2).start()

    def stage(self, i):
        if i >= 40:
            self.third((i - 39) % Z_CHIPS)
        elif i >= 30:
            self.second(i - 30)
        elif i == 6:
            self.fin_in(2).wait_recv()
            self.fin_copy(3).start()
        elif i == 7:
            self.fin_own().wait()
            self.fin_in(1).wait_recv()
            self.fin_in(3).wait_recv()
        elif self.order != "zxy":
            if i == 1:
                self.core_add(0)
                for k in range(Z_CHIPS):
                    zd = (self.z + k + 1) % Z_CHIPS
                    (self.x_copy(zd) if self.order[0] == "x" else self.y_copy(zd)).start()
            elif i == 2:
                self.core_add(1)
            elif i == 3:
                for k in range(Z_CHIPS):
                    self.second(k)
            elif i == 4 and self.order == "xzy":
                total = self.acc[self.z, self.x].astype(f32)
                for k in range(1, Z_CHIPS):
                    self.z_copy(k).wait_recv()
                    total = total + self.zbuf[k - 1].astype(f32)
                self.acc[self.z, self.x] = total.astype(bf16)
                self.y_copy(self.z).start()
            elif i == 4:
                for k in (1, 2, 3, 0):
                    self.third(k)
            elif i == 5 and self.order == "xzy":
                self.y_copy(self.z).wait_recv()
                self.publish(self.acc[self.z, self.x, self.mine].astype(f32) + self.ybuf[0].astype(f32))
            elif i == 5:
                total = self.acc[self.z, self.x, self.mine].astype(f32)
                for k in range(1, Z_CHIPS):
                    self.z_copy(k).wait_recv()
                    total = total + self.zbuf[k - 1].astype(f32)
                self.publish(total)
        else:
            if i == 3:
                for k in range(1, Z_CHIPS):
                    self.z_copy(k).wait_recv()
                for xd in range(2):
                    total = self.acc[self.z, xd].astype(f32)
                    for k in range(1, Z_CHIPS):
                        total = total + self.zbuf[k - 1, xd].astype(f32)
                    self.acc[self.z, xd] = total.astype(bf16)
                self.x_copy(self.z).start()
            elif i == 4:
                self.x_copy(self.z).wait_recv()
                total = self.acc[self.z, self.x].astype(f32) + self.xbuf[0].astype(f32)
                self.acc[self.z, self.x] = total.astype(bf16)
                self.y_copy(self.z).start()
            elif i == 5:
                self.y_copy(self.z).wait_recv()
                self.publish(self.acc[self.z, self.x, self.mine].astype(f32) + self.ybuf[0].astype(f32))

    def settle(self):
        for k in range(1, Z_CHIPS):
            self.z_copy(k).wait_send()
        for k in range(1, 4):
            self.fin_copy(k).wait_send()
        for k in range(1 if self.order == "zxy" else Z_CHIPS):
            self.x_copy((self.z + k) % Z_CHIPS).wait_send()
        for k in range(1 if self.order[2] == "y" else Z_CHIPS):
            self.y_copy((self.z + k) % Z_CHIPS).wait_send()


class Returns:
    def __init__(self, rows_ref, long_out, short_out, send, recv, local):
        self.rows_ref, self.long_out, self.short_out = rows_ref, long_out, short_out
        self.send, self.recv, self.local = send, recv, local
        self.dp, self.s = lax.axis_index("dp"), lax.axis_index("seq")

    def pieces(self, target, source):
        yield self.rows_ref.at[target, pl.ds(0, 128)], self.long_out.at[source // 2, source % 2]
        yield self.rows_ref.at[target, pl.ds(128, 64)], self.short_out.at[0, source]
        yield self.rows_ref.at[target, pl.ds(192, 64)], self.short_out.at[1, source]

    copies, own, start, finish, settle = Tokens.copies, Tokens.own, Tokens.start, Tokens.finish, Tokens.settle


def sums_window(d):
    return jnp.minimum(d * 96 // 128, 4) * 128


class Sums:
    def __init__(self, src, sbuf, part, dbuf, out, sems):
        self.src, self.sbuf, self.part, self.dbuf, self.out = src, sbuf, part, dbuf, out
        self.s_send, self.s_recv, self.d_send, self.d_recv = sems
        self.dp, self.s = lax.axis_index("dp"), lax.axis_index("seq")

    def s_copy(self, k, source):
        return remote(self.src, self.sbuf.at[source], self.s_send.at[k], self.s_recv.at[k], (self.dp, (self.s + k) % 4))

    def window(self, d):
        return self.part.at[:, pl.ds(pl.multiple_of(sums_window(d), 128), 256)]

    def d_copy(self, k, source):
        target = (self.dp + k) % 8
        return remote(self.window(target), self.dbuf.at[source], self.d_send.at[k], self.d_recv.at[k], (target, self.s))

    def stage(self, i):
        if i == 0:
            for k in range(1, 4):
                self.s_copy(k, self.s).start()
            self.sbuf[self.s] = self.src[...]
        elif i == 1:
            for k in range(1, 4):
                self.s_copy(k, (self.s + 4 - k) % 4).wait_recv()
            self.part[...] = (self.sbuf[0] + self.sbuf[1]) + (self.sbuf[2] + self.sbuf[3])
            for k in range(1, 8):
                self.d_copy(k, self.dp).start()
            self.dbuf[self.dp] = self.window(self.dp)[...]
        elif i == 2:
            for k in range(1, 8):
                self.d_copy(k, (self.dp + 8 - k) % 8).wait_recv()
            total = self.dbuf[0]
            for d in range(1, 8):
                total = total + self.dbuf[d]
            self.out[...] = total

    def settle(self):
        for k in range(1, 4):
            self.s_copy(k, self.s).wait_send()
        for k in range(1, 8):
            self.d_copy(k, self.dp).wait_send()


PIECES = (
    (384, D, "xzy"),
    (192, D, "yxz"),
    (192, D, "xyz"),
    (96, D, "xzy"),
    (96, D, "xzy"),
    (96, D, "xzy"),
    (96, D, "xzy"),
)


MIDDLE_JOBS = {
    0: (),
    1: (),
    2: ((0, 30),),
    3: (),
}
ONE_JOBS = ((2, 1), (1, 1),)
O_JOBS = ((0, 31), (1, 2),)
BEFORE_PAIR = {
    0: (),
    1: (),
    2: ((0, 32),),
    3: ((2, 2), (2, 30), (1, 30), (1, 31), (3, 2), (4, 1), (3, 30),),
    4: ((3, 32), (1, 33), (5, 1), (1, 40), (4, 2), (3, 33), (2, 32), (1, 41), (2, 33), (4, 30), (0, 4),),
    5: ((3, 4), (5, 2), (2, 40), (5, 30), (4, 31), (0, 5), (5, 31),),
}
AFTER_GROUP = (
    ((3, 1),),
    ((3, 31), (2, 31), (1, 32), (0, 33),),
    ((1, 42),),
)
LAST_JOBS = ((5, 32), (6, 1), (6, 2), (1, 43), (3, 5), (5, 33), (6, 30), (4, 32), (4, 33), (6, 31), (6, 32), (6, 33), (5, 4), (2, 41), (4, 4), (1, 5), (2, 42), (5, 5), (0, 6), (6, 4), (4, 5), (5, 6), (6, 5), (2, 43), (2, 5), (3, 6), (6, 6), (1, 6), (4, 6), (2, 6),)


def backward_kernel(*refs):
    refs = list(refs)

    def take(n):
        out = refs[:n]
        del refs[:n]
        return out

    short_len_ref, long_len_ref, vec_ref, sums_in = take(4)
    act_hbm, slope_hbm, y1b_hbm, norm_hbm, inv_hbm, dz_hbm, dfb_hbm, att_hbm, qkv_hbm, probs_hbm = take(10)
    tok_hbm, w_hbm, wo_hbm, w1_hbm, w2_hbm, out_rows = take(6)
    fins = take(len(PIECES))
    (sums_out,) = take(1)
    short_out, long_out, short_back, long_back = take(4)
    (theirs_a,) = take(1)
    bufs = [take(6) for _ in PIECES]
    big, dfb_s, y1b_s, att_s, at_s, first_s, second_s, wo_s, dub_s, dh_s, dob_s, inv_s, dqkv_s = take(13)
    sums_s, sbuf, part, dbuf = take(4)
    sems = take(11)
    s_sems = take(4)
    t_send, t_recv, local, load_sem, big_sem = take(5)

    dp, s, z, x, y, c = place()
    lens_ref = own_lengths(short_len_ref, long_len_ref)
    greet()
    outs = Returns(out_rows, long_out, short_out, t_send.at[0], t_recv.at[0], local.at[0])
    backs = Returns(y1b_s, long_back, short_back, t_send.at[1], t_recv.at[1], local.at[1])

    def load(i, *pairs):
        copies = [pltpu.make_async_copy(src, dst, load_sem.at[i + j]) for j, (src, dst) in enumerate(pairs)]
        for copy in copies:
            copy.start()
        return copies

    def done(copies):
        for copy in copies:
            copy.wait()

    def big_copy(src, slot):
        return pltpu.make_async_copy(src, big.at[slot], big_sem.at[slot])

    def act_chunk(k):
        return act_hbm.at[(z + k) % Z_CHIPS]

    chunk = lambda i: pl.ds(i * D, D)
    big_copy(act_chunk(1), 1).start()
    load_dfb = load(0, (dfb_hbm, dfb_s))
    load_w2 = load(1, (w2_hbm, second_s))
    load_w1 = load(2, *[(w1_hbm.at[:, chunk(k)], first_s.at[chunk(k)]) for k in range(4)])
    load_mid = load(6, (dz_hbm, dh_s), (norm_hbm, dob_s), (inv_hbm, inv_s), (wo_hbm, wo_s))
    load_y1b = load(10, (y1b_hbm, y1b_s))
    load_att = load(11, (att_hbm, att_s))

    pieces = []
    for i, (rows, cols, order) in enumerate(PIECES):
        first = (0, 0, 192, 0, 96, 192, 288)[i]
        theirs = theirs_a.at[:, :, pl.ds(first, rows), :]
        pieces.append(Grad(theirs, *bufs[i], fins[i], [r.at[i] for r in sems], order))
    down, one_a, one_b, o_piece = pieces[:4]
    sums = Sums(sums_s, sbuf, part, dbuf, sums_out, s_sems)
    outs.start()

    def run(jobs):
        for index, stage in jobs:
            pieces[index].stage(stage)

    def during(i, plan):
        for when, jobs in plan.items():

            @pl.when(i == when)
            def _():
                run(jobs)

    def columns(core):
        return pl.ds(pl.multiple_of(core * (D // 2), 128), D // 2)

    sums_s[...] = sums_in[...]
    done(load_dfb)

    def down_block(k, carry):
        zd = (z + k) % Z_CHIPS
        slot = k % 2
        big_copy(act_chunk(k), slot).wait()

        @pl.when(k < Z_CHIPS)
        def _():
            big_copy(act_chunk(k + 1), 1 - slot).start()

        @pl.when(k == Z_CHIPS)
        def _():
            big_copy(slope_hbm.at[0], 1 - slot).start()

        at_s[...] = jnp.transpose(big[slot])
        theirs_a[zd] = dot_nn(at_s[...], dfb_s[:, :, columns(1 - c)].reshape(1024, D // 2)).astype(bf16).reshape(2, 384, D // 2)
        down.core_copy(zd).start()
        down.acc[zd] = dot_nn(at_s[...], dfb_s[:, :, columns(c)].reshape(1024, D // 2)).astype(bf16).reshape(2, 384, D // 2)
        for j in range(2, Z_CHIPS + 1):

            @pl.when(k == j)
            def _():
                down.z_block(j - 1)

        return carry

    lax.fori_loop(1, Z_CHIPS + 1, down_block, 0)
    done(load_w2)
    done(load_w1)
    done(load_mid)
    row_vec = lambda i: vec_ref[i : i + 1, :]

    def add(index, v):
        sums_s[index : index + 1, :] += jnp.sum(v, axis=0, keepdims=True)

    def middle_back(r, carry):
        slot = (r + 1) % 2
        big_copy(slope_hbm.at[r], slot).wait()

        @pl.when(r < 3)
        def _():
            big_copy(slope_hbm.at[r + 1], 1 - slot).start()

        @pl.when(r == 0)
        def _():
            down.z_block(Z_CHIPS)

        during(r, MIDDLE_JOBS)
        at = pl.ds(pl.multiple_of(r * 256, 256), 256)
        dfb = dfb_s[r]
        dy1 = dh_s[r]
        for k in range(FF // D):
            slope = big[slot, k * 256 : (k + 1) * 256].astype(f32)
            dub = (dot_nt(dfb, second_s[k * D : (k + 1) * D]) * slope).astype(bf16)
            dub_s[k, at] = dub
            add(8 + k, dub.astype(f32))
            dy1 = dy1 + dot_nt(dub, first_s[k * D : (k + 1) * D])
        normed = dob_s[r].astype(f32)
        add(3, dy1 * normed)
        add(4, dy1)
        dh = layer_norm_back(dy1 * row_vec(3), normed, inv_s[r][:, 0:1])
        dab = dh.astype(bf16)
        dh_s[r] = dh
        dfb_s[r] = dab
        add(2, dab.astype(f32))
        dob_s[r] = dot_nt(dab, wo_s[...]).astype(bf16)
        return carry

    lax.fori_loop(0, 4, middle_back, 0)
    qkv_loads = load(1, *[(qkv_hbm.at[:, :, chunk(j)], first_s.at[pl.ds(j * 1024, 1024)].reshape(4, 256, D)) for j in range(3)])
    w_loads = load(4, *[(w_hbm.at[:, chunk(j)], second_s.at[chunk(j)]) for j in range(3)])

    def probs_copy(i, slot):
        return big_copy(probs_hbm.at[i], slot)

    probs_copy(0, 0).start()

    done(load_y1b)
    at_s[...] = jnp.transpose(y1b_s[...].reshape(1024, D))
    load_tok = load(10, (tok_hbm, y1b_s))
    down.core_sent()

    def one_block(k, carry):
        core = jnp.where(k < 2, 1 - c, c)
        grad = dot_nn(at_s[...], dub_s[core * 2 + k % 2]).astype(bf16)
        for e in range(2):
            half = grad[:, e * (D // 2) : (e + 1) * (D // 2)].reshape(4, 2, 96, D // 2)
            rows = pl.ds(e * 96, 96)
            for j, ref in enumerate((one_a.theirs, one_b.theirs, one_a.acc, one_b.acc)):

                @pl.when(k == j)
                def _():
                    ref[:, :, rows, :] = half

        for j, piece in ((0, one_a), (1, one_b)):

            @pl.when(k == j)
            def _():
                piece.core_start()

        return carry

    lax.fori_loop(0, 4, one_block, 0)
    run(ONE_JOBS)
    one_a.core_sent()
    one_b.core_sent()

    def small_grad(piece, right):
        piece.theirs[...] = dot_nn(at_s[...], right(1 - c)).astype(bf16).reshape(4, 2, 96, D // 2)
        piece.core_start()
        piece.acc[...] = dot_nn(at_s[...], right(c)).astype(bf16).reshape(4, 2, 96, D // 2)

    done(load_att)
    at_s[...] = jnp.transpose(att_s[...].reshape(1024, D))
    small_grad(o_piece, lambda core: dfb_s[:, :, columns(core)].reshape(1024, D // 2))
    run(O_JOBS)

    done(load_tok)
    at_s[...] = jnp.transpose(y1b_s[...].reshape(1024, D))
    done(qkv_loads)
    done(w_loads)
    pairs = D // PAIR

    for g in range(3):

        def pair(i, carry, g=g):
            during(i, {j: BEFORE_PAIR[j] for j in (2 * g, 2 * g + 1)})
            slot = i % 2
            probs_copy(i, slot).wait()

            @pl.when(i + 1 < pairs)
            def _():
                probs_copy(i + 1, 1 - slot).start()

            lanes = pl.ds(pl.multiple_of(i * PAIR, PAIR), PAIR)
            sum_q = jnp.zeros((1, PAIR), f32)
            sum_v = jnp.zeros((1, PAIR), f32)
            for first, rows, length, index in SEQS:
                q, k, v = [
                    first_s[j * 1024 : (j + 1) * 1024, lanes].reshape(4, 256, PAIR)[:, first : first + rows].reshape(length, PAIR)
                    for j in range(3)
                ]
                do, o = [r[:, first : first + rows, lanes].reshape(length, PAIR) for r in (dob_s, att_s)]

                def kept(h, index=index):
                    if index == 0:
                        return big[slot, h * LONG_L : (h + 1) * LONG_L, 0:LONG_L]
                    row = (2 * h + index - 1) * SHORT_L
                    return big[slot, row : row + SHORT_L, LONG_L : LONG_L + SHORT_L]

                grads = attend_back(q, k, v, do, o, lens_ref[index], kept)
                sum_q = sum_q + jnp.sum(grads[0].astype(f32), axis=0, keepdims=True)
                sum_v = sum_v + jnp.sum(grads[2].astype(f32), axis=0, keepdims=True)
                for j in range(3):
                    dst = pl.ds(pl.multiple_of(j * 256 + (i % 2) * PAIR, PAIR), PAIR)
                    dqkv_s[:, first : first + rows, dst] = grads[j].reshape(4, rows, PAIR)
            sums_s[0:1, lanes] = sum_q
            sums_s[1:2, lanes] = sum_v
            return carry

        lax.fori_loop(2 * g, 2 * g + 2, pair, 0)
        small_grad(pieces[4 + g], lambda core: dqkv_s[:, :, columns(core)].reshape(1024, D // 2))
        if g == 2:
            sums.stage(0)

        def rows_back(r, carry, g=g):
            total = dh_s[r]
            for j in range(3):
                total = total + dot_nt(
                    dqkv_s[r, :, j * 256 : (j + 1) * 256], second_s[j * D : (j + 1) * D, g * 256 : (g + 1) * 256]
                )
            if g < 2:
                dh_s[r] = total
            else:
                y1b_s[r] = total.astype(bf16)
            return carry

        if g == 2:
            lax.fori_loop(0, 4, rows_back, 0)
            backs.start()
            run(AFTER_GROUP[g])
        else:
            run(AFTER_GROUP[g])
            lax.fori_loop(0, 4, rows_back, 0)

    sums.stage(1)
    run(LAST_JOBS)
    sums.stage(2)
    run([(i, 7) for i in range(len(PIECES))])
    outs.finish()
    backs.finish()
    for i, piece in enumerate(pieces):
        if i > 2:
            piece.core_sent()
        piece.settle()
    sums.settle()
    outs.settle()
    backs.settle()


def backward(short_len, long_len, vec, sums, arrays, out_rows):
    any_spec = pl.BlockSpec(memory_space=pl.ANY)
    vmem = pl.BlockSpec(memory_space=pltpu.VMEM)
    smem = pl.BlockSpec(memory_space=pltpu.SMEM)
    shape = jax.ShapeDtypeStruct
    dma = pltpu.SemaphoreType.DMA
    count = len(PIECES)
    vm = lambda dims, t=bf16: pltpu.VMEM(dims, t)
    bufs = []
    for rows, cols, order in PIECES:
        half, cut = cols // 2, rows // 2
        bufs += [vm((4, 2, rows, half)), vm((4, 2, rows, half))]
        bufs += {
            "xyz": [vm((4, rows, half)), vm((4, cut, half)), vm((3, cut, half))],
            "yxz": [vm((4, cut, half)), vm((4, 2, cut, half)), vm((3, cut, half))],
            "xzy": [vm((4, rows, half)), vm((1, cut, half)), vm((3, rows, half))],
            "zxy": [vm((1, rows, half)), vm((1, cut, half)), vm((3, 2, rows, half))],
        }[order]
        bufs.append(vm((cut, half)))
    tok = (4, 256, D)
    return pl.pallas_call(
        backward_kernel,
        in_specs=[smem, smem, vmem, vmem] + [any_spec] * (len(arrays) + 1),
        out_specs=[any_spec] * count + [vmem] + [any_spec] * 4,
        out_shape=[shape((rows, cols), bf16) for rows, cols, _ in PIECES]
        + [
            shape((16, 256), f32),
            shape((2, 4, 64, D), bf16),
            shape((2, 2, 128, D), bf16),
            shape((2, 4, 64, D), bf16),
            shape((2, 2, 128, D), bf16),
        ],
        scratch_shapes=[vm((4, 2, 384, D // 2))]
        + bufs
        + [
            vm((2, 1024, D)),
            vm(tok),
            vm(tok),
            vm(tok),
            vm((D, 1024)),
            vm((FF, D)),
            vm((FF, D)),
            vm((D, D)),
            vm((4, 1024, D)),
            vm(tok, f32),
            vm(tok),
            vm((4, 256, 128), f32),
            vm(tok),
            vm((16, D), f32),
            vm((4, 16, D), f32),
            vm((16, D), f32),
            vm((8, 16, 256), f32),
        ]
        + [dma((count, 4))] * 10
        + [dma((count,))]
        + [dma((4,)), dma((4,)), dma((8,)), dma((8,))]
        + [dma((2, 4, 3)), dma((2, 4, 3)), dma((2, 3)), dma((12,)), dma((2,))],
        compiler_params=pltpu.CompilerParams(
            vmem_limit_bytes=VMEM_BYTES, collective_id=1, has_side_effects=True
        ),
        name="backward",
    )(short_len, long_len, vec, sums, *arrays, out_rows)


def transpose_dot(left, right):
    return jnp.einsum("ra,rb->ab", left, right, preferred_element_type=f32)


def right_dot(left, right):
    return jnp.einsum("ra,ba->rb", left, right, preferred_element_type=f32)


def flip(v, axis, bit):
    n = lax.axis_size(axis)
    return lax.ppermute(v, axis, [(i, i ^ bit) for i in range(n)])


def half_of(v, dim, which):
    size = v.shape[dim] // 2
    return lax.dynamic_slice_in_dim(v, which * size, size, dim)


def halve(v, axis, bit, dim):
    mine = (lax.axis_index(axis) // bit) % 2
    other = flip(half_of(v, dim, 1 - mine), axis, bit)
    return (half_of(v, dim, mine).astype(f32) + other.astype(f32)).astype(bf16)


def double(v, axis, bit, dim):
    mine = (lax.axis_index(axis) // bit) % 2
    other = flip(v, axis, bit)
    return jnp.where(
        mine == 0, jnp.concatenate([v, other], axis=dim), jnp.concatenate([other, v], axis=dim)
    )


def reduce_rows(grad):
    rows, cols = grad.shape
    dp = lax.axis_size("dp")
    v = grad.reshape(dp, rows // dp, cols)
    v = halve(v, "seq", 1, 2)
    v = halve(v, "seq", 2, 2)
    bit = 1
    while bit < dp:
        blocks = v.shape[0]
        v = v.reshape(blocks // 2, 2, v.shape[1], v.shape[2]) if v.ndim == 3 else v
        v = halve(v, "dp", bit, 1)[:, 0]
        bit *= 2
    v = v[0]
    v = double(v, "seq", 2, 1)
    v = double(v, "seq", 1, 1)
    return v.astype(f32)


def update(master, reduced_grad, moment, average):
    step_grad = reduced_grad + decay_weight * master
    velocity = momentum_rate * moment + step_grad
    updated = master - learning_rate * (step_grad + momentum_rate * velocity)
    averaged = average_rate * average + (1.0 - average_rate) * updated
    return (velocity, averaged, updated, updated.astype(jnp.bfloat16))


UPDATE_STEPS = 8


def update_kernel(*refs):
    refs = list(refs)

    def take(n):
        out = refs[:n]
        del refs[:n]
        return out

    down_low, one_a, one_b, o_low, low_0, low_1, low_2 = take(7)
    wide_state, down_state, passed = take(3), take(3), take(4)
    wide_out, down_out, passed_out = take(5), take(5), take(4)
    (grad_s,) = take(1)
    i = pl.program_id(0)
    for src, dst in zip(passed, passed_out):
        dst[...] = src[...]
    half = D // 2
    for b in range(UPDATE_STEPS):

        @pl.when(i == b)
        def _():
            if b < 3:
                for g, low in enumerate((low_0, low_1, low_2)):
                    grad_s[:, g * 256 : (g + 1) * 256] = low[:, b * 256 : (b + 1) * 256]
            elif b == 3:
                grad_s[...] = o_low[...]
            else:
                rows, core = grad_s.shape[0], (b - 4) // 2
                low = (one_a, one_b)[b % 2]
                for k in range(2):
                    part = low[k * rows : (k + 1) * rows, core * half : (core + 1) * half]
                    grad_s[:, k * half : (k + 1) * half] = part

    def step(grad, state, outs):
        master, moment, average = state
        outs[0][...] = grad
        for ref, v in zip(outs[1:], update(master[...], grad, moment[...], average[...])):
            ref[...] = v

    step(grad_s[...].astype(f32), wide_state, wide_out)
    rows = down_state[0].shape[0]
    step(down_low[pl.ds(pl.multiple_of(i * rows, 16), rows)].astype(f32), down_state, down_out)


def update_all(lows, wide, down, passed):
    rows, cols = wide[0].shape
    down_rows = down[0].shape[0]
    vmem = pl.BlockSpec(memory_space=pltpu.VMEM)
    short_spec = pl.BlockSpec((1, 1, 64, D), lambda i: (i // 4, i % 4, 0, 0))
    long_spec = pl.BlockSpec((1, 1, 64, D), lambda i: (i // 4, i % 4 // 2, i % 2, 0))
    passed_specs = [short_spec, long_spec, short_spec, long_spec]
    shape = jax.ShapeDtypeStruct
    wide_spec = pl.BlockSpec((rows, cols // UPDATE_STEPS), lambda i: (0, i))
    down_spec = pl.BlockSpec((down_rows // UPDATE_STEPS, D), lambda i: (i, 0))
    types = (f32, f32, f32, f32, bf16)
    return pl.pallas_call(
        update_kernel,
        grid=(UPDATE_STEPS,),
        in_specs=[vmem] * len(lows) + [wide_spec] * 3 + [down_spec] * 3 + passed_specs,
        out_specs=[wide_spec] * 5 + [down_spec] * 5 + passed_specs,
        out_shape=[shape((rows, cols), t) for t in types]
        + [shape((down_rows, D), t) for t in types]
        + [shape(p.shape, p.dtype) for p in passed],
        scratch_shapes=[pltpu.VMEM((rows, D), bf16)],
        compiler_params=params(),
        name="update",
    )(*lows, *wide, *down, *passed)


def spread_rows(long_part, short_part):
    long_blocks = long_part.reshape(4, 128, D)
    short_blocks = jnp.transpose(short_part, (1, 0, 2, 3)).reshape(4, 128, D)
    return jnp.concatenate([long_blocks, short_blocks], axis=1)


def exchange(v):
    return lax.all_to_all(v, "seq", split_axis=0, concat_axis=0, tiled=True)


def collect_rows(v):
    long_part = v[:, :128].reshape(2, 2, 128, D)
    short_part = jnp.transpose(v[:, 128:].reshape(4, 2, 64, D), (1, 0, 2, 3))
    return short_part, long_part


def body(
    short_in,
    long_in,
    short_cot,
    long_cot,
    short_len,
    long_len,
    wide_master,
    down_master,
    vector_master,
    wide_moment,
    down_moment,
    vector_moment,
    wide_average,
    down_average,
    vector_average,
):
    s = lax.axis_index("seq")
    own_rows = vector_master.shape[0]
    if lax.axis_size("dp") == 8:
        vec_own = jnp.pad(jnp.transpose(vector_master).astype(bf16), ((0, 4), (0, 0)))
        vec_block = lax.dynamic_update_slice(
            jnp.zeros((16, D), bf16), vec_own, (0, lax.axis_index("dp") * own_rows)
        )
        (w_qkv, w_o, w_1, w_2, tokens, qkv, attended, probs, act, slope, y1b, norm, inv, dz, dfb, out, vec, sums) = forward(
            short_len, long_len, wide_master, down_master, vec_block, long_in, short_in, long_cot, short_cot
        )
        w_qkv, w_o, w_1, w_2 = [w.reshape(-1, w.shape[2]) for w in (w_qkv, w_o, w_1, w_2)]
        arrays = (act, slope, y1b, norm, inv, dz, dfb, attended, qkv, probs, tokens, w_qkv, w_o, w_1, w_2)
        *lows, sums_own, short_out, long_out, short_back, long_back = backward(
            short_len, long_len, vec, sums, arrays, out
        )
        index = lax.axis_index("dp")
        own_sums = lax.dynamic_slice(sums_own, (0, index * own_rows - sums_window(index)), (12, own_rows))
        vector_reduced = jnp.transpose(own_sums)
        results = update_all(
            lows,
            (wide_master, wide_moment, wide_average),
            (down_master, down_moment, down_average),
            (short_out, long_out, short_back, long_back),
        )
        wide_reduced, *wide_new = results[:5]
        down_reduced, *down_new = results[5:10]
        short_out, long_out, short_back, long_back = results[10:]
    else:
        lens = jnp.stack([long_len[s // 2, 0, s % 2], short_len[0, 0, s], short_len[1, 0, s]])
        tokens = exchange(spread_rows(long_in, short_in))
        cotangent = exchange(spread_rows(long_cot, short_cot))
        wide_w = lax.all_gather(wide_master.astype(bf16), "dp", axis=0, tiled=True)
        w_2 = lax.all_gather(down_master.astype(bf16), "dp", axis=0, tiled=True)
        vector_w = lax.all_gather(vector_master.astype(bf16), "dp", axis=0, tiled=True)
        vec = jnp.transpose(vector_w.astype(f32))
        w_qkv = wide_w[:, : 3 * D]
        w_o = wide_w[:, 3 * D : 4 * D]
        w_1 = wide_w[:, 4 * D :]
        rows = tokens.reshape(1024, D)
        proj_bias = jnp.concatenate([vec[0], jnp.zeros((D,), f32), vec[1]])
        qkv = (jnp.dot(rows, w_qkv, preferred_element_type=f32) + proj_bias).astype(bf16)
        qkv = qkv.reshape(4, 256, 3 * D)
        attended, long_probs, short_probs = attn_forward(lens, qkv)
        flat_attended = attended.reshape(1024, D)
        out, y1b, act, dfb, dub, dab, dob, dh, sums = middle(
            lens, flat_attended, rows, cotangent.reshape(1024, D), w_o, w_1, w_2, vec
        )
        d_down = transpose_dot(act, dfb).astype(bf16)
        d_one = transpose_dot(y1b, dub).astype(bf16)
        d_o = transpose_dot(flat_attended, dab).astype(bf16)
        dq, dk, dv, qv_sums = attn_backward(
            lens, qkv, dob.reshape(4, 256, D), attended, long_probs, short_probs
        )
        d_qkv = jnp.concatenate([dq, dk, dv], axis=2).reshape(1024, 3 * D)
        d_wqkv = transpose_dot(rows, d_qkv).astype(bf16)
        back = (dh + right_dot(d_qkv, w_qkv)).astype(bf16).reshape(4, 256, D)
        vector_total = jnp.concatenate([qv_sums[:2], sums[2:12]], axis=0)
        vector_sum = jnp.transpose(lax.psum(vector_total, ("dp", "seq")))
        vector_reduced = lax.dynamic_slice_in_dim(vector_sum, lax.axis_index("dp") * own_rows, own_rows, 0)
        wide_reduced = jnp.concatenate([reduce_rows(d_wqkv), reduce_rows(d_o), reduce_rows(d_one)], axis=1)
        down_reduced = reduce_rows(d_down)
        short_out, long_out = collect_rows(exchange(out.reshape(4, 256, D)))
        short_back, long_back = collect_rows(exchange(back))
        wide_new = update(wide_master, wide_reduced, wide_moment, wide_average)
        down_new = update(down_master, down_reduced, down_moment, down_average)
    vector_new = update(vector_master, vector_reduced, vector_moment, vector_average)
    return (
        short_out,
        long_out,
        short_back,
        long_back,
        wide_reduced,
        down_reduced,
        vector_reduced,
        wide_new[0],
        down_new[0],
        vector_new[0],
        wide_new[1],
        down_new[1],
        vector_new[1],
        wide_new[2],
        down_new[2],
        vector_new[2],
        wide_new[3],
        down_new[3],
        vector_new[3],
    )


def solution(mesh):
    tok = P(None, "dp", "seq", None)
    lengths = P(None, "dp", None)
    state = P("dp", None)
    return jax.shard_map(
        body,
        mesh=mesh,
        in_specs=(tok,) * 4 + (lengths,) * 2 + (state,) * 9,
        out_specs=(tok,) * 4 + (state,) * 15,
        check_vma=False,
    )
```

```python
import jax
import jax.numpy as jnp
from jax import lax
from jax.experimental import pallas as pl
from jax.experimental.pallas import tpu as pltpu
from jax.sharding import PartitionSpec as P

D = 768
HEAD_DIM = 64
FF = 3072
PAIR = 128
LONG_L = 512
SHORT_L = 256
VMEM_BYTES = 62 * 1024 * 1024

norm_eps = 1e-12
mask_fill = -10000.0
learning_rate = 0.0002
momentum_rate = 0.9
decay_weight = 0.0001
average_rate = 0.9
score_scale = HEAD_DIM ** (-0.5)
FILL_PARTS = (-9984.0, -16.0)
f32 = jnp.float32
bf16 = jnp.bfloat16


def params():
    return pltpu.CompilerParams(vmem_limit_bytes=VMEM_BYTES)


def dot_nn(a, b):
    return lax.dot_general(a, b, (((1,), (0,)), ((), ())), preferred_element_type=f32)


def dot_nt(a, b):
    return lax.dot_general(a, b, (((1,), (1,)), ((), ())), preferred_element_type=f32)


SEQS = ((0, 128, LONG_L, 0), (128, 64, SHORT_L, 1), (192, 64, SHORT_L, 2))


def attend(q, k, v, limit, keep_probs):
    length = q.shape[0]
    v_t = jnp.transpose(v)
    head_lane = lax.broadcasted_iota(jnp.int32, (length, PAIR), 1) // HEAD_DIM
    live = lax.broadcasted_iota(jnp.int32, (length, length), 0) < limit
    parts = []
    for h in range(2):
        k_h = jnp.where(head_lane == h, k, jnp.zeros_like(k))
        scores = jnp.where(live, dot_nt(k_h, q) * score_scale, mask_fill)
        top = jnp.max(scores, axis=0, keepdims=True)
        exponent = jnp.exp(scores - top)
        total = jnp.sum(exponent, axis=0, keepdims=True)
        probs = (exponent * (1.0 / total)).astype(bf16)
        keep_probs(h, probs)
        parts.append(dot_nn(v_t[h * HEAD_DIM : (h + 1) * HEAD_DIM], probs))
    return jnp.transpose(jnp.concatenate(parts, axis=0)).astype(bf16)


def attn_forward_kernel(lens_ref, q_ref, k_ref, v_ref, o_ref, long_ref, short_ref):
    for first, rows, length, index in SEQS:
        q, k, v = [r[:, first : first + rows, :].reshape(length, PAIR) for r in (q_ref, k_ref, v_ref)]

        def keep_probs(h, probs, index=index):
            if index == 0:
                long_ref[h] = probs
            else:
                short_ref[h, index - 1] = probs

        o = attend(q, k, v, lens_ref[index], keep_probs)
        o_ref[:, first : first + rows, :] = o.reshape(4, rows, PAIR)


def attn_forward(lens, qkv):
    pairs = D // PAIR
    col = lambda base: pl.BlockSpec((4, 256, PAIR), lambda i, base=base: (0, 0, base + i))
    return pl.pallas_call(
        attn_forward_kernel,
        grid=(pairs,),
        in_specs=[
            pl.BlockSpec(memory_space=pltpu.SMEM),
            col(0),
            col(pairs),
            col(2 * pairs),
        ],
        out_specs=[
            pl.BlockSpec((4, 256, PAIR), lambda i: (0, 0, i)),
            pl.BlockSpec((2, LONG_L, LONG_L), lambda i: (i, 0, 0)),
            pl.BlockSpec((2, 2, SHORT_L, SHORT_L), lambda i: (i, 0, 0, 0)),
        ],
        out_shape=[
            jax.ShapeDtypeStruct((4, 256, D), bf16),
            jax.ShapeDtypeStruct((2 * pairs, LONG_L, LONG_L), bf16),
            jax.ShapeDtypeStruct((2 * pairs, 2, SHORT_L, SHORT_L), bf16),
        ],
        compiler_params=params(),
        name="attn_forward",
    )(lens, qkv, qkv, qkv)


def attend_back(q, k, v, do, o, limit, kept_probs):
    length = q.shape[0]
    k_t = jnp.transpose(k)
    inner = jnp.transpose(do.astype(f32) * o.astype(f32))
    head_lane = lax.broadcasted_iota(jnp.int32, (length, PAIR), 1) // HEAD_DIM
    live = lax.broadcasted_iota(jnp.int32, (length, length), 0) < limit
    dq_parts = []
    dk = jnp.zeros((length, PAIR), f32)
    dv = jnp.zeros((length, PAIR), f32)
    for h in range(2):
        keep = head_lane == h
        v_h, do_h, q_h = [jnp.where(keep, m, jnp.zeros_like(m)) for m in (v, do, q)]
        probs = kept_probs(h)
        delta = jnp.sum(inner[h * HEAD_DIM : (h + 1) * HEAD_DIM], axis=0, keepdims=True)
        d_probs = dot_nt(v_h, do)
        d_scores = jnp.where(live, probs.astype(f32) * (d_probs - delta), 0.0).astype(bf16)
        dv = dv + dot_nn(probs, do_h)
        dk = dk + dot_nn(d_scores, q_h)
        dq_parts.append(dot_nn(k_t[h * HEAD_DIM : (h + 1) * HEAD_DIM], d_scores))
    dq = jnp.transpose(jnp.concatenate(dq_parts, axis=0)) * score_scale
    return dq.astype(bf16), (dk * score_scale).astype(bf16), dv.astype(bf16)


def attn_backward_kernel(
    lens_ref, q_ref, k_ref, v_ref, do_ref, o_ref, long_ref, short_ref, dq_ref, dk_ref, dv_ref, sum_ref
):
    sum_q = jnp.zeros((1, PAIR), f32)
    sum_v = jnp.zeros((1, PAIR), f32)
    for first, rows, length, index in SEQS:
        args = [r[:, first : first + rows, :].reshape(length, PAIR) for r in (q_ref, k_ref, v_ref, do_ref, o_ref)]
        kept = lambda h, index=index: long_ref[h] if index == 0 else short_ref[h, index - 1]
        dq, dk, dv = attend_back(*args, lens_ref[index], kept)
        sum_q = sum_q + jnp.sum(dq.astype(f32), axis=0, keepdims=True)
        sum_v = sum_v + jnp.sum(dv.astype(f32), axis=0, keepdims=True)
        for ref, v in ((dq_ref, dq), (dk_ref, dk), (dv_ref, dv)):
            ref[:, first : first + rows, :] = v.reshape(4, rows, PAIR)
    sum_ref[0:1, :] = sum_q
    sum_ref[1:2, :] = sum_v
    sum_ref[2:8, :] = jnp.zeros((6, PAIR), f32)


def attn_backward(lens, qkv, d_attended, attended, long_probs, short_probs):
    pairs = D // PAIR
    col = lambda base: pl.BlockSpec((4, 256, PAIR), lambda i, base=base: (0, 0, base + i))
    return pl.pallas_call(
        attn_backward_kernel,
        grid=(pairs,),
        in_specs=[
            pl.BlockSpec(memory_space=pltpu.SMEM),
            col(0),
            col(pairs),
            col(2 * pairs),
            col(0),
            col(0),
            pl.BlockSpec((2, LONG_L, LONG_L), lambda i: (i, 0, 0)),
            pl.BlockSpec((2, 2, SHORT_L, SHORT_L), lambda i: (i, 0, 0, 0)),
        ],
        out_specs=[col(0), col(0), col(0), pl.BlockSpec((8, PAIR), lambda i: (0, i))],
        out_shape=[jax.ShapeDtypeStruct((4, 256, D), bf16)] * 3 + [jax.ShapeDtypeStruct((8, D), f32)],
        compiler_params=params(),
        name="attn_backward",
    )(lens, qkv, qkv, qkv, d_attended, attended, long_probs, short_probs)


def gelu_pair(u):
    t = 1.0 / (1.0 + (0.3275911 * 0.5**0.5) * jnp.abs(u))
    e = jnp.exp2((u * u) * (-0.5 * 1.4426950408889634))
    poly = 0.5 * -0.284496736 + t * (0.5 * 1.421413741 + t * (0.5 * -1.453152027 + t * (0.5 * 1.061405429)))
    tail = (t * (0.5 * 0.254829592 + t * poly)) * e
    cdf = jnp.where(u < 0.0, tail, 1.0 - tail)
    return u * cdf, cdf + (u * (0.5 / jnp.pi) ** 0.5) * e


def row_mean(v):
    return jnp.mean(v, axis=-1, keepdims=True)


def middle_kernel(
    lens_ref,
    o_ref,
    x_ref,
    cot_ref,
    wo_ref,
    w1_ref,
    w2_ref,
    vec_ref,
    out_ref,
    y1b_ref,
    g_ref,
    dfb_ref,
    dub_ref,
    dab_ref,
    dob_ref,
    dh_ref,
    sum_ref,
    slope_ref,
):
    r = pl.program_id(0)
    rows = o_ref.shape[0]

    @pl.when(r == 0)
    def _():
        sum_ref[...] = jnp.zeros_like(sum_ref)

    def add(index, v):
        sum_ref[index : index + 1, :] += jnp.sum(v, axis=0, keepdims=True)

    vec = lambda i: vec_ref[i : i + 1, :]
    h = x_ref[...].astype(f32) + (dot_nn(o_ref[...], wo_ref[...]) + vec(2))
    centred = h - row_mean(h)
    inv1 = lax.rsqrt(row_mean(centred * centred) + norm_eps)
    norm1 = centred * inv1
    y1 = norm1 * vec(3) + vec(4)
    y1b = y1.astype(bf16)
    y1b_ref[...] = y1b
    z = y1 + vec(5)
    for c in range(FF // D):
        cols = slice(c * D, (c + 1) * D)
        act, slope = gelu_pair(dot_nn(y1b, w1_ref[:, cols]) + vec(8 + c))
        act = act.astype(bf16)
        g_ref[:, cols] = act
        slope_ref[:, cols] = slope
        z = z + dot_nn(act, w2_ref[cols, :])
    centred2 = z - row_mean(z)
    inv2 = lax.rsqrt(row_mean(centred2 * centred2) + norm_eps)
    norm2 = centred2 * inv2
    out_ref[...] = (norm2 * vec(6) + vec(7)).astype(bf16)

    j = lax.broadcasted_iota(jnp.int32, (rows, 1), 0)
    long_end = lens_ref[0] - r * 128
    short_end = [lens_ref[i] - r * 64 + first for i, first in ((1, 128), (2, 192))]
    live = j < jnp.where(j < 128, long_end, jnp.where(j < 192, short_end[0], short_end[1]))
    dr = jnp.where(live, cot_ref[...].astype(f32), 0.0)
    e2 = dr * vec(6)
    dz = inv2 * (e2 - row_mean(e2) - norm2 * row_mean(e2 * norm2))
    dfb = dz.astype(bf16)
    dfb_ref[...] = dfb
    add(6, dr * norm2)
    add(7, dr)
    add(5, dfb.astype(f32))
    dy1 = dz
    for c in range(FF // D):
        cols = slice(c * D, (c + 1) * D)
        dub = (dot_nt(dfb, w2_ref[cols, :]) * slope_ref[:, cols]).astype(bf16)
        dub_ref[:, cols] = dub
        add(8 + c, dub.astype(f32))
        dy1 = dy1 + dot_nt(dub, w1_ref[:, cols])
    add(3, dy1 * norm1)
    add(4, dy1)
    e1 = dy1 * vec(3)
    dh = inv1 * (e1 - row_mean(e1) - norm1 * row_mean(e1 * norm1))
    dab = dh.astype(bf16)
    dh_ref[...] = dh
    dab_ref[...] = dab
    add(2, dab.astype(f32))
    dob_ref[...] = dot_nt(dab, wo_ref[...]).astype(bf16)


def middle(lens, attended, tokens, cotangent, w_o, w_1, w_2, vec):
    n = tokens.shape[0]
    rows = 256
    row = lambda width: pl.BlockSpec((rows, width), lambda i: (i, 0))
    whole = lambda a: pl.BlockSpec(a.shape, lambda i: (0, 0), pipeline_mode=pl.Buffered(1))
    shape = jax.ShapeDtypeStruct
    return pl.pallas_call(
        middle_kernel,
        grid=(n // rows,),
        in_specs=[
            pl.BlockSpec(memory_space=pltpu.SMEM),
            row(D),
            row(D),
            row(D),
            whole(w_o),
            whole(w_1),
            whole(w_2),
            whole(vec),
        ],
        out_specs=[
            row(D),
            row(D),
            row(FF),
            row(D),
            row(FF),
            row(D),
            row(D),
            row(D),
            pl.BlockSpec((16, D), lambda i: (0, 0)),
        ],
        out_shape=[
            shape((n, D), bf16),
            shape((n, D), bf16),
            shape((n, FF), bf16),
            shape((n, D), bf16),
            shape((n, FF), bf16),
            shape((n, D), bf16),
            shape((n, D), bf16),
            shape((n, D), f32),
            shape((16, D), f32),
        ],
        scratch_shapes=[pltpu.VMEM((rows, FF), f32)],
        compiler_params=params(),
        name="middle",
    )(lens, attended, tokens, cotangent, w_o, w_1, w_2, vec)


MESH = pl.DeviceIdType.MESH
Z_CHIPS = 4


def place():
    dp = lax.axis_index("dp")
    s = lax.axis_index("seq")
    return dp, s, dp // 2, dp % 2, s // 2, s % 2


def remote(src, dst, send, recv, device):
    return pltpu.make_async_remote_copy(
        src_ref=src, dst_ref=dst, send_sem=send, recv_sem=recv, device_id=device, device_id_type=MESH
    )


def greet():
    dp, s = lax.axis_index("dp"), lax.axis_index("seq")
    barrier = pltpu.get_barrier_semaphore()
    for k in range(1, 8):
        pl.semaphore_signal(barrier, inc=1, device_id=((dp + k) % 8, s), device_id_type=MESH)
    for k in range(1, 4):
        pl.semaphore_signal(barrier, inc=1, device_id=(dp, (s + k) % 4), device_id_type=MESH)
    pl.semaphore_wait(barrier, 10)


def head_operands(q, k, limit, h):
    lane = lax.broadcasted_iota(jnp.int32, q.shape, 1)
    live = lax.broadcasted_iota(jnp.int32, q.shape, 0) < limit
    keep = lane // HEAD_DIM == h
    spare = (1 - h) * HEAD_DIM
    zero = jnp.zeros_like(q)
    fill = jnp.where(lane == spare, jnp.full_like(q, FILL_PARTS[0]), zero)
    fill = jnp.where(lane == spare + 1, jnp.full_like(q, FILL_PARTS[1]), fill)
    k_h = jnp.where(live, jnp.where(keep, k, zero), fill)
    ones = jnp.where((lane == spare) | (lane == spare + 1), jnp.ones_like(q), zero)
    return jnp.where(keep, q * bf16(score_scale), ones), k_h


def attend_sums(q, k, v, limit, keep_exps):
    length = q.shape[0]
    v_t = jnp.transpose(v)
    parts = []
    inverses = []
    for h in range(2):
        q_h, k_h = head_operands(q, k, limit, h)
        scores = dot_nt(k_h, q_h)
        exponent = jnp.exp(scores - jnp.max(scores, axis=0, keepdims=True))
        inverse = 1.0 / jnp.sum(exponent, axis=0, keepdims=True)
        exps = exponent.astype(bf16)
        keep_exps(h, exps)
        parts.append(dot_nn(v_t[h * HEAD_DIM : (h + 1) * HEAD_DIM], exps) * inverse)
        inverses.append(jnp.broadcast_to(inverse, (HEAD_DIM, length)))
    o = jnp.transpose(jnp.concatenate(parts, axis=0)).astype(bf16)
    return o, jnp.transpose(jnp.concatenate(inverses, axis=0))


def attend_sums_back(q, k, v, do, o, limit, kept_exps):
    length = q.shape[0]
    lane = lax.broadcasted_iota(jnp.int32, (length, PAIR), 1)
    live = lax.broadcasted_iota(jnp.int32, (length, PAIR), 0) < limit
    k_t = jnp.transpose(jnp.where(live, k, jnp.zeros_like(k)))
    inner = jnp.transpose(do.astype(f32) * o.astype(f32))
    dq_parts = []
    dk = jnp.zeros((length, PAIR), f32)
    dv = jnp.zeros((length, PAIR), f32)
    for h in range(2):
        keep = lane // HEAD_DIM == h
        v_h, do_h, q_h = [jnp.where(keep, m, jnp.zeros_like(m)) for m in (v, do, q)]
        exps = kept_exps(h)
        delta = jnp.sum(inner[h * HEAD_DIM : (h + 1) * HEAD_DIM], axis=0, keepdims=True)
        d_scores = (exps.astype(f32) * (dot_nt(v_h, do) - delta)).astype(bf16)
        dv = dv + dot_nn(exps, do_h)
        dk = dk + dot_nn(d_scores, q_h)
        dq_parts.append(dot_nn(k_t[h * HEAD_DIM : (h + 1) * HEAD_DIM], d_scores))
    dq = jnp.transpose(jnp.concatenate(dq_parts, axis=0)) * score_scale
    dk = jnp.where(live, dk * score_scale, 0.0)
    return dq.astype(bf16), dk.astype(bf16), dv.astype(bf16)


def own_lengths(short_ref, long_ref):
    s = lax.axis_index("seq")
    return long_ref[s // 2, 0, s % 2], short_ref[0, 0, s], short_ref[1, 0, s]


class Part:
    def __init__(self, own, out, sems, direct=False):
        self.own, self.out, self.direct = own, out, direct
        self.z_send, self.z_recv, self.x_send, self.x_recv, self.y_send, self.y_recv, self.c_send, self.c_recv = sems
        self.dp, self.s, self.z, self.x, self.y, self.c = place()
        self.rows, cols = own.shape
        self.half_rows, self.half_cols = self.rows // 2, cols // 2

    def cols(self, core):
        return pl.ds(pl.multiple_of(core * self.half_cols, 128), self.half_cols)

    def some(self, q):
        return pl.ds(pl.multiple_of(q * self.half_rows, 16), self.half_rows)

    def block(self, zs, x, core, q=None):
        rows = slice(None) if q is None else self.some(q)
        return self.out.at[zs * 2 + x, rows, self.cols(core)]

    def source(self, zs, own, q=None):
        if own:
            rows = slice(None) if q is None else self.some(q)
            return self.own.at[rows, self.cols(self.c)]
        return self.block(zs, self.x, self.c, q)

    def up(self, zs, own=False):
        dst = self.block(zs, self.x, self.c)
        return remote(self.source(zs, own), dst, self.z_send.at[zs, 0], self.z_recv.at[zs], (self.dp + 2, self.s))

    def down(self, zs, own=False):
        dst = self.block(zs, self.x, self.c)
        return remote(self.source(zs, own), dst, self.z_send.at[zs, 1], self.z_recv.at[zs], (self.dp - 2, self.s))

    def across(self, zs, own=False):
        q = None if self.direct else self.y
        dst = self.block(zs, self.x, self.c, q)
        device = (self.z * 2 + 1 - self.x, self.s)
        return remote(self.source(zs, own, q), dst, self.x_send.at[zs], self.x_recv.at[zs], device)

    def across_in(self, zs):
        ref = self.block(zs, 1 - self.x, self.c, None if self.direct else self.y)
        return remote(ref, ref, self.x_send.at[zs], self.x_recv.at[zs], (self.dp, self.s))

    def over(self, zs):
        ref = self.block(zs, 1 - self.x, self.c, self.y)
        return remote(ref, ref, self.y_send.at[zs], self.y_recv.at[zs], (self.dp, (1 - self.y) * 2 + self.c))

    def over_in(self, zs):
        ref = self.block(zs, 1 - self.x, self.c, 1 - self.y)
        return remote(ref, ref, self.y_send.at[zs], self.y_recv.at[zs], (self.dp, self.s))

    def share(self, kind, zs, core):
        if kind == 0:
            ref = self.block(zs, self.x, core)
        else:
            q = self.y if kind == 1 else 1 - self.y
            ref = self.block(zs, 1 - self.x, core, None if self.direct else q)
        j = kind * Z_CHIPS + zs
        return remote(ref, ref, self.c_send.at[j], self.c_recv.at[j], (self.dp, self.s + 1 - 2 * self.c))

    def each(self, k, what):
        if k == 0:
            what(self.z)
            return

        @pl.when(self.z >= k)
        def _():
            what(self.z - k)

        @pl.when(self.z + k < Z_CHIPS)
        def _():
            what(self.z + k)

    def stage(self, k):
        if k == 0:

            @pl.when(self.z < Z_CHIPS - 1)
            def _():
                self.up(self.z, True).start()

            @pl.when(self.z > 0)
            def _():
                self.down(self.z, True).start()

            self.across(self.z, True).start()
        elif k < Z_CHIPS:

            @pl.when(self.z >= k)
            def _():
                zs = self.z - k
                self.up(zs).wait_recv()

                @pl.when(self.z < Z_CHIPS - 1)
                def _():
                    self.up(zs).start()

                self.across(zs).start()
                self.share(0, zs, self.c).start()

            @pl.when(self.z + k < Z_CHIPS)
            def _():
                zs = self.z + k
                self.down(zs).wait_recv()

                @pl.when(self.z > 0)
                def _():
                    self.down(zs).start()

                self.across(zs).start()
                self.share(0, zs, self.c).start()

        if 1 <= k <= Z_CHIPS:

            def pass_x(zs):
                self.across_in(zs).wait_recv()
                if not self.direct:
                    self.over(zs).start()
                self.share(1, zs, self.c).start()

            self.each(k - 1, pass_x)
        if 2 <= k <= Z_CHIPS + 1 and not self.direct:

            def pass_y(zs):
                self.over_in(zs).wait_recv()
                self.share(2, zs, self.c).start()

            self.each(k - 2, pass_y)

    stages = Z_CHIPS + 2

    def finish(self):
        for kind in range(2 if self.direct else 3):
            for k in range(1 if kind == 0 else 0, Z_CHIPS):
                self.each(k, lambda zs, kind=kind: self.share(kind, zs, 1 - self.c).wait_recv())

    def settle(self):
        for k in range(Z_CHIPS):

            @pl.when((self.z >= k) & (self.z < Z_CHIPS - 1))
            def _():
                self.up(self.z - k, k == 0).wait_send()

            @pl.when((self.z + k < Z_CHIPS) & (self.z > 0))
            def _():
                self.down(self.z + k, k == 0).wait_send()

            self.each(k, lambda zs, k=k: self.across(zs, k == 0).wait_send())
            if not self.direct:
                self.each(k, lambda zs: self.over(zs).wait_send())
            for kind in range(2 if self.direct else 3):
                if kind > 0 or k > 0:
                    self.each(k, lambda zs, kind=kind: self.share(kind, zs, self.c).wait_send())


class Tokens:
    def __init__(self, long_ref, short_ref, out, send, recv, local):
        self.long_ref, self.short_ref, self.out, self.send, self.recv, self.local = long_ref, short_ref, out, send, recv, local
        self.dp, self.s = lax.axis_index("dp"), lax.axis_index("seq")

    def pieces(self, target, source):
        yield self.long_ref.at[target // 2, target % 2], self.out.at[source, pl.ds(0, 128)]
        yield self.short_ref.at[0, target], self.out.at[source, pl.ds(128, 64)]
        yield self.short_ref.at[1, target], self.out.at[source, pl.ds(192, 64)]

    def copies(self, k):
        target = (self.s + k) % 4
        for j, (src, dst) in enumerate(self.pieces(target, self.s)):
            yield remote(src, dst, self.send.at[k, j], self.recv.at[k, j], (self.dp, target))

    def own(self):
        for j, (src, dst) in enumerate(self.pieces(self.s, self.s)):
            yield pltpu.make_async_copy(src, dst, self.local.at[j])

    def start(self):
        for k in range(1, 4):
            for copy in self.copies(k):
                copy.start()
        for copy in self.own():
            copy.start()

    def finish(self):
        for copy in self.own():
            copy.wait()
        for k in range(1, 4):
            source = (self.s + 4 - k) % 4
            for j, (src, dst) in enumerate(self.pieces(self.s, source)):
                remote(src, dst, self.send.at[k, j], self.recv.at[k, j], (self.dp, self.s)).wait_recv()

    def settle(self):
        for k in range(1, 4):
            for copy in self.copies(k):
                copy.wait_send()


def layer_norm_back(grad, normed, inverse):
    return inverse * (grad - row_mean(grad) - normed * row_mean(grad * normed))


def live_rows(r, lens_ref):
    j = lax.broadcasted_iota(jnp.int32, (256, 1), 0)
    ends = [lens_ref[0] - r * 128] + [lens_ref[i] - r * 64 + first for i, first in ((1, 128), (2, 192))]
    return j < jnp.where(j < 128, ends[0], jnp.where(j < 192, ends[1], ends[2]))


DIRECT = (False, False, False, True)
FIRST_JOBS = ((0, 1), (1, 0), (0, 2), (2, 0), (0, 3), (1, 1), (0, 4), (2, 1), (0, 5), (1, 2),)
PROJECT_JOBS = {
    5: ((2, 2),),
    7: ((1, 3),),
    8: ((3, 0),),
}
ATTENTION_JOBS = {
    1: ((2, 3),),
    2: ((1, 4),),
    3: ((3, 1), (1, 5), (2, 4), (4, 0),),
    5: ((2, 5),),
}
INNER_FIRST_JOBS = ((3, 2),)
INNER_JOBS = {
    2: ((3, 3),),
}
OUTER_FIRST_JOBS = ((3, 4),)


def forward_kernel(*refs):
    refs = list(refs)

    def take(n):
        out = refs[:n]
        del refs[:n]
        return out

    short_len_ref, long_len_ref, wide_hbm, down_hbm, vec_ref = take(5)
    long_in, short_in, long_cot, short_cot = take(4)
    qkv_w_out, wo_out, w1_out, w2_out, tok_out, qkv_out, att_out, probs_out = take(8)
    act_out, slope_out, y1b_out, norm_out, inv_out, dz_out, dfb_out, out_out = take(8)
    (ainv_out,) = take(1)
    vec_out, sums_out = take(2)
    own_wide, own_down, w_s, wo_s, w1_s, w2_s, x_s, cot_s, qkv_s, att_s, vec_s, bias_s = take(12)
    stage_s, act_s, y1_s, y1b_s, norm_s, inv_s, dfb_s, out_s = take(8)
    z_send, z_recv, x_send, x_recv, y_send, y_recv, c_send, c_recv, v_send, v_recv, t_send, t_recv = take(12)
    local, keep_sem, stage_sem = take(3)
    wide_ref, down_ref, state_sem, ainv_s = take(4)

    dp, s, z, x, y, c = place()
    lens_ref = own_lengths(short_len_ref, long_len_ref)
    ranges = ((0, 3 * D), (3 * D, D + FF))
    load_wide = [
        pltpu.make_async_copy(
            wide_hbm.at[:, pl.ds(first, cols)], wide_ref.at[:, pl.ds(first, cols)], state_sem.at[i]
        )
        for i, (first, cols) in enumerate(ranges)
    ]
    load_down = pltpu.make_async_copy(down_hbm, down_ref, state_sem.at[2])
    for copy in load_wide + [load_down]:
        copy.start()
    greet()
    tokens = Tokens(long_in, short_in, x_s, t_send.at[0], t_recv.at[0], local.at[0])
    cots = Tokens(long_cot, short_cot, cot_s, t_send.at[1], t_recv.at[1], local.at[1])
    tokens.start()
    load_wide[0].wait()
    own_wide[:, 0 : 3 * D] = wide_ref[:, 0 : 3 * D].astype(bf16)

    def vec_copy(k, source, target):
        return remote(vec_ref, vec_s.at[source], v_send.at[k], v_recv.at[k], (target, s))

    sems = lambda i: [
        r.at[i] for r in (z_send, z_recv, x_send, x_recv, y_send, y_recv, c_send, c_recv)
    ]
    owns = [own_wide.at[:, pl.ds(first, cols)] for first, cols in ((0, 3 * D), (3 * D, D), (4 * D, FF))] + [own_down]
    parts = [
        Part(own, out, sems(i), direct=DIRECT[i]) for i, (own, out) in enumerate(zip(owns, (w_s, wo_s, w1_s, w2_s)))
    ]

    def run(jobs):
        for index, stage in jobs:
            if index == len(parts):
                cots.start()
            else:
                parts[index].stage(stage)

    first = parts[0]
    first.stage(0)
    load_wide[1].wait()
    load_down.wait()
    for k in range(1, 8):
        vec_copy(k, dp, (dp + k) % 8).start()
    own_wide[:, 3 * D :] = wide_ref[:, 3 * D :].astype(bf16)
    own_down[...] = down_ref[...].astype(bf16)
    own_copies = [
        pltpu.make_async_copy(part.own, part.out.at[dp], local.at[2, i]) for i, part in enumerate(parts)
    ]
    own_copies.append(pltpu.make_async_copy(vec_ref, vec_s.at[dp], local.at[2, 4]))
    for copy in own_copies:
        copy.start()
    run(FIRST_JOBS)
    for copy in own_copies:
        copy.wait()
    for k in range(1, 8):
        vec_copy(k, (dp + 8 - k) % 8, dp).wait_recv()
    vec = vec_s[0].astype(f32)
    for d in range(1, 8):
        vec = vec + vec_s[d].astype(f32)
    vec_out[...] = vec
    bias_s[:, 0:D] = jnp.broadcast_to(vec[0:1, :], (8, D))
    bias_s[:, D : 2 * D] = jnp.zeros((8, D), f32)
    bias_s[:, 2 * D : 3 * D] = jnp.broadcast_to(vec[1:2, :], (8, D))
    sums_out[...] = jnp.zeros_like(sums_out)
    tokens.finish()
    first.finish()
    kept = []

    def keep(src, dst):
        copy = pltpu.make_async_copy(src, dst, keep_sem.at[len(kept)])
        copy.start()
        kept.append(copy)

    keep(x_s, tok_out)
    keep(w_s, qkv_w_out)

    def during(i, plan):
        for when, jobs in plan.items():

            @pl.when(i == when)
            def _():
                run(jobs)

    def project(j, carry):
        during(j, PROJECT_JOBS)
        cols = pl.ds(pl.multiple_of(j * 256, 256), 256)
        w = w_s[:, :, cols].reshape(D, 256)
        rows = x_s[...].reshape(1024, D)
        qkv_s[:, :, cols] = (dot_nn(rows, w) + bias_s[0:1, cols]).astype(bf16).reshape(4, 256, 256)
        return carry

    lax.fori_loop(0, 3 * D // 256, project, 0)
    keep(qkv_s, qkv_out)
    pairs = D // PAIR

    def probs_copy(i, slot):
        return pltpu.make_async_copy(stage_s.at[slot], probs_out.at[i], stage_sem.at[slot])

    def attention(i, carry):
        during(i, ATTENTION_JOBS)
        slot = i % 2

        @pl.when(i >= 2)
        def _():
            probs_copy(i - 2, slot).wait()

        lanes = pl.ds(pl.multiple_of(i * PAIR, PAIR), PAIR)
        for first_row, rows, length, index in SEQS:
            q, k, v = [
                qkv_s[:, first_row : first_row + rows, pl.ds(pl.multiple_of(base + i * PAIR, PAIR), PAIR)].reshape(
                    length, PAIR
                )
                for base in (0, D, 2 * D)
            ]

            def keep_probs(h, probs, index=index):
                if index == 0:
                    stage_s[slot, h * LONG_L : (h + 1) * LONG_L, 0:LONG_L] = probs
                else:
                    row = (2 * h + index - 1) * SHORT_L
                    stage_s[slot, row : row + SHORT_L, LONG_L : LONG_L + SHORT_L] = probs

            o, inverse = attend_sums(q, k, v, lens_ref[index], keep_probs)
            att_s[:, first_row : first_row + rows, lanes] = o.reshape(4, rows, PAIR)
            ainv_s[:, first_row : first_row + rows, lanes] = inverse.reshape(4, rows, PAIR)
        probs_copy(i, slot).start()
        return carry

    lax.fori_loop(0, pairs, attention, 0)
    keep(att_s, att_out)
    keep(ainv_s, ainv_out)
    run(INNER_FIRST_JOBS)
    parts[1].finish()
    parts[2].finish()
    keep(wo_s, wo_out)
    keep(w1_s, w1_out)
    row_vec = lambda i: vec_out[i : i + 1, :]

    def slope_copy(r, slot):
        return pltpu.make_async_copy(stage_s.at[slot], slope_out.at[r], stage_sem.at[slot])

    def inner(r, carry):
        during(r, INNER_JOBS)
        slot = r % 2

        @pl.when(r < 2)
        def _():
            probs_copy(pairs - 2 + r, slot).wait()

        @pl.when(r >= 2)
        def _():
            slope_copy(r - 2, slot).wait()

        h = x_s[r].astype(f32) + (dot_nn(att_s[r], wo_s[...].reshape(D, D)) + row_vec(2))
        centred = h - row_mean(h)
        inverse = lax.rsqrt(row_mean(centred * centred) + norm_eps)
        normed = centred * inverse
        y1 = normed * row_vec(3) + row_vec(4)
        y1b = y1.astype(bf16)
        y1_s[r] = y1
        y1b_s[r] = y1b
        norm_s[r] = normed.astype(bf16)
        inv_s[r] = jnp.broadcast_to(inverse, (256, 128))
        at = pl.ds(pl.multiple_of(r * 256, 256), 256)
        for k in range(FF // D):
            w = w1_s[:, :, k * D : (k + 1) * D].reshape(D, D)
            act, slope = gelu_pair(dot_nn(y1b, w) + row_vec(8 + k))
            act_s[k, at] = act.astype(bf16)
            stage_s[slot, k * 256 : (k + 1) * 256] = slope.astype(bf16)
        slope_copy(r, slot).start()
        return carry

    lax.fori_loop(0, 4, inner, 0)
    for src, dst in ((act_s, act_out), (y1b_s, y1b_out), (norm_s, norm_out), (inv_s, inv_out)):
        keep(src, dst)
    run(OUTER_FIRST_JOBS)
    parts[3].finish()
    keep(w2_s, w2_out)
    cots.finish()

    def outer(r, carry):
        at = pl.ds(pl.multiple_of(r * 256, 256), 256)
        total = y1_s[r] + row_vec(5)
        for k in range(FF // D):
            total = total + dot_nn(act_s[k, at], w2_s[2 * k : 2 * k + 2].reshape(D, D))
        centred = total - row_mean(total)
        inverse = lax.rsqrt(row_mean(centred * centred) + norm_eps)
        normed = centred * inverse
        out_s[r] = (normed * row_vec(6) + row_vec(7)).astype(bf16)
        dr = jnp.where(live_rows(r, lens_ref), cot_s[r].astype(f32), 0.0)
        dz = layer_norm_back(dr * row_vec(6), normed, inverse)
        dfb = dz.astype(bf16)
        y1_s[r] = dz
        dfb_s[r] = dfb
        for i, v in ((5, dfb.astype(f32)), (6, dr * normed), (7, dr)):
            sums_out[i : i + 1, :] += jnp.sum(v, axis=0, keepdims=True)
        return carry

    lax.fori_loop(0, 4, outer, 0)
    for src, dst in ((y1_s, dz_out), (dfb_s, dfb_out), (out_s, out_out)):
        keep(src, dst)
    for copy in kept:
        copy.wait()
    for r in (2, 3):
        slope_copy(r, r % 2).wait()
    for k in range(1, 8):
        vec_copy(k, dp, (dp + k) % 8).wait_send()
    for part in parts:
        part.settle()
    tokens.settle()
    cots.settle()


def forward(short_len, long_len, wide_master, down_master, vec_block, long_in, short_in, long_cot, short_cot):
    any_spec = pl.BlockSpec(memory_space=pl.ANY)
    vmem = pl.BlockSpec(memory_space=pltpu.VMEM)
    smem = pl.BlockSpec(memory_space=pltpu.SMEM)
    shape = jax.ShapeDtypeStruct
    rows, down_rows = wide_master.shape[0], down_master.shape[0]
    dma = pltpu.SemaphoreType.DMA
    tok = (4, 256, D)
    outs = [
        ((8, rows, 3 * D), bf16),
        ((8, rows, D), bf16),
        ((8, rows, FF), bf16),
        ((8, down_rows, D), bf16),
        (tok, bf16),
        ((4, 256, 3 * D), bf16),
        (tok, bf16),
        ((D // PAIR, 1024, D), bf16),
        ((4, 1024, D), bf16),
        ((4, 1024, D), bf16),
        (tok, bf16),
        (tok, bf16),
        ((4, 256, 128), f32),
        (tok, f32),
        (tok, bf16),
        (tok, bf16),
        (tok, f32),
    ]
    vm = lambda dims, t=bf16: pltpu.VMEM(dims, t)
    return pl.pallas_call(
        forward_kernel,
        in_specs=[smem, smem, any_spec, any_spec, vmem] + [any_spec] * 4,
        out_specs=[any_spec] * len(outs) + [vmem] * 2,
        out_shape=[shape(dims, t) for dims, t in outs] + [shape((16, D), f32)] * 2,
        scratch_shapes=[
            vm((rows, 4 * D + FF)),
            vm((down_rows, D)),
            vm((8, rows, 3 * D)),
            vm((8, rows, D)),
            vm((8, rows, FF)),
            vm((8, down_rows, D)),
            vm(tok),
            vm(tok),
            vm((4, 256, 3 * D)),
            vm(tok),
            vm((8, 16, D)),
            vm((8, 3 * D), f32),
            vm((2, 1024, D)),
            vm((4, 1024, D)),
            vm(tok, f32),
            vm(tok),
            vm(tok),
            vm((4, 256, 128), f32),
            vm(tok),
            vm(tok),
            dma((4, 4, 2)),
            dma((4, 4)),
            dma((4, 4)),
            dma((4, 4)),
            dma((4, 4)),
            dma((4, 4)),
            dma((4, 12)),
            dma((4, 12)),
            dma((8,)),
            dma((8,)),
            dma((2, 4, 3)),
            dma((2, 4, 3)),
            dma((3, 5)),
            dma((16,)),
            dma((2,)),
            vm((rows, 4 * D + FF), f32),
            vm((down_rows, D), f32),
            dma((3,)),
            vm(tok, f32),
        ],
        compiler_params=pltpu.CompilerParams(
            vmem_limit_bytes=VMEM_BYTES, collective_id=0, has_side_effects=True
        ),
        name="forward",
    )(short_len, long_len, wide_master, down_master, vec_block, long_in, short_in, long_cot, short_cot)


class Grad:
    def __init__(self, theirs, acc, cbuf, xbuf, ybuf, zbuf, quarter, fin, sems, order):
        self.theirs, self.acc, self.cbuf, self.xbuf, self.ybuf, self.zbuf = theirs, acc, cbuf, xbuf, ybuf, zbuf
        self.quarter, self.fin, self.order = quarter, fin, order
        self.c_send, self.c_recv, self.x_send, self.x_recv, self.y_send, self.y_recv = sems[:6]
        self.z_send, self.z_recv, self.f_send, self.f_recv, self.local = sems[6:]
        self.dp, self.s, self.z, self.x, self.y, self.c = place()
        self.rows, cols = fin.shape
        self.half_rows, self.half_cols = self.rows // 2, cols // 2
        self.by_z = self.rows == 384
        self.core_pieces = 4 if self.by_z else 2
        self.mine = self.some(self.y)

    def cols(self, core):
        return pl.ds(pl.multiple_of(core * self.half_cols, 128), self.half_cols)

    def some(self, q):
        return pl.ds(pl.multiple_of(q * self.half_rows, 16), self.half_rows)

    def core_view(self, ref, j):
        if self.by_z:
            return ref.at[j]
        if self.order[0] != "y":
            return ref.at[:, (1 - self.x) if j == 0 else self.x]
        return ref.at[:, :, self.some((1 - self.y) if j == 0 else self.y)]

    def core_copy(self, j):
        return remote(
            self.core_view(self.theirs, j),
            self.core_view(self.cbuf, j),
            self.c_send.at[j],
            self.c_recv.at[j],
            (self.dp, self.s + 1 - 2 * self.c),
        )

    def x_copy(self, zd):
        device = (self.z * 2 + 1 - self.x, self.s)
        j = 0 if self.order == "zxy" else zd
        src = self.acc.at[zd, 1 - self.x, self.mine] if self.order == "yxz" else self.acc.at[zd, 1 - self.x]
        return remote(src, self.xbuf.at[j], self.x_send.at[j], self.x_recv.at[j], device)

    def y_copy(self, zd):
        device = (self.dp, (1 - self.y) * 2 + self.c)
        j = 0 if self.order[2] == "y" else zd
        rows = self.some(1 - self.y)
        src = self.acc.at[zd, :, rows] if self.order == "yxz" else self.acc.at[zd, self.x, rows]
        return remote(src, self.ybuf.at[j], self.y_send.at[j], self.y_recv.at[j], device)

    def z_copy(self, k):
        zd = (self.z + k) % Z_CHIPS
        src = self.acc.at[zd, self.x, self.mine]
        if self.order == "zxy":
            src = self.acc.at[zd]
        elif self.order == "xzy":
            src = self.acc.at[zd, self.x]
        return remote(
            src, self.zbuf.at[k - 1], self.z_send.at[k], self.z_recv.at[k], (zd * 2 + self.x, self.s)
        )

    def fin_quarter(self, y, core):
        return self.fin.at[self.some(y), self.cols(core)]

    def fin_copy(self, k):
        device = (self.dp, (1 - self.y) * 2 + self.c) if k == 2 else (self.dp, self.s + 1 - 2 * self.c)
        y = 1 - self.y if k == 3 else self.y
        dst = self.fin_quarter(y, self.c)
        return remote(dst if k == 3 else self.quarter, dst, self.f_send.at[k], self.f_recv.at[k], device)

    def fin_in(self, k):
        ref = self.fin_quarter(self.y if k == 1 else 1 - self.y, self.c if k == 2 else 1 - self.c)
        return remote(self.quarter, ref, self.f_send.at[k], self.f_recv.at[k], (self.dp, self.s))

    def fin_own(self):
        return pltpu.make_async_copy(self.quarter, self.fin_quarter(self.y, self.c), self.local)

    def core_start(self):
        for j in range(self.core_pieces):
            self.core_copy(j).start()

    def core_sent(self):
        for j in range(self.core_pieces):
            self.core_copy(j).wait_send()

    def z_block(self, k):
        zd = (self.z + k) % Z_CHIPS
        self.core_copy(zd).wait_recv()
        for xd in range(2):
            self.acc[zd, xd] = (self.acc[zd, xd].astype(f32) + self.cbuf[zd, xd].astype(f32)).astype(bf16)
        if self.order[0] == "x":
            self.x_copy(zd).start()
        elif k % Z_CHIPS:
            self.z_copy(k % Z_CHIPS).start()

    def core_add(self, j):
        self.core_copy(j).wait_recv()
        if self.order[0] != "y":
            xd = (1 - self.x) if j == 0 else self.x

            def one(zd, carry):
                self.acc[zd, xd] = (self.acc[zd, xd].astype(f32) + self.cbuf[zd, xd].astype(f32)).astype(bf16)
                return carry

        else:
            rows = self.some((1 - self.y) if j == 0 else self.y)

            def one(zd, carry):
                for xd in range(2):
                    self.acc[zd, xd, rows] = (
                        self.acc[zd, xd, rows].astype(f32) + self.cbuf[zd, xd, rows].astype(f32)
                    ).astype(bf16)
                return carry

        lax.fori_loop(0, Z_CHIPS, one, 0)

    def second(self, k):
        zd = (self.z + k + 1) % Z_CHIPS
        if self.order[0] == "x":
            self.x_copy(zd).wait_recv()
            self.acc[zd, self.x] = (self.acc[zd, self.x].astype(f32) + self.xbuf[zd].astype(f32)).astype(bf16)
            if self.order == "xyz":
                self.y_copy(zd).start()
            elif k < 3:
                self.z_copy(k + 1).start()
        else:
            self.y_copy(zd).wait_recv()
            for xd in range(2):
                self.acc[zd, xd, self.mine] = (
                    self.acc[zd, xd, self.mine].astype(f32) + self.ybuf[zd, xd].astype(f32)
                ).astype(bf16)
            self.x_copy(zd).start()

    def third(self, k):
        zd = (self.z + k) % Z_CHIPS
        if self.order == "xyz":
            self.y_copy(zd).wait_recv()
            came = self.ybuf
        else:
            self.x_copy(zd).wait_recv()
            came = self.xbuf
        self.acc[zd, self.x, self.mine] = (
            self.acc[zd, self.x, self.mine].astype(f32) + came[zd].astype(f32)
        ).astype(bf16)
        if k:
            self.z_copy(k).start()

    def publish(self, total):
        self.quarter[...] = total.astype(bf16)
        self.fin_own().start()
        self.fin_copy(1).start()
        self.fin_copy(2).start()

    def stage(self, i):
        if i >= 40:
            self.third((i - 39) % Z_CHIPS)
        elif i >= 30:
            self.second(i - 30)
        elif i == 6:
            self.fin_in(2).wait_recv()
            self.fin_copy(3).start()
        elif i == 7:
            self.fin_own().wait()
            self.fin_in(1).wait_recv()
            self.fin_in(3).wait_recv()
        elif self.order != "zxy":
            if i == 1:
                self.core_add(0)
                for k in range(Z_CHIPS):
                    zd = (self.z + k + 1) % Z_CHIPS
                    (self.x_copy(zd) if self.order[0] == "x" else self.y_copy(zd)).start()
            elif i == 2:
                self.core_add(1)
            elif i == 3:
                for k in range(Z_CHIPS):
                    self.second(k)
            elif i == 4 and self.order == "xzy":
                total = self.acc[self.z, self.x].astype(f32)
                for k in range(1, Z_CHIPS):
                    self.z_copy(k).wait_recv()
                    total = total + self.zbuf[k - 1].astype(f32)
                self.acc[self.z, self.x] = total.astype(bf16)
                self.y_copy(self.z).start()
            elif i == 4:
                for k in (1, 2, 3, 0):
                    self.third(k)
            elif i == 5 and self.order == "xzy":
                self.y_copy(self.z).wait_recv()
                self.publish(self.acc[self.z, self.x, self.mine].astype(f32) + self.ybuf[0].astype(f32))
            elif i == 5:
                total = self.acc[self.z, self.x, self.mine].astype(f32)
                for k in range(1, Z_CHIPS):
                    self.z_copy(k).wait_recv()
                    total = total + self.zbuf[k - 1].astype(f32)
                self.publish(total)
        else:
            if i == 1:
                self.core_add(0)
            elif i == 2:
                self.core_add(1)
                for k in range(1, Z_CHIPS):
                    self.z_copy(k).start()
            elif i == 3:
                for k in range(1, Z_CHIPS):
                    self.z_copy(k).wait_recv()
                for xd in range(2):
                    total = self.acc[self.z, xd].astype(f32)
                    for k in range(1, Z_CHIPS):
                        total = total + self.zbuf[k - 1, xd].astype(f32)
                    self.acc[self.z, xd] = total.astype(bf16)
                self.x_copy(self.z).start()
            elif i == 4:
                self.x_copy(self.z).wait_recv()
                total = self.acc[self.z, self.x].astype(f32) + self.xbuf[0].astype(f32)
                self.acc[self.z, self.x] = total.astype(bf16)
                self.y_copy(self.z).start()
            elif i == 5:
                self.y_copy(self.z).wait_recv()
                self.publish(self.acc[self.z, self.x, self.mine].astype(f32) + self.ybuf[0].astype(f32))

    def settle(self):
        for k in range(1, Z_CHIPS):
            self.z_copy(k).wait_send()
        for k in range(1, 4):
            self.fin_copy(k).wait_send()
        for k in range(1 if self.order == "zxy" else Z_CHIPS):
            self.x_copy((self.z + k) % Z_CHIPS).wait_send()
        for k in range(1 if self.order[2] == "y" else Z_CHIPS):
            self.y_copy((self.z + k) % Z_CHIPS).wait_send()


class Returns:
    def __init__(self, rows_ref, long_out, short_out, send, recv, local, own_rows=None):
        self.rows_ref, self.long_out, self.short_out = rows_ref, long_out, short_out
        self.send, self.recv, self.local = send, recv, local
        self.dp, self.s = lax.axis_index("dp"), lax.axis_index("seq")
        self.own_rows = rows_ref.at[self.s] if own_rows is None else own_rows

    def own(self):
        for j, (first, rows, (_, dst)) in enumerate(zip((0, 128, 192), (128, 64, 64), self.pieces(self.s, self.s))):
            yield pltpu.make_async_copy(self.own_rows.at[pl.ds(first, rows)], dst, self.local.at[j])

    def pieces(self, target, source):
        yield self.rows_ref.at[target, pl.ds(0, 128)], self.long_out.at[source // 2, source % 2]
        yield self.rows_ref.at[target, pl.ds(128, 64)], self.short_out.at[0, source]
        yield self.rows_ref.at[target, pl.ds(192, 64)], self.short_out.at[1, source]

    copies, start, finish, settle = Tokens.copies, Tokens.start, Tokens.finish, Tokens.settle


def sums_window(d):
    return jnp.minimum(d * 96 // 128, 4) * 128


class Sums:
    def __init__(self, src, sbuf, part, dbuf, out, sems):
        self.src, self.sbuf, self.part, self.dbuf, self.out = src, sbuf, part, dbuf, out
        self.s_send, self.s_recv, self.d_send, self.d_recv = sems
        self.dp, self.s = lax.axis_index("dp"), lax.axis_index("seq")

    def s_copy(self, k, source):
        return remote(self.src, self.sbuf.at[source], self.s_send.at[k], self.s_recv.at[k], (self.dp, (self.s + k) % 4))

    def window(self, d):
        return self.part.at[:, pl.ds(pl.multiple_of(sums_window(d), 128), 256)]

    def d_copy(self, k, source):
        target = (self.dp + k) % 8
        return remote(self.window(target), self.dbuf.at[source], self.d_send.at[k], self.d_recv.at[k], (target, self.s))

    def stage(self, i):
        if i == 0:
            for k in range(1, 4):
                self.s_copy(k, self.s).start()
            self.sbuf[self.s] = self.src[...]
        elif i == 1:
            for k in range(1, 4):
                self.s_copy(k, (self.s + 4 - k) % 4).wait_recv()
            self.part[...] = (self.sbuf[0] + self.sbuf[1]) + (self.sbuf[2] + self.sbuf[3])
            for k in range(1, 8):
                self.d_copy(k, self.dp).start()
            self.dbuf[self.dp] = self.window(self.dp)[...]
        elif i == 2:
            for k in range(1, 8):
                self.d_copy(k, (self.dp + 8 - k) % 8).wait_recv()
            total = self.dbuf[0]
            for d in range(1, 8):
                total = total + self.dbuf[d]
            self.out[...] = total

    def settle(self):
        for k in range(1, 4):
            self.s_copy(k, self.s).wait_send()
        for k in range(1, 8):
            self.d_copy(k, self.dp).wait_send()


PIECES = (
    (384, D, "xzy"),
    (192, D, "yxz"),
    (192, D, "xyz"),
    (96, D, "xzy"),
    (96, D, "xzy"),
    (96, D, "xzy"),
    (96, D, "xzy"),
)


MIDDLE_JOBS = {
    0: (),
    1: ((0, 30),),
    2: ((0, 31),),
    3: (),
}
ONE_JOBS = ((2, 1),)
O_JOBS = ((1, 1),)
BEFORE_PAIR = {
    0: (),
    1: (),
    2: ((3, 1), (1, 2), (3, 2), (0, 32), (1, 30), (2, 2), (0, 33),),
    3: ((1, 31), (4, 1),),
    4: ((3, 31), (2, 30), (5, 1), (1, 33), (1, 40), (5, 2), (1, 41), (4, 30), (2, 31),),
    5: ((2, 32), (2, 33), (5, 30), (2, 40), (5, 31), (0, 5),),
}
AFTER_GROUP = (
    (),
    ((4, 2), (0, 4), (3, 30), (1, 32),),
    ((5, 32), (2, 41), (4, 31), (3, 32), (5, 33), (6, 1), (6, 2), (4, 32), (3, 33), (4, 33), (5, 4), (6, 30), (1, 42), (4, 4), (6, 31), (3, 4), (1, 43), (6, 32), (2, 42), (0, 6), (5, 5), (2, 43), (1, 5), (4, 5), (5, 6), (6, 33), (3, 5), (6, 4),),
)
LAST_JOBS = ((1, 6), (2, 5), (3, 6), (6, 5), (2, 6), (4, 6), (6, 6),)


def backward_kernel(*refs):
    refs = list(refs)

    def take(n):
        out = refs[:n]
        del refs[:n]
        return out

    short_len_ref, long_len_ref, vec_ref, sums_in = take(4)
    act_hbm, slope_hbm, y1b_hbm, norm_hbm, inv_hbm, ainv_hbm, dz_hbm, dfb_hbm, att_hbm, qkv_hbm, probs_hbm = take(11)
    tok_hbm, w_hbm, wo_hbm, w1_hbm, w2_hbm, out_rows = take(6)
    fins = take(len(PIECES))
    (sums_out,) = take(1)
    short_out, long_out, short_back, long_back = take(4)
    (theirs_a,) = take(1)
    bufs = [take(6) for _ in PIECES]
    big, dfb_s, y1b_s, att_s, at_s, first_s, second_s, wo_s, dub_s, dh_s, dob_s, inv_s, dqkv_s = take(13)
    sums_s, sbuf, part, dbuf = take(4)
    sems = take(11)
    s_sems = take(4)
    t_send, t_recv, local, load_sem, big_sem, ainv_s, ainv_sem, out_s = take(8)

    dp, s, z, x, y, c = place()
    lens_ref = own_lengths(short_len_ref, long_len_ref)
    greet()
    outs = Returns(out_rows, long_out, short_out, t_send.at[0], t_recv.at[0], local.at[0], out_s)
    backs = Returns(y1b_s, long_back, short_back, t_send.at[1], t_recv.at[1], local.at[1])

    def plan(i, *pairs):
        return [pltpu.make_async_copy(src, dst, load_sem.at[i + j]) for j, (src, dst) in enumerate(pairs)]

    def begin(copies):
        for copy in copies:
            copy.start()
        return copies

    def load(i, *pairs):
        return begin(plan(i, *pairs))

    def done(copies):
        for copy in copies:
            copy.wait()

    def big_copy(src, slot):
        return pltpu.make_async_copy(src, big.at[slot], big_sem.at[slot])

    def act_chunk(k):
        return act_hbm.at[(z + k) % Z_CHIPS]

    chunk = lambda i: pl.ds(i * D, D)
    big_copy(act_chunk(1), 1).start()
    load_dfb = load(0, (dfb_hbm, dfb_s))
    load_out = load(12, (out_rows.at[s], out_s))
    load_w2 = plan(1, (w2_hbm, second_s))
    load_w1 = plan(2, *[(w1_hbm.at[:, chunk(k)], first_s.at[chunk(k)]) for k in range(4)])
    load_mid = plan(6, (dz_hbm, dh_s), (norm_hbm, dob_s), (inv_hbm, inv_s), (wo_hbm, wo_s))
    load_y1b = plan(10, (y1b_hbm, y1b_s))
    load_att = plan(11, (att_hbm, att_s))

    pieces = []
    for i, (rows, cols, order) in enumerate(PIECES):
        first = (0, 0, 192, 0, 96, 192, 288)[i]
        theirs = theirs_a.at[:, :, pl.ds(first, rows), :]
        pieces.append(Grad(theirs, *bufs[i], fins[i], [r.at[i] for r in sems], order))
    down, one_a, one_b, o_piece = pieces[:4]
    sums = Sums(sums_s, sbuf, part, dbuf, sums_out, s_sems)
    done(load_out)
    outs.start()

    def run(jobs):
        for index, stage in jobs:
            pieces[index].stage(stage)

    def during(i, plan):
        for when, jobs in plan.items():

            @pl.when(i == when)
            def _():
                run(jobs)

    def columns(core):
        return pl.ds(pl.multiple_of(core * (D // 2), 128), D // 2)

    sums_s[...] = sums_in[...]
    done(load_dfb)

    def down_block(k, carry):
        zd = (z + k) % Z_CHIPS
        slot = k % 2
        big_copy(act_chunk(k), slot).wait()

        @pl.when(k < Z_CHIPS)
        def _():
            big_copy(act_chunk(k + 1), 1 - slot).start()

        @pl.when(k == Z_CHIPS)
        def _():
            big_copy(slope_hbm.at[0], 1 - slot).start()

        for j, later in ((1, load_w2), (2, load_w1), (3, load_mid), (4, load_y1b + load_att)):

            @pl.when(k == j)
            def _():
                begin(later)

        at_s[...] = jnp.transpose(big[slot])
        theirs_a[zd] = dot_nn(at_s[...], dfb_s[:, :, columns(1 - c)].reshape(1024, D // 2)).astype(bf16).reshape(2, 384, D // 2)
        down.core_copy(zd).start()
        down.acc[zd] = dot_nn(at_s[...], dfb_s[:, :, columns(c)].reshape(1024, D // 2)).astype(bf16).reshape(2, 384, D // 2)
        for j in range(2, Z_CHIPS + 1):

            @pl.when(k == j)
            def _():
                down.z_block(j - 1)

        return carry

    def ainv_copy(r, slot):
        return pltpu.make_async_copy(ainv_hbm.at[r], ainv_s.at[slot], ainv_sem.at[slot])

    lax.fori_loop(1, Z_CHIPS + 1, down_block, 0)
    ainv_copy(0, 0).start()
    done(load_w2)
    done(load_w1)
    done(load_mid)
    row_vec = lambda i: vec_ref[i : i + 1, :]

    def add(index, v):
        sums_s[index : index + 1, :] += jnp.sum(v, axis=0, keepdims=True)

    def middle_back(r, carry):
        slot = (r + 1) % 2
        big_copy(slope_hbm.at[r], slot).wait()

        @pl.when(r < 3)
        def _():
            big_copy(slope_hbm.at[r + 1], 1 - slot).start()

        @pl.when(r == 0)
        def _():
            down.z_block(Z_CHIPS)

        during(r, MIDDLE_JOBS)
        ainv_copy(r, r % 2).wait()

        @pl.when(r < 3)
        def _():
            ainv_copy(r + 1, (r + 1) % 2).start()

        at = pl.ds(pl.multiple_of(r * 256, 256), 256)
        dfb = dfb_s[r]
        dy1 = dh_s[r]
        for k in range(FF // D):
            slope = big[slot, k * 256 : (k + 1) * 256].astype(f32)
            dub = (dot_nt(dfb, second_s[k * D : (k + 1) * D]) * slope).astype(bf16)
            dub_s[k, at] = dub
            add(8 + k, dub.astype(f32))
            dy1 = dy1 + dot_nt(dub, first_s[k * D : (k + 1) * D])
        normed = dob_s[r].astype(f32)
        add(3, dy1 * normed)
        add(4, dy1)
        dh = layer_norm_back(dy1 * row_vec(3), normed, inv_s[r][:, 0:1])
        dab = dh.astype(bf16)
        dh_s[r] = dh
        dfb_s[r] = dab
        add(2, dab.astype(f32))
        dob_s[r] = (dot_nt(dab, wo_s[...]) * ainv_s[r % 2]).astype(bf16)
        return carry

    lax.fori_loop(0, 4, middle_back, 0)
    qkv_loads = load(1, *[(qkv_hbm.at[:, :, chunk(j)], first_s.at[pl.ds(j * 1024, 1024)].reshape(4, 256, D)) for j in range(3)])
    w_loads = load(4, *[(w_hbm.at[:, chunk(j)], second_s.at[chunk(j)]) for j in range(3)])

    def probs_copy(i, slot):
        return big_copy(probs_hbm.at[i], slot)

    probs_copy(0, 0).start()

    done(load_y1b)
    at_s[...] = jnp.transpose(y1b_s[...].reshape(1024, D))
    load_tok = load(10, (tok_hbm, y1b_s))
    down.core_sent()

    def one_block(k, carry):
        core = jnp.where(k < 2, 1 - c, c)
        grad = dot_nn(at_s[...], dub_s[core * 2 + k % 2]).astype(bf16)
        for e in range(2):
            half = grad[:, e * (D // 2) : (e + 1) * (D // 2)].reshape(4, 2, 96, D // 2)
            rows = pl.ds(e * 96, 96)
            for j, ref in enumerate((one_a.theirs, one_b.theirs, one_a.acc, one_b.acc)):

                @pl.when(k == j)
                def _():
                    ref[:, :, rows, :] = half

        for j, piece in ((0, one_a), (1, one_b)):

            @pl.when(k == j)
            def _():
                piece.core_start()

        return carry

    lax.fori_loop(0, 4, one_block, 0)
    run(ONE_JOBS)
    one_a.core_sent()
    one_b.core_sent()

    def small_grad(piece, right):
        piece.theirs[...] = dot_nn(at_s[...], right(1 - c)).astype(bf16).reshape(4, 2, 96, D // 2)
        piece.core_start()
        piece.acc[...] = dot_nn(at_s[...], right(c)).astype(bf16).reshape(4, 2, 96, D // 2)

    done(load_att)
    at_s[...] = jnp.transpose(att_s[...].reshape(1024, D))
    small_grad(o_piece, lambda core: dfb_s[:, :, columns(core)].reshape(1024, D // 2))
    run(O_JOBS)

    done(load_tok)
    at_s[...] = jnp.transpose(y1b_s[...].reshape(1024, D))
    done(qkv_loads)
    done(w_loads)
    pairs = D // PAIR

    for g in range(3):

        def pair(i, carry, g=g):
            during(i, {j: BEFORE_PAIR[j] for j in (2 * g, 2 * g + 1)})
            slot = i % 2
            probs_copy(i, slot).wait()

            @pl.when(i + 1 < pairs)
            def _():
                probs_copy(i + 1, 1 - slot).start()

            lanes = pl.ds(pl.multiple_of(i * PAIR, PAIR), PAIR)
            sum_q = jnp.zeros((1, PAIR), f32)
            sum_v = jnp.zeros((1, PAIR), f32)
            for first, rows, length, index in SEQS:
                q, k, v = [
                    first_s[j * 1024 : (j + 1) * 1024, lanes].reshape(4, 256, PAIR)[:, first : first + rows].reshape(length, PAIR)
                    for j in range(3)
                ]
                do, o = [r[:, first : first + rows, lanes].reshape(length, PAIR) for r in (dob_s, att_s)]

                def kept(h, index=index):
                    if index == 0:
                        return big[slot, h * LONG_L : (h + 1) * LONG_L, 0:LONG_L]
                    row = (2 * h + index - 1) * SHORT_L
                    return big[slot, row : row + SHORT_L, LONG_L : LONG_L + SHORT_L]

                grads = attend_sums_back(q, k, v, do, o, lens_ref[index], kept)
                sum_q = sum_q + jnp.sum(grads[0].astype(f32), axis=0, keepdims=True)
                sum_v = sum_v + jnp.sum(grads[2].astype(f32), axis=0, keepdims=True)
                for j in range(3):
                    dst = pl.ds(pl.multiple_of(j * 256 + (i % 2) * PAIR, PAIR), PAIR)
                    dqkv_s[:, first : first + rows, dst] = grads[j].reshape(4, rows, PAIR)
            sums_s[0:1, lanes] = sum_q
            sums_s[1:2, lanes] = sum_v
            return carry

        lax.fori_loop(2 * g, 2 * g + 2, pair, 0)
        small_grad(pieces[4 + g], lambda core: dqkv_s[:, :, columns(core)].reshape(1024, D // 2))
        if g == 2:
            sums.stage(0)

        def rows_back(r, carry, g=g):
            total = dh_s[r]
            for j in range(3):
                total = total + dot_nt(
                    dqkv_s[r, :, j * 256 : (j + 1) * 256], second_s[j * D : (j + 1) * D, g * 256 : (g + 1) * 256]
                )
            if g < 2:
                dh_s[r] = total
            else:
                y1b_s[r] = total.astype(bf16)
            return carry

        if g == 2:
            lax.fori_loop(0, 4, rows_back, 0)
            backs.start()
            run(AFTER_GROUP[g])
        else:
            run(AFTER_GROUP[g])
            lax.fori_loop(0, 4, rows_back, 0)

    sums.stage(1)
    run(LAST_JOBS)
    sums.stage(2)
    run([(i, 7) for i in range(len(PIECES))])
    outs.finish()
    backs.finish()
    for i, piece in enumerate(pieces):
        if i > 2:
            piece.core_sent()
        piece.settle()
    sums.settle()
    outs.settle()
    backs.settle()


def backward(short_len, long_len, vec, sums, arrays, out_rows):
    any_spec = pl.BlockSpec(memory_space=pl.ANY)
    vmem = pl.BlockSpec(memory_space=pltpu.VMEM)
    smem = pl.BlockSpec(memory_space=pltpu.SMEM)
    shape = jax.ShapeDtypeStruct
    dma = pltpu.SemaphoreType.DMA
    count = len(PIECES)
    vm = lambda dims, t=bf16: pltpu.VMEM(dims, t)
    bufs = []
    for rows, cols, order in PIECES:
        half, cut = cols // 2, rows // 2
        bufs += [vm((4, 2, rows, half)), vm((4, 2, rows, half))]
        bufs += {
            "xyz": [vm((4, rows, half)), vm((4, cut, half)), vm((3, cut, half))],
            "yxz": [vm((4, cut, half)), vm((4, 2, cut, half)), vm((3, cut, half))],
            "xzy": [vm((4, rows, half)), vm((1, cut, half)), vm((3, rows, half))],
            "zxy": [vm((1, rows, half)), vm((1, cut, half)), vm((3, 2, rows, half))],
        }[order]
        bufs.append(vm((cut, half)))
    tok = (4, 256, D)
    return pl.pallas_call(
        backward_kernel,
        in_specs=[smem, smem, vmem, vmem] + [any_spec] * (len(arrays) + 1),
        out_specs=[any_spec] * count + [vmem] + [any_spec] * 4,
        out_shape=[shape((rows, cols), bf16) for rows, cols, _ in PIECES]
        + [
            shape((16, 256), f32),
            shape((2, 4, 64, D), bf16),
            shape((2, 2, 128, D), bf16),
            shape((2, 4, 64, D), bf16),
            shape((2, 2, 128, D), bf16),
        ],
        scratch_shapes=[vm((4, 2, 384, D // 2))]
        + bufs
        + [
            vm((2, 1024, D)),
            vm(tok),
            vm(tok),
            vm(tok),
            vm((D, 1024)),
            vm((FF, D)),
            vm((FF, D)),
            vm((D, D)),
            vm((4, 1024, D)),
            vm(tok, f32),
            vm(tok),
            vm((4, 256, 128), f32),
            vm(tok),
            vm((16, D), f32),
            vm((4, 16, D), f32),
            vm((16, D), f32),
            vm((8, 16, 256), f32),
        ]
        + [dma((count, 4))] * 10
        + [dma((count,))]
        + [dma((4,)), dma((4,)), dma((8,)), dma((8,))]
        + [dma((2, 4, 3)), dma((2, 4, 3)), dma((2, 3)), dma((13,)), dma((2,)), vm((2, 256, D), f32), dma((2,)), vm((256, D))],
        compiler_params=pltpu.CompilerParams(
            vmem_limit_bytes=VMEM_BYTES, collective_id=1, has_side_effects=True
        ),
        name="backward",
    )(short_len, long_len, vec, sums, *arrays, out_rows)


def transpose_dot(left, right):
    return jnp.einsum("ra,rb->ab", left, right, preferred_element_type=f32)


def right_dot(left, right):
    return jnp.einsum("ra,ba->rb", left, right, preferred_element_type=f32)


def flip(v, axis, bit):
    n = lax.axis_size(axis)
    return lax.ppermute(v, axis, [(i, i ^ bit) for i in range(n)])


def half_of(v, dim, which):
    size = v.shape[dim] // 2
    return lax.dynamic_slice_in_dim(v, which * size, size, dim)


def halve(v, axis, bit, dim):
    mine = (lax.axis_index(axis) // bit) % 2
    other = flip(half_of(v, dim, 1 - mine), axis, bit)
    return (half_of(v, dim, mine).astype(f32) + other.astype(f32)).astype(bf16)


def double(v, axis, bit, dim):
    mine = (lax.axis_index(axis) // bit) % 2
    other = flip(v, axis, bit)
    return jnp.where(
        mine == 0, jnp.concatenate([v, other], axis=dim), jnp.concatenate([other, v], axis=dim)
    )


def reduce_rows(grad):
    rows, cols = grad.shape
    dp = lax.axis_size("dp")
    v = grad.reshape(dp, rows // dp, cols)
    v = halve(v, "seq", 1, 2)
    v = halve(v, "seq", 2, 2)
    bit = 1
    while bit < dp:
        blocks = v.shape[0]
        v = v.reshape(blocks // 2, 2, v.shape[1], v.shape[2]) if v.ndim == 3 else v
        v = halve(v, "dp", bit, 1)[:, 0]
        bit *= 2
    v = v[0]
    v = double(v, "seq", 2, 1)
    v = double(v, "seq", 1, 1)
    return v.astype(f32)


def update(master, reduced_grad, moment, average):
    step_grad = reduced_grad + decay_weight * master
    velocity = momentum_rate * moment + step_grad
    updated = master - learning_rate * (step_grad + momentum_rate * velocity)
    averaged = average_rate * average + (1.0 - average_rate) * updated
    return (velocity, averaged, updated, updated.astype(jnp.bfloat16))


UPDATE_STEPS = 8


def update_kernel(*refs):
    refs = list(refs)

    def take(n):
        out = refs[:n]
        del refs[:n]
        return out

    down_low, one_a, one_b, o_low, low_0, low_1, low_2 = take(7)
    wide_state, down_state, passed = take(3), take(3), take(4)
    wide_out, down_out, passed_out = take(5), take(5), take(4)
    (grad_s,) = take(1)
    i = pl.program_id(0)
    for src, dst in zip(passed, passed_out):
        dst[...] = src[...]
    half = D // 2
    for b in range(UPDATE_STEPS):

        @pl.when(i == b)
        def _():
            if b < 3:
                for g, low in enumerate((low_0, low_1, low_2)):
                    grad_s[:, g * 256 : (g + 1) * 256] = low[:, b * 256 : (b + 1) * 256]
            elif b == 3:
                grad_s[...] = o_low[...]
            else:
                rows, core = grad_s.shape[0], (b - 4) // 2
                low = (one_a, one_b)[b % 2]
                for k in range(2):
                    part = low[k * rows : (k + 1) * rows, core * half : (core + 1) * half]
                    grad_s[:, k * half : (k + 1) * half] = part

    def step(grad, state, outs):
        master, moment, average = state
        outs[0][...] = grad
        for ref, v in zip(outs[1:], update(master[...], grad, moment[...], average[...])):
            ref[...] = v

    step(grad_s[...].astype(f32), wide_state, wide_out)
    rows = down_state[0].shape[0]
    step(down_low[pl.ds(pl.multiple_of(i * rows, 16), rows)].astype(f32), down_state, down_out)


def update_all(lows, wide, down, passed):
    rows, cols = wide[0].shape
    down_rows = down[0].shape[0]
    vmem = pl.BlockSpec(memory_space=pltpu.VMEM)
    short_spec = pl.BlockSpec((1, 1, 64, D), lambda i: (i // 4, i % 4, 0, 0))
    long_spec = pl.BlockSpec((1, 1, 64, D), lambda i: (i // 4, i % 4 // 2, i % 2, 0))
    passed_specs = [short_spec, long_spec, short_spec, long_spec]
    shape = jax.ShapeDtypeStruct
    wide_spec = pl.BlockSpec((rows, cols // UPDATE_STEPS), lambda i: (0, i))
    down_spec = pl.BlockSpec((down_rows // UPDATE_STEPS, D), lambda i: (i, 0))
    types = (f32, f32, f32, f32, bf16)
    return pl.pallas_call(
        update_kernel,
        grid=(UPDATE_STEPS,),
        in_specs=[vmem] * len(lows) + [wide_spec] * 3 + [down_spec] * 3 + passed_specs,
        out_specs=[wide_spec] * 5 + [down_spec] * 5 + passed_specs,
        out_shape=[shape((rows, cols), t) for t in types]
        + [shape((down_rows, D), t) for t in types]
        + [shape(p.shape, p.dtype) for p in passed],
        scratch_shapes=[pltpu.VMEM((rows, D), bf16)],
        compiler_params=params(),
        name="update",
    )(*lows, *wide, *down, *passed)


def spread_rows(long_part, short_part):
    long_blocks = long_part.reshape(4, 128, D)
    short_blocks = jnp.transpose(short_part, (1, 0, 2, 3)).reshape(4, 128, D)
    return jnp.concatenate([long_blocks, short_blocks], axis=1)


def exchange(v):
    return lax.all_to_all(v, "seq", split_axis=0, concat_axis=0, tiled=True)


def collect_rows(v):
    long_part = v[:, :128].reshape(2, 2, 128, D)
    short_part = jnp.transpose(v[:, 128:].reshape(4, 2, 64, D), (1, 0, 2, 3))
    return short_part, long_part


def body(
    short_in,
    long_in,
    short_cot,
    long_cot,
    short_len,
    long_len,
    wide_master,
    down_master,
    vector_master,
    wide_moment,
    down_moment,
    vector_moment,
    wide_average,
    down_average,
    vector_average,
):
    s = lax.axis_index("seq")
    own_rows = vector_master.shape[0]
    if lax.axis_size("dp") == 8:
        vec_own = jnp.pad(jnp.transpose(vector_master).astype(bf16), ((0, 4), (0, 0)))
        vec_block = lax.dynamic_update_slice(
            jnp.zeros((16, D), bf16), vec_own, (0, lax.axis_index("dp") * own_rows)
        )
        (w_qkv, w_o, w_1, w_2, tokens, qkv, attended, probs, act, slope, y1b, norm, inv, dz, dfb, out, att_inv, vec, sums) = forward(
            short_len, long_len, wide_master, down_master, vec_block, long_in, short_in, long_cot, short_cot
        )
        w_qkv, w_o, w_1, w_2 = [w.reshape(-1, w.shape[2]) for w in (w_qkv, w_o, w_1, w_2)]
        arrays = (act, slope, y1b, norm, inv, att_inv, dz, dfb, attended, qkv, probs, tokens, w_qkv, w_o, w_1, w_2)
        *lows, sums_own, short_out, long_out, short_back, long_back = backward(
            short_len, long_len, vec, sums, arrays, out
        )
        index = lax.axis_index("dp")
        own_sums = lax.dynamic_slice(sums_own, (0, index * own_rows - sums_window(index)), (12, own_rows))
        vector_reduced = jnp.transpose(own_sums)
        results = update_all(
            lows,
            (wide_master, wide_moment, wide_average),
            (down_master, down_moment, down_average),
            (short_out, long_out, short_back, long_back),
        )
        wide_reduced, *wide_new = results[:5]
        down_reduced, *down_new = results[5:10]
        short_out, long_out, short_back, long_back = results[10:]
    else:
        lens = jnp.stack([long_len[s // 2, 0, s % 2], short_len[0, 0, s], short_len[1, 0, s]])
        tokens = exchange(spread_rows(long_in, short_in))
        cotangent = exchange(spread_rows(long_cot, short_cot))
        wide_w = lax.all_gather(wide_master.astype(bf16), "dp", axis=0, tiled=True)
        w_2 = lax.all_gather(down_master.astype(bf16), "dp", axis=0, tiled=True)
        vector_w = lax.all_gather(vector_master.astype(bf16), "dp", axis=0, tiled=True)
        vec = jnp.transpose(vector_w.astype(f32))
        w_qkv = wide_w[:, : 3 * D]
        w_o = wide_w[:, 3 * D : 4 * D]
        w_1 = wide_w[:, 4 * D :]
        rows = tokens.reshape(1024, D)
        proj_bias = jnp.concatenate([vec[0], jnp.zeros((D,), f32), vec[1]])
        qkv = (jnp.dot(rows, w_qkv, preferred_element_type=f32) + proj_bias).astype(bf16)
        qkv = qkv.reshape(4, 256, 3 * D)
        attended, long_probs, short_probs = attn_forward(lens, qkv)
        flat_attended = attended.reshape(1024, D)
        out, y1b, act, dfb, dub, dab, dob, dh, sums = middle(
            lens, flat_attended, rows, cotangent.reshape(1024, D), w_o, w_1, w_2, vec
        )
        d_down = transpose_dot(act, dfb).astype(bf16)
        d_one = transpose_dot(y1b, dub).astype(bf16)
        d_o = transpose_dot(flat_attended, dab).astype(bf16)
        dq, dk, dv, qv_sums = attn_backward(
            lens, qkv, dob.reshape(4, 256, D), attended, long_probs, short_probs
        )
        d_qkv = jnp.concatenate([dq, dk, dv], axis=2).reshape(1024, 3 * D)
        d_wqkv = transpose_dot(rows, d_qkv).astype(bf16)
        back = (dh + right_dot(d_qkv, w_qkv)).astype(bf16).reshape(4, 256, D)
        vector_total = jnp.concatenate([qv_sums[:2], sums[2:12]], axis=0)
        vector_sum = jnp.transpose(lax.psum(vector_total, ("dp", "seq")))
        vector_reduced = lax.dynamic_slice_in_dim(vector_sum, lax.axis_index("dp") * own_rows, own_rows, 0)
        wide_reduced = jnp.concatenate([reduce_rows(d_wqkv), reduce_rows(d_o), reduce_rows(d_one)], axis=1)
        down_reduced = reduce_rows(d_down)
        short_out, long_out = collect_rows(exchange(out.reshape(4, 256, D)))
        short_back, long_back = collect_rows(exchange(back))
        wide_new = update(wide_master, wide_reduced, wide_moment, wide_average)
        down_new = update(down_master, down_reduced, down_moment, down_average)
    vector_new = update(vector_master, vector_reduced, vector_moment, vector_average)
    return (
        short_out,
        long_out,
        short_back,
        long_back,
        wide_reduced,
        down_reduced,
        vector_reduced,
        wide_new[0],
        down_new[0],
        vector_new[0],
        wide_new[1],
        down_new[1],
        vector_new[1],
        wide_new[2],
        down_new[2],
        vector_new[2],
        wide_new[3],
        down_new[3],
        vector_new[3],
    )


def solution(mesh):
    tok = P(None, "dp", "seq", None)
    lengths = P(None, "dp", None)
    state = P("dp", None)
    return jax.shard_map(
        body,
        mesh=mesh,
        in_specs=(tok,) * 4 + (lengths,) * 2 + (state,) * 9,
        out_specs=(tok,) * 4 + (state,) * 15,
        check_vma=False,
    )
```

```python
import jax
import jax.numpy as jnp
from jax import lax
from jax.experimental import pallas as pl
from jax.experimental.pallas import tpu as pltpu
from jax.sharding import PartitionSpec as P

D = 768
HEAD_DIM = 64
FF = 3072
PAIR = 128
LONG_L = 512
SHORT_L = 256
VMEM_BYTES = 62 * 1024 * 1024

norm_eps = 1e-12
mask_fill = -10000.0
learning_rate = 0.0002
momentum_rate = 0.9
decay_weight = 0.0001
average_rate = 0.9
score_scale = HEAD_DIM ** (-0.5)
FILL_PARTS = (-9984.0, -16.0)
f32 = jnp.float32
bf16 = jnp.bfloat16


def params():
    return pltpu.CompilerParams(vmem_limit_bytes=VMEM_BYTES)


def dot_nn(a, b):
    return lax.dot_general(a, b, (((1,), (0,)), ((), ())), preferred_element_type=f32)


def dot_nt(a, b):
    return lax.dot_general(a, b, (((1,), (1,)), ((), ())), preferred_element_type=f32)


SEQS = ((0, 128, LONG_L, 0), (128, 64, SHORT_L, 1), (192, 64, SHORT_L, 2))


def attend(q, k, v, limit, keep_probs):
    length = q.shape[0]
    v_t = jnp.transpose(v)
    head_lane = lax.broadcasted_iota(jnp.int32, (length, PAIR), 1) // HEAD_DIM
    live = lax.broadcasted_iota(jnp.int32, (length, length), 0) < limit
    parts = []
    for h in range(2):
        k_h = jnp.where(head_lane == h, k, jnp.zeros_like(k))
        scores = jnp.where(live, dot_nt(k_h, q) * score_scale, mask_fill)
        top = jnp.max(scores, axis=0, keepdims=True)
        exponent = jnp.exp(scores - top)
        total = jnp.sum(exponent, axis=0, keepdims=True)
        probs = (exponent * (1.0 / total)).astype(bf16)
        keep_probs(h, probs)
        parts.append(dot_nn(v_t[h * HEAD_DIM : (h + 1) * HEAD_DIM], probs))
    return jnp.transpose(jnp.concatenate(parts, axis=0)).astype(bf16)


def attn_forward_kernel(lens_ref, q_ref, k_ref, v_ref, o_ref, long_ref, short_ref):
    for first, rows, length, index in SEQS:
        q, k, v = [r[:, first : first + rows, :].reshape(length, PAIR) for r in (q_ref, k_ref, v_ref)]

        def keep_probs(h, probs, index=index):
            if index == 0:
                long_ref[h] = probs
            else:
                short_ref[h, index - 1] = probs

        o = attend(q, k, v, lens_ref[index], keep_probs)
        o_ref[:, first : first + rows, :] = o.reshape(4, rows, PAIR)


def attn_forward(lens, qkv):
    pairs = D // PAIR
    col = lambda base: pl.BlockSpec((4, 256, PAIR), lambda i, base=base: (0, 0, base + i))
    return pl.pallas_call(
        attn_forward_kernel,
        grid=(pairs,),
        in_specs=[
            pl.BlockSpec(memory_space=pltpu.SMEM),
            col(0),
            col(pairs),
            col(2 * pairs),
        ],
        out_specs=[
            pl.BlockSpec((4, 256, PAIR), lambda i: (0, 0, i)),
            pl.BlockSpec((2, LONG_L, LONG_L), lambda i: (i, 0, 0)),
            pl.BlockSpec((2, 2, SHORT_L, SHORT_L), lambda i: (i, 0, 0, 0)),
        ],
        out_shape=[
            jax.ShapeDtypeStruct((4, 256, D), bf16),
            jax.ShapeDtypeStruct((2 * pairs, LONG_L, LONG_L), bf16),
            jax.ShapeDtypeStruct((2 * pairs, 2, SHORT_L, SHORT_L), bf16),
        ],
        compiler_params=params(),
        name="attn_forward",
    )(lens, qkv, qkv, qkv)


def attend_back(q, k, v, do, o, limit, kept_probs):
    length = q.shape[0]
    k_t = jnp.transpose(k)
    inner = jnp.transpose(do.astype(f32) * o.astype(f32))
    head_lane = lax.broadcasted_iota(jnp.int32, (length, PAIR), 1) // HEAD_DIM
    live = lax.broadcasted_iota(jnp.int32, (length, length), 0) < limit
    dq_parts = []
    dk = jnp.zeros((length, PAIR), f32)
    dv = jnp.zeros((length, PAIR), f32)
    for h in range(2):
        keep = head_lane == h
        v_h, do_h, q_h = [jnp.where(keep, m, jnp.zeros_like(m)) for m in (v, do, q)]
        probs = kept_probs(h)
        delta = jnp.sum(inner[h * HEAD_DIM : (h + 1) * HEAD_DIM], axis=0, keepdims=True)
        d_probs = dot_nt(v_h, do)
        d_scores = jnp.where(live, probs.astype(f32) * (d_probs - delta), 0.0).astype(bf16)
        dv = dv + dot_nn(probs, do_h)
        dk = dk + dot_nn(d_scores, q_h)
        dq_parts.append(dot_nn(k_t[h * HEAD_DIM : (h + 1) * HEAD_DIM], d_scores))
    dq = jnp.transpose(jnp.concatenate(dq_parts, axis=0)) * score_scale
    return dq.astype(bf16), (dk * score_scale).astype(bf16), dv.astype(bf16)


def attn_backward_kernel(
    lens_ref, q_ref, k_ref, v_ref, do_ref, o_ref, long_ref, short_ref, dq_ref, dk_ref, dv_ref, sum_ref
):
    sum_q = jnp.zeros((1, PAIR), f32)
    sum_v = jnp.zeros((1, PAIR), f32)
    for first, rows, length, index in SEQS:
        args = [r[:, first : first + rows, :].reshape(length, PAIR) for r in (q_ref, k_ref, v_ref, do_ref, o_ref)]
        kept = lambda h, index=index: long_ref[h] if index == 0 else short_ref[h, index - 1]
        dq, dk, dv = attend_back(*args, lens_ref[index], kept)
        sum_q = sum_q + jnp.sum(dq.astype(f32), axis=0, keepdims=True)
        sum_v = sum_v + jnp.sum(dv.astype(f32), axis=0, keepdims=True)
        for ref, v in ((dq_ref, dq), (dk_ref, dk), (dv_ref, dv)):
            ref[:, first : first + rows, :] = v.reshape(4, rows, PAIR)
    sum_ref[0:1, :] = sum_q
    sum_ref[1:2, :] = sum_v
    sum_ref[2:8, :] = jnp.zeros((6, PAIR), f32)


def attn_backward(lens, qkv, d_attended, attended, long_probs, short_probs):
    pairs = D // PAIR
    col = lambda base: pl.BlockSpec((4, 256, PAIR), lambda i, base=base: (0, 0, base + i))
    return pl.pallas_call(
        attn_backward_kernel,
        grid=(pairs,),
        in_specs=[
            pl.BlockSpec(memory_space=pltpu.SMEM),
            col(0),
            col(pairs),
            col(2 * pairs),
            col(0),
            col(0),
            pl.BlockSpec((2, LONG_L, LONG_L), lambda i: (i, 0, 0)),
            pl.BlockSpec((2, 2, SHORT_L, SHORT_L), lambda i: (i, 0, 0, 0)),
        ],
        out_specs=[col(0), col(0), col(0), pl.BlockSpec((8, PAIR), lambda i: (0, i))],
        out_shape=[jax.ShapeDtypeStruct((4, 256, D), bf16)] * 3 + [jax.ShapeDtypeStruct((8, D), f32)],
        compiler_params=params(),
        name="attn_backward",
    )(lens, qkv, qkv, qkv, d_attended, attended, long_probs, short_probs)


def gelu_pair(u):
    t = 1.0 / (1.0 + (0.3275911 * 0.5**0.5) * jnp.abs(u))
    e = jnp.exp2((u * u) * (-0.5 * 1.4426950408889634))
    poly = 0.5 * -0.284496736 + t * (0.5 * 1.421413741 + t * (0.5 * -1.453152027 + t * (0.5 * 1.061405429)))
    tail = (t * (0.5 * 0.254829592 + t * poly)) * e
    cdf = jnp.where(u < 0.0, tail, 1.0 - tail)
    return u * cdf, cdf + (u * (0.5 / jnp.pi) ** 0.5) * e


def row_mean(v):
    return jnp.mean(v, axis=-1, keepdims=True)


def middle_kernel(
    lens_ref,
    o_ref,
    x_ref,
    cot_ref,
    wo_ref,
    w1_ref,
    w2_ref,
    vec_ref,
    out_ref,
    y1b_ref,
    g_ref,
    dfb_ref,
    dub_ref,
    dab_ref,
    dob_ref,
    dh_ref,
    sum_ref,
    slope_ref,
):
    r = pl.program_id(0)
    rows = o_ref.shape[0]

    @pl.when(r == 0)
    def _():
        sum_ref[...] = jnp.zeros_like(sum_ref)

    def add(index, v):
        sum_ref[index : index + 1, :] += jnp.sum(v, axis=0, keepdims=True)

    vec = lambda i: vec_ref[i : i + 1, :]
    h = x_ref[...].astype(f32) + (dot_nn(o_ref[...], wo_ref[...]) + vec(2))
    centred = h - row_mean(h)
    inv1 = lax.rsqrt(row_mean(centred * centred) + norm_eps)
    norm1 = centred * inv1
    y1 = norm1 * vec(3) + vec(4)
    y1b = y1.astype(bf16)
    y1b_ref[...] = y1b
    z = y1 + vec(5)
    for c in range(FF // D):
        cols = slice(c * D, (c + 1) * D)
        act, slope = gelu_pair(dot_nn(y1b, w1_ref[:, cols]) + vec(8 + c))
        act = act.astype(bf16)
        g_ref[:, cols] = act
        slope_ref[:, cols] = slope
        z = z + dot_nn(act, w2_ref[cols, :])
    centred2 = z - row_mean(z)
    inv2 = lax.rsqrt(row_mean(centred2 * centred2) + norm_eps)
    norm2 = centred2 * inv2
    out_ref[...] = (norm2 * vec(6) + vec(7)).astype(bf16)

    j = lax.broadcasted_iota(jnp.int32, (rows, 1), 0)
    long_end = lens_ref[0] - r * 128
    short_end = [lens_ref[i] - r * 64 + first for i, first in ((1, 128), (2, 192))]
    live = j < jnp.where(j < 128, long_end, jnp.where(j < 192, short_end[0], short_end[1]))
    dr = jnp.where(live, cot_ref[...].astype(f32), 0.0)
    e2 = dr * vec(6)
    dz = inv2 * (e2 - row_mean(e2) - norm2 * row_mean(e2 * norm2))
    dfb = dz.astype(bf16)
    dfb_ref[...] = dfb
    add(6, dr * norm2)
    add(7, dr)
    add(5, dfb.astype(f32))
    dy1 = dz
    for c in range(FF // D):
        cols = slice(c * D, (c + 1) * D)
        dub = (dot_nt(dfb, w2_ref[cols, :]) * slope_ref[:, cols]).astype(bf16)
        dub_ref[:, cols] = dub
        add(8 + c, dub.astype(f32))
        dy1 = dy1 + dot_nt(dub, w1_ref[:, cols])
    add(3, dy1 * norm1)
    add(4, dy1)
    e1 = dy1 * vec(3)
    dh = inv1 * (e1 - row_mean(e1) - norm1 * row_mean(e1 * norm1))
    dab = dh.astype(bf16)
    dh_ref[...] = dh
    dab_ref[...] = dab
    add(2, dab.astype(f32))
    dob_ref[...] = dot_nt(dab, wo_ref[...]).astype(bf16)


def middle(lens, attended, tokens, cotangent, w_o, w_1, w_2, vec):
    n = tokens.shape[0]
    rows = 256
    row = lambda width: pl.BlockSpec((rows, width), lambda i: (i, 0))
    whole = lambda a: pl.BlockSpec(a.shape, lambda i: (0, 0), pipeline_mode=pl.Buffered(1))
    shape = jax.ShapeDtypeStruct
    return pl.pallas_call(
        middle_kernel,
        grid=(n // rows,),
        in_specs=[
            pl.BlockSpec(memory_space=pltpu.SMEM),
            row(D),
            row(D),
            row(D),
            whole(w_o),
            whole(w_1),
            whole(w_2),
            whole(vec),
        ],
        out_specs=[
            row(D),
            row(D),
            row(FF),
            row(D),
            row(FF),
            row(D),
            row(D),
            row(D),
            pl.BlockSpec((16, D), lambda i: (0, 0)),
        ],
        out_shape=[
            shape((n, D), bf16),
            shape((n, D), bf16),
            shape((n, FF), bf16),
            shape((n, D), bf16),
            shape((n, FF), bf16),
            shape((n, D), bf16),
            shape((n, D), bf16),
            shape((n, D), f32),
            shape((16, D), f32),
        ],
        scratch_shapes=[pltpu.VMEM((rows, FF), f32)],
        compiler_params=params(),
        name="middle",
    )(lens, attended, tokens, cotangent, w_o, w_1, w_2, vec)


MESH = pl.DeviceIdType.MESH
Z_CHIPS = 4


def place():
    dp = lax.axis_index("dp")
    s = lax.axis_index("seq")
    return dp, s, dp // 2, dp % 2, s // 2, s % 2


def remote(src, dst, send, recv, device):
    return pltpu.make_async_remote_copy(
        src_ref=src, dst_ref=dst, send_sem=send, recv_sem=recv, device_id=device, device_id_type=MESH
    )


def greet():
    dp, s = lax.axis_index("dp"), lax.axis_index("seq")
    barrier = pltpu.get_barrier_semaphore()
    for k in range(1, 8):
        pl.semaphore_signal(barrier, inc=1, device_id=((dp + k) % 8, s), device_id_type=MESH)
    for k in range(1, 4):
        pl.semaphore_signal(barrier, inc=1, device_id=(dp, (s + k) % 4), device_id_type=MESH)
    pl.semaphore_wait(barrier, 10)


def head_operands(q, k, limit, h):
    lane = lax.broadcasted_iota(jnp.int32, q.shape, 1)
    live = lax.broadcasted_iota(jnp.int32, q.shape, 0) < limit
    keep = lane // HEAD_DIM == h
    spare = (1 - h) * HEAD_DIM
    zero = jnp.zeros_like(q)
    fill = jnp.where(lane == spare, jnp.full_like(q, FILL_PARTS[0]), zero)
    fill = jnp.where(lane == spare + 1, jnp.full_like(q, FILL_PARTS[1]), fill)
    k_h = jnp.where(live, jnp.where(keep, k, zero), fill)
    ones = jnp.where((lane == spare) | (lane == spare + 1), jnp.ones_like(q), zero)
    return jnp.where(keep, q * bf16(score_scale), ones), k_h


def attend_sums(q, k, v, limit, keep_exps):
    length = q.shape[0]
    v_t = jnp.transpose(v)
    parts = []
    inverses = []
    for h in range(2):
        q_h, k_h = head_operands(q, k, limit, h)
        scores = dot_nt(k_h, q_h)
        exponent = jnp.exp(scores - jnp.max(scores, axis=0, keepdims=True))
        inverse = 1.0 / jnp.sum(exponent, axis=0, keepdims=True)
        exps = exponent.astype(bf16)
        keep_exps(h, exps)
        parts.append(dot_nn(v_t[h * HEAD_DIM : (h + 1) * HEAD_DIM], exps) * inverse)
        inverses.append(jnp.broadcast_to(inverse, (HEAD_DIM, length)))
    o = jnp.transpose(jnp.concatenate(parts, axis=0)).astype(bf16)
    return o, jnp.transpose(jnp.concatenate(inverses, axis=0))


def attend_sums_back(q, k, v, do, o, limit, kept_exps):
    length = q.shape[0]
    lane = lax.broadcasted_iota(jnp.int32, (length, PAIR), 1)
    live = lax.broadcasted_iota(jnp.int32, (length, PAIR), 0) < limit
    k_t = jnp.transpose(jnp.where(live, k, jnp.zeros_like(k)))
    inner = jnp.transpose(do.astype(f32) * o.astype(f32))
    dq_parts = []
    dk = jnp.zeros((length, PAIR), f32)
    dv = jnp.zeros((length, PAIR), f32)
    for h in range(2):
        keep = lane // HEAD_DIM == h
        v_h, do_h, q_h = [jnp.where(keep, m, jnp.zeros_like(m)) for m in (v, do, q)]
        exps = kept_exps(h)
        delta = jnp.sum(inner[h * HEAD_DIM : (h + 1) * HEAD_DIM], axis=0, keepdims=True)
        d_scores = (exps.astype(f32) * (dot_nt(v_h, do) - delta)).astype(bf16)
        dv = dv + dot_nn(exps, do_h)
        dk = dk + dot_nn(d_scores, q_h)
        dq_parts.append(dot_nn(k_t[h * HEAD_DIM : (h + 1) * HEAD_DIM], d_scores))
    dq = jnp.transpose(jnp.concatenate(dq_parts, axis=0)) * score_scale
    dk = jnp.where(live, dk * score_scale, 0.0)
    return dq.astype(bf16), dk.astype(bf16), dv.astype(bf16)


def own_lengths(short_ref, long_ref):
    s = lax.axis_index("seq")
    return long_ref[s // 2, 0, s % 2], short_ref[0, 0, s], short_ref[1, 0, s]


class Part:
    def __init__(self, own, out, sems, direct=False):
        self.own, self.out, self.direct = own, out, direct
        self.z_send, self.z_recv, self.x_send, self.x_recv, self.y_send, self.y_recv, self.c_send, self.c_recv = sems
        self.dp, self.s, self.z, self.x, self.y, self.c = place()
        self.rows, cols = own.shape
        self.half_rows, self.half_cols = self.rows // 2, cols // 2

    def cols(self, core):
        return pl.ds(pl.multiple_of(core * self.half_cols, 128), self.half_cols)

    def some(self, q):
        return pl.ds(pl.multiple_of(q * self.half_rows, 16), self.half_rows)

    def block(self, zs, x, core, q=None):
        rows = slice(None) if q is None else self.some(q)
        return self.out.at[zs * 2 + x, rows, self.cols(core)]

    def source(self, zs, own, q=None):
        if own:
            rows = slice(None) if q is None else self.some(q)
            return self.own.at[rows, self.cols(self.c)]
        return self.block(zs, self.x, self.c, q)

    def up(self, zs, own=False):
        dst = self.block(zs, self.x, self.c)
        return remote(self.source(zs, own), dst, self.z_send.at[zs, 0], self.z_recv.at[zs], (self.dp + 2, self.s))

    def down(self, zs, own=False):
        dst = self.block(zs, self.x, self.c)
        return remote(self.source(zs, own), dst, self.z_send.at[zs, 1], self.z_recv.at[zs], (self.dp - 2, self.s))

    def across(self, zs, own=False):
        q = None if self.direct else self.y
        dst = self.block(zs, self.x, self.c, q)
        device = (self.z * 2 + 1 - self.x, self.s)
        return remote(self.source(zs, own, q), dst, self.x_send.at[zs], self.x_recv.at[zs], device)

    def across_in(self, zs):
        ref = self.block(zs, 1 - self.x, self.c, None if self.direct else self.y)
        return remote(ref, ref, self.x_send.at[zs], self.x_recv.at[zs], (self.dp, self.s))

    def over(self, zs):
        ref = self.block(zs, 1 - self.x, self.c, self.y)
        return remote(ref, ref, self.y_send.at[zs], self.y_recv.at[zs], (self.dp, (1 - self.y) * 2 + self.c))

    def over_in(self, zs):
        ref = self.block(zs, 1 - self.x, self.c, 1 - self.y)
        return remote(ref, ref, self.y_send.at[zs], self.y_recv.at[zs], (self.dp, self.s))

    def share(self, kind, zs, core):
        if kind == 0:
            ref = self.block(zs, self.x, core)
        else:
            q = self.y if kind == 1 else 1 - self.y
            ref = self.block(zs, 1 - self.x, core, None if self.direct else q)
        j = kind * Z_CHIPS + zs
        return remote(ref, ref, self.c_send.at[j], self.c_recv.at[j], (self.dp, self.s + 1 - 2 * self.c))

    def each(self, k, what):
        if k == 0:
            what(self.z)
            return

        @pl.when(self.z >= k)
        def _():
            what(self.z - k)

        @pl.when(self.z + k < Z_CHIPS)
        def _():
            what(self.z + k)

    def stage(self, k):
        if k == 0:

            @pl.when(self.z < Z_CHIPS - 1)
            def _():
                self.up(self.z, True).start()

            @pl.when(self.z > 0)
            def _():
                self.down(self.z, True).start()

            self.across(self.z, True).start()
        elif k < Z_CHIPS:

            @pl.when(self.z >= k)
            def _():
                zs = self.z - k
                self.up(zs).wait_recv()

                @pl.when(self.z < Z_CHIPS - 1)
                def _():
                    self.up(zs).start()

                self.across(zs).start()
                self.share(0, zs, self.c).start()

            @pl.when(self.z + k < Z_CHIPS)
            def _():
                zs = self.z + k
                self.down(zs).wait_recv()

                @pl.when(self.z > 0)
                def _():
                    self.down(zs).start()

                self.across(zs).start()
                self.share(0, zs, self.c).start()

        if 1 <= k <= Z_CHIPS:

            def pass_x(zs):
                self.across_in(zs).wait_recv()
                if not self.direct:
                    self.over(zs).start()
                self.share(1, zs, self.c).start()

            self.each(k - 1, pass_x)
        if 2 <= k <= Z_CHIPS + 1 and not self.direct:

            def pass_y(zs):
                self.over_in(zs).wait_recv()
                self.share(2, zs, self.c).start()

            self.each(k - 2, pass_y)

    stages = Z_CHIPS + 2

    def finish(self):
        for kind in range(2 if self.direct else 3):
            for k in range(1 if kind == 0 else 0, Z_CHIPS):
                self.each(k, lambda zs, kind=kind: self.share(kind, zs, 1 - self.c).wait_recv())

    def settle(self):
        for k in range(Z_CHIPS):

            @pl.when((self.z >= k) & (self.z < Z_CHIPS - 1))
            def _():
                self.up(self.z - k, k == 0).wait_send()

            @pl.when((self.z + k < Z_CHIPS) & (self.z > 0))
            def _():
                self.down(self.z + k, k == 0).wait_send()

            self.each(k, lambda zs, k=k: self.across(zs, k == 0).wait_send())
            if not self.direct:
                self.each(k, lambda zs: self.over(zs).wait_send())
            for kind in range(2 if self.direct else 3):
                if kind > 0 or k > 0:
                    self.each(k, lambda zs, kind=kind: self.share(kind, zs, self.c).wait_send())


class Tokens:
    def __init__(self, long_ref, short_ref, out, send, recv, local):
        self.long_ref, self.short_ref, self.out, self.send, self.recv, self.local = long_ref, short_ref, out, send, recv, local
        self.dp, self.s = lax.axis_index("dp"), lax.axis_index("seq")

    def pieces(self, target, source):
        yield self.long_ref.at[target // 2, target % 2], self.out.at[source, pl.ds(0, 128)]
        yield self.short_ref.at[0, target], self.out.at[source, pl.ds(128, 64)]
        yield self.short_ref.at[1, target], self.out.at[source, pl.ds(192, 64)]

    def copies(self, k):
        target = (self.s + k) % 4
        for j, (src, dst) in enumerate(self.pieces(target, self.s)):
            yield remote(src, dst, self.send.at[k, j], self.recv.at[k, j], (self.dp, target))

    def own(self):
        for j, (src, dst) in enumerate(self.pieces(self.s, self.s)):
            yield pltpu.make_async_copy(src, dst, self.local.at[j])

    def start(self):
        for k in range(1, 4):
            for copy in self.copies(k):
                copy.start()
        for copy in self.own():
            copy.start()

    def finish(self):
        for copy in self.own():
            copy.wait()
        for k in range(1, 4):
            source = (self.s + 4 - k) % 4
            for j, (src, dst) in enumerate(self.pieces(self.s, source)):
                remote(src, dst, self.send.at[k, j], self.recv.at[k, j], (self.dp, self.s)).wait_recv()

    def settle(self):
        for k in range(1, 4):
            for copy in self.copies(k):
                copy.wait_send()


def layer_norm_back(grad, normed, inverse):
    return inverse * (grad - row_mean(grad) - normed * row_mean(grad * normed))


def live_rows(r, lens_ref):
    j = lax.broadcasted_iota(jnp.int32, (256, 1), 0)
    ends = [lens_ref[0] - r * 128] + [lens_ref[i] - r * 64 + first for i, first in ((1, 128), (2, 192))]
    return j < jnp.where(j < 128, ends[0], jnp.where(j < 192, ends[1], ends[2]))


DIRECT = (True, False, False, False)
FIRST_JOBS = ((4, 0), (0, 1), (1, 0), (0, 2), (2, 0), (0, 3), (0, 4), (1, 1),)
PROJECT_JOBS = {
    0: ((2, 1),),
    3: ((1, 2),),
    4: ((2, 2),),
    6: ((1, 3), (3, 0),),
}
ATTENTION_JOBS = {
    1: ((2, 3),),
    2: ((1, 4), (3, 1),),
    3: ((2, 4),),
    4: ((1, 5),),
    5: ((3, 2), (2, 5),),
}
INNER_FIRST_JOBS = ()
INNER_JOBS = {
    1: ((3, 3),),
    2: ((3, 4),),
    3: ((3, 5),),
}
OUTER_FIRST_JOBS = ()


def forward_kernel(*refs):
    refs = list(refs)

    def take(n):
        out = refs[:n]
        del refs[:n]
        return out

    short_len_ref, long_len_ref, wide_hbm, down_hbm, vec_ref = take(5)
    long_in, short_in, long_cot, short_cot = take(4)
    qkv_w_out, wo_out, w1_out, w2_out, tok_out, qkv_out, att_out, probs_out = take(8)
    act_out, slope_out, y1b_out, norm_out, inv_out, dz_out, dfb_out, out_out = take(8)
    (ainv_out,) = take(1)
    vec_out, sums_out = take(2)
    own_wide, own_down, w_s, wo_s, w1_s, w2_s, x_s, cot_s, qkv_s, att_s, vec_s, bias_s = take(12)
    stage_s, act_s, y1_s, y1b_s, norm_s, inv_s, dfb_s, out_s = take(8)
    z_send, z_recv, x_send, x_recv, y_send, y_recv, c_send, c_recv, v_send, v_recv, t_send, t_recv = take(12)
    local, keep_sem, stage_sem = take(3)
    wide_ref, down_ref, state_sem, ainv_s = take(4)

    dp, s, z, x, y, c = place()
    lens_ref = own_lengths(short_len_ref, long_len_ref)
    ranges = ((0, 3 * D), (3 * D, D + FF))
    load_wide = [
        pltpu.make_async_copy(
            wide_hbm.at[:, pl.ds(first, cols)], wide_ref.at[:, pl.ds(first, cols)], state_sem.at[i]
        )
        for i, (first, cols) in enumerate(ranges)
    ]
    load_down = pltpu.make_async_copy(down_hbm, down_ref, state_sem.at[2])
    for copy in load_wide + [load_down]:
        copy.start()
    greet()
    tokens = Tokens(long_in, short_in, x_s, t_send.at[0], t_recv.at[0], local.at[0])
    cots = Tokens(long_cot, short_cot, cot_s, t_send.at[1], t_recv.at[1], local.at[1])
    tokens.start()
    load_wide[0].wait()
    own_wide[:, 0 : 3 * D] = wide_ref[:, 0 : 3 * D].astype(bf16)

    def vec_copy(k, source, target):
        return remote(vec_ref, vec_s.at[source], v_send.at[k], v_recv.at[k], (target, s))

    sems = lambda i: [
        r.at[i] for r in (z_send, z_recv, x_send, x_recv, y_send, y_recv, c_send, c_recv)
    ]
    owns = [own_wide.at[:, pl.ds(first, cols)] for first, cols in ((0, 3 * D), (3 * D, D), (4 * D, FF))] + [own_down]
    parts = [
        Part(own, out, sems(i), direct=DIRECT[i]) for i, (own, out) in enumerate(zip(owns, (w_s, wo_s, w1_s, w2_s)))
    ]

    def run(jobs):
        for index, stage in jobs:
            if index == len(parts):
                cots.start()
            else:
                parts[index].stage(stage)

    first = parts[0]
    first.stage(0)
    load_wide[1].wait()
    load_down.wait()
    for k in range(1, 8):
        vec_copy(k, dp, (dp + k) % 8).start()
    own_wide[:, 3 * D :] = wide_ref[:, 3 * D :].astype(bf16)
    own_down[...] = down_ref[...].astype(bf16)
    own_copies = [
        pltpu.make_async_copy(part.own, part.out.at[dp], local.at[2, i]) for i, part in enumerate(parts)
    ]
    own_copies.append(pltpu.make_async_copy(vec_ref, vec_s.at[dp], local.at[2, 4]))
    for copy in own_copies:
        copy.start()
    run(FIRST_JOBS)
    for copy in own_copies:
        copy.wait()
    for k in range(1, 8):
        vec_copy(k, (dp + 8 - k) % 8, dp).wait_recv()
    vec = vec_s[0].astype(f32)
    for d in range(1, 8):
        vec = vec + vec_s[d].astype(f32)
    vec_out[...] = vec
    bias_s[:, 0:D] = jnp.broadcast_to(vec[0:1, :], (8, D))
    bias_s[:, D : 2 * D] = jnp.zeros((8, D), f32)
    bias_s[:, 2 * D : 3 * D] = jnp.broadcast_to(vec[1:2, :], (8, D))
    sums_out[...] = jnp.zeros_like(sums_out)
    tokens.finish()
    first.finish()
    kept = []

    def keep(src, dst):
        copy = pltpu.make_async_copy(src, dst, keep_sem.at[len(kept)])
        copy.start()
        kept.append(copy)

    keep(x_s, tok_out)
    keep(w_s, qkv_w_out)

    def during(i, plan):
        for when, jobs in plan.items():

            @pl.when(i == when)
            def _():
                run(jobs)

    def project(j, carry):
        during(j, PROJECT_JOBS)
        cols = pl.ds(pl.multiple_of(j * 256, 256), 256)
        w = w_s[:, :, cols].reshape(D, 256)
        rows = x_s[...].reshape(1024, D)
        qkv_s[:, :, cols] = (dot_nn(rows, w) + bias_s[0:1, cols]).astype(bf16).reshape(4, 256, 256)
        return carry

    lax.fori_loop(0, 3 * D // 256, project, 0)
    keep(qkv_s, qkv_out)
    pairs = D // PAIR

    def probs_copy(i, slot):
        return pltpu.make_async_copy(stage_s.at[slot], probs_out.at[i], stage_sem.at[slot])

    def attention(i, carry):
        during(i, ATTENTION_JOBS)
        slot = i % 2

        @pl.when(i >= 2)
        def _():
            probs_copy(i - 2, slot).wait()

        lanes = pl.ds(pl.multiple_of(i * PAIR, PAIR), PAIR)
        for first_row, rows, length, index in SEQS:
            q, k, v = [
                qkv_s[:, first_row : first_row + rows, pl.ds(pl.multiple_of(base + i * PAIR, PAIR), PAIR)].reshape(
                    length, PAIR
                )
                for base in (0, D, 2 * D)
            ]

            def keep_probs(h, probs, index=index):
                if index == 0:
                    stage_s[slot, h * LONG_L : (h + 1) * LONG_L, 0:LONG_L] = probs
                else:
                    row = (2 * h + index - 1) * SHORT_L
                    stage_s[slot, row : row + SHORT_L, LONG_L : LONG_L + SHORT_L] = probs

            o, inverse = attend_sums(q, k, v, lens_ref[index], keep_probs)
            att_s[:, first_row : first_row + rows, lanes] = o.reshape(4, rows, PAIR)
            ainv_s[:, first_row : first_row + rows, lanes] = inverse.reshape(4, rows, PAIR)
        probs_copy(i, slot).start()
        return carry

    lax.fori_loop(0, pairs, attention, 0)
    keep(att_s, att_out)
    keep(ainv_s, ainv_out)
    run(INNER_FIRST_JOBS)
    parts[1].finish()
    parts[2].finish()
    keep(wo_s, wo_out)
    keep(w1_s, w1_out)
    row_vec = lambda i: vec_out[i : i + 1, :]

    def slope_copy(r, slot):
        return pltpu.make_async_copy(stage_s.at[slot], slope_out.at[r], stage_sem.at[slot])

    def inner(r, carry):
        during(r, INNER_JOBS)
        slot = r % 2

        @pl.when(r < 2)
        def _():
            probs_copy(pairs - 2 + r, slot).wait()

        @pl.when(r >= 2)
        def _():
            slope_copy(r - 2, slot).wait()

        h = x_s[r].astype(f32) + (dot_nn(att_s[r], wo_s[...].reshape(D, D)) + row_vec(2))
        centred = h - row_mean(h)
        inverse = lax.rsqrt(row_mean(centred * centred) + norm_eps)
        normed = centred * inverse
        y1 = normed * row_vec(3) + row_vec(4)
        y1b = y1.astype(bf16)
        y1_s[r] = y1
        y1b_s[r] = y1b
        norm_s[r] = normed.astype(bf16)
        inv_s[r] = jnp.broadcast_to(inverse, (256, 128))
        at = pl.ds(pl.multiple_of(r * 256, 256), 256)
        for k in range(FF // D):
            w = w1_s[:, :, k * D : (k + 1) * D].reshape(D, D)
            act, slope = gelu_pair(dot_nn(y1b, w) + row_vec(8 + k))
            act_s[k, at] = act.astype(bf16)
            stage_s[slot, k * 256 : (k + 1) * 256] = slope.astype(bf16)
        slope_copy(r, slot).start()
        return carry

    lax.fori_loop(0, 4, inner, 0)
    for src, dst in ((act_s, act_out), (y1b_s, y1b_out), (norm_s, norm_out), (inv_s, inv_out)):
        keep(src, dst)
    run(OUTER_FIRST_JOBS)
    parts[3].finish()
    keep(w2_s, w2_out)
    cots.finish()

    def outer(r, carry):
        at = pl.ds(pl.multiple_of(r * 256, 256), 256)
        total = y1_s[r] + row_vec(5)
        for k in range(FF // D):
            total = total + dot_nn(act_s[k, at], w2_s[2 * k : 2 * k + 2].reshape(D, D))
        centred = total - row_mean(total)
        inverse = lax.rsqrt(row_mean(centred * centred) + norm_eps)
        normed = centred * inverse
        out_s[r] = (normed * row_vec(6) + row_vec(7)).astype(bf16)
        dr = jnp.where(live_rows(r, lens_ref), cot_s[r].astype(f32), 0.0)
        dz = layer_norm_back(dr * row_vec(6), normed, inverse)
        dfb = dz.astype(bf16)
        y1_s[r] = dz
        dfb_s[r] = dfb
        for i, v in ((5, dfb.astype(f32)), (6, dr * normed), (7, dr)):
            sums_out[i : i + 1, :] += jnp.sum(v, axis=0, keepdims=True)
        return carry

    lax.fori_loop(0, 4, outer, 0)
    for src, dst in ((y1_s, dz_out), (dfb_s, dfb_out), (out_s, out_out)):
        keep(src, dst)
    for copy in kept:
        copy.wait()
    for r in (2, 3):
        slope_copy(r, r % 2).wait()
    for k in range(1, 8):
        vec_copy(k, dp, (dp + k) % 8).wait_send()
    for part in parts:
        part.settle()
    tokens.settle()
    cots.settle()


def forward(short_len, long_len, wide_master, down_master, vec_block, long_in, short_in, long_cot, short_cot):
    any_spec = pl.BlockSpec(memory_space=pl.ANY)
    vmem = pl.BlockSpec(memory_space=pltpu.VMEM)
    smem = pl.BlockSpec(memory_space=pltpu.SMEM)
    shape = jax.ShapeDtypeStruct
    rows, down_rows = wide_master.shape[0], down_master.shape[0]
    dma = pltpu.SemaphoreType.DMA
    tok = (4, 256, D)
    outs = [
        ((8, rows, 3 * D), bf16),
        ((8, rows, D), bf16),
        ((8, rows, FF), bf16),
        ((8, down_rows, D), bf16),
        (tok, bf16),
        ((4, 256, 3 * D), bf16),
        (tok, bf16),
        ((D // PAIR, 1024, D), bf16),
        ((4, 1024, D), bf16),
        ((4, 1024, D), bf16),
        (tok, bf16),
        (tok, bf16),
        ((4, 256, 128), f32),
        (tok, f32),
        (tok, bf16),
        (tok, bf16),
        (tok, f32),
    ]
    vm = lambda dims, t=bf16: pltpu.VMEM(dims, t)
    return pl.pallas_call(
        forward_kernel,
        in_specs=[smem, smem, any_spec, any_spec, vmem] + [any_spec] * 4,
        out_specs=[any_spec] * len(outs) + [vmem] * 2,
        out_shape=[shape(dims, t) for dims, t in outs] + [shape((16, D), f32)] * 2,
        scratch_shapes=[
            vm((rows, 4 * D + FF)),
            vm((down_rows, D)),
            vm((8, rows, 3 * D)),
            vm((8, rows, D)),
            vm((8, rows, FF)),
            vm((8, down_rows, D)),
            vm(tok),
            vm(tok),
            vm((4, 256, 3 * D)),
            vm(tok),
            vm((8, 16, D)),
            vm((8, 3 * D), f32),
            vm((2, 1024, D)),
            vm((4, 1024, D)),
            vm(tok, f32),
            vm(tok),
            vm(tok),
            vm((4, 256, 128), f32),
            vm(tok),
            vm(tok),
            dma((4, 4, 2)),
            dma((4, 4)),
            dma((4, 4)),
            dma((4, 4)),
            dma((4, 4)),
            dma((4, 4)),
            dma((4, 12)),
            dma((4, 12)),
            dma((8,)),
            dma((8,)),
            dma((2, 4, 3)),
            dma((2, 4, 3)),
            dma((3, 5)),
            dma((16,)),
            dma((2,)),
            vm((rows, 4 * D + FF), f32),
            vm((down_rows, D), f32),
            dma((3,)),
            vm(tok, f32),
        ],
        compiler_params=pltpu.CompilerParams(
            vmem_limit_bytes=VMEM_BYTES, collective_id=0, has_side_effects=True
        ),
        name="forward",
    )(short_len, long_len, wide_master, down_master, vec_block, long_in, short_in, long_cot, short_cot)


class Grad:
    def __init__(self, theirs, acc, cbuf, xbuf, ybuf, zbuf, quarter, fin, sems, order):
        self.theirs, self.acc, self.cbuf, self.xbuf, self.ybuf, self.zbuf = theirs, acc, cbuf, xbuf, ybuf, zbuf
        self.quarter, self.fin, self.order = quarter, fin, order
        self.c_send, self.c_recv, self.x_send, self.x_recv, self.y_send, self.y_recv = sems[:6]
        self.z_send, self.z_recv, self.f_send, self.f_recv, self.local = sems[6:]
        self.dp, self.s, self.z, self.x, self.y, self.c = place()
        self.rows, cols = fin.shape
        self.half_rows, self.half_cols = self.rows // 2, cols // 2
        self.by_z = self.rows == 384
        self.core_pieces = 4 if self.by_z else 2
        self.mine = self.some(self.y)

    def cols(self, core):
        return pl.ds(pl.multiple_of(core * self.half_cols, 128), self.half_cols)

    def some(self, q):
        return pl.ds(pl.multiple_of(q * self.half_rows, 16), self.half_rows)

    def core_view(self, ref, j):
        if self.by_z:
            return ref.at[j]
        if self.order[0] != "y":
            return ref.at[:, (1 - self.x) if j == 0 else self.x]
        return ref.at[:, :, self.some((1 - self.y) if j == 0 else self.y)]

    def core_copy(self, j):
        return remote(
            self.core_view(self.theirs, j),
            self.core_view(self.cbuf, j),
            self.c_send.at[j],
            self.c_recv.at[j],
            (self.dp, self.s + 1 - 2 * self.c),
        )

    def x_copy(self, zd):
        device = (self.z * 2 + 1 - self.x, self.s)
        j = 0 if self.order == "zxy" else zd
        src = self.acc.at[zd, 1 - self.x, self.mine] if self.order == "yxz" else self.acc.at[zd, 1 - self.x]
        return remote(src, self.xbuf.at[j], self.x_send.at[j], self.x_recv.at[j], device)

    def y_copy(self, zd):
        device = (self.dp, (1 - self.y) * 2 + self.c)
        j = 0 if self.order[2] == "y" else zd
        rows = self.some(1 - self.y)
        src = self.acc.at[zd, :, rows] if self.order == "yxz" else self.acc.at[zd, self.x, rows]
        return remote(src, self.ybuf.at[j], self.y_send.at[j], self.y_recv.at[j], device)

    def z_copy(self, k):
        zd = (self.z + k) % Z_CHIPS
        src = self.acc.at[zd, self.x, self.mine]
        if self.order == "zxy":
            src = self.acc.at[zd]
        elif self.order == "xzy":
            src = self.acc.at[zd, self.x]
        return remote(
            src, self.zbuf.at[k - 1], self.z_send.at[k], self.z_recv.at[k], (zd * 2 + self.x, self.s)
        )

    def fin_quarter(self, y, core):
        return self.fin.at[self.some(y), self.cols(core)]

    def fin_copy(self, k):
        device = (self.dp, (1 - self.y) * 2 + self.c) if k == 2 else (self.dp, self.s + 1 - 2 * self.c)
        y = 1 - self.y if k == 3 else self.y
        dst = self.fin_quarter(y, self.c)
        return remote(dst if k == 3 else self.quarter, dst, self.f_send.at[k], self.f_recv.at[k], device)

    def fin_in(self, k):
        ref = self.fin_quarter(self.y if k == 1 else 1 - self.y, self.c if k == 2 else 1 - self.c)
        return remote(self.quarter, ref, self.f_send.at[k], self.f_recv.at[k], (self.dp, self.s))

    def fin_own(self):
        return pltpu.make_async_copy(self.quarter, self.fin_quarter(self.y, self.c), self.local)

    def core_start(self):
        for j in range(self.core_pieces):
            self.core_copy(j).start()

    def core_sent(self):
        for j in range(self.core_pieces):
            self.core_copy(j).wait_send()

    def z_block(self, k):
        zd = (self.z + k) % Z_CHIPS
        self.core_copy(zd).wait_recv()
        for xd in range(2):
            self.acc[zd, xd] = (self.acc[zd, xd].astype(f32) + self.cbuf[zd, xd].astype(f32)).astype(bf16)
        if self.order[0] == "x":
            self.x_copy(zd).start()
        elif k % Z_CHIPS:
            self.z_copy(k % Z_CHIPS).start()

    def core_add(self, j):
        self.core_copy(j).wait_recv()
        if self.order[0] != "y":
            xd = (1 - self.x) if j == 0 else self.x

            def one(zd, carry):
                self.acc[zd, xd] = (self.acc[zd, xd].astype(f32) + self.cbuf[zd, xd].astype(f32)).astype(bf16)
                return carry

        else:
            rows = self.some((1 - self.y) if j == 0 else self.y)

            def one(zd, carry):
                for xd in range(2):
                    self.acc[zd, xd, rows] = (
                        self.acc[zd, xd, rows].astype(f32) + self.cbuf[zd, xd, rows].astype(f32)
                    ).astype(bf16)
                return carry

        lax.fori_loop(0, Z_CHIPS, one, 0)

    def second(self, k):
        zd = (self.z + k + 1) % Z_CHIPS
        if self.order[0] == "x":
            self.x_copy(zd).wait_recv()
            self.acc[zd, self.x] = (self.acc[zd, self.x].astype(f32) + self.xbuf[zd].astype(f32)).astype(bf16)
            if self.order == "xyz":
                self.y_copy(zd).start()
            elif k < 3:
                self.z_copy(k + 1).start()
        else:
            self.y_copy(zd).wait_recv()
            for xd in range(2):
                self.acc[zd, xd, self.mine] = (
                    self.acc[zd, xd, self.mine].astype(f32) + self.ybuf[zd, xd].astype(f32)
                ).astype(bf16)
            self.x_copy(zd).start()

    def third(self, k):
        zd = (self.z + k) % Z_CHIPS
        if self.order == "xyz":
            self.y_copy(zd).wait_recv()
            came = self.ybuf
        else:
            self.x_copy(zd).wait_recv()
            came = self.xbuf
        self.acc[zd, self.x, self.mine] = (
            self.acc[zd, self.x, self.mine].astype(f32) + came[zd].astype(f32)
        ).astype(bf16)
        if k:
            self.z_copy(k).start()

    def publish(self, total):
        self.quarter[...] = total.astype(bf16)
        self.fin_own().start()
        self.fin_copy(1).start()
        self.fin_copy(2).start()

    def stage(self, i):
        if i >= 40:
            self.third((i - 39) % Z_CHIPS)
        elif i >= 30:
            self.second(i - 30)
        elif i == 6:
            self.fin_in(2).wait_recv()
            self.fin_copy(3).start()
        elif i == 7:
            self.fin_own().wait()
            self.fin_in(1).wait_recv()
            self.fin_in(3).wait_recv()
        elif self.order != "zxy":
            if i == 1:
                self.core_add(0)
                for k in range(Z_CHIPS):
                    zd = (self.z + k + 1) % Z_CHIPS
                    (self.x_copy(zd) if self.order[0] == "x" else self.y_copy(zd)).start()
            elif i == 2:
                self.core_add(1)
            elif i == 3:
                for k in range(Z_CHIPS):
                    self.second(k)
            elif i == 4 and self.order == "xzy":
                total = self.acc[self.z, self.x].astype(f32)
                for k in range(1, Z_CHIPS):
                    self.z_copy(k).wait_recv()
                    total = total + self.zbuf[k - 1].astype(f32)
                self.acc[self.z, self.x] = total.astype(bf16)
                self.y_copy(self.z).start()
            elif i == 4:
                for k in (1, 2, 3, 0):
                    self.third(k)
            elif i == 5 and self.order == "xzy":
                self.y_copy(self.z).wait_recv()
                self.publish(self.acc[self.z, self.x, self.mine].astype(f32) + self.ybuf[0].astype(f32))
            elif i == 5:
                total = self.acc[self.z, self.x, self.mine].astype(f32)
                for k in range(1, Z_CHIPS):
                    self.z_copy(k).wait_recv()
                    total = total + self.zbuf[k - 1].astype(f32)
                self.publish(total)
        else:
            if i == 1:
                self.core_add(0)
            elif i == 2:
                self.core_add(1)
                for k in range(1, Z_CHIPS):
                    self.z_copy(k).start()
            elif i == 3:
                for k in range(1, Z_CHIPS):
                    self.z_copy(k).wait_recv()
                for xd in range(2):
                    total = self.acc[self.z, xd].astype(f32)
                    for k in range(1, Z_CHIPS):
                        total = total + self.zbuf[k - 1, xd].astype(f32)
                    self.acc[self.z, xd] = total.astype(bf16)
                self.x_copy(self.z).start()
            elif i == 4:
                self.x_copy(self.z).wait_recv()
                total = self.acc[self.z, self.x].astype(f32) + self.xbuf[0].astype(f32)
                self.acc[self.z, self.x] = total.astype(bf16)
                self.y_copy(self.z).start()
            elif i == 5:
                self.y_copy(self.z).wait_recv()
                self.publish(self.acc[self.z, self.x, self.mine].astype(f32) + self.ybuf[0].astype(f32))

    def settle(self):
        for k in range(1, Z_CHIPS):
            self.z_copy(k).wait_send()
        for k in range(1, 4):
            self.fin_copy(k).wait_send()
        for k in range(1 if self.order == "zxy" else Z_CHIPS):
            self.x_copy((self.z + k) % Z_CHIPS).wait_send()
        for k in range(1 if self.order[2] == "y" else Z_CHIPS):
            self.y_copy((self.z + k) % Z_CHIPS).wait_send()


class Returns:
    def __init__(self, rows_ref, long_out, short_out, send, recv, local, own_rows=None):
        self.rows_ref, self.long_out, self.short_out = rows_ref, long_out, short_out
        self.send, self.recv, self.local = send, recv, local
        self.dp, self.s = lax.axis_index("dp"), lax.axis_index("seq")
        self.own_rows = rows_ref.at[self.s] if own_rows is None else own_rows

    def own(self):
        for j, (first, rows, (_, dst)) in enumerate(zip((0, 128, 192), (128, 64, 64), self.pieces(self.s, self.s))):
            yield pltpu.make_async_copy(self.own_rows.at[pl.ds(first, rows)], dst, self.local.at[j])

    def pieces(self, target, source):
        yield self.rows_ref.at[target, pl.ds(0, 128)], self.long_out.at[source // 2, source % 2]
        yield self.rows_ref.at[target, pl.ds(128, 64)], self.short_out.at[0, source]
        yield self.rows_ref.at[target, pl.ds(192, 64)], self.short_out.at[1, source]

    copies, start, finish, settle = Tokens.copies, Tokens.start, Tokens.finish, Tokens.settle


def sums_window(d):
    return jnp.minimum(d * 96 // 128, 4) * 128


class Sums:
    def __init__(self, src, sbuf, part, dbuf, out, sems):
        self.src, self.sbuf, self.part, self.dbuf, self.out = src, sbuf, part, dbuf, out
        self.s_send, self.s_recv, self.d_send, self.d_recv = sems
        self.dp, self.s = lax.axis_index("dp"), lax.axis_index("seq")

    def s_copy(self, k, source):
        return remote(self.src, self.sbuf.at[source], self.s_send.at[k], self.s_recv.at[k], (self.dp, (self.s + k) % 4))

    def window(self, d):
        return self.part.at[:, pl.ds(pl.multiple_of(sums_window(d), 128), 256)]

    def d_copy(self, k, source):
        target = (self.dp + k) % 8
        return remote(self.window(target), self.dbuf.at[source], self.d_send.at[k], self.d_recv.at[k], (target, self.s))

    def stage(self, i):
        if i == 0:
            for k in range(1, 4):
                self.s_copy(k, self.s).start()
            self.sbuf[self.s] = self.src[...]
        elif i == 1:
            for k in range(1, 4):
                self.s_copy(k, (self.s + 4 - k) % 4).wait_recv()
            self.part[...] = (self.sbuf[0] + self.sbuf[1]) + (self.sbuf[2] + self.sbuf[3])
            for k in range(1, 8):
                self.d_copy(k, self.dp).start()
            self.dbuf[self.dp] = self.window(self.dp)[...]
        elif i == 2:
            for k in range(1, 8):
                self.d_copy(k, (self.dp + 8 - k) % 8).wait_recv()
            total = self.dbuf[0]
            for d in range(1, 8):
                total = total + self.dbuf[d]
            self.out[...] = total

    def settle(self):
        for k in range(1, 4):
            self.s_copy(k, self.s).wait_send()
        for k in range(1, 8):
            self.d_copy(k, self.dp).wait_send()


PIECES = (
    (384, D, "xzy"),
    (192, D, "yxz"),
    (192, D, "xyz"),
    (96, D, "zxy"),
    (96, D, "xzy"),
    (96, D, "xzy"),
    (96, D, "xzy"),
)


MIDDLE_JOBS = {
    0: ((0, 30),),
    1: (),
    2: ((0, 31), (1, 1), (1, 2),),
    3: ((0, 32),),
}
ONE_JOBS = ((1, 30), (2, 1), (2, 2), (1, 31),)
O_JOBS = ((0, 33), (2, 30), (3, 1), (1, 32), (3, 2),)
BEFORE_PAIR = {
    0: (),
    1: (),
    2: ((2, 32), (1, 33),),
    3: ((4, 1),),
    4: ((1, 41), (5, 1),),
    5: ((4, 30), (4, 31), (0, 5), (5, 2),),
}
AFTER_GROUP = (
    ((0, 4), (2, 31),),
    ((1, 40), (4, 2),),
    ((5, 30), (5, 31), (2, 33),),
)
LAST_JOBS = ((6, 1), (6, 2), (4, 32), (5, 32), (6, 30), (2, 40), (3, 3), (2, 41), (4, 33), (3, 4), (2, 42), (5, 33), (2, 43), (4, 4), (1, 42), (6, 31), (1, 43), (5, 4), (0, 6), (6, 32), (1, 5), (5, 5), (6, 33), (3, 5), (4, 5), (6, 4), (5, 6), (2, 5), (6, 5), (4, 6), (3, 6), (1, 6), (2, 6), (6, 6),)


def backward_kernel(*refs):
    refs = list(refs)

    def take(n):
        out = refs[:n]
        del refs[:n]
        return out

    short_len_ref, long_len_ref, vec_ref, sums_in = take(4)
    act_hbm, slope_hbm, y1b_hbm, norm_hbm, inv_hbm, ainv_hbm, dz_hbm, dfb_hbm, att_hbm, qkv_hbm, probs_hbm = take(11)
    tok_hbm, w_hbm, wo_hbm, w1_hbm, w2_hbm, out_rows = take(6)
    fins = take(len(PIECES))
    (sums_out,) = take(1)
    short_out, long_out, short_back, long_back = take(4)
    (theirs_a,) = take(1)
    bufs = [take(6) for _ in PIECES]
    big, dfb_s, y1b_s, att_s, at_s, first_s, second_s, wo_s, dub_s, dh_s, dob_s, inv_s, dqkv_s = take(13)
    sums_s, sbuf, part, dbuf = take(4)
    sems = take(11)
    s_sems = take(4)
    t_send, t_recv, local, load_sem, big_sem, ainv_s, ainv_sem, out_s = take(8)

    dp, s, z, x, y, c = place()
    lens_ref = own_lengths(short_len_ref, long_len_ref)
    greet()
    outs = Returns(out_rows, long_out, short_out, t_send.at[0], t_recv.at[0], local.at[0], out_s)
    backs = Returns(y1b_s, long_back, short_back, t_send.at[1], t_recv.at[1], local.at[1])

    def plan(i, *pairs):
        return [pltpu.make_async_copy(src, dst, load_sem.at[i + j]) for j, (src, dst) in enumerate(pairs)]

    def begin(copies):
        for copy in copies:
            copy.start()
        return copies

    def load(i, *pairs):
        return begin(plan(i, *pairs))

    def done(copies):
        for copy in copies:
            copy.wait()

    def big_copy(src, slot):
        return pltpu.make_async_copy(src, big.at[slot], big_sem.at[slot])

    def act_chunk(k):
        return act_hbm.at[(z + k) % Z_CHIPS]

    def up_chunk(k):
        return jnp.where(k % 2 == 0, 1 - c, c) * 2 + k // 2

    def slope_copy(k, slot):
        rows = pl.ds(pl.multiple_of(up_chunk(k) * 256, 256), 256)
        return pltpu.make_async_copy(slope_hbm.at[:, rows], big.at[slot].reshape(4, 256, D), big_sem.at[slot])

    chunk = lambda i: pl.ds(i * D, D)
    big_copy(act_chunk(1), 1).start()
    load_dfb = load(0, (dfb_hbm, dfb_s))
    load_out = load(12, (out_rows.at[s], out_s))
    load_w2 = plan(1, (w2_hbm, second_s))
    load_w1 = plan(2, *[(w1_hbm.at[:, chunk(k)], first_s.at[chunk(k)]) for k in range(4)])
    load_mid = plan(6, (dz_hbm, dh_s), (norm_hbm, dob_s), (inv_hbm, inv_s), (wo_hbm, wo_s))
    load_y1b = plan(10, (y1b_hbm, y1b_s))
    load_att = plan(11, (att_hbm, att_s))

    pieces = []
    for i, (rows, cols, order) in enumerate(PIECES):
        first = (0, 0, 192, 0, 96, 192, 288)[i]
        theirs = theirs_a.at[:, :, pl.ds(first, rows), :]
        pieces.append(Grad(theirs, *bufs[i], fins[i], [r.at[i] for r in sems], order))
    down, one_a, one_b, o_piece = pieces[:4]
    sums = Sums(sums_s, sbuf, part, dbuf, sums_out, s_sems)
    done(load_out)
    outs.start()

    def run(jobs):
        for index, stage in jobs:
            pieces[index].stage(stage)

    def during(i, plan):
        for when, jobs in plan.items():

            @pl.when(i == when)
            def _():
                run(jobs)

    def columns(core):
        return pl.ds(pl.multiple_of(core * (D // 2), 128), D // 2)

    sums_s[...] = sums_in[...]
    done(load_dfb)

    def down_block(k, carry):
        zd = (z + k) % Z_CHIPS
        slot = k % 2
        big_copy(act_chunk(k), slot).wait()

        @pl.when(k < Z_CHIPS)
        def _():
            big_copy(act_chunk(k + 1), 1 - slot).start()

        @pl.when(k == Z_CHIPS)
        def _():
            slope_copy(0, 1 - slot).start()

        for j, later in ((1, load_w2), (2, load_w1), (3, load_mid), (4, load_y1b + load_att)):

            @pl.when(k == j)
            def _():
                begin(later)

        at_s[...] = jnp.transpose(big[slot])
        theirs_a[zd] = dot_nn(at_s[...], dfb_s[:, :, columns(1 - c)].reshape(1024, D // 2)).astype(bf16).reshape(2, 384, D // 2)
        down.core_copy(zd).start()
        down.acc[zd] = dot_nn(at_s[...], dfb_s[:, :, columns(c)].reshape(1024, D // 2)).astype(bf16).reshape(2, 384, D // 2)
        for j in range(2, Z_CHIPS + 1):

            @pl.when(k == j)
            def _():
                down.z_block(j - 1)

        return carry

    def ainv_copy(r, slot):
        return pltpu.make_async_copy(ainv_hbm.at[r], ainv_s.at[slot], ainv_sem.at[slot])

    lax.fori_loop(1, Z_CHIPS + 1, down_block, 0)
    ainv_copy(0, 0).start()
    done(load_w2)
    done(load_w1)
    done(load_mid)
    row_vec = lambda i: vec_ref[i : i + 1, :]

    def add(index, v):
        sums_s[index : index + 1, :] += jnp.sum(v, axis=0, keepdims=True)

    done(load_y1b)
    at_s[...] = jnp.transpose(y1b_s[...].reshape(1024, D))
    load_tok = load(10, (tok_hbm, y1b_s))

    def up_block(k, carry):
        slot = (k + 1) % 2
        slope_copy(k, slot).wait()

        @pl.when(k < 3)
        def _():
            slope_copy(k + 1, 1 - slot).start()

        @pl.when(k == 0)
        def _():
            down.z_block(Z_CHIPS)
            down.core_sent()

        during(k, MIDDLE_JOBS)
        chunk_rows = pl.ds(pl.multiple_of(up_chunk(k) * D, D), D)

        def up_rows(r, carry):
            slope = big[slot, pl.ds(pl.multiple_of(r * 256, 256), 256)].astype(f32)
            dub = (dot_nt(dfb_s[r], second_s[chunk_rows]) * slope).astype(bf16)
            dub_s[r] = dub
            dh_s[r] += dot_nt(dub, first_s[chunk_rows])
            return carry + jnp.sum(dub.astype(f32), axis=0, keepdims=True)

        hidden_sum = lax.fori_loop(0, 4, up_rows, jnp.zeros((1, D), f32))
        for j in range(4):

            @pl.when(up_chunk(k) == j)
            def _():
                sums_s[8 + j : 9 + j, :] = hidden_sum

        grad = dot_nn(at_s[...], dub_s[...].reshape(1024, D)).astype(bf16)
        for e in range(2):
            half = grad[:, e * (D // 2) : (e + 1) * (D // 2)].reshape(4, 2, 96, D // 2)
            for j, ref in enumerate((one_a.theirs, one_a.acc, one_b.theirs, one_b.acc)):

                @pl.when(k == j)
                def _():
                    ref[:, :, e * 96 : (e + 1) * 96, :] = half

        for j, piece in ((0, one_a), (2, one_b)):

            @pl.when(k == j)
            def _():
                piece.core_start()

        return carry

    lax.fori_loop(0, 4, up_block, 0)
    run(ONE_JOBS)

    def middle_back(r, carry):
        ainv_copy(r, r % 2).wait()

        @pl.when(r < 3)
        def _():
            ainv_copy(r + 1, (r + 1) % 2).start()

        dy1 = dh_s[r]
        normed = dob_s[r].astype(f32)
        add(3, dy1 * normed)
        add(4, dy1)
        dh = layer_norm_back(dy1 * row_vec(3), normed, inv_s[r][:, 0:1])
        dab = dh.astype(bf16)
        dh_s[r] = dh
        dfb_s[r] = dab
        add(2, dab.astype(f32))
        dob_s[r] = (dot_nt(dab, wo_s[...]) * ainv_s[r % 2]).astype(bf16)
        return carry

    lax.fori_loop(0, 4, middle_back, 0)
    one_a.core_sent()
    one_b.core_sent()
    qkv_loads = load(1, *[(qkv_hbm.at[:, :, chunk(j)], first_s.at[pl.ds(j * 1024, 1024)].reshape(4, 256, D)) for j in range(3)])
    w_loads = load(4, *[(w_hbm.at[:, chunk(j)], second_s.at[chunk(j)]) for j in range(3)])

    def probs_copy(i, slot):
        return big_copy(probs_hbm.at[i], slot)

    probs_copy(0, 0).start()

    def small_grad(piece, right):
        piece.theirs[...] = dot_nn(at_s[...], right(1 - c)).astype(bf16).reshape(4, 2, 96, D // 2)
        piece.core_start()
        piece.acc[...] = dot_nn(at_s[...], right(c)).astype(bf16).reshape(4, 2, 96, D // 2)

    done(load_att)
    at_s[...] = jnp.transpose(att_s[...].reshape(1024, D))
    small_grad(o_piece, lambda core: dfb_s[:, :, columns(core)].reshape(1024, D // 2))
    run(O_JOBS)

    done(load_tok)
    at_s[...] = jnp.transpose(y1b_s[...].reshape(1024, D))
    done(qkv_loads)
    done(w_loads)
    pairs = D // PAIR

    for g in range(3):

        def pair(i, carry, g=g):
            during(i, {j: BEFORE_PAIR[j] for j in (2 * g, 2 * g + 1)})
            slot = i % 2
            probs_copy(i, slot).wait()

            @pl.when(i + 1 < pairs)
            def _():
                probs_copy(i + 1, 1 - slot).start()

            lanes = pl.ds(pl.multiple_of(i * PAIR, PAIR), PAIR)
            sum_q = jnp.zeros((1, PAIR), f32)
            sum_v = jnp.zeros((1, PAIR), f32)
            for first, rows, length, index in SEQS:
                q, k, v = [
                    first_s[j * 1024 : (j + 1) * 1024, lanes].reshape(4, 256, PAIR)[:, first : first + rows].reshape(length, PAIR)
                    for j in range(3)
                ]
                do, o = [r[:, first : first + rows, lanes].reshape(length, PAIR) for r in (dob_s, att_s)]

                def kept(h, index=index):
                    if index == 0:
                        return big[slot, h * LONG_L : (h + 1) * LONG_L, 0:LONG_L]
                    row = (2 * h + index - 1) * SHORT_L
                    return big[slot, row : row + SHORT_L, LONG_L : LONG_L + SHORT_L]

                grads = attend_sums_back(q, k, v, do, o, lens_ref[index], kept)
                sum_q = sum_q + jnp.sum(grads[0].astype(f32), axis=0, keepdims=True)
                sum_v = sum_v + jnp.sum(grads[2].astype(f32), axis=0, keepdims=True)
                for j in range(3):
                    dst = pl.ds(pl.multiple_of(j * 256 + (i % 2) * PAIR, PAIR), PAIR)
                    dqkv_s[g, :, first : first + rows, dst] = grads[j].reshape(4, rows, PAIR)
            sums_s[0:1, lanes] = sum_q
            sums_s[1:2, lanes] = sum_v
            return carry

        lax.fori_loop(2 * g, 2 * g + 2, pair, 0)
        small_grad(pieces[4 + g], lambda core, g=g: dqkv_s[g, :, :, columns(core)].reshape(1024, D // 2))
        if g == 2:
            sums.stage(0)
        run(AFTER_GROUP[g])

    def rows_back(r, carry):
        total = dh_s[r]
        for g in range(3):
            for j in range(3):
                total = total + dot_nt(
                    dqkv_s[g, r, :, j * 256 : (j + 1) * 256], second_s[j * D : (j + 1) * D, g * 256 : (g + 1) * 256]
                )
        y1b_s[r] = total.astype(bf16)
        return carry

    lax.fori_loop(0, 4, rows_back, 0)
    backs.start()
    sums.stage(1)
    run(LAST_JOBS)
    sums.stage(2)
    run([(i, 7) for i in range(len(PIECES))])
    outs.finish()
    backs.finish()
    for i, piece in enumerate(pieces):
        if i > 2:
            piece.core_sent()
        piece.settle()
    sums.settle()
    outs.settle()
    backs.settle()


def backward(short_len, long_len, vec, sums, arrays, out_rows):
    any_spec = pl.BlockSpec(memory_space=pl.ANY)
    vmem = pl.BlockSpec(memory_space=pltpu.VMEM)
    smem = pl.BlockSpec(memory_space=pltpu.SMEM)
    shape = jax.ShapeDtypeStruct
    dma = pltpu.SemaphoreType.DMA
    count = len(PIECES)
    vm = lambda dims, t=bf16: pltpu.VMEM(dims, t)
    bufs = []
    for rows, cols, order in PIECES:
        half, cut = cols // 2, rows // 2
        bufs += [vm((4, 2, rows, half)), vm((4, 2, rows, half))]
        bufs += {
            "xyz": [vm((4, rows, half)), vm((4, cut, half)), vm((3, cut, half))],
            "yxz": [vm((4, cut, half)), vm((4, 2, cut, half)), vm((3, cut, half))],
            "xzy": [vm((4, rows, half)), vm((1, cut, half)), vm((3, rows, half))],
            "zxy": [vm((1, rows, half)), vm((1, cut, half)), vm((3, 2, rows, half))],
        }[order]
        bufs.append(vm((cut, half)))
    tok = (4, 256, D)
    return pl.pallas_call(
        backward_kernel,
        in_specs=[smem, smem, vmem, vmem] + [any_spec] * (len(arrays) + 1),
        out_specs=[any_spec] * count + [vmem] + [any_spec] * 4,
        out_shape=[shape((rows, cols), bf16) for rows, cols, _ in PIECES]
        + [
            shape((16, 256), f32),
            shape((2, 4, 64, D), bf16),
            shape((2, 2, 128, D), bf16),
            shape((2, 4, 64, D), bf16),
            shape((2, 2, 128, D), bf16),
        ],
        scratch_shapes=[vm((4, 2, 384, D // 2))]
        + bufs
        + [
            vm((2, 1024, D)),
            vm(tok),
            vm(tok),
            vm(tok),
            vm((D, 1024)),
            vm((FF, D)),
            vm((FF, D)),
            vm((D, D)),
            vm(tok),
            vm(tok, f32),
            vm(tok),
            vm((4, 256, 128), f32),
            vm((3, 4, 256, D)),
            vm((16, D), f32),
            vm((4, 16, D), f32),
            vm((16, D), f32),
            vm((8, 16, 256), f32),
        ]
        + [dma((count, 4))] * 10
        + [dma((count,))]
        + [dma((4,)), dma((4,)), dma((8,)), dma((8,))]
        + [dma((2, 4, 3)), dma((2, 4, 3)), dma((2, 3)), dma((13,)), dma((2,)), vm((2, 256, D), f32), dma((2,)), vm((256, D))],
        compiler_params=pltpu.CompilerParams(
            vmem_limit_bytes=VMEM_BYTES, collective_id=1, has_side_effects=True
        ),
        name="backward",
    )(short_len, long_len, vec, sums, *arrays, out_rows)


def transpose_dot(left, right):
    return jnp.einsum("ra,rb->ab", left, right, preferred_element_type=f32)


def right_dot(left, right):
    return jnp.einsum("ra,ba->rb", left, right, preferred_element_type=f32)


def flip(v, axis, bit):
    n = lax.axis_size(axis)
    return lax.ppermute(v, axis, [(i, i ^ bit) for i in range(n)])


def half_of(v, dim, which):
    size = v.shape[dim] // 2
    return lax.dynamic_slice_in_dim(v, which * size, size, dim)


def halve(v, axis, bit, dim):
    mine = (lax.axis_index(axis) // bit) % 2
    other = flip(half_of(v, dim, 1 - mine), axis, bit)
    return (half_of(v, dim, mine).astype(f32) + other.astype(f32)).astype(bf16)


def double(v, axis, bit, dim):
    mine = (lax.axis_index(axis) // bit) % 2
    other = flip(v, axis, bit)
    return jnp.where(
        mine == 0, jnp.concatenate([v, other], axis=dim), jnp.concatenate([other, v], axis=dim)
    )


def reduce_rows(grad):
    rows, cols = grad.shape
    dp = lax.axis_size("dp")
    v = grad.reshape(dp, rows // dp, cols)
    v = halve(v, "seq", 1, 2)
    v = halve(v, "seq", 2, 2)
    bit = 1
    while bit < dp:
        blocks = v.shape[0]
        v = v.reshape(blocks // 2, 2, v.shape[1], v.shape[2]) if v.ndim == 3 else v
        v = halve(v, "dp", bit, 1)[:, 0]
        bit *= 2
    v = v[0]
    v = double(v, "seq", 2, 1)
    v = double(v, "seq", 1, 1)
    return v.astype(f32)


def update(master, reduced_grad, moment, average):
    step_grad = reduced_grad + decay_weight * master
    velocity = momentum_rate * moment + step_grad
    updated = master - learning_rate * (step_grad + momentum_rate * velocity)
    averaged = average_rate * average + (1.0 - average_rate) * updated
    return (velocity, averaged, updated, updated.astype(jnp.bfloat16))


UPDATE_STEPS = 4


def update_kernel(*refs):
    refs = list(refs)

    def take(n):
        out = refs[:n]
        del refs[:n]
        return out

    down_low, one_a, one_b, o_low, low_0, low_1, low_2 = take(7)
    wide_state, down_state, passed = take(3), take(3), take(4)
    wide_out, down_out, passed_out = take(5), take(5), take(4)
    (grad_s,) = take(1)
    i = pl.program_id(0)
    for src, dst in zip(passed, passed_out):
        dst[...] = src[...]
    half, width = D // 2, grad_s.shape[1] // D
    for b in range(UPDATE_STEPS * width):
        first = b % width * D

        @pl.when(i == b // width)
        def _():
            if b < 3:
                for g, low in enumerate((low_0, low_1, low_2)):
                    grad_s[:, first + g * 256 : first + (g + 1) * 256] = low[:, b * 256 : (b + 1) * 256]
            elif b == 3:
                grad_s[:, first : first + D] = o_low[...]
            else:
                rows, core = grad_s.shape[0], (b - 4) // 2
                low = (one_a, one_b)[b % 2]
                for k in range(2):
                    part = low[k * rows : (k + 1) * rows, core * half : (core + 1) * half]
                    grad_s[:, first + k * half : first + (k + 1) * half] = part

    def step(grad, state, outs):
        master, moment, average = state
        outs[0][...] = grad
        for ref, v in zip(outs[1:], update(master[...], grad, moment[...], average[...])):
            ref[...] = v

    step(grad_s[...].astype(f32), wide_state, wide_out)
    rows = down_state[0].shape[0]
    step(down_low[pl.ds(pl.multiple_of(i * rows, 16), rows)].astype(f32), down_state, down_out)


def update_all(lows, wide, down, passed):
    rows, cols = wide[0].shape
    down_rows = down[0].shape[0]
    vmem = pl.BlockSpec(memory_space=pltpu.VMEM)
    halves = UPDATE_STEPS // 2
    short_spec = pl.BlockSpec((1, 4 // halves, 64, D), lambda i: (i // halves, i % halves, 0, 0))
    long_spec = pl.BlockSpec((1, 2 // halves, 128, D), lambda i: (i // halves, i % halves, 0, 0))
    passed_specs = [short_spec, long_spec, short_spec, long_spec]
    shape = jax.ShapeDtypeStruct
    wide_spec = pl.BlockSpec((rows, cols // UPDATE_STEPS), lambda i: (0, i))
    down_spec = pl.BlockSpec((down_rows // UPDATE_STEPS, D), lambda i: (i, 0))
    types = (f32, f32, f32, f32, bf16)
    return pl.pallas_call(
        update_kernel,
        grid=(UPDATE_STEPS,),
        in_specs=[vmem] * len(lows) + [wide_spec] * 3 + [down_spec] * 3 + passed_specs,
        out_specs=[wide_spec] * 5 + [down_spec] * 5 + passed_specs,
        out_shape=[shape((rows, cols), t) for t in types]
        + [shape((down_rows, D), t) for t in types]
        + [shape(p.shape, p.dtype) for p in passed],
        scratch_shapes=[pltpu.VMEM((rows, cols // UPDATE_STEPS), bf16)],
        compiler_params=params(),
        name="update",
    )(*lows, *wide, *down, *passed)


def spread_rows(long_part, short_part):
    long_blocks = long_part.reshape(4, 128, D)
    short_blocks = jnp.transpose(short_part, (1, 0, 2, 3)).reshape(4, 128, D)
    return jnp.concatenate([long_blocks, short_blocks], axis=1)


def exchange(v):
    return lax.all_to_all(v, "seq", split_axis=0, concat_axis=0, tiled=True)


def collect_rows(v):
    long_part = v[:, :128].reshape(2, 2, 128, D)
    short_part = jnp.transpose(v[:, 128:].reshape(4, 2, 64, D), (1, 0, 2, 3))
    return short_part, long_part


def body(
    short_in,
    long_in,
    short_cot,
    long_cot,
    short_len,
    long_len,
    wide_master,
    down_master,
    vector_master,
    wide_moment,
    down_moment,
    vector_moment,
    wide_average,
    down_average,
    vector_average,
):
    s = lax.axis_index("seq")
    own_rows = vector_master.shape[0]
    if lax.axis_size("dp") == 8:
        vec_own = jnp.pad(jnp.transpose(vector_master).astype(bf16), ((0, 4), (0, 0)))
        vec_block = lax.dynamic_update_slice(
            jnp.zeros((16, D), bf16), vec_own, (0, lax.axis_index("dp") * own_rows)
        )
        (w_qkv, w_o, w_1, w_2, tokens, qkv, attended, probs, act, slope, y1b, norm, inv, dz, dfb, out, att_inv, vec, sums) = forward(
            short_len, long_len, wide_master, down_master, vec_block, long_in, short_in, long_cot, short_cot
        )
        w_qkv, w_o, w_1, w_2 = [w.reshape(-1, w.shape[2]) for w in (w_qkv, w_o, w_1, w_2)]
        arrays = (act, slope, y1b, norm, inv, att_inv, dz, dfb, attended, qkv, probs, tokens, w_qkv, w_o, w_1, w_2)
        *lows, sums_own, short_out, long_out, short_back, long_back = backward(
            short_len, long_len, vec, sums, arrays, out
        )
        index = lax.axis_index("dp")
        own_sums = lax.dynamic_slice(sums_own, (0, index * own_rows - sums_window(index)), (12, own_rows))
        vector_reduced = jnp.transpose(own_sums)
        results = update_all(
            lows,
            (wide_master, wide_moment, wide_average),
            (down_master, down_moment, down_average),
            (short_out, long_out, short_back, long_back),
        )
        wide_reduced, *wide_new = results[:5]
        down_reduced, *down_new = results[5:10]
        short_out, long_out, short_back, long_back = results[10:]
    else:
        lens = jnp.stack([long_len[s // 2, 0, s % 2], short_len[0, 0, s], short_len[1, 0, s]])
        tokens = exchange(spread_rows(long_in, short_in))
        cotangent = exchange(spread_rows(long_cot, short_cot))
        wide_w = lax.all_gather(wide_master.astype(bf16), "dp", axis=0, tiled=True)
        w_2 = lax.all_gather(down_master.astype(bf16), "dp", axis=0, tiled=True)
        vector_w = lax.all_gather(vector_master.astype(bf16), "dp", axis=0, tiled=True)
        vec = jnp.transpose(vector_w.astype(f32))
        w_qkv = wide_w[:, : 3 * D]
        w_o = wide_w[:, 3 * D : 4 * D]
        w_1 = wide_w[:, 4 * D :]
        rows = tokens.reshape(1024, D)
        proj_bias = jnp.concatenate([vec[0], jnp.zeros((D,), f32), vec[1]])
        qkv = (jnp.dot(rows, w_qkv, preferred_element_type=f32) + proj_bias).astype(bf16)
        qkv = qkv.reshape(4, 256, 3 * D)
        attended, long_probs, short_probs = attn_forward(lens, qkv)
        flat_attended = attended.reshape(1024, D)
        out, y1b, act, dfb, dub, dab, dob, dh, sums = middle(
            lens, flat_attended, rows, cotangent.reshape(1024, D), w_o, w_1, w_2, vec
        )
        d_down = transpose_dot(act, dfb).astype(bf16)
        d_one = transpose_dot(y1b, dub).astype(bf16)
        d_o = transpose_dot(flat_attended, dab).astype(bf16)
        dq, dk, dv, qv_sums = attn_backward(
            lens, qkv, dob.reshape(4, 256, D), attended, long_probs, short_probs
        )
        d_qkv = jnp.concatenate([dq, dk, dv], axis=2).reshape(1024, 3 * D)
        d_wqkv = transpose_dot(rows, d_qkv).astype(bf16)
        back = (dh + right_dot(d_qkv, w_qkv)).astype(bf16).reshape(4, 256, D)
        vector_total = jnp.concatenate([qv_sums[:2], sums[2:12]], axis=0)
        vector_sum = jnp.transpose(lax.psum(vector_total, ("dp", "seq")))
        vector_reduced = lax.dynamic_slice_in_dim(vector_sum, lax.axis_index("dp") * own_rows, own_rows, 0)
        wide_reduced = jnp.concatenate([reduce_rows(d_wqkv), reduce_rows(d_o), reduce_rows(d_one)], axis=1)
        down_reduced = reduce_rows(d_down)
        short_out, long_out = collect_rows(exchange(out.reshape(4, 256, D)))
        short_back, long_back = collect_rows(exchange(back))
        wide_new = update(wide_master, wide_reduced, wide_moment, wide_average)
        down_new = update(down_master, down_reduced, down_moment, down_average)
    vector_new = update(vector_master, vector_reduced, vector_moment, vector_average)
    return (
        short_out,
        long_out,
        short_back,
        long_back,
        wide_reduced,
        down_reduced,
        vector_reduced,
        wide_new[0],
        down_new[0],
        vector_new[0],
        wide_new[1],
        down_new[1],
        vector_new[1],
        wide_new[2],
        down_new[2],
        vector_new[2],
        wide_new[3],
        down_new[3],
        vector_new[3],
    )


def solution(mesh):
    tok = P(None, "dp", "seq", None)
    lengths = P(None, "dp", None)
    state = P("dp", None)
    return jax.shard_map(
        body,
        mesh=mesh,
        in_specs=(tok,) * 4 + (lengths,) * 2 + (state,) * 9,
        out_specs=(tok,) * 4 + (state,) * 15,
        check_vma=False,
    )
```

```python
import jax
import jax.numpy as jnp
from jax import lax
from jax.experimental import pallas as pl
from jax.experimental.pallas import tpu as pltpu
from jax.sharding import PartitionSpec as P

D = 768
HEAD_DIM = 64
FF = 3072
PAIR = 128
LONG_L = 512
SHORT_L = 256
VMEM_BYTES = 62 * 1024 * 1024

norm_eps = 1e-12
mask_fill = -10000.0
learning_rate = 0.0002
momentum_rate = 0.9
decay_weight = 0.0001
average_rate = 0.9
score_scale = HEAD_DIM ** (-0.5)
FILL_PARTS = (-9984.0, -16.0)
f32 = jnp.float32
bf16 = jnp.bfloat16


def params():
    return pltpu.CompilerParams(vmem_limit_bytes=VMEM_BYTES)


def dot_nn(a, b):
    return lax.dot_general(a, b, (((1,), (0,)), ((), ())), preferred_element_type=f32)


def dot_nt(a, b):
    return lax.dot_general(a, b, (((1,), (1,)), ((), ())), preferred_element_type=f32)


SEQS = ((0, 128, LONG_L, 0), (128, 64, SHORT_L, 1), (192, 64, SHORT_L, 2))


def attend(q, k, v, limit, keep_probs):
    length = q.shape[0]
    v_t = jnp.transpose(v)
    head_lane = lax.broadcasted_iota(jnp.int32, (length, PAIR), 1) // HEAD_DIM
    live = lax.broadcasted_iota(jnp.int32, (length, length), 0) < limit
    parts = []
    for h in range(2):
        k_h = jnp.where(head_lane == h, k, jnp.zeros_like(k))
        scores = jnp.where(live, dot_nt(k_h, q) * score_scale, mask_fill)
        top = jnp.max(scores, axis=0, keepdims=True)
        exponent = jnp.exp(scores - top)
        total = jnp.sum(exponent, axis=0, keepdims=True)
        probs = (exponent * (1.0 / total)).astype(bf16)
        keep_probs(h, probs)
        parts.append(dot_nn(v_t[h * HEAD_DIM : (h + 1) * HEAD_DIM], probs))
    return jnp.transpose(jnp.concatenate(parts, axis=0)).astype(bf16)


def attn_forward_kernel(lens_ref, q_ref, k_ref, v_ref, o_ref, long_ref, short_ref):
    for first, rows, length, index in SEQS:
        q, k, v = [r[:, first : first + rows, :].reshape(length, PAIR) for r in (q_ref, k_ref, v_ref)]

        def keep_probs(h, probs, index=index):
            if index == 0:
                long_ref[h] = probs
            else:
                short_ref[h, index - 1] = probs

        o = attend(q, k, v, lens_ref[index], keep_probs)
        o_ref[:, first : first + rows, :] = o.reshape(4, rows, PAIR)


def attn_forward(lens, qkv):
    pairs = D // PAIR
    col = lambda base: pl.BlockSpec((4, 256, PAIR), lambda i, base=base: (0, 0, base + i))
    return pl.pallas_call(
        attn_forward_kernel,
        grid=(pairs,),
        in_specs=[
            pl.BlockSpec(memory_space=pltpu.SMEM),
            col(0),
            col(pairs),
            col(2 * pairs),
        ],
        out_specs=[
            pl.BlockSpec((4, 256, PAIR), lambda i: (0, 0, i)),
            pl.BlockSpec((2, LONG_L, LONG_L), lambda i: (i, 0, 0)),
            pl.BlockSpec((2, 2, SHORT_L, SHORT_L), lambda i: (i, 0, 0, 0)),
        ],
        out_shape=[
            jax.ShapeDtypeStruct((4, 256, D), bf16),
            jax.ShapeDtypeStruct((2 * pairs, LONG_L, LONG_L), bf16),
            jax.ShapeDtypeStruct((2 * pairs, 2, SHORT_L, SHORT_L), bf16),
        ],
        compiler_params=params(),
        name="attn_forward",
    )(lens, qkv, qkv, qkv)


def attend_back(q, k, v, do, o, limit, kept_probs):
    length = q.shape[0]
    k_t = jnp.transpose(k)
    inner = jnp.transpose(do.astype(f32) * o.astype(f32))
    head_lane = lax.broadcasted_iota(jnp.int32, (length, PAIR), 1) // HEAD_DIM
    live = lax.broadcasted_iota(jnp.int32, (length, length), 0) < limit
    dq_parts = []
    dk = jnp.zeros((length, PAIR), f32)
    dv = jnp.zeros((length, PAIR), f32)
    for h in range(2):
        keep = head_lane == h
        v_h, do_h, q_h = [jnp.where(keep, m, jnp.zeros_like(m)) for m in (v, do, q)]
        probs = kept_probs(h)
        delta = jnp.sum(inner[h * HEAD_DIM : (h + 1) * HEAD_DIM], axis=0, keepdims=True)
        d_probs = dot_nt(v_h, do)
        d_scores = jnp.where(live, probs.astype(f32) * (d_probs - delta), 0.0).astype(bf16)
        dv = dv + dot_nn(probs, do_h)
        dk = dk + dot_nn(d_scores, q_h)
        dq_parts.append(dot_nn(k_t[h * HEAD_DIM : (h + 1) * HEAD_DIM], d_scores))
    dq = jnp.transpose(jnp.concatenate(dq_parts, axis=0)) * score_scale
    return dq.astype(bf16), (dk * score_scale).astype(bf16), dv.astype(bf16)


def attn_backward_kernel(
    lens_ref, q_ref, k_ref, v_ref, do_ref, o_ref, long_ref, short_ref, dq_ref, dk_ref, dv_ref, sum_ref
):
    sum_q = jnp.zeros((1, PAIR), f32)
    sum_v = jnp.zeros((1, PAIR), f32)
    for first, rows, length, index in SEQS:
        args = [r[:, first : first + rows, :].reshape(length, PAIR) for r in (q_ref, k_ref, v_ref, do_ref, o_ref)]
        kept = lambda h, index=index: long_ref[h] if index == 0 else short_ref[h, index - 1]
        dq, dk, dv = attend_back(*args, lens_ref[index], kept)
        sum_q = sum_q + jnp.sum(dq.astype(f32), axis=0, keepdims=True)
        sum_v = sum_v + jnp.sum(dv.astype(f32), axis=0, keepdims=True)
        for ref, v in ((dq_ref, dq), (dk_ref, dk), (dv_ref, dv)):
            ref[:, first : first + rows, :] = v.reshape(4, rows, PAIR)
    sum_ref[0:1, :] = sum_q
    sum_ref[1:2, :] = sum_v
    sum_ref[2:8, :] = jnp.zeros((6, PAIR), f32)


def attn_backward(lens, qkv, d_attended, attended, long_probs, short_probs):
    pairs = D // PAIR
    col = lambda base: pl.BlockSpec((4, 256, PAIR), lambda i, base=base: (0, 0, base + i))
    return pl.pallas_call(
        attn_backward_kernel,
        grid=(pairs,),
        in_specs=[
            pl.BlockSpec(memory_space=pltpu.SMEM),
            col(0),
            col(pairs),
            col(2 * pairs),
            col(0),
            col(0),
            pl.BlockSpec((2, LONG_L, LONG_L), lambda i: (i, 0, 0)),
            pl.BlockSpec((2, 2, SHORT_L, SHORT_L), lambda i: (i, 0, 0, 0)),
        ],
        out_specs=[col(0), col(0), col(0), pl.BlockSpec((8, PAIR), lambda i: (0, i))],
        out_shape=[jax.ShapeDtypeStruct((4, 256, D), bf16)] * 3 + [jax.ShapeDtypeStruct((8, D), f32)],
        compiler_params=params(),
        name="attn_backward",
    )(lens, qkv, qkv, qkv, d_attended, attended, long_probs, short_probs)


def gelu_pair(u):
    t = 1.0 / (1.0 + (0.3275911 * 0.5**0.5) * jnp.abs(u))
    e = jnp.exp2((u * u) * (-0.5 * 1.4426950408889634))
    poly = 0.5 * -0.284496736 + t * (0.5 * 1.421413741 + t * (0.5 * -1.453152027 + t * (0.5 * 1.061405429)))
    tail = (t * (0.5 * 0.254829592 + t * poly)) * e
    cdf = jnp.where(u < 0.0, tail, 1.0 - tail)
    return u * cdf, cdf + (u * (0.5 / jnp.pi) ** 0.5) * e


def row_mean(v):
    return jnp.mean(v, axis=-1, keepdims=True)


def middle_kernel(
    lens_ref,
    o_ref,
    x_ref,
    cot_ref,
    wo_ref,
    w1_ref,
    w2_ref,
    vec_ref,
    out_ref,
    y1b_ref,
    g_ref,
    dfb_ref,
    dub_ref,
    dab_ref,
    dob_ref,
    dh_ref,
    sum_ref,
    slope_ref,
):
    r = pl.program_id(0)
    rows = o_ref.shape[0]

    @pl.when(r == 0)
    def _():
        sum_ref[...] = jnp.zeros_like(sum_ref)

    def add(index, v):
        sum_ref[index : index + 1, :] += jnp.sum(v, axis=0, keepdims=True)

    vec = lambda i: vec_ref[i : i + 1, :]
    h = x_ref[...].astype(f32) + (dot_nn(o_ref[...], wo_ref[...]) + vec(2))
    centred = h - row_mean(h)
    inv1 = lax.rsqrt(row_mean(centred * centred) + norm_eps)
    norm1 = centred * inv1
    y1 = norm1 * vec(3) + vec(4)
    y1b = y1.astype(bf16)
    y1b_ref[...] = y1b
    z = y1 + vec(5)
    for c in range(FF // D):
        cols = slice(c * D, (c + 1) * D)
        act, slope = gelu_pair(dot_nn(y1b, w1_ref[:, cols]) + vec(8 + c))
        act = act.astype(bf16)
        g_ref[:, cols] = act
        slope_ref[:, cols] = slope
        z = z + dot_nn(act, w2_ref[cols, :])
    centred2 = z - row_mean(z)
    inv2 = lax.rsqrt(row_mean(centred2 * centred2) + norm_eps)
    norm2 = centred2 * inv2
    out_ref[...] = (norm2 * vec(6) + vec(7)).astype(bf16)

    j = lax.broadcasted_iota(jnp.int32, (rows, 1), 0)
    long_end = lens_ref[0] - r * 128
    short_end = [lens_ref[i] - r * 64 + first for i, first in ((1, 128), (2, 192))]
    live = j < jnp.where(j < 128, long_end, jnp.where(j < 192, short_end[0], short_end[1]))
    dr = jnp.where(live, cot_ref[...].astype(f32), 0.0)
    e2 = dr * vec(6)
    dz = inv2 * (e2 - row_mean(e2) - norm2 * row_mean(e2 * norm2))
    dfb = dz.astype(bf16)
    dfb_ref[...] = dfb
    add(6, dr * norm2)
    add(7, dr)
    add(5, dfb.astype(f32))
    dy1 = dz
    for c in range(FF // D):
        cols = slice(c * D, (c + 1) * D)
        dub = (dot_nt(dfb, w2_ref[cols, :]) * slope_ref[:, cols]).astype(bf16)
        dub_ref[:, cols] = dub
        add(8 + c, dub.astype(f32))
        dy1 = dy1 + dot_nt(dub, w1_ref[:, cols])
    add(3, dy1 * norm1)
    add(4, dy1)
    e1 = dy1 * vec(3)
    dh = inv1 * (e1 - row_mean(e1) - norm1 * row_mean(e1 * norm1))
    dab = dh.astype(bf16)
    dh_ref[...] = dh
    dab_ref[...] = dab
    add(2, dab.astype(f32))
    dob_ref[...] = dot_nt(dab, wo_ref[...]).astype(bf16)


def middle(lens, attended, tokens, cotangent, w_o, w_1, w_2, vec):
    n = tokens.shape[0]
    rows = 256
    row = lambda width: pl.BlockSpec((rows, width), lambda i: (i, 0))
    whole = lambda a: pl.BlockSpec(a.shape, lambda i: (0, 0), pipeline_mode=pl.Buffered(1))
    shape = jax.ShapeDtypeStruct
    return pl.pallas_call(
        middle_kernel,
        grid=(n // rows,),
        in_specs=[
            pl.BlockSpec(memory_space=pltpu.SMEM),
            row(D),
            row(D),
            row(D),
            whole(w_o),
            whole(w_1),
            whole(w_2),
            whole(vec),
        ],
        out_specs=[
            row(D),
            row(D),
            row(FF),
            row(D),
            row(FF),
            row(D),
            row(D),
            row(D),
            pl.BlockSpec((16, D), lambda i: (0, 0)),
        ],
        out_shape=[
            shape((n, D), bf16),
            shape((n, D), bf16),
            shape((n, FF), bf16),
            shape((n, D), bf16),
            shape((n, FF), bf16),
            shape((n, D), bf16),
            shape((n, D), bf16),
            shape((n, D), f32),
            shape((16, D), f32),
        ],
        scratch_shapes=[pltpu.VMEM((rows, FF), f32)],
        compiler_params=params(),
        name="middle",
    )(lens, attended, tokens, cotangent, w_o, w_1, w_2, vec)


MESH = pl.DeviceIdType.MESH
Z_CHIPS = 4


def place():
    dp = lax.axis_index("dp")
    s = lax.axis_index("seq")
    return dp, s, dp // 2, dp % 2, s // 2, s % 2


def remote(src, dst, send, recv, device):
    return pltpu.make_async_remote_copy(
        src_ref=src, dst_ref=dst, send_sem=send, recv_sem=recv, device_id=device, device_id_type=MESH
    )


def greet():
    dp, s = lax.axis_index("dp"), lax.axis_index("seq")
    barrier = pltpu.get_barrier_semaphore()
    for k in range(1, 8):
        pl.semaphore_signal(barrier, inc=1, device_id=((dp + k) % 8, s), device_id_type=MESH)
    for k in range(1, 4):
        pl.semaphore_signal(barrier, inc=1, device_id=(dp, (s + k) % 4), device_id_type=MESH)
    pl.semaphore_wait(barrier, 10)


def head_operands(q, k, limit, h):
    lane = lax.broadcasted_iota(jnp.int32, q.shape, 1)
    live = lax.broadcasted_iota(jnp.int32, q.shape, 0) < limit
    keep = lane // HEAD_DIM == h
    spare = (1 - h) * HEAD_DIM
    zero = jnp.zeros_like(q)
    fill = jnp.where(lane == spare, jnp.full_like(q, FILL_PARTS[0]), zero)
    fill = jnp.where(lane == spare + 1, jnp.full_like(q, FILL_PARTS[1]), fill)
    k_h = jnp.where(live, jnp.where(keep, k, zero), fill)
    ones = jnp.where((lane == spare) | (lane == spare + 1), jnp.ones_like(q), zero)
    return jnp.where(keep, q * bf16(score_scale), ones), k_h


def attend_sums(q, k, v, limit, keep_exps):
    length = q.shape[0]
    v_t = jnp.transpose(v)
    parts = []
    inverses = []
    for h in range(2):
        q_h, k_h = head_operands(q, k, limit, h)
        scores = dot_nt(k_h, q_h)
        exponent = jnp.exp(scores - jnp.max(scores, axis=0, keepdims=True))
        inverse = 1.0 / jnp.sum(exponent, axis=0, keepdims=True)
        exps = exponent.astype(bf16)
        keep_exps(h, exps)
        parts.append(dot_nn(v_t[h * HEAD_DIM : (h + 1) * HEAD_DIM], exps) * inverse)
        inverses.append(jnp.broadcast_to(inverse, (HEAD_DIM, length)))
    o = jnp.transpose(jnp.concatenate(parts, axis=0)).astype(bf16)
    return o, jnp.transpose(jnp.concatenate(inverses, axis=0))


def attend_sums_back(q, k, v, do, o, limit, kept_exps):
    length = q.shape[0]
    lane = lax.broadcasted_iota(jnp.int32, (length, PAIR), 1)
    live = lax.broadcasted_iota(jnp.int32, (length, PAIR), 0) < limit
    k_t = jnp.transpose(jnp.where(live, k, jnp.zeros_like(k)))
    inner = jnp.transpose(do.astype(f32) * o.astype(f32))
    dq_parts = []
    dk = jnp.zeros((length, PAIR), f32)
    dv = jnp.zeros((length, PAIR), f32)
    for h in range(2):
        keep = lane // HEAD_DIM == h
        v_h, do_h, q_h = [jnp.where(keep, m, jnp.zeros_like(m)) for m in (v, do, q)]
        exps = kept_exps(h)
        delta = jnp.sum(inner[h * HEAD_DIM : (h + 1) * HEAD_DIM], axis=0, keepdims=True)
        d_scores = (exps.astype(f32) * (dot_nt(v_h, do) - delta)).astype(bf16)
        dv = dv + dot_nn(exps, do_h)
        dk = dk + dot_nn(d_scores, q_h)
        dq_parts.append(dot_nn(k_t[h * HEAD_DIM : (h + 1) * HEAD_DIM], d_scores))
    dq = jnp.transpose(jnp.concatenate(dq_parts, axis=0)) * score_scale
    dk = jnp.where(live, dk * score_scale, 0.0)
    return dq.astype(bf16), dk.astype(bf16), dv.astype(bf16)


def own_lengths(short_ref, long_ref):
    s = lax.axis_index("seq")
    return long_ref[s // 2, 0, s % 2], short_ref[0, 0, s], short_ref[1, 0, s]


class Part:
    def __init__(self, own, out, sems, direct=False):
        self.own, self.out, self.direct = own, out, direct
        self.z_send, self.z_recv, self.x_send, self.x_recv, self.y_send, self.y_recv, self.c_send, self.c_recv = sems
        self.dp, self.s, self.z, self.x, self.y, self.c = place()
        self.rows, cols = own.shape
        self.half_rows, self.half_cols = self.rows // 2, cols // 2

    def cols(self, core):
        return pl.ds(pl.multiple_of(core * self.half_cols, 128), self.half_cols)

    def some(self, q):
        return pl.ds(pl.multiple_of(q * self.half_rows, 16), self.half_rows)

    def block(self, zs, x, core, q=None):
        rows = slice(None) if q is None else self.some(q)
        return self.out.at[zs * 2 + x, rows, self.cols(core)]

    def source(self, zs, own, q=None):
        if own:
            rows = slice(None) if q is None else self.some(q)
            return self.own.at[rows, self.cols(self.c)]
        return self.block(zs, self.x, self.c, q)

    def up(self, zs, own=False):
        dst = self.block(zs, self.x, self.c)
        return remote(self.source(zs, own), dst, self.z_send.at[zs, 0], self.z_recv.at[zs], (self.dp + 2, self.s))

    def down(self, zs, own=False):
        dst = self.block(zs, self.x, self.c)
        return remote(self.source(zs, own), dst, self.z_send.at[zs, 1], self.z_recv.at[zs], (self.dp - 2, self.s))

    def across(self, zs, own=False):
        q = None if self.direct else self.y
        dst = self.block(zs, self.x, self.c, q)
        device = (self.z * 2 + 1 - self.x, self.s)
        return remote(self.source(zs, own, q), dst, self.x_send.at[zs], self.x_recv.at[zs], device)

    def across_in(self, zs):
        ref = self.block(zs, 1 - self.x, self.c, None if self.direct else self.y)
        return remote(ref, ref, self.x_send.at[zs], self.x_recv.at[zs], (self.dp, self.s))

    def over(self, zs):
        ref = self.block(zs, 1 - self.x, self.c, self.y)
        return remote(ref, ref, self.y_send.at[zs], self.y_recv.at[zs], (self.dp, (1 - self.y) * 2 + self.c))

    def over_in(self, zs):
        ref = self.block(zs, 1 - self.x, self.c, 1 - self.y)
        return remote(ref, ref, self.y_send.at[zs], self.y_recv.at[zs], (self.dp, self.s))

    def share(self, kind, zs, core):
        if kind == 0:
            ref = self.block(zs, self.x, core)
        else:
            q = self.y if kind == 1 else 1 - self.y
            ref = self.block(zs, 1 - self.x, core, None if self.direct else q)
        j = kind * Z_CHIPS + zs
        return remote(ref, ref, self.c_send.at[j], self.c_recv.at[j], (self.dp, self.s + 1 - 2 * self.c))

    def each(self, k, what):
        if k == 0:
            what(self.z)
            return

        @pl.when(self.z >= k)
        def _():
            what(self.z - k)

        @pl.when(self.z + k < Z_CHIPS)
        def _():
            what(self.z + k)

    def stage(self, k):
        if k == 0:

            @pl.when(self.z < Z_CHIPS - 1)
            def _():
                self.up(self.z, True).start()

            @pl.when(self.z > 0)
            def _():
                self.down(self.z, True).start()

            self.across(self.z, True).start()
        elif k < Z_CHIPS:

            @pl.when(self.z >= k)
            def _():
                zs = self.z - k
                self.up(zs).wait_recv()

                @pl.when(self.z < Z_CHIPS - 1)
                def _():
                    self.up(zs).start()

                self.across(zs).start()
                self.share(0, zs, self.c).start()

            @pl.when(self.z + k < Z_CHIPS)
            def _():
                zs = self.z + k
                self.down(zs).wait_recv()

                @pl.when(self.z > 0)
                def _():
                    self.down(zs).start()

                self.across(zs).start()
                self.share(0, zs, self.c).start()

        if 1 <= k <= Z_CHIPS:

            def pass_x(zs):
                self.across_in(zs).wait_recv()
                if not self.direct:
                    self.over(zs).start()
                self.share(1, zs, self.c).start()

            self.each(k - 1, pass_x)
        if 2 <= k <= Z_CHIPS + 1 and not self.direct:

            def pass_y(zs):
                self.over_in(zs).wait_recv()
                self.share(2, zs, self.c).start()

            self.each(k - 2, pass_y)

    stages = Z_CHIPS + 2

    def finish(self):
        for kind in range(2 if self.direct else 3):
            for k in range(1 if kind == 0 else 0, Z_CHIPS):
                self.each(k, lambda zs, kind=kind: self.share(kind, zs, 1 - self.c).wait_recv())

    def settle(self):
        for k in range(Z_CHIPS):

            @pl.when((self.z >= k) & (self.z < Z_CHIPS - 1))
            def _():
                self.up(self.z - k, k == 0).wait_send()

            @pl.when((self.z + k < Z_CHIPS) & (self.z > 0))
            def _():
                self.down(self.z + k, k == 0).wait_send()

            self.each(k, lambda zs, k=k: self.across(zs, k == 0).wait_send())
            if not self.direct:
                self.each(k, lambda zs: self.over(zs).wait_send())
            for kind in range(2 if self.direct else 3):
                if kind > 0 or k > 0:
                    self.each(k, lambda zs, kind=kind: self.share(kind, zs, self.c).wait_send())


class Tokens:
    def __init__(self, long_ref, short_ref, out, send, recv, local):
        self.long_ref, self.short_ref, self.out, self.send, self.recv, self.local = long_ref, short_ref, out, send, recv, local
        self.dp, self.s = lax.axis_index("dp"), lax.axis_index("seq")

    def pieces(self, target, source):
        yield self.long_ref.at[target // 2, target % 2], self.out.at[source, pl.ds(0, 128)]
        yield self.short_ref.at[0, target], self.out.at[source, pl.ds(128, 64)]
        yield self.short_ref.at[1, target], self.out.at[source, pl.ds(192, 64)]

    def copies(self, k):
        target = (self.s + k) % 4
        for j, (src, dst) in enumerate(self.pieces(target, self.s)):
            yield remote(src, dst, self.send.at[k, j], self.recv.at[k, j], (self.dp, target))

    def own(self):
        for j, (src, dst) in enumerate(self.pieces(self.s, self.s)):
            yield pltpu.make_async_copy(src, dst, self.local.at[j])

    def start(self):
        for k in range(1, 4):
            for copy in self.copies(k):
                copy.start()
        for copy in self.own():
            copy.start()

    def finish(self):
        for copy in self.own():
            copy.wait()
        for k in range(1, 4):
            source = (self.s + 4 - k) % 4
            for j, (src, dst) in enumerate(self.pieces(self.s, source)):
                remote(src, dst, self.send.at[k, j], self.recv.at[k, j], (self.dp, self.s)).wait_recv()

    def settle(self):
        for k in range(1, 4):
            for copy in self.copies(k):
                copy.wait_send()


def layer_norm_back(grad, normed, inverse):
    return inverse * (grad - row_mean(grad) - normed * row_mean(grad * normed))


def live_rows(r, lens_ref):
    j = lax.broadcasted_iota(jnp.int32, (256, 1), 0)
    ends = [lens_ref[0] - r * 128] + [lens_ref[i] - r * 64 + first for i, first in ((1, 128), (2, 192))]
    return j < jnp.where(j < 128, ends[0], jnp.where(j < 192, ends[1], ends[2]))


DIRECT = (True, False, False, False)
FIRST_JOBS = ((4, 0), (0, 1), (1, 0), (0, 2), (2, 0), (0, 3), (0, 4), (1, 1),)
PROJECT_JOBS = {
    0: ((2, 1),),
    3: ((1, 2),),
    4: ((2, 2),),
    6: ((1, 3), (3, 0),),
}
ATTENTION_JOBS = {
    1: ((2, 3),),
    2: ((1, 4), (3, 1),),
    3: ((2, 4),),
    4: ((1, 5),),
    5: ((3, 2), (2, 5),),
}
INNER_FIRST_JOBS = ()
INNER_JOBS = {
    1: ((3, 3),),
    2: ((3, 4),),
    3: ((3, 5),),
}
OUTER_FIRST_JOBS = ()


def forward_kernel(*refs):
    refs = list(refs)

    def take(n):
        out = refs[:n]
        del refs[:n]
        return out

    short_len_ref, long_len_ref, wide_hbm, down_hbm, vec_ref = take(5)
    long_in, short_in, long_cot, short_cot = take(4)
    qkv_w_out, wo_out, w1_out, w2_out, tok_out, qkv_out, att_out, probs_out = take(8)
    act_out, slope_out, y1b_out, norm_out, inv_out, dz_out, dfb_out, out_out = take(8)
    (ainv_out,) = take(1)
    vec_out, sums_out = take(2)
    own_wide, own_down, w_s, wo_s, w1_s, w2_s, x_s, cot_s, qkv_s, att_s, vec_s, bias_s = take(12)
    stage_s, act_s, y1_s, y1b_s, norm_s, inv_s, dfb_s, out_s = take(8)
    z_send, z_recv, x_send, x_recv, y_send, y_recv, c_send, c_recv, v_send, v_recv, t_send, t_recv = take(12)
    local, keep_sem, stage_sem = take(3)
    wide_ref, down_ref, state_sem, ainv_s = take(4)

    dp, s, z, x, y, c = place()
    lens_ref = own_lengths(short_len_ref, long_len_ref)
    ranges = ((0, 3 * D), (3 * D, D + FF))
    load_wide = [
        pltpu.make_async_copy(
            wide_hbm.at[:, pl.ds(first, cols)], wide_ref.at[:, pl.ds(first, cols)], state_sem.at[i]
        )
        for i, (first, cols) in enumerate(ranges)
    ]
    load_down = pltpu.make_async_copy(down_hbm, down_ref, state_sem.at[2])
    for copy in load_wide + [load_down]:
        copy.start()
    greet()
    tokens = Tokens(long_in, short_in, x_s, t_send.at[0], t_recv.at[0], local.at[0])
    cots = Tokens(long_cot, short_cot, cot_s, t_send.at[1], t_recv.at[1], local.at[1])
    tokens.start()
    load_wide[0].wait()
    own_wide[:, 0 : 3 * D] = wide_ref[:, 0 : 3 * D].astype(bf16)

    def vec_copy(k, source, target):
        return remote(vec_ref, vec_s.at[source], v_send.at[k], v_recv.at[k], (target, s))

    sems = lambda i: [
        r.at[i] for r in (z_send, z_recv, x_send, x_recv, y_send, y_recv, c_send, c_recv)
    ]
    owns = [own_wide.at[:, pl.ds(first, cols)] for first, cols in ((0, 3 * D), (3 * D, D), (4 * D, FF))] + [own_down]
    parts = [
        Part(own, out, sems(i), direct=DIRECT[i]) for i, (own, out) in enumerate(zip(owns, (w_s, wo_s, w1_s, w2_s)))
    ]

    def run(jobs):
        for index, stage in jobs:
            if index == len(parts):
                cots.start()
            else:
                parts[index].stage(stage)

    first = parts[0]
    first.stage(0)
    load_wide[1].wait()
    load_down.wait()
    for k in range(1, 8):
        vec_copy(k, dp, (dp + k) % 8).start()
    own_wide[:, 3 * D :] = wide_ref[:, 3 * D :].astype(bf16)
    own_down[...] = down_ref[...].astype(bf16)
    own_copies = [
        pltpu.make_async_copy(part.own, part.out.at[dp], local.at[2, i]) for i, part in enumerate(parts)
    ]
    own_copies.append(pltpu.make_async_copy(vec_ref, vec_s.at[dp], local.at[2, 4]))
    for copy in own_copies:
        copy.start()
    run(FIRST_JOBS)
    for copy in own_copies:
        copy.wait()
    for k in range(1, 8):
        vec_copy(k, (dp + 8 - k) % 8, dp).wait_recv()
    vec = vec_s[0].astype(f32)
    for d in range(1, 8):
        vec = vec + vec_s[d].astype(f32)
    vec_out[...] = vec
    bias_s[:, 0:D] = jnp.broadcast_to(vec[0:1, :], (8, D))
    bias_s[:, D : 2 * D] = jnp.zeros((8, D), f32)
    bias_s[:, 2 * D : 3 * D] = jnp.broadcast_to(vec[1:2, :], (8, D))
    sums_out[...] = jnp.zeros_like(sums_out)
    tokens.finish()
    first.finish()
    kept = []

    def keep(src, dst):
        copy = pltpu.make_async_copy(src, dst, keep_sem.at[len(kept)])
        copy.start()
        kept.append(copy)

    keep(x_s, tok_out)
    keep(w_s, qkv_w_out)

    def during(i, plan):
        for when, jobs in plan.items():

            @pl.when(i == when)
            def _():
                run(jobs)

    def project(j, carry):
        during(j, PROJECT_JOBS)
        cols = pl.ds(pl.multiple_of(j * 256, 256), 256)
        w = w_s[:, :, cols].reshape(D, 256)
        rows = x_s[...].reshape(1024, D)
        qkv_s[:, :, cols] = (dot_nn(rows, w) + bias_s[0:1, cols]).astype(bf16).reshape(4, 256, 256)
        return carry

    lax.fori_loop(0, 3 * D // 256, project, 0)
    keep(qkv_s, qkv_out)
    pairs = D // PAIR

    def probs_copy(i, slot):
        return pltpu.make_async_copy(stage_s.at[slot], probs_out.at[i], stage_sem.at[slot])

    def attention(i, carry):
        during(i, ATTENTION_JOBS)
        slot = i % 2

        @pl.when(i >= 2)
        def _():
            probs_copy(i - 2, slot).wait()

        lanes = pl.ds(pl.multiple_of(i * PAIR, PAIR), PAIR)
        for first_row, rows, length, index in SEQS:
            q, k, v = [
                qkv_s[:, first_row : first_row + rows, pl.ds(pl.multiple_of(base + i * PAIR, PAIR), PAIR)].reshape(
                    length, PAIR
                )
                for base in (0, D, 2 * D)
            ]

            def keep_probs(h, probs, index=index):
                if index == 0:
                    stage_s[slot, h * LONG_L : (h + 1) * LONG_L, 0:LONG_L] = probs
                else:
                    row = (2 * h + index - 1) * SHORT_L
                    stage_s[slot, row : row + SHORT_L, LONG_L : LONG_L + SHORT_L] = probs

            o, inverse = attend_sums(q, k, v, lens_ref[index], keep_probs)
            att_s[:, first_row : first_row + rows, lanes] = o.reshape(4, rows, PAIR)
            ainv_s[:, first_row : first_row + rows, lanes] = inverse.reshape(4, rows, PAIR)
        probs_copy(i, slot).start()
        return carry

    lax.fori_loop(0, pairs, attention, 0)
    keep(att_s, att_out)
    keep(ainv_s, ainv_out)
    run(INNER_FIRST_JOBS)
    parts[1].finish()
    parts[2].finish()
    keep(wo_s, wo_out)
    keep(w1_s, w1_out)
    row_vec = lambda i: vec_out[i : i + 1, :]

    def slope_copy(r, slot):
        return pltpu.make_async_copy(stage_s.at[slot], slope_out.at[r], stage_sem.at[slot])

    def inner(r, carry):
        during(r, INNER_JOBS)
        slot = r % 2

        @pl.when(r < 2)
        def _():
            probs_copy(pairs - 2 + r, slot).wait()

        @pl.when(r >= 2)
        def _():
            slope_copy(r - 2, slot).wait()

        h = x_s[r].astype(f32) + (dot_nn(att_s[r], wo_s[...].reshape(D, D)) + row_vec(2))
        centred = h - row_mean(h)
        inverse = lax.rsqrt(row_mean(centred * centred) + norm_eps)
        normed = centred * inverse
        y1 = normed * row_vec(3) + row_vec(4)
        y1b = y1.astype(bf16)
        y1_s[r] = y1
        y1b_s[r] = y1b
        norm_s[r] = normed.astype(bf16)
        inv_s[r] = jnp.broadcast_to(inverse, (256, 128))
        at = pl.ds(pl.multiple_of(r * 256, 256), 256)
        for k in range(FF // D):
            w = w1_s[:, :, k * D : (k + 1) * D].reshape(D, D)
            act, slope = gelu_pair(dot_nn(y1b, w) + row_vec(8 + k))
            act_s[k, at] = act.astype(bf16)
            stage_s[slot, k * 256 : (k + 1) * 256] = slope.astype(bf16)
        slope_copy(r, slot).start()
        return carry

    lax.fori_loop(0, 4, inner, 0)
    for src, dst in ((act_s, act_out), (y1b_s, y1b_out), (norm_s, norm_out), (inv_s, inv_out)):
        keep(src, dst)
    run(OUTER_FIRST_JOBS)
    parts[3].finish()
    keep(w2_s, w2_out)
    cots.finish()

    def outer(r, carry):
        at = pl.ds(pl.multiple_of(r * 256, 256), 256)
        total = y1_s[r] + row_vec(5)
        for k in range(FF // D):
            total = total + dot_nn(act_s[k, at], w2_s[2 * k : 2 * k + 2].reshape(D, D))
        centred = total - row_mean(total)
        inverse = lax.rsqrt(row_mean(centred * centred) + norm_eps)
        normed = centred * inverse
        out_s[r] = (normed * row_vec(6) + row_vec(7)).astype(bf16)
        dr = jnp.where(live_rows(r, lens_ref), cot_s[r].astype(f32), 0.0)
        dz = layer_norm_back(dr * row_vec(6), normed, inverse)
        dfb = dz.astype(bf16)
        y1_s[r] = dz
        dfb_s[r] = dfb
        for i, v in ((5, dfb.astype(f32)), (6, dr * normed), (7, dr)):
            sums_out[i : i + 1, :] += jnp.sum(v, axis=0, keepdims=True)
        return carry

    lax.fori_loop(0, 4, outer, 0)
    for src, dst in ((y1_s, dz_out), (dfb_s, dfb_out), (out_s, out_out)):
        keep(src, dst)
    for copy in kept:
        copy.wait()
    for r in (2, 3):
        slope_copy(r, r % 2).wait()
    for k in range(1, 8):
        vec_copy(k, dp, (dp + k) % 8).wait_send()
    for part in parts:
        part.settle()
    tokens.settle()
    cots.settle()


def forward(short_len, long_len, wide_master, down_master, vec_block, long_in, short_in, long_cot, short_cot):
    any_spec = pl.BlockSpec(memory_space=pl.ANY)
    vmem = pl.BlockSpec(memory_space=pltpu.VMEM)
    smem = pl.BlockSpec(memory_space=pltpu.SMEM)
    shape = jax.ShapeDtypeStruct
    rows, down_rows = wide_master.shape[0], down_master.shape[0]
    dma = pltpu.SemaphoreType.DMA
    tok = (4, 256, D)
    outs = [
        ((8, rows, 3 * D), bf16),
        ((8, rows, D), bf16),
        ((8, rows, FF), bf16),
        ((8, down_rows, D), bf16),
        (tok, bf16),
        ((4, 256, 3 * D), bf16),
        (tok, bf16),
        ((D // PAIR, 1024, D), bf16),
        ((4, 1024, D), bf16),
        ((4, 1024, D), bf16),
        (tok, bf16),
        (tok, bf16),
        ((4, 256, 128), f32),
        (tok, f32),
        (tok, bf16),
        (tok, bf16),
        (tok, f32),
    ]
    vm = lambda dims, t=bf16: pltpu.VMEM(dims, t)
    return pl.pallas_call(
        forward_kernel,
        in_specs=[smem, smem, any_spec, any_spec, vmem] + [any_spec] * 4,
        out_specs=[any_spec] * len(outs) + [vmem] * 2,
        out_shape=[shape(dims, t) for dims, t in outs] + [shape((16, D), f32)] * 2,
        scratch_shapes=[
            vm((rows, 4 * D + FF)),
            vm((down_rows, D)),
            vm((8, rows, 3 * D)),
            vm((8, rows, D)),
            vm((8, rows, FF)),
            vm((8, down_rows, D)),
            vm(tok),
            vm(tok),
            vm((4, 256, 3 * D)),
            vm(tok),
            vm((8, 16, D)),
            vm((8, 3 * D), f32),
            vm((2, 1024, D)),
            vm((4, 1024, D)),
            vm(tok, f32),
            vm(tok),
            vm(tok),
            vm((4, 256, 128), f32),
            vm(tok),
            vm(tok),
            dma((4, 4, 2)),
            dma((4, 4)),
            dma((4, 4)),
            dma((4, 4)),
            dma((4, 4)),
            dma((4, 4)),
            dma((4, 12)),
            dma((4, 12)),
            dma((8,)),
            dma((8,)),
            dma((2, 4, 3)),
            dma((2, 4, 3)),
            dma((3, 5)),
            dma((16,)),
            dma((2,)),
            vm((rows, 4 * D + FF), f32),
            vm((down_rows, D), f32),
            dma((3,)),
            vm(tok, f32),
        ],
        compiler_params=pltpu.CompilerParams(
            vmem_limit_bytes=VMEM_BYTES, collective_id=0, has_side_effects=True
        ),
        name="forward",
    )(short_len, long_len, wide_master, down_master, vec_block, long_in, short_in, long_cot, short_cot)


class Grad:
    def __init__(self, theirs, acc, cbuf, xbuf, ybuf, zbuf, quarter, fin, sems, order):
        self.theirs, self.acc, self.cbuf, self.xbuf, self.ybuf, self.zbuf = theirs, acc, cbuf, xbuf, ybuf, zbuf
        self.quarter, self.fin, self.order = quarter, fin, order
        self.c_send, self.c_recv, self.x_send, self.x_recv, self.y_send, self.y_recv = sems[:6]
        self.z_send, self.z_recv, self.f_send, self.f_recv, self.local = sems[6:]
        self.dp, self.s, self.z, self.x, self.y, self.c = place()
        self.rows, cols = fin.shape
        self.half_rows, self.half_cols = self.rows // 2, cols // 2
        self.by_z = self.rows == 384
        self.core_pieces = 4 if self.by_z else 2
        self.mine = self.some(self.y)

    def cols(self, core):
        return pl.ds(pl.multiple_of(core * self.half_cols, 128), self.half_cols)

    def some(self, q):
        return pl.ds(pl.multiple_of(q * self.half_rows, 16), self.half_rows)

    def core_view(self, ref, j):
        if self.by_z:
            return ref.at[j]
        if self.order[0] != "y":
            return ref.at[:, (1 - self.x) if j == 0 else self.x]
        return ref.at[:, :, self.some((1 - self.y) if j == 0 else self.y)]

    def core_copy(self, j):
        return remote(
            self.core_view(self.theirs, j),
            self.core_view(self.cbuf, j),
            self.c_send.at[j],
            self.c_recv.at[j],
            (self.dp, self.s + 1 - 2 * self.c),
        )

    def x_copy(self, zd):
        device = (self.z * 2 + 1 - self.x, self.s)
        j = 0 if self.order == "zxy" else zd
        src = self.acc.at[zd, 1 - self.x, self.mine] if self.order == "yxz" else self.acc.at[zd, 1 - self.x]
        return remote(src, self.xbuf.at[j], self.x_send.at[j], self.x_recv.at[j], device)

    def y_copy(self, zd):
        device = (self.dp, (1 - self.y) * 2 + self.c)
        j = 0 if self.order[2] == "y" else zd
        rows = self.some(1 - self.y)
        src = self.acc.at[zd, :, rows] if self.order == "yxz" else self.acc.at[zd, self.x, rows]
        return remote(src, self.ybuf.at[j], self.y_send.at[j], self.y_recv.at[j], device)

    def z_copy(self, k):
        zd = (self.z + k) % Z_CHIPS
        src = self.acc.at[zd, self.x, self.mine]
        if self.order == "zxy":
            src = self.acc.at[zd]
        elif self.order == "xzy":
            src = self.acc.at[zd, self.x]
        return remote(
            src, self.zbuf.at[k - 1], self.z_send.at[k], self.z_recv.at[k], (zd * 2 + self.x, self.s)
        )

    def fin_quarter(self, y, core):
        return self.fin.at[self.some(y), self.cols(core)]

    def fin_copy(self, k):
        device = (self.dp, (1 - self.y) * 2 + self.c) if k == 2 else (self.dp, self.s + 1 - 2 * self.c)
        y = 1 - self.y if k == 3 else self.y
        dst = self.fin_quarter(y, self.c)
        return remote(dst if k == 3 else self.quarter, dst, self.f_send.at[k], self.f_recv.at[k], device)

    def fin_in(self, k):
        ref = self.fin_quarter(self.y if k == 1 else 1 - self.y, self.c if k == 2 else 1 - self.c)
        return remote(self.quarter, ref, self.f_send.at[k], self.f_recv.at[k], (self.dp, self.s))

    def fin_own(self):
        return pltpu.make_async_copy(self.quarter, self.fin_quarter(self.y, self.c), self.local)

    def core_start(self):
        for j in range(self.core_pieces):
            self.core_copy(j).start()

    def core_sent(self):
        for j in range(self.core_pieces):
            self.core_copy(j).wait_send()

    def z_block(self, k):
        zd = (self.z + k) % Z_CHIPS
        self.core_copy(zd).wait_recv()
        for xd in range(2):
            self.acc[zd, xd] = (self.acc[zd, xd].astype(f32) + self.cbuf[zd, xd].astype(f32)).astype(bf16)
        if self.order[0] == "x":
            self.x_copy(zd).start()
        elif k % Z_CHIPS:
            self.z_copy(k % Z_CHIPS).start()

    def core_add(self, j):
        self.core_copy(j).wait_recv()
        if self.order[0] != "y":
            xd = (1 - self.x) if j == 0 else self.x

            def one(zd, carry):
                self.acc[zd, xd] = (self.acc[zd, xd].astype(f32) + self.cbuf[zd, xd].astype(f32)).astype(bf16)
                return carry

        else:
            rows = self.some((1 - self.y) if j == 0 else self.y)

            def one(zd, carry):
                for xd in range(2):
                    self.acc[zd, xd, rows] = (
                        self.acc[zd, xd, rows].astype(f32) + self.cbuf[zd, xd, rows].astype(f32)
                    ).astype(bf16)
                return carry

        lax.fori_loop(0, Z_CHIPS, one, 0)

    def second(self, k):
        zd = (self.z + k + 1) % Z_CHIPS
        if self.order[0] == "x":
            self.x_copy(zd).wait_recv()
            self.acc[zd, self.x] = (self.acc[zd, self.x].astype(f32) + self.xbuf[zd].astype(f32)).astype(bf16)
            if self.order == "xyz":
                self.y_copy(zd).start()
            elif k < 3:
                self.z_copy(k + 1).start()
        else:
            self.y_copy(zd).wait_recv()
            for xd in range(2):
                self.acc[zd, xd, self.mine] = (
                    self.acc[zd, xd, self.mine].astype(f32) + self.ybuf[zd, xd].astype(f32)
                ).astype(bf16)
            self.x_copy(zd).start()

    def third(self, k):
        zd = (self.z + k) % Z_CHIPS
        if self.order == "xyz":
            self.y_copy(zd).wait_recv()
            came = self.ybuf
        else:
            self.x_copy(zd).wait_recv()
            came = self.xbuf
        self.acc[zd, self.x, self.mine] = (
            self.acc[zd, self.x, self.mine].astype(f32) + came[zd].astype(f32)
        ).astype(bf16)
        if k:
            self.z_copy(k).start()

    def publish(self, total):
        self.quarter[...] = total.astype(bf16)
        self.fin_own().start()
        self.fin_copy(1).start()
        self.fin_copy(2).start()

    def stage(self, i):
        if i >= 40:
            self.third((i - 39) % Z_CHIPS)
        elif i >= 30:
            self.second(i - 30)
        elif i == 6:
            self.fin_in(2).wait_recv()
            self.fin_copy(3).start()
        elif i == 7:
            self.fin_own().wait()
            self.fin_in(1).wait_recv()
            self.fin_in(3).wait_recv()
        elif self.order != "zxy":
            if i == 1:
                self.core_add(0)
                for k in range(Z_CHIPS):
                    zd = (self.z + k + 1) % Z_CHIPS
                    (self.x_copy(zd) if self.order[0] == "x" else self.y_copy(zd)).start()
            elif i == 2:
                self.core_add(1)
            elif i == 3:
                for k in range(Z_CHIPS):
                    self.second(k)
            elif i == 4 and self.order == "xzy":
                total = self.acc[self.z, self.x].astype(f32)
                for k in range(1, Z_CHIPS):
                    self.z_copy(k).wait_recv()
                    total = total + self.zbuf[k - 1].astype(f32)
                self.acc[self.z, self.x] = total.astype(bf16)
                self.y_copy(self.z).start()
            elif i == 4:
                for k in (1, 2, 3, 0):
                    self.third(k)
            elif i == 5 and self.order == "xzy":
                self.y_copy(self.z).wait_recv()
                self.publish(self.acc[self.z, self.x, self.mine].astype(f32) + self.ybuf[0].astype(f32))
            elif i == 5:
                total = self.acc[self.z, self.x, self.mine].astype(f32)
                for k in range(1, Z_CHIPS):
                    self.z_copy(k).wait_recv()
                    total = total + self.zbuf[k - 1].astype(f32)
                self.publish(total)
        else:
            if i == 1:
                self.core_add(0)
            elif i == 2:
                self.core_add(1)
                for k in range(1, Z_CHIPS):
                    self.z_copy(k).start()
            elif i == 3:
                for k in range(1, Z_CHIPS):
                    self.z_copy(k).wait_recv()
                for xd in range(2):
                    total = self.acc[self.z, xd].astype(f32)
                    for k in range(1, Z_CHIPS):
                        total = total + self.zbuf[k - 1, xd].astype(f32)
                    self.acc[self.z, xd] = total.astype(bf16)
                self.x_copy(self.z).start()
            elif i == 4:
                self.x_copy(self.z).wait_recv()
                total = self.acc[self.z, self.x].astype(f32) + self.xbuf[0].astype(f32)
                self.acc[self.z, self.x] = total.astype(bf16)
                self.y_copy(self.z).start()
            elif i == 5:
                self.y_copy(self.z).wait_recv()
                self.publish(self.acc[self.z, self.x, self.mine].astype(f32) + self.ybuf[0].astype(f32))

    def settle(self):
        for k in range(1, Z_CHIPS):
            self.z_copy(k).wait_send()
        for k in range(1, 4):
            self.fin_copy(k).wait_send()
        for k in range(1 if self.order == "zxy" else Z_CHIPS):
            self.x_copy((self.z + k) % Z_CHIPS).wait_send()
        for k in range(1 if self.order[2] == "y" else Z_CHIPS):
            self.y_copy((self.z + k) % Z_CHIPS).wait_send()


class Returns:
    def __init__(self, rows_ref, long_out, short_out, send, recv, local, own_rows=None):
        self.rows_ref, self.long_out, self.short_out = rows_ref, long_out, short_out
        self.send, self.recv, self.local = send, recv, local
        self.dp, self.s = lax.axis_index("dp"), lax.axis_index("seq")
        self.own_rows = rows_ref.at[self.s] if own_rows is None else own_rows

    def own(self):
        for j, (first, rows, (_, dst)) in enumerate(zip((0, 128, 192), (128, 64, 64), self.pieces(self.s, self.s))):
            yield pltpu.make_async_copy(self.own_rows.at[pl.ds(first, rows)], dst, self.local.at[j])

    def pieces(self, target, source):
        yield self.rows_ref.at[target, pl.ds(0, 128)], self.long_out.at[source // 2, source % 2]
        yield self.rows_ref.at[target, pl.ds(128, 64)], self.short_out.at[0, source]
        yield self.rows_ref.at[target, pl.ds(192, 64)], self.short_out.at[1, source]

    copies, start, finish, settle = Tokens.copies, Tokens.start, Tokens.finish, Tokens.settle


def sums_window(d):
    return jnp.minimum(d * 96 // 128, 4) * 128


class Sums:
    def __init__(self, src, sbuf, part, dbuf, out, sems):
        self.src, self.sbuf, self.part, self.dbuf, self.out = src, sbuf, part, dbuf, out
        self.s_send, self.s_recv, self.d_send, self.d_recv = sems
        self.dp, self.s = lax.axis_index("dp"), lax.axis_index("seq")

    def s_copy(self, k, source):
        return remote(self.src, self.sbuf.at[source], self.s_send.at[k], self.s_recv.at[k], (self.dp, (self.s + k) % 4))

    def window(self, d):
        return self.part.at[:, pl.ds(pl.multiple_of(sums_window(d), 128), 256)]

    def d_copy(self, k, source):
        target = (self.dp + k) % 8
        return remote(self.window(target), self.dbuf.at[source], self.d_send.at[k], self.d_recv.at[k], (target, self.s))

    def stage(self, i):
        if i == 0:
            for k in range(1, 4):
                self.s_copy(k, self.s).start()
            self.sbuf[self.s] = self.src[...]
        elif i == 1:
            for k in range(1, 4):
                self.s_copy(k, (self.s + 4 - k) % 4).wait_recv()
            self.part[...] = (self.sbuf[0] + self.sbuf[1]) + (self.sbuf[2] + self.sbuf[3])
            for k in range(1, 8):
                self.d_copy(k, self.dp).start()
            self.dbuf[self.dp] = self.window(self.dp)[...]
        elif i == 2:
            for k in range(1, 8):
                self.d_copy(k, (self.dp + 8 - k) % 8).wait_recv()
            total = self.dbuf[0]
            for d in range(1, 8):
                total = total + self.dbuf[d]
            self.out[...] = total

    def settle(self):
        for k in range(1, 4):
            self.s_copy(k, self.s).wait_send()
        for k in range(1, 8):
            self.d_copy(k, self.dp).wait_send()


PIECES = (
    (384, D, "xzy"),
    (192, D, "yxz"),
    (192, D, "xyz"),
    (96, D, "zxy"),
    (96, D, "xzy"),
    (96, D, "xzy"),
    (96, D, "xzy"),
)


MIDDLE_JOBS = {
    0: ((0, 30),),
    1: (),
    2: ((0, 31), (1, 1), (1, 2),),
    3: ((0, 32),),
}
ONE_JOBS = ((1, 30), (2, 1), (2, 2), (1, 31),)
O_JOBS = ((0, 33), (2, 30), (3, 1), (1, 32), (3, 2),)
BEFORE_PAIR = {
    0: (),
    1: (),
    2: ((2, 32), (1, 33),),
    3: ((4, 1),),
    4: ((1, 41), (5, 1),),
    5: ((4, 30), (4, 31), (0, 5), (5, 2),),
}
AFTER_GROUP = (
    ((0, 4), (2, 31),),
    ((1, 40), (4, 2),),
    ((5, 30), (5, 31), (2, 33),),
)
LAST_JOBS = ((6, 1), (6, 2), (4, 32), (5, 32), (6, 30), (2, 40), (3, 3), (2, 41), (4, 33), (3, 4), (2, 42), (5, 33), (2, 43), (4, 4), (1, 42), (6, 31), (1, 43), (5, 4), (0, 6), (6, 32), (1, 5), (5, 5), (6, 33), (3, 5), (4, 5), (6, 4), (5, 6), (2, 5), (6, 5), (4, 6), (3, 6), (1, 6), (2, 6), (6, 6),)


def backward_kernel(*refs):
    refs = list(refs)

    def take(n):
        out = refs[:n]
        del refs[:n]
        return out

    short_len_ref, long_len_ref, vec_ref, sums_in = take(4)
    act_hbm, slope_hbm, y1b_hbm, norm_hbm, inv_hbm, ainv_hbm, dz_hbm, dfb_hbm, att_hbm, qkv_hbm, probs_hbm = take(11)
    tok_hbm, w_hbm, wo_hbm, w1_hbm, w2_hbm, out_rows = take(6)
    fins = take(len(PIECES))
    (sums_out,) = take(1)
    short_out, long_out, short_back, long_back = take(4)
    (theirs_a,) = take(1)
    bufs = [take(6) for _ in PIECES]
    big, dfb_s, y1b_s, att_s, at_s, first_s, second_s, wo_s, dub_s, dh_s, dob_s, inv_s, dqkv_s = take(13)
    sums_s, sbuf, part, dbuf = take(4)
    sems = take(11)
    s_sems = take(4)
    t_send, t_recv, local, load_sem, big_sem, ainv_s, ainv_sem, out_s = take(8)

    dp, s, z, x, y, c = place()
    lens_ref = own_lengths(short_len_ref, long_len_ref)
    greet()
    outs = Returns(out_rows, long_out, short_out, t_send.at[0], t_recv.at[0], local.at[0], out_s)
    backs = Returns(y1b_s, long_back, short_back, t_send.at[1], t_recv.at[1], local.at[1])

    def plan(i, *pairs):
        return [pltpu.make_async_copy(src, dst, load_sem.at[i + j]) for j, (src, dst) in enumerate(pairs)]

    def begin(copies):
        for copy in copies:
            copy.start()
        return copies

    def load(i, *pairs):
        return begin(plan(i, *pairs))

    def done(copies):
        for copy in copies:
            copy.wait()

    def big_copy(src, slot):
        return pltpu.make_async_copy(src, big.at[slot], big_sem.at[slot])

    def act_chunk(k):
        return act_hbm.at[(z + k) % Z_CHIPS]

    def up_chunk(k):
        return jnp.where(k % 2 == 0, 1 - c, c) * 2 + k // 2

    def slope_copy(k, slot):
        rows = pl.ds(pl.multiple_of(up_chunk(k) * 256, 256), 256)
        return pltpu.make_async_copy(slope_hbm.at[:, rows], big.at[slot].reshape(4, 256, D), big_sem.at[slot])

    chunk = lambda i: pl.ds(i * D, D)
    big_copy(act_chunk(1), 1).start()
    load_dfb = load(0, (dfb_hbm, dfb_s))
    load_out = load(12, (out_rows.at[s], out_s))
    load_w2 = plan(1, (w2_hbm, second_s))
    load_w1 = plan(2, *[(w1_hbm.at[:, chunk(k)], first_s.at[chunk(k)]) for k in range(4)])
    load_mid = plan(6, (dz_hbm, dh_s), (norm_hbm, dob_s), (inv_hbm, inv_s), (wo_hbm, wo_s))
    load_y1b = plan(10, (y1b_hbm, y1b_s))
    load_att = plan(11, (att_hbm, att_s))

    pieces = []
    for i, (rows, cols, order) in enumerate(PIECES):
        first = (0, 0, 192, 0, 96, 192, 288)[i]
        theirs = theirs_a.at[:, :, pl.ds(first, rows), :]
        pieces.append(Grad(theirs, *bufs[i], fins[i], [r.at[i] for r in sems], order))
    down, one_a, one_b, o_piece = pieces[:4]
    sums = Sums(sums_s, sbuf, part, dbuf, sums_out, s_sems)
    done(load_out)
    outs.start()

    def run(jobs):
        for index, stage in jobs:
            pieces[index].stage(stage)

    def during(i, plan):
        for when, jobs in plan.items():

            @pl.when(i == when)
            def _():
                run(jobs)

    def columns(core):
        return pl.ds(pl.multiple_of(core * (D // 2), 128), D // 2)

    sums_s[...] = sums_in[...]
    done(load_dfb)

    def down_block(k, carry):
        zd = (z + k) % Z_CHIPS
        slot = k % 2
        big_copy(act_chunk(k), slot).wait()

        @pl.when(k < Z_CHIPS)
        def _():
            big_copy(act_chunk(k + 1), 1 - slot).start()

        @pl.when(k == Z_CHIPS)
        def _():
            slope_copy(0, 1 - slot).start()

        for j, later in ((1, load_w2), (2, load_w1), (3, load_mid), (4, load_y1b + load_att)):

            @pl.when(k == j)
            def _():
                begin(later)

        at_s[...] = jnp.transpose(big[slot])
        theirs_a[zd] = dot_nn(at_s[...], dfb_s[:, :, columns(1 - c)].reshape(1024, D // 2)).astype(bf16).reshape(2, 384, D // 2)
        down.core_copy(zd).start()
        down.acc[zd] = dot_nn(at_s[...], dfb_s[:, :, columns(c)].reshape(1024, D // 2)).astype(bf16).reshape(2, 384, D // 2)
        for j in range(2, Z_CHIPS + 1):

            @pl.when(k == j)
            def _():
                down.z_block(j - 1)

        return carry

    def ainv_copy(r, slot):
        return pltpu.make_async_copy(ainv_hbm.at[r], ainv_s.at[slot], ainv_sem.at[slot])

    lax.fori_loop(1, Z_CHIPS + 1, down_block, 0)
    ainv_copy(0, 0).start()
    done(load_w2)
    done(load_w1)
    done(load_mid)
    row_vec = lambda i: vec_ref[i : i + 1, :]

    def add(index, v):
        sums_s[index : index + 1, :] += jnp.sum(v, axis=0, keepdims=True)

    done(load_y1b)
    at_s[...] = jnp.transpose(y1b_s[...].reshape(1024, D))
    load_tok = load(10, (tok_hbm, y1b_s))

    def up_block(k, carry):
        slot = (k + 1) % 2
        slope_copy(k, slot).wait()

        @pl.when(k < 3)
        def _():
            slope_copy(k + 1, 1 - slot).start()

        @pl.when(k == 0)
        def _():
            down.z_block(Z_CHIPS)
            down.core_sent()

        during(k, MIDDLE_JOBS)
        chunk_rows = pl.ds(pl.multiple_of(up_chunk(k) * D, D), D)

        def up_rows(r, carry):
            slope = big[slot, pl.ds(pl.multiple_of(r * 256, 256), 256)].astype(f32)
            dub = (dot_nt(dfb_s[r], second_s[chunk_rows]) * slope).astype(bf16)
            dub_s[r] = dub
            dh_s[r] += dot_nt(dub, first_s[chunk_rows])
            return carry + jnp.sum(dub.astype(f32), axis=0, keepdims=True)

        hidden_sum = lax.fori_loop(0, 4, up_rows, jnp.zeros((1, D), f32))
        for j in range(4):

            @pl.when(up_chunk(k) == j)
            def _():
                sums_s[8 + j : 9 + j, :] = hidden_sum

        grad = dot_nn(at_s[...], dub_s[...].reshape(1024, D)).astype(bf16)
        for e in range(2):
            half = grad[:, e * (D // 2) : (e + 1) * (D // 2)].reshape(4, 2, 96, D // 2)
            for j, ref in enumerate((one_a.theirs, one_a.acc, one_b.theirs, one_b.acc)):

                @pl.when(k == j)
                def _():
                    ref[:, :, e * 96 : (e + 1) * 96, :] = half

        for j, piece in ((0, one_a), (2, one_b)):

            @pl.when(k == j)
            def _():
                piece.core_start()

        return carry

    lax.fori_loop(0, 4, up_block, 0)
    run(ONE_JOBS)

    def middle_back(r, carry):
        ainv_copy(r, r % 2).wait()

        @pl.when(r < 3)
        def _():
            ainv_copy(r + 1, (r + 1) % 2).start()

        dy1 = dh_s[r]
        normed = dob_s[r].astype(f32)
        add(3, dy1 * normed)
        add(4, dy1)
        dh = layer_norm_back(dy1 * row_vec(3), normed, inv_s[r][:, 0:1])
        dab = dh.astype(bf16)
        dh_s[r] = dh
        dfb_s[r] = dab
        add(2, dab.astype(f32))
        dob_s[r] = (dot_nt(dab, wo_s[...]) * ainv_s[r % 2]).astype(bf16)
        return carry

    lax.fori_loop(0, 4, middle_back, 0)
    one_a.core_sent()
    one_b.core_sent()
    qkv_loads = load(1, *[(qkv_hbm.at[:, :, chunk(j)], first_s.at[pl.ds(j * 1024, 1024)].reshape(4, 256, D)) for j in range(3)])
    w_loads = load(4, *[(w_hbm.at[:, chunk(j)], second_s.at[chunk(j)]) for j in range(3)])

    def probs_copy(i, slot):
        return big_copy(probs_hbm.at[i], slot)

    probs_copy(0, 0).start()

    def small_grad(piece, right):
        piece.theirs[...] = dot_nn(at_s[...], right(1 - c)).astype(bf16).reshape(4, 2, 96, D // 2)
        piece.core_start()
        piece.acc[...] = dot_nn(at_s[...], right(c)).astype(bf16).reshape(4, 2, 96, D // 2)

    done(load_att)
    at_s[...] = jnp.transpose(att_s[...].reshape(1024, D))
    small_grad(o_piece, lambda core: dfb_s[:, :, columns(core)].reshape(1024, D // 2))
    run(O_JOBS)

    done(load_tok)
    at_s[...] = jnp.transpose(y1b_s[...].reshape(1024, D))
    done(qkv_loads)
    done(w_loads)
    pairs = D // PAIR

    for g in range(3):

        def pair(i, carry, g=g):
            during(i, {j: BEFORE_PAIR[j] for j in (2 * g, 2 * g + 1)})
            slot = i % 2
            probs_copy(i, slot).wait()

            @pl.when(i + 1 < pairs)
            def _():
                probs_copy(i + 1, 1 - slot).start()

            lanes = pl.ds(pl.multiple_of(i * PAIR, PAIR), PAIR)
            sum_q = jnp.zeros((1, PAIR), f32)
            sum_v = jnp.zeros((1, PAIR), f32)
            for first, rows, length, index in SEQS:
                q, k, v = [
                    first_s[j * 1024 : (j + 1) * 1024, lanes].reshape(4, 256, PAIR)[:, first : first + rows].reshape(length, PAIR)
                    for j in range(3)
                ]
                do, o = [r[:, first : first + rows, lanes].reshape(length, PAIR) for r in (dob_s, att_s)]

                def kept(h, index=index):
                    if index == 0:
                        return big[slot, h * LONG_L : (h + 1) * LONG_L, 0:LONG_L]
                    row = (2 * h + index - 1) * SHORT_L
                    return big[slot, row : row + SHORT_L, LONG_L : LONG_L + SHORT_L]

                grads = attend_sums_back(q, k, v, do, o, lens_ref[index], kept)
                sum_q = sum_q + jnp.sum(grads[0].astype(f32), axis=0, keepdims=True)
                sum_v = sum_v + jnp.sum(grads[2].astype(f32), axis=0, keepdims=True)
                for j in range(3):
                    dst = pl.ds(pl.multiple_of(j * 256 + (i % 2) * PAIR, PAIR), PAIR)
                    dqkv_s[g, :, first : first + rows, dst] = grads[j].reshape(4, rows, PAIR)
            sums_s[0:1, lanes] = sum_q
            sums_s[1:2, lanes] = sum_v
            return carry

        lax.fori_loop(2 * g, 2 * g + 2, pair, 0)
        small_grad(pieces[4 + g], lambda core, g=g: dqkv_s[g, :, :, columns(core)].reshape(1024, D // 2))
        if g == 2:
            sums.stage(0)
        run(AFTER_GROUP[g])

    def rows_back(i, carry):
        r = (s + 1 + i) % 4
        total = dh_s[r]
        for g in range(3):
            for j in range(3):
                total = total + dot_nt(
                    dqkv_s[g, r, :, j * 256 : (j + 1) * 256], second_s[j * D : (j + 1) * D, g * 256 : (g + 1) * 256]
                )
        y1b_s[r] = total.astype(bf16)
        for k in range(1, 4):

            @pl.when(i == k - 1)
            def _():
                for copy in backs.copies(k):
                    copy.start()

        return carry

    lax.fori_loop(0, 4, rows_back, 0)
    for copy in backs.own():
        copy.start()
    sums.stage(1)
    run(LAST_JOBS)
    sums.stage(2)
    run([(i, 7) for i in range(len(PIECES))])
    outs.finish()
    backs.finish()
    for i, piece in enumerate(pieces):
        if i > 2:
            piece.core_sent()
        piece.settle()
    sums.settle()
    outs.settle()
    backs.settle()


def backward(short_len, long_len, vec, sums, arrays, out_rows):
    any_spec = pl.BlockSpec(memory_space=pl.ANY)
    vmem = pl.BlockSpec(memory_space=pltpu.VMEM)
    smem = pl.BlockSpec(memory_space=pltpu.SMEM)
    shape = jax.ShapeDtypeStruct
    dma = pltpu.SemaphoreType.DMA
    count = len(PIECES)
    vm = lambda dims, t=bf16: pltpu.VMEM(dims, t)
    bufs = []
    for rows, cols, order in PIECES:
        half, cut = cols // 2, rows // 2
        bufs += [vm((4, 2, rows, half)), vm((4, 2, rows, half))]
        bufs += {
            "xyz": [vm((4, rows, half)), vm((4, cut, half)), vm((3, cut, half))],
            "yxz": [vm((4, cut, half)), vm((4, 2, cut, half)), vm((3, cut, half))],
            "xzy": [vm((4, rows, half)), vm((1, cut, half)), vm((3, rows, half))],
            "zxy": [vm((1, rows, half)), vm((1, cut, half)), vm((3, 2, rows, half))],
        }[order]
        bufs.append(vm((cut, half)))
    tok = (4, 256, D)
    return pl.pallas_call(
        backward_kernel,
        in_specs=[smem, smem, vmem, vmem] + [any_spec] * (len(arrays) + 1),
        out_specs=[any_spec] * count + [vmem] + [any_spec] * 4,
        out_shape=[shape((rows, cols), bf16) for rows, cols, _ in PIECES]
        + [
            shape((16, 256), f32),
            shape((2, 4, 64, D), bf16),
            shape((2, 2, 128, D), bf16),
            shape((2, 4, 64, D), bf16),
            shape((2, 2, 128, D), bf16),
        ],
        scratch_shapes=[vm((4, 2, 384, D // 2))]
        + bufs
        + [
            vm((2, 1024, D)),
            vm(tok),
            vm(tok),
            vm(tok),
            vm((D, 1024)),
            vm((FF, D)),
            vm((FF, D)),
            vm((D, D)),
            vm(tok),
            vm(tok, f32),
            vm(tok),
            vm((4, 256, 128), f32),
            vm((3, 4, 256, D)),
            vm((16, D), f32),
            vm((4, 16, D), f32),
            vm((16, D), f32),
            vm((8, 16, 256), f32),
        ]
        + [dma((count, 4))] * 10
        + [dma((count,))]
        + [dma((4,)), dma((4,)), dma((8,)), dma((8,))]
        + [dma((2, 4, 3)), dma((2, 4, 3)), dma((2, 3)), dma((13,)), dma((2,)), vm((2, 256, D), f32), dma((2,)), vm((256, D))],
        compiler_params=pltpu.CompilerParams(
            vmem_limit_bytes=VMEM_BYTES, collective_id=1, has_side_effects=True
        ),
        name="backward",
    )(short_len, long_len, vec, sums, *arrays, out_rows)


def transpose_dot(left, right):
    return jnp.einsum("ra,rb->ab", left, right, preferred_element_type=f32)


def right_dot(left, right):
    return jnp.einsum("ra,ba->rb", left, right, preferred_element_type=f32)


def flip(v, axis, bit):
    n = lax.axis_size(axis)
    return lax.ppermute(v, axis, [(i, i ^ bit) for i in range(n)])


def half_of(v, dim, which):
    size = v.shape[dim] // 2
    return lax.dynamic_slice_in_dim(v, which * size, size, dim)


def halve(v, axis, bit, dim):
    mine = (lax.axis_index(axis) // bit) % 2
    other = flip(half_of(v, dim, 1 - mine), axis, bit)
    return (half_of(v, dim, mine).astype(f32) + other.astype(f32)).astype(bf16)


def double(v, axis, bit, dim):
    mine = (lax.axis_index(axis) // bit) % 2
    other = flip(v, axis, bit)
    return jnp.where(
        mine == 0, jnp.concatenate([v, other], axis=dim), jnp.concatenate([other, v], axis=dim)
    )


def reduce_rows(grad):
    rows, cols = grad.shape
    dp = lax.axis_size("dp")
    v = grad.reshape(dp, rows // dp, cols)
    v = halve(v, "seq", 1, 2)
    v = halve(v, "seq", 2, 2)
    bit = 1
    while bit < dp:
        blocks = v.shape[0]
        v = v.reshape(blocks // 2, 2, v.shape[1], v.shape[2]) if v.ndim == 3 else v
        v = halve(v, "dp", bit, 1)[:, 0]
        bit *= 2
    v = v[0]
    v = double(v, "seq", 2, 1)
    v = double(v, "seq", 1, 1)
    return v.astype(f32)


def update(master, reduced_grad, moment, average):
    step_grad = reduced_grad + decay_weight * master
    velocity = momentum_rate * moment + step_grad
    updated = master - learning_rate * (step_grad + momentum_rate * velocity)
    averaged = average_rate * average + (1.0 - average_rate) * updated
    return (velocity, averaged, updated, updated.astype(jnp.bfloat16))


UPDATE_STEPS = 4


def update_kernel(*refs):
    refs = list(refs)

    def take(n):
        out = refs[:n]
        del refs[:n]
        return out

    down_low, one_a, one_b, o_low, low_0, low_1, low_2 = take(7)
    wide_state, down_state, passed = take(3), take(3), take(4)
    wide_out, down_out, passed_out = take(5), take(5), take(4)
    (grad_s,) = take(1)
    i = pl.program_id(0)
    for src, dst in zip(passed, passed_out):
        dst[...] = src[...]
    half, width = D // 2, grad_s.shape[1] // D
    for b in range(UPDATE_STEPS * width):
        first = b % width * D

        @pl.when(i == b // width)
        def _():
            if b < 3:
                for g, low in enumerate((low_0, low_1, low_2)):
                    grad_s[:, first + g * 256 : first + (g + 1) * 256] = low[:, b * 256 : (b + 1) * 256]
            elif b == 3:
                grad_s[:, first : first + D] = o_low[...]
            else:
                rows, core = grad_s.shape[0], (b - 4) // 2
                low = (one_a, one_b)[b % 2]
                for k in range(2):
                    part = low[k * rows : (k + 1) * rows, core * half : (core + 1) * half]
                    grad_s[:, first + k * half : first + (k + 1) * half] = part

    def step(grad, state, outs):
        master, moment, average = state
        outs[0][...] = grad
        for ref, v in zip(outs[1:], update(master[...], grad, moment[...], average[...])):
            ref[...] = v

    step(grad_s[...].astype(f32), wide_state, wide_out)
    rows = down_state[0].shape[0]
    step(down_low[pl.ds(pl.multiple_of(i * rows, 16), rows)].astype(f32), down_state, down_out)


def update_all(lows, wide, down, passed):
    rows, cols = wide[0].shape
    down_rows = down[0].shape[0]
    vmem = pl.BlockSpec(memory_space=pltpu.VMEM)
    halves = UPDATE_STEPS // 2
    short_spec = pl.BlockSpec((1, 4 // halves, 64, D), lambda i: (i // halves, i % halves, 0, 0))
    long_spec = pl.BlockSpec((1, 2 // halves, 128, D), lambda i: (i // halves, i % halves, 0, 0))
    passed_specs = [short_spec, long_spec, short_spec, long_spec]
    shape = jax.ShapeDtypeStruct
    wide_spec = pl.BlockSpec((rows, cols // UPDATE_STEPS), lambda i: (0, i))
    down_spec = pl.BlockSpec((down_rows // UPDATE_STEPS, D), lambda i: (i, 0))
    types = (f32, f32, f32, f32, bf16)
    return pl.pallas_call(
        update_kernel,
        grid=(UPDATE_STEPS,),
        in_specs=[vmem] * len(lows) + [wide_spec] * 3 + [down_spec] * 3 + passed_specs,
        out_specs=[wide_spec] * 5 + [down_spec] * 5 + passed_specs,
        out_shape=[shape((rows, cols), t) for t in types]
        + [shape((down_rows, D), t) for t in types]
        + [shape(p.shape, p.dtype) for p in passed],
        scratch_shapes=[pltpu.VMEM((rows, cols // UPDATE_STEPS), bf16)],
        compiler_params=params(),
        name="update",
    )(*lows, *wide, *down, *passed)


def spread_rows(long_part, short_part):
    long_blocks = long_part.reshape(4, 128, D)
    short_blocks = jnp.transpose(short_part, (1, 0, 2, 3)).reshape(4, 128, D)
    return jnp.concatenate([long_blocks, short_blocks], axis=1)


def exchange(v):
    return lax.all_to_all(v, "seq", split_axis=0, concat_axis=0, tiled=True)


def collect_rows(v):
    long_part = v[:, :128].reshape(2, 2, 128, D)
    short_part = jnp.transpose(v[:, 128:].reshape(4, 2, 64, D), (1, 0, 2, 3))
    return short_part, long_part


def body(
    short_in,
    long_in,
    short_cot,
    long_cot,
    short_len,
    long_len,
    wide_master,
    down_master,
    vector_master,
    wide_moment,
    down_moment,
    vector_moment,
    wide_average,
    down_average,
    vector_average,
):
    s = lax.axis_index("seq")
    own_rows = vector_master.shape[0]
    if lax.axis_size("dp") == 8:
        vec_own = jnp.pad(jnp.transpose(vector_master).astype(bf16), ((0, 4), (0, 0)))
        vec_block = lax.dynamic_update_slice(
            jnp.zeros((16, D), bf16), vec_own, (0, lax.axis_index("dp") * own_rows)
        )
        (w_qkv, w_o, w_1, w_2, tokens, qkv, attended, probs, act, slope, y1b, norm, inv, dz, dfb, out, att_inv, vec, sums) = forward(
            short_len, long_len, wide_master, down_master, vec_block, long_in, short_in, long_cot, short_cot
        )
        w_qkv, w_o, w_1, w_2 = [w.reshape(-1, w.shape[2]) for w in (w_qkv, w_o, w_1, w_2)]
        arrays = (act, slope, y1b, norm, inv, att_inv, dz, dfb, attended, qkv, probs, tokens, w_qkv, w_o, w_1, w_2)
        *lows, sums_own, short_out, long_out, short_back, long_back = backward(
            short_len, long_len, vec, sums, arrays, out
        )
        index = lax.axis_index("dp")
        own_sums = lax.dynamic_slice(sums_own, (0, index * own_rows - sums_window(index)), (12, own_rows))
        vector_reduced = jnp.transpose(own_sums)
        results = update_all(
            lows,
            (wide_master, wide_moment, wide_average),
            (down_master, down_moment, down_average),
            (short_out, long_out, short_back, long_back),
        )
        wide_reduced, *wide_new = results[:5]
        down_reduced, *down_new = results[5:10]
        short_out, long_out, short_back, long_back = results[10:]
    else:
        lens = jnp.stack([long_len[s // 2, 0, s % 2], short_len[0, 0, s], short_len[1, 0, s]])
        tokens = exchange(spread_rows(long_in, short_in))
        cotangent = exchange(spread_rows(long_cot, short_cot))
        wide_w = lax.all_gather(wide_master.astype(bf16), "dp", axis=0, tiled=True)
        w_2 = lax.all_gather(down_master.astype(bf16), "dp", axis=0, tiled=True)
        vector_w = lax.all_gather(vector_master.astype(bf16), "dp", axis=0, tiled=True)
        vec = jnp.transpose(vector_w.astype(f32))
        w_qkv = wide_w[:, : 3 * D]
        w_o = wide_w[:, 3 * D : 4 * D]
        w_1 = wide_w[:, 4 * D :]
        rows = tokens.reshape(1024, D)
        proj_bias = jnp.concatenate([vec[0], jnp.zeros((D,), f32), vec[1]])
        qkv = (jnp.dot(rows, w_qkv, preferred_element_type=f32) + proj_bias).astype(bf16)
        qkv = qkv.reshape(4, 256, 3 * D)
        attended, long_probs, short_probs = attn_forward(lens, qkv)
        flat_attended = attended.reshape(1024, D)
        out, y1b, act, dfb, dub, dab, dob, dh, sums = middle(
            lens, flat_attended, rows, cotangent.reshape(1024, D), w_o, w_1, w_2, vec
        )
        d_down = transpose_dot(act, dfb).astype(bf16)
        d_one = transpose_dot(y1b, dub).astype(bf16)
        d_o = transpose_dot(flat_attended, dab).astype(bf16)
        dq, dk, dv, qv_sums = attn_backward(
            lens, qkv, dob.reshape(4, 256, D), attended, long_probs, short_probs
        )
        d_qkv = jnp.concatenate([dq, dk, dv], axis=2).reshape(1024, 3 * D)
        d_wqkv = transpose_dot(rows, d_qkv).astype(bf16)
        back = (dh + right_dot(d_qkv, w_qkv)).astype(bf16).reshape(4, 256, D)
        vector_total = jnp.concatenate([qv_sums[:2], sums[2:12]], axis=0)
        vector_sum = jnp.transpose(lax.psum(vector_total, ("dp", "seq")))
        vector_reduced = lax.dynamic_slice_in_dim(vector_sum, lax.axis_index("dp") * own_rows, own_rows, 0)
        wide_reduced = jnp.concatenate([reduce_rows(d_wqkv), reduce_rows(d_o), reduce_rows(d_one)], axis=1)
        down_reduced = reduce_rows(d_down)
        short_out, long_out = collect_rows(exchange(out.reshape(4, 256, D)))
        short_back, long_back = collect_rows(exchange(back))
        wide_new = update(wide_master, wide_reduced, wide_moment, wide_average)
        down_new = update(down_master, down_reduced, down_moment, down_average)
    vector_new = update(vector_master, vector_reduced, vector_moment, vector_average)
    return (
        short_out,
        long_out,
        short_back,
        long_back,
        wide_reduced,
        down_reduced,
        vector_reduced,
        wide_new[0],
        down_new[0],
        vector_new[0],
        wide_new[1],
        down_new[1],
        vector_new[1],
        wide_new[2],
        down_new[2],
        vector_new[2],
        wide_new[3],
        down_new[3],
        vector_new[3],
    )


def solution(mesh):
    tok = P(None, "dp", "seq", None)
    lengths = P(None, "dp", None)
    state = P("dp", None)
    return jax.shard_map(
        body,
        mesh=mesh,
        in_specs=(tok,) * 4 + (lengths,) * 2 + (state,) * 9,
        out_specs=(tok,) * 4 + (state,) * 15,
        check_vma=False,
    )
```
